32 devices in a mesh: fsdp: 32 (over z, y, x, core).
Axes of the slice: x: 2, y: 2, z: 4, core: 2. Of those that a mesh axis runs over, the one named last changes fastest.
Arguments:
- layer_input: bfloat16 [4096, 1536], P('fsdp'), may hold values from -6 to 6
- cotangent: bfloat16 [4096, 1536], P('fsdp'), may hold values from -6 to 6
- sequence_ids: int32 [4096], P('fsdp'), may hold values from 0 to 3, as said below
- expert_ids: int32 [4096, 8], P('fsdp'), may hold values from 0 to 39, all different within a row; in each aligned block of 128 rows (0 to 127, 128 to 255, ...) at most 32 rows name the same one
- attention_gain: bfloat16 [1536], P('fsdp'), may hold values from 0.5 to 1.5
- qkv_weight: bfloat16 [1536, 2560], P('fsdp'), may hold values from -2 to 2
- output_weight: bfloat16 [1536, 1536], P('fsdp'), may hold values from -3.59375 to 3.59375
- moe_gain: bfloat16 [1536], P('fsdp'), may hold values from 0.5 to 1.5
- router: bfloat16 [1536, 40], P('fsdp'), may hold values from -1 to 1
- gate_up: bfloat16 [1536, 40, 1024], P('fsdp'), may hold values from -0.15625 to 0.15625
- down_proj: bfloat16 [1536, 40, 512], P('fsdp'), may hold values from -24 to 24
Outputs:
- layer_output: bfloat16 [4096, 1536], P('fsdp')
- input_grad: bfloat16 [4096, 1536], P('fsdp')
- attention_gain_grad: float32 [1536], P('fsdp')
- qkv_weight_grad: float32 [1536, 2560], P('fsdp')
- output_weight_grad: float32 [1536, 1536], P('fsdp')
- moe_gain_grad: float32 [1536], P('fsdp')
- router_grad: float32 [1536, 40], P('fsdp')
- gate_up_grad: float32 [1536, 40, 1024], P('fsdp')
- down_grad: float32 [1536, 40, 512], P('fsdp')
The draws below stay inside these ranges and needn't reach their ends.
Inputs may be any that keep to these rules, and one draw needn't show every extreme that they name: `sequence_ids`: along one device's 128 tokens the numbers never fall; a run of equal numbers is one sequence; some device holds a single sequence of 128 tokens. `expert_ids`: among the 128 rows of one device no expert is named by more than 32 rows.
All inputs are finite; a program needn't handle non-finite values.
Results may differ from the reference program's by a relative error of at most 0.014.
Values may be sent and summed in bfloat16 or wider, within the bound.
A program may use at most 448 MiB of HBM per device.

```python
import math
import jax
import jax.numpy as jnp
import numpy as np
from jax import lax

MODEL_WIDTH = 1536
QUERY_HEADS = 24
KEY_VALUE_HEADS = 8
HEAD_WIDTH = 64
E = 40
F = 512
TOP = 8
TOK_DEV = 128
CAP = 32
TOKENS = 4096


def draw_sequence_ids(key, part):
    devices = TOKENS // TOK_DEV
    grain = max(TOK_DEV // 8, 1)
    cut_points = grain * jax.random.randint(jax.random.fold_in(key, 1), (devices, 3), 1, TOK_DEV // grain)
    kept_cuts = jax.random.randint(jax.random.fold_in(key, 2), (devices, 3), 0, 2)
    single_device = jax.random.randint(jax.random.fold_in(key, 3), (), 0, devices)
    device_rows = jnp.arange(devices, dtype=jnp.int32)[:, None]
    kept_cuts = jnp.where(device_rows == single_device, 0, kept_cuts)
    kept_cuts = jnp.where(device_rows == (single_device + 1) % devices, 1, kept_cuts)
    token_index = jnp.arange(TOK_DEV, dtype=jnp.int32)
    handed_along = (token_index[None, :, None] >= cut_points[:, None, :]).astype(jnp.int32)
    numbers = jnp.sum(kept_cuts[:, None, :] * handed_along, axis=-1)
    return numbers.reshape(devices * TOK_DEV).astype(jnp.int32)


def unit_sample(key, shape, spread_limit):
    return jnp.clip(jax.random.normal(key, shape, jnp.float32), -spread_limit, spread_limit)


def draw_qkv_weight(key, part):
    key = jax.random.fold_in(key, 11)
    query_feature_width = QUERY_HEADS * HEAD_WIDTH
    key_feature_width = KEY_VALUE_HEADS * HEAD_WIDTH
    normal_sample_base = unit_sample(key, (MODEL_WIDTH, query_feature_width + 2 * key_feature_width), 5.0)
    width_square_root = math.sqrt(MODEL_WIDTH)
    query_slice = normal_sample_base[:, :query_feature_width] * (3.0 / width_square_root)
    key_part = normal_sample_base[:, query_feature_width:query_feature_width + key_feature_width] * (3.0 / width_square_root)
    value_part = normal_sample_base[:, query_feature_width + key_feature_width:] * (1.0 / width_square_root)
    return jnp.concatenate([query_slice, key_part, value_part], axis=1).astype(jnp.bfloat16)


def draw_router(key, part):
    key = jax.random.fold_in(key, 13)
    normal_sample_base = unit_sample(key, (MODEL_WIDTH, E), 5.0)
    return (normal_sample_base * (0.5 / math.sqrt(MODEL_WIDTH))).astype(jnp.bfloat16)


def raised(result, own_key, source, target, shards_of, factor):
    owner, partner = [(jnp.arange(result.shape[dim]) // (result.shape[dim] // shards_of)).reshape([-1 if axis == dim else 1 for axis in range(result.ndim)]) for dim in (source, target)]
    chosen = jax.random.permutation(own_key, shards_of)[partner]
    strong = (owner == chosen) | (owner == (partner + shards_of // 2) % shards_of)
    return jnp.where(strong, factor * result, result)


def shard_levels(stream_key, dims, split, low, high):
    gain = 1.0
    for dim, parts in split:
        steps = jax.random.uniform(jax.random.fold_in(jax.random.fold_in(stream_key, 6), dim), (parts,), jnp.float32, low / len(split), high / len(split))
        gain = gain * jnp.repeat(jnp.exp(steps), dims[dim] // parts).reshape((-1,) + (1,) * (len(dims) - 1 - dim))
    return gain


def shared_out(own_key, own, number, rows, count, top, limit, slope):
    sequence = jax.random.permutation(own_key, count)
    heavy_load, usual = shares(count, rows * top, limit, slope, True), shares(count, rows * top, limit, slope, False)
    places = jnp.arange(count)

    def named(sizes, rotation):
        used = int((sizes > 0).sum())
        fixed = max(1, used // 4)
        passed = fixed + (places - fixed + rotation * (used - fixed)) % max(1, count - fixed)
        return jnp.zeros((count,), jnp.int32).at[sequence[jnp.where(places < fixed, places, passed)]].set(jnp.asarray(sizes, jnp.int32))

    sizes = jnp.where(number % 4 == 0, named(heavy_load, number // 4), named(usual, number - number // 4 - 1))
    mixed = jax.random.permutation(jax.random.fold_in(own, 3), count)
    giver, taker = mixed[0:count // 2 * 2:2], mixed[1:count // 2 * 2:2]
    slack = jnp.minimum(sizes[giver] - 1, limit - sizes[taker]) // 2
    slack = jnp.where((giver == sequence[0]) | (taker == sequence[0]) | (sizes[taker] == 0), 0, jnp.maximum(slack, 0))
    passed = jax.random.randint(jax.random.fold_in(own, 4), (count // 2,), 0, 1 << 20) % (slack + 1)
    sizes = sizes.at[giver].add(-passed).at[taker].add(passed)
    labels = jnp.searchsorted(jnp.cumsum(sizes), jnp.arange(rows * top), side="right").astype(jnp.int32)
    grid = labels.reshape(top, rows).T
    grid = grid[jax.random.permutation(jax.random.fold_in(own, 1), rows)]
    rotation = jax.random.randint(jax.random.fold_in(own, 2), (rows, 1), 0, top)
    return jnp.take_along_axis(grid, (jnp.arange(top)[None, :] + rotation) % top, axis=1)


def shares(amount, total, bound, skew, full):
    portions = [(1 << 20) // math.isqrt(grade ** skew) + 1 for grade in range(1, amount + 1)]
    largest = bound if full else min(bound, max(-(-total // amount), total * portions[0] // sum(portions)))
    least = 1 if total - largest >= amount - 1 else 0
    holding, surplus = [largest] + [least] * (amount - 1), total - largest - least * (amount - 1)
    while surplus > 0:
        movable = [i for i in range(1, amount) if holding[i] < largest] or [i for i in range(1, amount) if holding[i] < bound]
        whole, left = sum([portions[i] for i in movable]), surplus
        for i in movable:
            addition = min(bound - holding[i], max(1, left * portions[i] // whole), surplus)
            holding[i] = holding[i] + addition
            surplus = surplus - addition
    return np.array(holding)


def noise(stream_key, dims, scale, bound, cuts=(), kind=jnp.bfloat16):
    loudness = shard_levels(stream_key, dims, cuts, -0.22, 0.18) if cuts else 1.0
    values = jax.random.normal(stream_key, dims, jnp.float32) * scale * loudness
    return jnp.minimum(jnp.maximum(values, -bound), bound).astype(kind)


def noise_with(rng, extent, spread, limit, shards, heavy, held_as=jnp.bfloat16):
    result = spread * jax.random.normal(rng, extent, jnp.float32)
    if shards:
        result = result * shard_levels(rng, extent, shards, -0.22, 0.18)
    return jnp.clip(raised(result, jax.random.fold_in(rng, 3), *heavy), -limit, limit).astype(held_as)


def setup_inputs(seed: int = 0) -> dict:
    key_list = jax.random.split(jax.random.key(seed), 12)
    layer_input = noise_with(key_list[0], (TOKENS, MODEL_WIDTH), 1.0, 6.0, ((0, 32),), (0, 1, 32, 2.75))
    cotangent = noise(key_list[1], (TOKENS, MODEL_WIDTH), 1.0, 6.0, ((0, 32),))
    sequence_ids = draw_sequence_ids(jax.random.fold_in(key_list[11], 71), 0)
    expert_ids_keys = jax.random.split(jax.random.fold_in(key_list[3], 1), TOKENS // TOK_DEV)
    expert_ids_turns = jax.random.permutation(jax.random.fold_in(key_list[3], 3), TOKENS // TOK_DEV)
    expert_ids = jax.vmap(lambda own, number: shared_out(jax.random.fold_in(key_list[3], 2), own, number, TOK_DEV, E, TOP, CAP, 1))(expert_ids_keys, expert_ids_turns).reshape((TOKENS, TOP))
    attention_gain = jnp.clip(1.0 + 0.1 * jax.random.normal(key_list[4], (MODEL_WIDTH,), jnp.float32), 0.5, 1.5).astype(jnp.bfloat16)
    qkv_weight = draw_qkv_weight(jax.random.fold_in(key_list[11], 71), 0)
    output_weight = noise(key_list[6], (QUERY_HEADS * HEAD_WIDTH, MODEL_WIDTH), 0.6, 3.59375, ((0, 32),))
    moe_gain = jnp.clip(1.0 + 0.1 * jax.random.normal(key_list[7], (MODEL_WIDTH,), jnp.float32), 0.5, 1.5).astype(jnp.bfloat16)
    router = draw_router(jax.random.fold_in(key_list[11], 71), 0)
    gate_up = noise(key_list[9], (MODEL_WIDTH, E, 2 * F), MODEL_WIDTH ** -0.5, 0.15625, ((0, 32),))
    down_proj = noise(key_list[10], (MODEL_WIDTH, E, F), 4.0, 24.0, ((0, 32),))
    return {"layer_input": layer_input, "cotangent": cotangent, "sequence_ids": sequence_ids, "expert_ids": expert_ids, "attention_gain": attention_gain, "qkv_weight": qkv_weight, "output_weight": output_weight, "moe_gain": moe_gain, "router": router, "gate_up": gate_up, "down_proj": down_proj}


EPSILON = 1e-06
ATTN_SCALE = 0.015625
RESIDUAL_SCALE = 0.22
ROPE_BASE = 10000.0
PRECISE_ARITHMETIC = lax.Precision.HIGHEST

def convert_halfprecision(value):
    return lax.optimization_barrier(value.astype(jnp.bfloat16))

def positions(sequence_ids):
    sequence_length = sequence_ids.shape[0]
    places = jnp.arange(sequence_length, dtype=jnp.int32)
    starts_new = jnp.concatenate([jnp.ones((1,), jnp.bool_), sequence_ids[1:] != sequence_ids[:-1]])
    begins = lax.cummax(jnp.where(starts_new, places, 0), axis=0)
    return (places - begins).astype(jnp.int32)

def rope_tables(places, head_size):
    half_size = head_size // 2
    exponents = jnp.arange(half_size, dtype=jnp.float32) * (2.0 / head_size)
    inverse = jnp.exp(exponents * -math.log(ROPE_BASE))
    angles = places.astype(jnp.float32)[:, None] * inverse[None, :]
    return (jnp.cos(angles), jnp.sin(angles))

def apply_rotary(tensor, cosine_lookup, sine_lookup):
    half_size = tensor.shape[-1] // 2
    first_half = tensor[..., :half_size]
    second_half = tensor[..., half_size:]
    cosine_rows = cosine_lookup[:, None, :]
    sine_rows = sine_lookup[:, None, :]
    return jnp.concatenate([first_half * cosine_rows - second_half * sine_rows, second_half * cosine_rows + first_half * sine_rows], axis=-1)

def rotate_back(tensor, cosine_lookup, sine_lookup):
    half_size = tensor.shape[-1] // 2
    first_half = tensor[..., :half_size]
    second_half = tensor[..., half_size:]
    cosine_rows = cosine_lookup[:, None, :]
    sine_rows = sine_lookup[:, None, :]
    return jnp.concatenate([first_half * cosine_rows + second_half * sine_rows, second_half * cosine_rows - first_half * sine_rows], axis=-1)

def norm_scale(hidden_state):
    return lax.rsqrt(lax.optimization_barrier(jnp.mean(hidden_state * hidden_state, axis=-1, keepdims=True)) + EPSILON)

def norm_back(hidden_state, gain_vector, scale_rows, upstream):
    weighted = upstream * gain_vector.astype(jnp.float32)
    inner_mean = lax.optimization_barrier(jnp.mean(weighted * hidden_state, axis=-1, keepdims=True))
    grad_hidden = scale_rows * weighted - hidden_state * scale_rows ** 3 * inner_mean
    grad_gain = lax.optimization_barrier(jnp.sum(upstream * hidden_state * scale_rows, axis=0))
    return (grad_hidden, grad_gain)

def expert_slots(expert_ids, experts, capacity):
    flat_ids = expert_ids.reshape(-1).astype(jnp.int32)
    onehot = (flat_ids[:, None] == jnp.arange(experts, dtype=jnp.int32)[None, :]).astype(jnp.int32)
    running = jnp.cumsum(onehot, axis=0, dtype=jnp.int32)
    ranks = lax.optimization_barrier(jnp.sum((running - 1) * onehot, axis=-1, dtype=jnp.int32))
    return (flat_ids * capacity + ranks).astype(jnp.int32)

def device_layer(weights, device_block):
    gain_one, qkv_full, out_full, gain_two, router_full, gate_up_gathered, down_wide = weights
    layer_input, cotangent, sequence_ids, expert_ids = device_block
    sequence_length = layer_input.shape[0]
    query_group_count = QUERY_HEADS // KEY_VALUE_HEADS
    query_feature_width = QUERY_HEADS * HEAD_WIDTH
    key_feature_width = KEY_VALUE_HEADS * HEAD_WIDTH
    inputs = layer_input.astype(jnp.float32)
    scale_one = norm_scale(inputs)
    normed_one = convert_halfprecision(inputs * scale_one * gain_one.astype(jnp.float32))
    joined_projection = jnp.dot(normed_one, qkv_full, preferred_element_type=jnp.float32)
    places = positions(sequence_ids)
    cosine_lookup, sine_lookup = rope_tables(places, HEAD_WIDTH)
    query_rows = convert_halfprecision(apply_rotary(joined_projection[:, :query_feature_width].reshape(sequence_length, QUERY_HEADS, HEAD_WIDTH), cosine_lookup, sine_lookup))
    rotated_keys = convert_halfprecision(apply_rotary(joined_projection[:, query_feature_width:query_feature_width + key_feature_width].reshape(sequence_length, KEY_VALUE_HEADS, HEAD_WIDTH), cosine_lookup, sine_lookup))
    value_inputs = convert_halfprecision(joined_projection[:, query_feature_width + key_feature_width:].reshape(sequence_length, KEY_VALUE_HEADS, HEAD_WIDTH))
    query_gathered = query_rows.astype(jnp.float32).reshape(sequence_length, KEY_VALUE_HEADS, query_group_count, HEAD_WIDTH)
    keys_wide = rotated_keys.astype(jnp.float32)
    values_wide = value_inputs.astype(jnp.float32)
    token_index = jnp.arange(sequence_length, dtype=jnp.int32)
    allowed = (sequence_ids[:, None] == sequence_ids[None, :]) & (token_index[None, :] <= token_index[:, None])
    scores = jnp.einsum('qkgd,tkd->kgqt', query_gathered, keys_wide, precision=PRECISE_ARITHMETIC) * ATTN_SCALE
    scores = jnp.where(allowed, scores, -jnp.inf)
    row_peak = lax.optimization_barrier(jnp.max(scores, axis=-1, keepdims=True))
    log_total = row_peak + jnp.log(lax.optimization_barrier(jnp.sum(jnp.exp(scores - row_peak), axis=-1, keepdims=True)))
    attn_probs = jnp.exp(scores - log_total)
    probs_half = convert_halfprecision(attn_probs).astype(jnp.float32)
    attention_output = convert_halfprecision(jnp.einsum('kgqt,tkd->qkgd', probs_half, values_wide, precision=PRECISE_ARITHMETIC).reshape(sequence_length, query_feature_width))
    branch = jnp.dot(attention_output, out_full, preferred_element_type=jnp.float32)
    middle = inputs + RESIDUAL_SCALE * branch
    scale_two = norm_scale(middle)
    normed_two = convert_halfprecision(middle * scale_two * gain_two.astype(jnp.float32))
    logits = jnp.dot(normed_two, router_full, preferred_element_type=jnp.float32)
    gate_probs = jax.nn.softmax(logits, axis=-1)
    picked = (expert_ids[:, :, None] == jnp.arange(E, dtype=jnp.int32)[None, None, :]).astype(jnp.float32)
    route_weight = jnp.einsum('tke,te->tk', picked, gate_probs, precision=PRECISE_ARITHMETIC)
    slot_rows = expert_slots(expert_ids, E, CAP)
    received_storage = jnp.zeros((E * CAP, MODEL_WIDTH), jnp.bfloat16).at[slot_rows].set(jnp.repeat(normed_two, TOP, axis=0)).reshape(E, CAP, MODEL_WIDTH)
    collected_storage = received_storage.astype(jnp.float32)
    gate_up_preactivation = jnp.einsum('anu,uax->anx', collected_storage, gate_up_gathered, precision=PRECISE_ARITHMETIC)
    gate_pre = gate_up_preactivation[..., :F]
    up_pre = gate_up_preactivation[..., F:]
    sigmoid_gate = jax.nn.sigmoid(gate_pre)
    activated = convert_halfprecision(gate_pre * sigmoid_gate * up_pre).astype(jnp.float32)
    buffer_out = jnp.einsum('ecf,def->ecd', activated, down_wide, precision=PRECISE_ARITHMETIC)
    routed_out = buffer_out.reshape(E * CAP, MODEL_WIDTH)[slot_rows].reshape(sequence_length, TOP, MODEL_WIDTH).astype(jnp.float32)
    combined = jnp.einsum('tk,tkd->td', route_weight, routed_out, precision=PRECISE_ARITHMETIC)
    layer_output = (middle + RESIDUAL_SCALE * combined).astype(jnp.bfloat16)
    upstream = cotangent.astype(jnp.float32)
    grad_mix = RESIDUAL_SCALE * upstream
    grad_weight = jnp.einsum('td,tkd->tk', grad_mix, routed_out, precision=PRECISE_ARITHMETIC)
    grad_rows = convert_halfprecision(route_weight[:, :, None] * grad_mix[:, None, :]).reshape(sequence_length * TOP, MODEL_WIDTH)
    buffer_grad = jnp.zeros((E * CAP, MODEL_WIDTH), jnp.bfloat16).at[slot_rows].set(grad_rows).reshape(E, CAP, MODEL_WIDTH).astype(jnp.float32)
    grad_act = jnp.einsum('ecd,def->ecf', buffer_grad, down_wide, precision=PRECISE_ARITHMETIC)
    down_part = jnp.einsum('ecd,ecf->def', buffer_grad, activated, precision=PRECISE_ARITHMETIC)
    silu_gate = gate_pre * sigmoid_gate
    grad_gate = grad_act * up_pre * sigmoid_gate * (1.0 + gate_pre * (1.0 - sigmoid_gate))
    grad_up = grad_act * silu_gate
    expansion_matrix_derivative = convert_halfprecision(jnp.concatenate([grad_gate, grad_up], axis=-1)).astype(jnp.float32)
    expansion_matrix_portion = jnp.einsum('ftb,ftw->bfw', collected_storage, expansion_matrix_derivative, precision=PRECISE_ARITHMETIC)
    backward_buffer = jnp.einsum('qys,hqs->qyh', expansion_matrix_derivative, gate_up_gathered, precision=PRECISE_ARITHMETIC)
    grad_normed = lax.optimization_barrier(jnp.sum(backward_buffer.reshape(E * CAP, MODEL_WIDTH)[slot_rows].reshape(sequence_length, TOP, MODEL_WIDTH), axis=1))
    grad_gates = jnp.einsum('tk,tke->te', grad_weight, picked, precision=PRECISE_ARITHMETIC)
    grad_logits = gate_probs * (grad_gates - lax.optimization_barrier(jnp.sum(gate_probs * grad_gates, axis=-1, keepdims=True)))
    router_wide = router_full.astype(jnp.float32)
    grad_normed = grad_normed + jnp.einsum('te,de->td', grad_logits, router_wide, precision=PRECISE_ARITHMETIC)
    router_part = jnp.einsum('td,te->de', normed_two.astype(jnp.float32), grad_logits, precision=PRECISE_ARITHMETIC)
    grad_middle, gain_two_part = norm_back(middle, gain_two, scale_two, grad_normed)
    grad_middle = grad_middle + upstream
    grad_branch = convert_halfprecision(RESIDUAL_SCALE * grad_middle)
    out_part = jnp.einsum('tq,td->qd', attention_output.astype(jnp.float32), grad_branch.astype(jnp.float32), precision=PRECISE_ARITHMETIC)
    attention_output_gradient = convert_halfprecision(jnp.einsum('td,qd->tq', grad_branch.astype(jnp.float32), out_full.astype(jnp.float32), precision=PRECISE_ARITHMETIC))
    head_gradient = attention_output_gradient.astype(jnp.float32).reshape(sequence_length, KEY_VALUE_HEADS, query_group_count, HEAD_WIDTH)
    attention_head_output = attention_output.astype(jnp.float32).reshape(sequence_length, KEY_VALUE_HEADS, query_group_count, HEAD_WIDTH)
    row_delta = jnp.transpose(lax.optimization_barrier(jnp.sum(head_gradient * attention_head_output, axis=-1)), (1, 2, 0))[..., None]
    value_gradient = jnp.einsum('kgqt,qkgd->tkd', probs_half, head_gradient, precision=PRECISE_ARITHMETIC)
    grad_probs = jnp.einsum('qkgd,tkd->kgqt', head_gradient, values_wide, precision=PRECISE_ARITHMETIC)
    grad_scores = convert_halfprecision(attn_probs * (grad_probs - row_delta) * ATTN_SCALE).astype(jnp.float32)
    grad_queries = jnp.einsum('kgqt,tkd->qkgd', grad_scores, keys_wide, precision=PRECISE_ARITHMETIC).reshape(sequence_length, QUERY_HEADS, HEAD_WIDTH)
    key_gradient = jnp.einsum('kgqt,qkgd->tkd', grad_scores, query_gathered, precision=PRECISE_ARITHMETIC)
    grad_joined = convert_halfprecision(jnp.concatenate([rotate_back(grad_queries, cosine_lookup, sine_lookup).reshape(sequence_length, query_feature_width), rotate_back(key_gradient, cosine_lookup, sine_lookup).reshape(sequence_length, key_feature_width), value_gradient.reshape(sequence_length, key_feature_width)], axis=-1))
    qkv_part = jnp.einsum('td,tm->dm', normed_one.astype(jnp.float32), grad_joined.astype(jnp.float32), precision=PRECISE_ARITHMETIC)
    grad_normed_one = jnp.einsum('tm,dm->td', grad_joined.astype(jnp.float32), qkv_full.astype(jnp.float32), precision=PRECISE_ARITHMETIC)
    grad_inputs, gain_one_part = norm_back(inputs, gain_one, scale_one, grad_normed_one)
    input_grad = (grad_inputs + grad_middle).astype(jnp.bfloat16)
    part_sums = (gain_one_part, qkv_part, out_part, gain_two_part, router_part, expansion_matrix_portion, down_part)
    return (layer_output, input_grad, part_sums)

def reference(layer_input, cotangent, sequence_ids, expert_ids, attention_gain, qkv_weight, output_weight, moe_gain, router, gate_up, down_proj):
    blocks = layer_input.shape[0] // TOK_DEV
    weights = (attention_gain, qkv_weight, output_weight, moe_gain, router, gate_up.astype(jnp.float32), down_proj.astype(jnp.float32))
    stacked = (layer_input.reshape(blocks, TOK_DEV, MODEL_WIDTH), cotangent.reshape(blocks, TOK_DEV, MODEL_WIDTH), sequence_ids.reshape(blocks, TOK_DEV), expert_ids.reshape(blocks, TOK_DEV, TOP))
    initial = (jnp.zeros((MODEL_WIDTH,), jnp.float32), jnp.zeros(qkv_weight.shape, jnp.float32), jnp.zeros(output_weight.shape, jnp.float32), jnp.zeros((MODEL_WIDTH,), jnp.float32), jnp.zeros((MODEL_WIDTH, E), jnp.float32), jnp.zeros((MODEL_WIDTH, E, 2 * F), jnp.float32), jnp.zeros((MODEL_WIDTH, E, F), jnp.float32))

    def scan_step(running, device_block):
        output_block, block_gradient, part_sums = device_layer(weights, device_block)
        return (tuple((total + part_now for total, part_now in zip(running, part_sums))), (output_block, block_gradient))
    totals, (outputs, grads_in) = lax.scan(scan_step, initial, stacked)
    return (outputs.reshape(blocks * TOK_DEV, MODEL_WIDTH), grads_in.reshape(blocks * TOK_DEV, MODEL_WIDTH), totals[0], totals[1], totals[2], totals[3], totals[4], totals[5], totals[6])
```

```python
import functools
import math
import jax
import jax.numpy as jnp
import numpy as np
from jax import lax
from jax.experimental import pallas as pl
from jax.experimental.pallas import tpu as pltpu
from jax.sharding import PartitionSpec as P

MODEL_WIDTH = 1536
QUERY_HEADS = 24
KEY_VALUE_HEADS = 8
HEAD_WIDTH = 64
E = 40
F = 512
TOP = 8
CAP = 32


EPSILON = 1e-06
ATTN_SCALE = 0.015625
RESIDUAL_SCALE = 0.22
ROPE_BASE = 10000.0
PRECISE_ARITHMETIC = lax.Precision.HIGHEST


def positions(sequence_ids):
    sequence_length = sequence_ids.shape[0]
    places = jnp.arange(sequence_length, dtype=jnp.int32)
    same = (sequence_ids[:, None] == sequence_ids[None, :]) & (places[None, :] < places[:, None])
    return jnp.sum(same.astype(jnp.int32), axis=1, dtype=jnp.int32)


def rope_tables(places, head_size):
    half_size = head_size // 2
    exponents = jnp.arange(half_size, dtype=jnp.float32) * (2.0 / head_size)
    inverse = jnp.exp(exponents * -math.log(ROPE_BASE))
    angles = places.astype(jnp.float32)[:, None] * inverse[None, :]
    return (jnp.cos(angles), jnp.sin(angles))


def apply_rotary(tensor, cosine_lookup, sine_lookup):
    half_size = tensor.shape[-1] // 2
    first_half = tensor[..., :half_size]
    second_half = tensor[..., half_size:]
    cosine_rows = cosine_lookup[:, None, :]
    sine_rows = sine_lookup[:, None, :]
    return jnp.concatenate(
        [
            first_half * cosine_rows - second_half * sine_rows,
            second_half * cosine_rows + first_half * sine_rows,
        ],
        axis=-1,
    )


def rotate_back(tensor, cosine_lookup, sine_lookup):
    half_size = tensor.shape[-1] // 2
    first_half = tensor[..., :half_size]
    second_half = tensor[..., half_size:]
    cosine_rows = cosine_lookup[:, None, :]
    sine_rows = sine_lookup[:, None, :]
    return jnp.concatenate(
        [
            first_half * cosine_rows + second_half * sine_rows,
            second_half * cosine_rows - first_half * sine_rows,
        ],
        axis=-1,
    )


def norm_scale(hidden_state):
    return lax.rsqrt(jnp.mean(hidden_state * hidden_state, axis=-1, keepdims=True) + EPSILON)


def norm_back(hidden_state, gain_vector, scale_rows, upstream):
    weighted = upstream * gain_vector.astype(jnp.float32)
    inner_mean = jnp.mean(weighted * hidden_state, axis=-1, keepdims=True)
    grad_hidden = scale_rows * weighted - hidden_state * scale_rows**3 * inner_mean
    grad_gain = jnp.sum(upstream * hidden_state * scale_rows, axis=0)
    return (grad_hidden, grad_gain)


def expert_slots(expert_ids, experts, capacity):
    rows = expert_ids.shape[0]
    picked = expert_ids[:, :, None] == jnp.arange(experts, dtype=jnp.int32)[None, None, :]
    named = jnp.any(picked, axis=1).astype(jnp.bfloat16)
    places = jnp.arange(rows, dtype=jnp.int32)
    before = (places[None, :] < places[:, None]).astype(jnp.bfloat16)
    ranks = jnp.dot(before, named, preferred_element_type=jnp.float32)
    ranks = jnp.sum(jnp.where(picked, ranks[:, None, :], 0.0), axis=-1).astype(jnp.int32)
    return (expert_ids * capacity + ranks).reshape(-1)


def owner_tables(devices):
    width_owned = E * F // devices
    span_count = (F + width_owned - 2) // F + 1
    first_expert = np.arange(devices) * width_owned // F
    send_table = np.minimum(first_expert[:, None] + np.arange(span_count)[None, :], E).reshape(-1)
    combine_table = (send_table[None, :] == np.arange(E)[:, None]).astype(np.float32)
    return (width_owned, span_count, send_table, combine_table)


def dispatch_rows(buffer_rows, send_table, devices, span_count):
    padded = jnp.concatenate(
        [buffer_rows, jnp.zeros((1, CAP, MODEL_WIDTH), buffer_rows.dtype)], axis=0
    )
    chosen = jnp.asarray(send_table[:, None] == np.arange(E + 1)[None, :], dtype=buffer_rows.dtype)
    picked_rows = jnp.einsum(
        "se,ecd->scd", chosen, padded, preferred_element_type=jnp.float32
    ).astype(buffer_rows.dtype)
    return picked_rows.reshape(devices, span_count, CAP, MODEL_WIDTH)


def merge_entries(returned, combine_table):
    flat_rows = returned.reshape(returned.shape[0] * returned.shape[1], CAP * MODEL_WIDTH)
    summed = jnp.dot(
        jnp.asarray(combine_table),
        flat_rows,
        precision=PRECISE_ARITHMETIC,
        preferred_element_type=jnp.float32,
    )
    return summed.reshape(E, CAP, MODEL_WIDTH)


def on_device(
    layer_input,
    cotangent,
    sequence_ids,
    expert_ids,
    attention_gain,
    qkv_weight,
    output_weight,
    moe_gain,
    router,
    gate_up,
    down_proj,
):
    sequence_length = layer_input.shape[0]
    shard_rows = gate_up.shape[0]
    query_group_count = QUERY_HEADS // KEY_VALUE_HEADS
    query_feature_width = QUERY_HEADS * HEAD_WIDTH
    key_feature_width = KEY_VALUE_HEADS * HEAD_WIDTH
    rows_per_block = min(512, sequence_length)
    devices = lax.axis_size("fsdp")
    dense_set = (
        lax.all_gather(attention_gain, "fsdp", axis=0, tiled=True),
        lax.all_gather(qkv_weight, "fsdp", axis=0, tiled=True),
        lax.all_gather(output_weight, "fsdp", axis=0, tiled=True),
        lax.all_gather(moe_gain, "fsdp", axis=0, tiled=True),
        lax.all_gather(router, "fsdp", axis=0, tiled=True),
    )
    gain_one, qkv_full, out_full, gain_two, router_full = dense_set
    width_owned, span_count, send_table, combine_table = owner_tables(devices)
    gate_cols = jnp.transpose(gate_up.reshape(shard_rows, E, 2, F), (0, 2, 1, 3)).reshape(
        shard_rows, 2, E * F
    )
    down_cols = down_proj.reshape(shard_rows, 1, E * F)
    owned_weights = lax.all_to_all(
        jnp.concatenate([gate_cols, down_cols], axis=1),
        "fsdp",
        split_axis=2,
        concat_axis=0,
        tiled=True,
    )
    owned_gate_up = owned_weights[:, :2, :]
    owned_down = owned_weights[:, 2, :]
    owner_index = lax.axis_index("fsdp")
    owned_start = owner_index * width_owned
    owned_columns = owned_start + jnp.arange(width_owned, dtype=jnp.int32)
    slot_of = owned_columns // F - owned_start // F
    column_mask = (slot_of[None, :] == jnp.arange(span_count, dtype=jnp.int32)[:, None]).astype(
        jnp.float32
    )
    inputs = layer_input.astype(jnp.float32)
    scale_one = norm_scale(inputs)
    normed_one = (inputs * scale_one * gain_one.astype(jnp.float32)).astype(jnp.bfloat16)
    joined_projection = jnp.dot(normed_one, qkv_full, preferred_element_type=jnp.float32)
    places = positions(sequence_ids)
    cosine_lookup, sine_lookup = rope_tables(places, HEAD_WIDTH)
    query_rows = apply_rotary(
        joined_projection[:, :query_feature_width].reshape(
            sequence_length, QUERY_HEADS, HEAD_WIDTH
        ),
        cosine_lookup,
        sine_lookup,
    ).astype(jnp.bfloat16)
    query_rows = query_rows.reshape(sequence_length, KEY_VALUE_HEADS, query_group_count, HEAD_WIDTH)
    rotated_keys = apply_rotary(
        joined_projection[:, query_feature_width : query_feature_width + key_feature_width].reshape(
            sequence_length, KEY_VALUE_HEADS, HEAD_WIDTH
        ),
        cosine_lookup,
        sine_lookup,
    ).astype(jnp.bfloat16)
    value_inputs = (
        joined_projection[:, query_feature_width + key_feature_width :]
        .reshape(sequence_length, KEY_VALUE_HEADS, HEAD_WIDTH)
        .astype(jnp.bfloat16)
    )
    token_index = jnp.arange(sequence_length, dtype=jnp.int32)

    def block_scores(offset):
        scores = (
            jnp.einsum(
                "qkgd,tkd->kgqt", query_rows, rotated_keys, preferred_element_type=jnp.float32
            )
            * ATTN_SCALE
        )
        allowed = (
            sequence_ids[offset : offset + rows_per_block, None] == sequence_ids[None, :]
        ) & (token_index[None, :] <= token_index[offset : offset + rows_per_block, None])
        return jnp.where(allowed, scores, -jnp.inf)

    offset = 0
    scores = block_scores(offset)
    row_peak = jnp.max(scores, axis=-1, keepdims=True)
    log_total = row_peak + jnp.log(jnp.sum(jnp.exp(scores - row_peak), axis=-1, keepdims=True))
    probs_half = jnp.exp(scores - log_total).astype(jnp.bfloat16)
    mixed_heads = jnp.einsum(
        "kgqt,tkd->qkgd", probs_half, value_inputs, preferred_element_type=jnp.float32
    )
    attention_output_list = mixed_heads.reshape(rows_per_block, query_feature_width).astype(
        jnp.bfloat16
    )
    total_list = [log_total]
    branch = jnp.dot(attention_output_list, out_full, preferred_element_type=jnp.float32)
    middle = inputs + RESIDUAL_SCALE * branch
    scale_two = norm_scale(middle)
    normed_two = (middle * scale_two * gain_two.astype(jnp.float32)).astype(jnp.bfloat16)
    logits = jnp.dot(normed_two, router_full, preferred_element_type=jnp.float32)
    gate_probs = jax.nn.softmax(logits, axis=-1)
    picked = (expert_ids[:, :, None] == jnp.arange(E, dtype=jnp.int32)[None, None, :]).astype(
        jnp.float32
    )
    route_weight = jnp.einsum("tke,te->tk", picked, gate_probs, precision=PRECISE_ARITHMETIC)
    slot_rows = expert_slots(expert_ids, E, CAP)
    received_storage = (
        jnp.zeros((E * CAP, MODEL_WIDTH), jnp.bfloat16)
        .at[slot_rows]
        .set(jnp.repeat(normed_two, TOP, axis=0))
        .reshape(E, CAP, MODEL_WIDTH)
    )
    send_in = dispatch_rows(received_storage, send_table, devices, span_count)
    pre_cols = jnp.einsum(
        "nrkd,dgw->nrkgw",
        lax.all_to_all(send_in, "fsdp", split_axis=0, concat_axis=0, tiled=True),
        owned_gate_up,
        preferred_element_type=jnp.float32,
    )
    pre_cols = pre_cols * column_mask[None, :, None, None, :]
    gate_cols_pre = pre_cols[..., 0, :]
    up_cols_pre = pre_cols[..., 1, :]
    acted = (gate_cols_pre * jax.nn.sigmoid(gate_cols_pre) * up_cols_pre).astype(jnp.bfloat16)
    partial_out = jnp.einsum("nrkw,dw->nrkd", acted, owned_down, preferred_element_type=jnp.float32)
    returned_out = lax.all_to_all(partial_out, "fsdp", split_axis=0, concat_axis=0, tiled=True)
    buffer_out = merge_entries(returned_out, combine_table)
    routed_out = buffer_out.reshape(E * CAP, MODEL_WIDTH)[slot_rows].reshape(
        sequence_length, TOP, MODEL_WIDTH
    )
    combined = jnp.einsum("tk,tkd->td", route_weight, routed_out, precision=PRECISE_ARITHMETIC)
    layer_output = (middle + RESIDUAL_SCALE * combined).astype(jnp.bfloat16)
    upstream = cotangent.astype(jnp.float32)
    grad_mix = RESIDUAL_SCALE * upstream
    grad_weight = jnp.einsum("td,tkd->tk", grad_mix, routed_out, precision=PRECISE_ARITHMETIC)
    grad_rows = (
        (route_weight[:, :, None] * grad_mix[:, None, :])
        .astype(jnp.bfloat16)
        .reshape(sequence_length * TOP, MODEL_WIDTH)
    )
    buffer_grad = (
        jnp.zeros((E * CAP, MODEL_WIDTH), jnp.bfloat16)
        .at[slot_rows]
        .set(grad_rows)
        .reshape(E, CAP, MODEL_WIDTH)
    )
    gain_one_back, qkv_back, out_back, gain_two_back, router_back = dense_set
    send_grad = dispatch_rows(buffer_grad, send_table, devices, span_count)
    rows_in = lax.all_to_all(send_in, "fsdp", split_axis=0, concat_axis=0, tiled=True)
    rows_grad = lax.all_to_all(send_grad, "fsdp", split_axis=0, concat_axis=0, tiled=True)
    pre_cols = jnp.einsum(
        "nrkd,dgw->nrkgw", rows_in, owned_gate_up, preferred_element_type=jnp.float32
    )
    pre_cols = pre_cols * column_mask[None, :, None, None, :]
    gate_cols_pre = pre_cols[..., 0, :]
    up_cols_pre = pre_cols[..., 1, :]
    sigmoid_cols = jax.nn.sigmoid(gate_cols_pre)
    silu_cols = gate_cols_pre * sigmoid_cols
    acted = (silu_cols * up_cols_pre).astype(jnp.bfloat16)
    grad_act_cols = jnp.einsum(
        "nrkd,dw->nrkw", rows_grad, owned_down, preferred_element_type=jnp.float32
    )
    grad_gate_cols = (
        grad_act_cols * up_cols_pre * sigmoid_cols * (1.0 + gate_cols_pre * (1.0 - sigmoid_cols))
    )
    grad_up_cols = grad_act_cols * silu_cols
    grad_pair = jnp.stack([grad_gate_cols, grad_up_cols], axis=3).astype(jnp.bfloat16)
    partial_back = jnp.einsum(
        "nrkgw,dgw->nrkd", grad_pair, owned_gate_up, preferred_element_type=jnp.float32
    )
    returned_back = lax.all_to_all(partial_back, "fsdp", split_axis=0, concat_axis=0, tiled=True)
    results = (returned_back, rows_in, rows_grad, grad_pair, acted)
    returned_back, rows_in_all, rows_grad_all, grad_pair_all, acted_all = results
    backward_buffer = merge_entries(returned_back, combine_table)
    owned_gate_up_grad = jnp.einsum(
        "nrkd,nrkgw->dgw", rows_in_all, grad_pair_all, preferred_element_type=jnp.float32
    )
    owned_down_grad = jnp.einsum(
        "nrkd,nrkw->dw", rows_grad_all, acted_all, preferred_element_type=jnp.float32
    )
    owned_grads = jnp.concatenate([owned_gate_up_grad, owned_down_grad[:, None, :]], axis=1)
    relaid = lax.all_to_all(owned_grads, "fsdp", split_axis=0, concat_axis=2, tiled=True)
    gate_up_grad = jnp.transpose(
        relaid[:, :2, :].reshape(shard_rows, 2, E, F), (0, 2, 1, 3)
    ).reshape(shard_rows, E, 2 * F)
    down_grad = relaid[:, 2, :].reshape(shard_rows, E, F)
    grad_normed = jnp.sum(
        backward_buffer.reshape(E * CAP, MODEL_WIDTH)[slot_rows].reshape(
            sequence_length, TOP, MODEL_WIDTH
        ),
        axis=1,
    )
    grad_gates = jnp.einsum("tk,tke->te", grad_weight, picked, precision=PRECISE_ARITHMETIC)
    grad_logits = gate_probs * (
        grad_gates - jnp.sum(gate_probs * grad_gates, axis=-1, keepdims=True)
    )
    grad_normed = grad_normed + jnp.einsum(
        "te,de->td", grad_logits, router_back.astype(jnp.float32), precision=PRECISE_ARITHMETIC
    )
    router_part = jnp.einsum(
        "td,te->de", normed_two.astype(jnp.float32), grad_logits, precision=PRECISE_ARITHMETIC
    )
    grad_middle, gain_two_part = norm_back(middle, gain_two_back, scale_two, grad_normed)
    grad_middle = grad_middle + upstream
    grad_branch = (RESIDUAL_SCALE * grad_middle).astype(jnp.bfloat16)
    out_part = jnp.einsum(
        "tq,td->qd", attention_output_list, grad_branch, preferred_element_type=jnp.float32
    )
    attention_output_gradient = jnp.einsum(
        "td,qd->tq", grad_branch, out_back, preferred_element_type=jnp.float32
    ).astype(jnp.bfloat16)
    value_gradient = jnp.zeros((sequence_length, KEY_VALUE_HEADS, HEAD_WIDTH), jnp.float32)
    key_gradient = jnp.zeros((sequence_length, KEY_VALUE_HEADS, HEAD_WIDTH), jnp.float32)
    query_grads = []
    for block_number, offset in enumerate(range(0, sequence_length, rows_per_block)):
        scores = block_scores(offset)
        attn_probs = jnp.exp(scores - total_list[block_number])
        block_gradient = attention_output_gradient.reshape(
            rows_per_block, KEY_VALUE_HEADS, query_group_count, HEAD_WIDTH
        )
        attention_output_block = attention_output_list.reshape(
            rows_per_block, KEY_VALUE_HEADS, query_group_count, HEAD_WIDTH
        )
        row_delta = jnp.sum(
            block_gradient.astype(jnp.float32) * attention_output_block.astype(jnp.float32), axis=-1
        )
        row_delta = jnp.transpose(row_delta, (1, 2, 0))[..., None]
        value_gradient = jnp.einsum(
            "kgqt,qkgd->tkd",
            attn_probs.astype(jnp.bfloat16),
            block_gradient,
            preferred_element_type=jnp.float32,
        )
        grad_probs = jnp.einsum(
            "qkgd,tkd->kgqt", block_gradient, value_inputs, preferred_element_type=jnp.float32
        )
        grad_scores = (attn_probs * (grad_probs - row_delta) * ATTN_SCALE).astype(jnp.bfloat16)
        query_grads.append(
            jnp.einsum(
                "kgqt,tkd->qkgd", grad_scores, rotated_keys, preferred_element_type=jnp.float32
            )
        )
        key_gradient = jnp.einsum(
            "kgqt,qkgd->tkd", grad_scores, query_rows, preferred_element_type=jnp.float32
        )
    grad_queries = query_grads[0].reshape(sequence_length, QUERY_HEADS, HEAD_WIDTH)
    grad_joined = jnp.concatenate(
        [
            rotate_back(grad_queries, cosine_lookup, sine_lookup).reshape(
                sequence_length, query_feature_width
            ),
            rotate_back(key_gradient, cosine_lookup, sine_lookup).reshape(
                sequence_length, key_feature_width
            ),
            value_gradient.reshape(sequence_length, key_feature_width),
        ],
        axis=-1,
    ).astype(jnp.bfloat16)
    qkv_part = jnp.einsum("td,tm->dm", normed_one, grad_joined, preferred_element_type=jnp.float32)
    grad_normed_one = jnp.einsum(
        "tm,dm->td", grad_joined, qkv_back, preferred_element_type=jnp.float32
    )
    grad_inputs, gain_one_part = norm_back(inputs, gain_one_back, scale_one, grad_normed_one)
    input_grad = (grad_inputs + grad_middle).astype(jnp.bfloat16)
    dense_grads = (
        lax.psum_scatter(gain_one_part, "fsdp", scatter_dimension=0, tiled=True),
        lax.psum_scatter(qkv_part, "fsdp", scatter_dimension=0, tiled=True),
        lax.psum_scatter(out_part, "fsdp", scatter_dimension=0, tiled=True),
        lax.psum_scatter(gain_two_part, "fsdp", scatter_dimension=0, tiled=True),
        lax.psum_scatter(router_part, "fsdp", scatter_dimension=0, tiled=True),
    )
    return (
        layer_output,
        input_grad,
        dense_grads[0],
        dense_grads[1],
        dense_grads[2],
        dense_grads[3],
        dense_grads[4],
        gate_up_grad,
        down_grad,
    )


MESH = pl.DeviceIdType.MESH

def place():
    me = lax.axis_index("fsdp")
    return me // 8, lax.rem(me // 4, 2), lax.rem(me // 2, 2), lax.rem(me, 2)

def dev(z, y, x, c):
    return ((z * 2 + y) * 2 + x) * 2 + c

def z_order(z, q):
    table = ((0, 1, 2, 3), (1, 0, 2, 3), (2, 3, 1, 0), (3, 2, 1, 0))
    v = jnp.int32(table[0][q])
    for k in range(1, 4):
        v = jnp.where(z == k, table[k][q], v)
    return v

def greet(z, near, up, down):
    barrier = pltpu.get_barrier_semaphore()
    for d in near:
        pl.semaphore_signal(barrier, inc=1, device_id=(d,), device_id_type=MESH)
    @pl.when(z < 3)
    def _():
        pl.semaphore_signal(barrier, inc=1, device_id=(up,), device_id_type=MESH)
    @pl.when(z > 0)
    def _():
        pl.semaphore_signal(barrier, inc=1, device_id=(down,), device_id_type=MESH)
    pl.semaphore_wait(barrier, len(near) + jnp.where(z < 3, 1, 0) + jnp.where(z > 0, 1, 0))

def gather_kernel(parts, count, *refs):
    shards, outs = refs[:count], refs[count:2 * count]
    (local_sem, zs, zs2, zr, fs, fr, s1s, s1r, s2s, s2r, cs, cr) = refs[2 * count:]
    z, y, x, c = place()
    sib, xn, yn = dev(z, y, x, 1 - c), dev(z, y, 1 - x, c), dev(z, 1 - y, x, c)
    up, down = dev(z + 1, y, x, c), dev(z - 1, y, x, c)
    greet(z, (sib, xn, yn), up, down)

    def at(p, d):
        a, c0, w, _ = parts[p]
        rows = shards[a].shape[0]
        return outs[a].at[pl.ds(pl.multiple_of(d * rows, rows), rows), pl.ds(c0, w)]

    def own(p):
        a, c0, w, _ = parts[p]
        return shards[a].at[:, pl.ds(c0, w)]

    def rc(src, dst, ss, rs, to):
        return pltpu.make_async_remote_copy(src_ref=src, dst_ref=dst, send_sem=ss, recv_sem=rs, device_id=(to,), device_id_type=MESH)

    me = dev(z, y, x, c)
    locals_ = []
    for a in range(count):
        rows = shards[a].shape[0]
        l = pltpu.make_async_copy(shards[a], outs[a].at[pl.ds(pl.multiple_of(me * rows, rows), rows)], local_sem.at[a])
        l.start(); locals_.append(l)
    P = len(parts)
    zq = [z_order(z, q) for q in range(4)]
    sends = []
    def go(copy):
        copy.start(); sends.append(copy)

    def stage1(q):
        for p in range(P):
            first, second = (xn, yn) if parts[p][3] == 0 else (yn, xn)
            d = dev(zq[q], y, x, c)
            here = at(p, d)
            if q == 0:
                src = own(p)
                @pl.when(z < 3)
                def _():
                    rc(src, here, zs.at[0, p], zr.at[z, p], up).start()
                @pl.when(z > 0)
                def _():
                    rc(src, here, zs2.at[p], zr.at[z, p], down).start()
            else:
                src = here
                rc(here, here, zs.at[q, p], zr.at[zq[q], p], up).wait_recv()
                @pl.when((zq[q] < z) & (z < 3))
                def _():
                    rc(src, here, zs.at[q, p], zr.at[zq[q], p], up).start()
                @pl.when((zq[q] > z) & (z > 0))
                def _():
                    rc(src, here, zs.at[q, p], zr.at[zq[q], p], down).start()
            go(rc(src, here, fs.at[q, p], fr.at[q, p], first))
            go(rc(src, here, s1s.at[q, p], s1r.at[q, p], second))
            go(rc(src, here, cs.at[0, q, p], cr.at[0, q, p], sib))

    def near(q, p):
        return dev(zq[q], y, 1 - x, c) if parts[p][3] == 0 else dev(zq[q], 1 - y, x, c)
    def side(q, p):
        return dev(zq[q], 1 - y, x, c) if parts[p][3] == 0 else dev(zq[q], y, 1 - x, c)

    def stage2(q):
        for p in range(P):
            first, second = (xn, yn) if parts[p][3] == 0 else (yn, xn)
            there = at(p, near(q, p))
            rc(there, there, fs.at[q, p], fr.at[q, p], first).wait_recv()
            go(rc(there, there, s2s.at[q, p], s2r.at[q, p], second))
            go(rc(there, there, cs.at[1, q, p], cr.at[1, q, p], sib))

    def stage3(q):
        for p in range(P):
            there = at(p, side(q, p))
            rc(there, there, s1s.at[q, p], s1r.at[q, p], sib).wait_recv()
            go(rc(there, there, cs.at[2, q, p], cr.at[2, q, p], sib))
        for p in range(P):
            there = at(p, dev(zq[q], 1 - y, 1 - x, c))
            rc(there, there, s2s.at[q, p], s2r.at[q, p], sib).wait_recv()
            go(rc(there, there, cs.at[3, q, p], cr.at[3, q, p], sib))

    stage1(0); stage1(1); stage2(0); stage1(2); stage2(1); stage3(0); stage1(3); stage2(2); stage3(1); stage2(3); stage3(2); stage3(3)
    for q in range(4):
        for p in range(P):
            for k, where in enumerate((dev(zq[q], y, x, 1 - c), None, None, None)):
                if k == 0: d = dev(zq[q], y, x, 1 - c)
                elif k == 1: d = near(q, p) + 1 - 2 * c
                elif k == 2: d = side(q, p) + 1 - 2 * c
                else: d = dev(zq[q], 1 - y, 1 - x, 1 - c)
                there = at(p, d)
                rc(there, there, cs.at[k, q, p], cr.at[k, q, p], sib).wait_recv()
    for copy in sends: copy.wait_send()
    for p in range(P):
        here = at(p, me)
        @pl.when(z < 3)
        def _():
            rc(here, here, zs.at[0, p], zr.at[z, p], up).wait_send()
        @pl.when(z > 0)
        def _():
            rc(here, here, zs2.at[p], zr.at[z, p], down).wait_send()
        for q in range(1, 4):
            @pl.when(((zq[q] < z) & (z < 3)) | ((zq[q] > z) & (z > 0)))
            def _():
                rc(here, here, zs.at[q, p], zr.at[zq[q], p], up).wait_send()
    for l in locals_: l.wait()

def gather(arrays, parts, collective_id):
    n = 32; k = len(arrays); P = len(parts)
    dma = pltpu.SemaphoreType.DMA
    return pl.pallas_call(
        functools.partial(gather_kernel, parts, k),
        out_shape=[jax.ShapeDtypeStruct((n * a.shape[0],) + a.shape[1:], a.dtype) for a in arrays],
        in_specs=[pl.BlockSpec(memory_space=pl.ANY)] * k,
        out_specs=[pl.BlockSpec(memory_space=pl.ANY)] * k,
        scratch_shapes=[dma((k,)), dma((4, P)), dma((P,)), dma((4, P)), dma((4, P)), dma((4, P)), dma((4, P)), dma((4, P)), dma((4, P)), dma((4, P)), dma((4, 4, P)), dma((4, 4, P))],
        compiler_params=pltpu.CompilerParams(collective_id=collective_id, has_side_effects=True),
    )(*arrays)


def scatter_kernel(parts, count, rows, *refs):
    fulls, outs = refs[:count], refs[count:2 * count]
    refs = refs[2 * count:]
    held, r0, r1, r2, r3 = (refs[i * count:(i + 1) * count] for i in range(5))
    (ls, s0, e0, s1, e1, s2, e2, s3, e3) = refs[5 * count:]
    z, y, x, c = place()
    sib, xn, yn = dev(z, y, x, 1 - c), dev(z, y, 1 - x, c), dev(z, 1 - y, x, c)
    up, down = dev(z + 1, y, x, c), dev(z - 1, y, x, c)
    greet(z, (sib, xn, yn), up, down)

    P = len(parts)
    zq = [z_order(z, q) for q in range(4)]
    sends = []
    def rc(src, dst, ss, rs, to):
        return pltpu.make_async_remote_copy(src_ref=src, dst_ref=dst, send_sem=ss, recv_sem=rs, device_id=(to,), device_id_type=MESH)
    def go(copy):
        copy.start(); sends.append(copy)
    def cut(p):
        return pl.ds(parts[p][1], parts[p][2])
    def spot(p, k):
        if parts[p][3] == 0:
            return ((1 - y, 1 - x), (1 - y, x), (y, 1 - x), (y, x))[k]
        return ((1 - y, 1 - x), (y, 1 - x), (1 - y, x), (y, x))[k]
    def slot(q, yy, xx):
        return (yy * 2 + xx) * 4 + zq[q]
    def source(p, q, k, core):
        a = parts[p][0]
        yy, xx = spot(p, k)
        d = dev(zq[q], yy, xx, core)
        return fulls[a].at[pl.ds(pl.multiple_of(d * rows[a], rows[a]), rows[a]), cut(p)]

    loads = {}
    for q in (3, 2, 1, 0):
        for k in range(4):
            for p in range(P):
                a = parts[p][0]
                go(rc(source(p, q, k, 1 - c), r0[a].at[slot(q, *spot(p, k)), :, cut(p)], s0.at[q, k, p], e0.at[q, k, p], sib))
                l = pltpu.make_async_copy(source(p, q, k, c), held[a].at[slot(q, *spot(p, k)), :, cut(p)], ls.at[q, k, p])
                l.start(); loads[q, k, p] = l

    def add(p, dst, s_dst, src, s_src, more=None, out=None):
        a, c0, w, _ = parts[p]
        step = 16
        def body(i, carry):
            r = pl.ds(pl.multiple_of(i * step, step), step)
            v = dst[s_dst, r, c0:c0 + w].astype(jnp.float32) + src[s_src, r, c0:c0 + w].astype(jnp.float32)
            dst[s_dst, r, c0:c0 + w] = v.astype(dst.dtype)
            return carry
        lax.fori_loop(0, rows[a] // step, body, 0)

    def stage1(q):
        for k in range(4):
            for p in range(P):
                a = parts[p][0]
                first = yn if parts[p][3] == 0 else xn
                s = slot(q, *spot(p, k))
                here = held[a].at[s, :, cut(p)]
                rc(here, r0[a].at[s, :, cut(p)], s0.at[q, k, p], e0.at[q, k, p], sib).wait_recv()
                loads[q, k, p].wait()
                add(p, held[a], s, r0[a], s)
                if k < 2:
                    go(rc(here, r1[a].at[q * 2 + k, :, cut(p)], s1.at[q, k, p], e1.at[q, k, p], first))

    def stage2(q):
        for k in range(2):
            for p in range(P):
                a = parts[p][0]
                second = xn if parts[p][3] == 0 else yn
                s = slot(q, *spot(p, k + 2))
                here = held[a].at[s, :, cut(p)]
                rc(here, r1[a].at[q * 2 + k, :, cut(p)], s1.at[q, k, p], e1.at[q, k, p], sib).wait_recv()
                add(p, held[a], s, r1[a], q * 2 + k)
                if k == 0:
                    go(rc(here, r2[a].at[q, :, cut(p)], s2.at[q, p], e2.at[q, p], second))

    def stage3(q):
        for p in range(P):
            a = parts[p][0]
            s = slot(q, y, x)
            here = held[a].at[s, :, cut(p)]
            rc(here, r2[a].at[q, :, cut(p)], s2.at[q, p], e2.at[q, p], sib).wait_recv()
            add(p, held[a], s, r2[a], q)
            if q > 0:
                @pl.when((zq[q] > z) & (z > 0) | (zq[q] < z) & (z < 3))
                def _():
                    land = r3[a].at[zq[q], :, cut(p)]
                    rc(here, land, s3.at[q, p], e3.at[zq[q], p], sib).wait_recv()
                    add(p, held[a], s, r3[a], zq[q])
                @pl.when(zq[q] > z)
                def _():
                    rc(here, r3[a].at[zq[q], :, cut(p)], s3.at[q, p], e3.at[zq[q], p], up).start()
                @pl.when((zq[q] < z) & (zq[q] == z - 1))
                def _():
                    rc(here, r3[a].at[4, :, cut(p)], s3.at[q, p], e3.at[4, p], down).start()
                @pl.when(zq[q] < z - 1)
                def _():
                    rc(here, r3[a].at[zq[q], :, cut(p)], s3.at[q, p], e3.at[zq[q], p], down).start()
            else:
                @pl.when(z > 0)
                def _():
                    rc(here, r3[a].at[z, :, cut(p)], s3.at[q, p], e3.at[z, p], sib).wait_recv()
                @pl.when(z < 3)
                def _():
                    rc(here, r3[a].at[4, :, cut(p)], s3.at[q, p], e3.at[4, p], sib).wait_recv()
                a_, c0, w, _m = parts[p]
                step = 16
                zero = jnp.float32(0)
                def body(i, carry):
                    r = pl.ds(pl.multiple_of(i * step, step), step)
                    v = held[a][s, r, c0:c0 + w].astype(jnp.float32)
                    outs[a][r, c0:c0 + w] = v.astype(outs[a].dtype)
                    return carry
                lax.fori_loop(0, rows[a] // step, body, 0)
                for cond, where in ((z > 0, z), (z < 3, 4)):
                    @pl.when(cond)
                    def _():
                        def more(i, carry):
                            r = pl.ds(pl.multiple_of(i * step, step), step)
                            outs[a][r, c0:c0 + w] += r3[a][where, r, c0:c0 + w].astype(jnp.float32)
                            return carry
                        lax.fori_loop(0, rows[a] // step, more, 0)

    for f, q in ((1, 3), (1, 2), (2, 3), (1, 1), (2, 2), (3, 3), (1, 0), (2, 1), (3, 2), (2, 0), (3, 1), (3, 0)):
        (stage1, stage2, stage3)[f - 1](q)
    for copy in sends: copy.wait_send()
    for q in range(1, 4):
        for p in range(P):
            a = parts[p][0]
            here = held[a].at[slot(q, y, x), :, cut(p)]
            rc(here, here, s3.at[q, p], e3.at[0, p], sib).wait_send()

def scatter(arrays, parts, collective_id):
    k = len(arrays); P = len(parts)
    dma = pltpu.SemaphoreType.DMA
    rows = [a.shape[0] // 32 for a in arrays]
    scr = []
    for cnt in (16, 16, 8, 4, 5):
        scr += [pltpu.VMEM((cnt, a.shape[0] // 32, a.shape[1]), a.dtype) for a in arrays]
    return pl.pallas_call(
        functools.partial(scatter_kernel, parts, k, rows),
        out_shape=[jax.ShapeDtypeStruct((a.shape[0] // 32, a.shape[1]), jnp.float32) for a in arrays],
        in_specs=[pl.BlockSpec(memory_space=pl.ANY)] * k,
        out_specs=[pl.BlockSpec(memory_space=pltpu.VMEM)] * k,
        scratch_shapes=scr + [dma((4, 4, P)), dma((4, 4, P)), dma((4, 4, P)), dma((4, 2, P)), dma((4, 2, P)), dma((4, P)), dma((4, P)), dma((4, P)), dma((5, P))],
        compiler_params=pltpu.CompilerParams(collective_id=collective_id, has_side_effects=True, vmem_limit_bytes=60 * 2**20),
    )(*arrays)


D = MODEL_WIDTH
SRC = 8
STEPS = 4
M = SRC * CAP
F32, BF16 = jnp.float32, jnp.bfloat16
HALVES = ((0, 512, 1280), (1024, 128, 1792))

def nt(a, b):
    return lax.dot_general(a, b, (((1,), (1,)), ((), ())), preferred_element_type=F32)
def nn(a, b):
    return lax.dot_general(a, b, (((1,), (0,)), ((), ())), preferred_element_type=F32)
def tn(a, b):
    return lax.dot_general(a, b, (((0,), (0,)), ((), ())), preferred_element_type=F32)

def expert_kernel(own_ref, t_ref, c_ref, pick_ref, router_ref, w_ref, out_ref, gin_ref, gg_ref, dw_ref,
                  x_ref, g_ref, rw_ref, act_ref, dgu_ref, actq_ref, dguq_ref, ow_ref, gi_ref):
    i = pl.program_id(0)
    mine = (own_ref[0], own_ref[1])
    logits = nt(router_ref[...], t_ref[...])
    row = lax.broadcasted_iota(jnp.int32, logits.shape, 0)
    logits = jnp.where(row < E, logits, -jnp.inf)
    e = jnp.exp(logits - jnp.max(logits, axis=0, keepdims=True))
    probs = e / jnp.sum(e, axis=0, keepdims=True)
    mineprob = [jnp.sum(jnp.where(row == m, probs, 0.0), axis=0, keepdims=True) for m in mine]
    at = pl.ds(pl.multiple_of(i * M, M), M)
    for s in range(SRC):
        pick = pick_ref[s * 64:s * 64 + 64, :]
        xs = nn(pick, t_ref[s * 128:s * 128 + 128, :]).astype(BF16)
        gs = nn(pick, c_ref[s * 128:s * 128 + 128, :]).astype(BF16)
        wide = pick.astype(F32)
        for k in range(2):
            to = pl.ds(pl.multiple_of(i * M + s * CAP, CAP), CAP)
            x_ref[k, to, :] = xs[k * 32:k * 32 + 32]
            g_ref[k, to, :] = gs[k * 32:k * 32 + 32]
            rw_ref[k, s * CAP:s * CAP + CAP, :] = jnp.broadcast_to(jnp.sum(wide[k * 32:k * 32 + 32] * mineprob[k][:, s * 128:(s + 1) * 128], axis=1, keepdims=True), (CAP, 128))
    gws = []
    for k, acts, dgus in ((0, act_ref, dgu_ref), (1, actq_ref, dguq_ref)):
        g0, w, d0 = HALVES[k]
        pre = nn(x_ref[k, at, :], w_ref[:, g0:g0 + 2 * w])
        gate, up = pre[:, :w], pre[:, w:]
        sig = jax.nn.sigmoid(gate)
        silu = gate * sig
        act = (silu * up).astype(BF16)
        acts[at, :] = act
        rw = rw_ref[k, :, 0:1]
        out = nt(act, w_ref[:, d0:d0 + w])
        mix = g_ref[k, at, :].astype(F32) * 0.22
        gws.append(jnp.sum(mix * out, axis=1, keepdims=True))
        ow_ref[k] = (rw * out).astype(BF16)
        g = (rw * mix).astype(BF16)
        g_ref[k, at, :] = g
        da = nn(g, w_ref[:, d0:d0 + w])
        dgu = jnp.concatenate([(da * up * sig * (1.0 + gate * (1.0 - sig))).astype(BF16), (da * silu).astype(BF16)], axis=1)
        dgus[at, :] = dgu
        gi_ref[k] = nt(dgu, w_ref[:, g0:g0 + 2 * w]).astype(BF16)
    for s in range(SRC):
        r = slice(s * CAP, s * CAP + CAP)
        pick = pick_ref[s * 64:s * 64 + 64, :]
        to = slice(s * 128, s * 128 + 128)
        out_ref[to, :] = tn(pick, jnp.concatenate([ow_ref[0, r, :], ow_ref[1, r, :]], axis=0)).astype(BF16)
        gin_ref[to, :] = tn(pick, jnp.concatenate([gi_ref[0, r, :], gi_ref[1, r, :]], axis=0)).astype(BF16)
        wide = pick.astype(F32)
        for k in range(2):
            gg_ref[s, k:k + 1, :] = jnp.sum(wide[k * 32:k * 32 + 32] * gws[k][r], axis=0, keepdims=True)
        gg_ref[s, 2:8, :] = jnp.zeros((6, 128), F32)

    @pl.when(i == STEPS - 1)
    def _():
        def body(j, carry):
            c = pl.ds(pl.multiple_of(j * 256, 256), 256)
            for k, acts, dgus in ((0, act_ref, dgu_ref), (1, actq_ref, dguq_ref)):
                g0, w, d0 = HALVES[k]
                dw_ref[c, g0:g0 + 2 * w] = tn(x_ref[k, :, c], dgus[...]).astype(BF16)
                dw_ref[c, d0:d0 + w] = tn(g_ref[k, :, c], acts[...]).astype(BF16)
            return carry
        lax.fori_loop(0, D // 256, body, 0)

def experts(owned, tokens, cot, picks, router_t, w):
    R = SRC * 128
    return pl.pallas_call(
        expert_kernel,
        grid=(STEPS,),
        in_specs=[
            pl.BlockSpec(memory_space=pltpu.SMEM),
            pl.BlockSpec((R, D), lambda i: (i, 0)),
            pl.BlockSpec((R, D), lambda i: (i, 0)),
            pl.BlockSpec((SRC * 64, 128), lambda i: (i, 0)),
            pl.BlockSpec((64, D), lambda i: (0, 0), pipeline_mode=pl.Buffered(1)),
            pl.BlockSpec((D, 1920), lambda i: (0, 0), pipeline_mode=pl.Buffered(1)),
        ],
        out_specs=[
            pl.BlockSpec((R, D), lambda i: (i, 0)),
            pl.BlockSpec((R, D), lambda i: (i, 0)),
            pl.BlockSpec((SRC, 8, 128), lambda i: (i, 0, 0)),
            pl.BlockSpec((D, 1920), lambda i: (0, 0), pipeline_mode=pl.Buffered(1)),
        ],
        out_shape=[
            jax.ShapeDtypeStruct((4096, D), BF16), jax.ShapeDtypeStruct((4096, D), BF16),
            jax.ShapeDtypeStruct((32, 8, 128), F32), jax.ShapeDtypeStruct((D, 1920), BF16),
        ],
        scratch_shapes=[
            pltpu.VMEM((2, 1024, D), BF16), pltpu.VMEM((2, 1024, D), BF16), pltpu.VMEM((2, M, 128), F32),
            pltpu.VMEM((1024, 512), BF16), pltpu.VMEM((1024, 1024), BF16), pltpu.VMEM((1024, 128), BF16), pltpu.VMEM((1024, 256), BF16),
            pltpu.VMEM((2, M, D), BF16), pltpu.VMEM((2, M, D), BF16),
        ],
        compiler_params=pltpu.CompilerParams(vmem_limit_bytes=62 * 2**20),
        cost_estimate=pl.CostEstimate(flops=22 * 10**9, bytes_accessed=62 * 10**6, transcendentals=0),
    )(owned, tokens, cot, picks, router_t, w)


GATHER_DENSE = ((0, 0, 1280, 0), (0, 1280, 1280, 1), (1, 0, 768, 0), (1, 768, 896, 1), (2, 0, 128, 0))
TOKEN_HALVES = ((0, 0, 768, 0), (0, 768, 768, 1))
GATHER_TOKENS = TOKEN_HALVES + ((1, 0, 768, 0), (1, 768, 768, 1))
SCATTER_LAST = ((0, 0, 1280, 0), (0, 1280, 1280, 1), (1, 0, 768, 0), (1, 768, 896, 1), (2, 0, 768, 0), (2, 768, 768, 1))


def fast(
    layer_input, cotangent, sequence_ids, expert_ids, attention_gain, qkv_weight, output_weight, moe_gain, router, gate_up, down_proj
):
    n, own_rows, T = 32, gate_up.shape[0], layer_input.shape[0]
    group = QUERY_HEADS // KEY_VALUE_HEADS
    q_width, k_width = QUERY_HEADS * HEAD_WIDTH, KEY_VALUE_HEADS * HEAD_WIDTH
    me = lax.axis_index("fsdp")
    small = jnp.concatenate(
        [router, attention_gain[:, None], moe_gain[:, None], jnp.zeros((own_rows, 86), BF16)], axis=1
    )
    qkv_full, out_small, ids_all = gather(
        [qkv_weight, jnp.concatenate([output_weight, small], axis=1), expert_ids.T], GATHER_DENSE, 0
    )
    out_full, small_full = out_small[:, :D], out_small[:, D:]
    router_full, gain_one, gain_two = small_full[:, :E], small_full[:, E].astype(F32), small_full[:, E + 1].astype(F32)

    gu = jnp.transpose(gate_up, (1, 0, 2)).reshape(8, 5, own_rows, 2 * F)
    dp = jnp.transpose(down_proj, (1, 0, 2)).reshape(8, 5, own_rows, F)
    gu_q = jnp.transpose(gu[:, 4].reshape(8, own_rows, 2, 4, 128), (0, 3, 1, 2, 4)).reshape(n, own_rows, 256)
    dp_q = jnp.transpose(dp[:, 4].reshape(8, own_rows, 4, 128), (0, 2, 1, 3)).reshape(n, own_rows, 128)
    pack = jnp.concatenate(
        [gu[:, :4].reshape(n, own_rows, 2 * F), gu_q, dp[:, :4].reshape(n, own_rows, F), dp_q], axis=2
    )
    pack, qkv_full = lax.optimization_barrier((pack, qkv_full))
    w = lax.all_to_all(pack, "fsdp", split_axis=0, concat_axis=0, tiled=True).reshape(D, 1920)

    inputs = layer_input.astype(F32)
    scale_one = norm_scale(inputs)
    normed_one = (inputs * scale_one * gain_one).astype(BF16)
    joined = jnp.dot(normed_one, qkv_full, preferred_element_type=F32)
    cosine, sine = rope_tables(positions(sequence_ids), HEAD_WIDTH)
    queries = apply_rotary(joined[:, :q_width].reshape(T, QUERY_HEADS, HEAD_WIDTH), cosine, sine).astype(BF16)
    queries = queries.reshape(T, KEY_VALUE_HEADS, group, HEAD_WIDTH)
    keys = apply_rotary(joined[:, q_width : q_width + k_width].reshape(T, KEY_VALUE_HEADS, HEAD_WIDTH), cosine, sine).astype(BF16)
    values = joined[:, q_width + k_width :].reshape(T, KEY_VALUE_HEADS, HEAD_WIDTH).astype(BF16)
    place_in = jnp.arange(T, dtype=jnp.int32)
    allowed = (sequence_ids[:, None] == sequence_ids[None, :]) & (place_in[None, :] <= place_in[:, None])
    scores = jnp.einsum("qkgd,tkd->kgqt", queries, keys, preferred_element_type=F32) * ATTN_SCALE
    scores = jnp.where(allowed, scores, -jnp.inf)
    peak = jnp.max(scores, axis=-1, keepdims=True)
    log_total = peak + jnp.log(jnp.sum(jnp.exp(scores - peak), axis=-1, keepdims=True))
    probs = jnp.exp(scores - log_total)
    probs_half = probs.astype(BF16)
    attended = jnp.einsum("kgqt,tkd->qkgd", probs_half, values, preferred_element_type=F32).reshape(T, q_width).astype(BF16)
    middle = inputs + RESIDUAL_SCALE * jnp.dot(attended, out_full, preferred_element_type=F32)
    scale_two = norm_scale(middle)
    normed_two = (middle * scale_two * gain_two).astype(BF16)

    tokens, cots = gather([normed_two, cotangent], GATHER_TOKENS, 1)
    whole, fifth = (me // 4) * 5 + lax.rem(me, 4), (me // 4) * 5 + 4
    owned = jnp.stack([whole, fifth])
    named = jnp.any(ids_all.reshape(n, TOP, T)[:, :, None, :] == owned[None, None, :, None], axis=1)
    before = (place_in[:, None] < place_in[None, :]).astype(BF16)
    ranks = jnp.dot(named.astype(BF16).reshape(2 * n, T), before, preferred_element_type=F32).reshape(n, 2, 1, T)
    picks = ((ranks == jnp.arange(CAP, dtype=F32)[:, None]) & named[:, :, None, :]).astype(BF16).reshape(n * 64, T)
    router_t = jnp.pad(router_full.T, ((0, 64 - E), (0, 0)))
    out_part, gin_part, gg, dw = experts(owned, tokens, cots, picks, router_t, w)
    gg_all = lax.all_to_all(gg, "fsdp", split_axis=0, concat_axis=0, tiled=True).reshape(8, 4, 8, T)
    grad_gates = jnp.concatenate([gg_all[:, :, 0], jnp.sum(gg_all[:, :, 1], axis=1, keepdims=True)], axis=1).reshape(E, T).T
    [gin] = scatter([gin_part], TOKEN_HALVES, 2)
    dw, gin = lax.optimization_barrier((dw, gin))
    dw = lax.all_to_all(dw.reshape(n, own_rows, 1920), "fsdp", split_axis=0, concat_axis=0, tiled=True)

    upstream = cotangent.astype(F32)
    logits = jnp.dot(normed_two, router_full, preferred_element_type=F32)
    gate_probs = jax.nn.softmax(logits, axis=-1)
    grad_logits = gate_probs * (grad_gates - jnp.sum(gate_probs * grad_gates, axis=-1, keepdims=True))
    grad_normed = gin + jnp.einsum("te,de->td", grad_logits, router_full.astype(F32), precision=PRECISE_ARITHMETIC)
    router_part = jnp.einsum("td,te->de", normed_two.astype(F32), grad_logits, precision=PRECISE_ARITHMETIC)
    grad_middle, gain_two_part = norm_back(middle, gain_two, scale_two, grad_normed)
    grad_middle = grad_middle + upstream
    grad_branch = (RESIDUAL_SCALE * grad_middle).astype(BF16)

    out_grad_part = jnp.einsum("tq,td->qd", attended, grad_branch, preferred_element_type=F32)
    grad_attended = jnp.einsum("td,qd->tq", grad_branch, out_full, preferred_element_type=F32).astype(BF16)
    grad_heads = grad_attended.reshape(T, KEY_VALUE_HEADS, group, HEAD_WIDTH)
    row_delta = jnp.sum(grad_heads.astype(F32) * attended.reshape(grad_heads.shape).astype(F32), axis=-1)
    row_delta = jnp.transpose(row_delta, (1, 2, 0))[..., None]
    grad_values = jnp.einsum("kgqt,qkgd->tkd", probs_half, grad_heads, preferred_element_type=F32)
    grad_probs = jnp.einsum("qkgd,tkd->kgqt", grad_heads, values, preferred_element_type=F32)
    grad_scores = (probs * (grad_probs - row_delta) * ATTN_SCALE).astype(BF16)
    grad_queries = jnp.einsum("kgqt,tkd->qkgd", grad_scores, keys, preferred_element_type=F32)
    grad_keys = jnp.einsum("kgqt,qkgd->tkd", grad_scores, queries, preferred_element_type=F32)
    grad_joined = jnp.concatenate(
        [
            rotate_back(grad_queries.reshape(T, QUERY_HEADS, HEAD_WIDTH), cosine, sine).reshape(T, q_width),
            rotate_back(grad_keys, cosine, sine).reshape(T, k_width),
            grad_values.reshape(T, k_width),
        ],
        axis=-1,
    ).astype(BF16)
    qkv_part = jnp.einsum("td,tm->dm", normed_one, grad_joined, preferred_element_type=F32)
    grad_normed_one = jnp.einsum("tm,dm->td", grad_joined, qkv_full, preferred_element_type=F32)
    grad_inputs, gain_one_part = norm_back(inputs, gain_one, scale_one, grad_normed_one)
    input_grad = (grad_inputs + grad_middle).astype(BF16)

    out_small_part = jnp.concatenate(
        [out_grad_part, router_part, gain_one_part[:, None], gain_two_part[:, None], jnp.zeros((D, 86), F32)], axis=1
    ).astype(BF16)
    qkv_grad, out_small_grad, combined = scatter([qkv_part.astype(BF16), out_small_part, out_part], SCATTER_LAST, 3)
    layer_output = (middle + RESIDUAL_SCALE * combined).astype(BF16)

    part = lambda c0, c1: dw[:, :, c0:c1]
    gu_w = part(0, 1024).reshape(8, 4, own_rows, 1024)
    gu_f = jnp.transpose(part(1024, 1280).reshape(8, 4, own_rows, 2, 128), (0, 2, 3, 1, 4)).reshape(8, 1, own_rows, 1024)
    gate_up_grad = jnp.transpose(jnp.concatenate([gu_w, gu_f], axis=1).reshape(E, own_rows, 1024), (1, 0, 2)).astype(F32)
    dp_w = part(1280, 1792).reshape(8, 4, own_rows, F)
    dp_f = jnp.transpose(part(1792, 1920).reshape(8, 4, own_rows, 128), (0, 2, 1, 3)).reshape(8, 1, own_rows, F)
    down_grad = jnp.transpose(jnp.concatenate([dp_w, dp_f], axis=1).reshape(E, own_rows, F), (1, 0, 2)).astype(F32)
    return (
        layer_output,
        input_grad,
        out_small_grad[:, D + E],
        qkv_grad,
        out_small_grad[:, :D],
        out_small_grad[:, D + E + 1],
        out_small_grad[:, D : D + E],
        gate_up_grad,
        down_grad,
    )


def solution(mesh):
    rows, flat, cube = P("fsdp", None), P("fsdp"), P("fsdp", None, None)
    return jax.shard_map(
        fast if mesh.shape["fsdp"] == 32 else on_device,
        mesh=mesh,
        in_specs=(rows, rows, flat, rows, flat, rows, rows, flat, rows, cube, cube),
        out_specs=(rows, rows, flat, rows, rows, flat, rows, cube, cube),
        check_vma=False,
    )
```

```python
import functools
import math
import jax
import jax.numpy as jnp
import numpy as np
from jax import lax
from jax.experimental import pallas as pl
from jax.experimental.pallas import tpu as pltpu
from jax.sharding import PartitionSpec as P

MODEL_WIDTH = 1536
QUERY_HEADS = 24
KEY_VALUE_HEADS = 8
HEAD_WIDTH = 64
E = 40
F = 512
TOP = 8
CAP = 32


EPSILON = 1e-06
ATTN_SCALE = 0.015625
RESIDUAL_SCALE = 0.22
ROPE_BASE = 10000.0
PRECISE_ARITHMETIC = lax.Precision.HIGHEST


def positions(sequence_ids):
    sequence_length = sequence_ids.shape[0]
    places = jnp.arange(sequence_length, dtype=jnp.int32)
    same = (sequence_ids[:, None] == sequence_ids[None, :]) & (places[None, :] < places[:, None])
    return jnp.sum(same.astype(jnp.int32), axis=1, dtype=jnp.int32)


def rope_tables(places, head_size):
    half_size = head_size // 2
    exponents = jnp.arange(half_size, dtype=jnp.float32) * (2.0 / head_size)
    inverse = jnp.exp(exponents * -math.log(ROPE_BASE))
    angles = places.astype(jnp.float32)[:, None] * inverse[None, :]
    return (jnp.cos(angles), jnp.sin(angles))


def apply_rotary(tensor, cosine_lookup, sine_lookup):
    half_size = tensor.shape[-1] // 2
    first_half = tensor[..., :half_size]
    second_half = tensor[..., half_size:]
    cosine_rows = cosine_lookup[:, None, :]
    sine_rows = sine_lookup[:, None, :]
    return jnp.concatenate(
        [
            first_half * cosine_rows - second_half * sine_rows,
            second_half * cosine_rows + first_half * sine_rows,
        ],
        axis=-1,
    )


def rotate_back(tensor, cosine_lookup, sine_lookup):
    half_size = tensor.shape[-1] // 2
    first_half = tensor[..., :half_size]
    second_half = tensor[..., half_size:]
    cosine_rows = cosine_lookup[:, None, :]
    sine_rows = sine_lookup[:, None, :]
    return jnp.concatenate(
        [
            first_half * cosine_rows + second_half * sine_rows,
            second_half * cosine_rows - first_half * sine_rows,
        ],
        axis=-1,
    )


def norm_scale(hidden_state):
    return lax.rsqrt(jnp.mean(hidden_state * hidden_state, axis=-1, keepdims=True) + EPSILON)


def norm_back(hidden_state, gain_vector, scale_rows, upstream):
    weighted = upstream * gain_vector.astype(jnp.float32)
    inner_mean = jnp.mean(weighted * hidden_state, axis=-1, keepdims=True)
    grad_hidden = scale_rows * weighted - hidden_state * scale_rows**3 * inner_mean
    grad_gain = jnp.sum(upstream * hidden_state * scale_rows, axis=0)
    return (grad_hidden, grad_gain)


def expert_slots(expert_ids, experts, capacity):
    rows = expert_ids.shape[0]
    picked = expert_ids[:, :, None] == jnp.arange(experts, dtype=jnp.int32)[None, None, :]
    named = jnp.any(picked, axis=1).astype(jnp.bfloat16)
    places = jnp.arange(rows, dtype=jnp.int32)
    before = (places[None, :] < places[:, None]).astype(jnp.bfloat16)
    ranks = jnp.dot(before, named, preferred_element_type=jnp.float32)
    ranks = jnp.sum(jnp.where(picked, ranks[:, None, :], 0.0), axis=-1).astype(jnp.int32)
    return (expert_ids * capacity + ranks).reshape(-1)


def owner_tables(devices):
    width_owned = E * F // devices
    span_count = (F + width_owned - 2) // F + 1
    first_expert = np.arange(devices) * width_owned // F
    send_table = np.minimum(first_expert[:, None] + np.arange(span_count)[None, :], E).reshape(-1)
    combine_table = (send_table[None, :] == np.arange(E)[:, None]).astype(np.float32)
    return (width_owned, span_count, send_table, combine_table)


def dispatch_rows(buffer_rows, send_table, devices, span_count):
    padded = jnp.concatenate(
        [buffer_rows, jnp.zeros((1, CAP, MODEL_WIDTH), buffer_rows.dtype)], axis=0
    )
    chosen = jnp.asarray(send_table[:, None] == np.arange(E + 1)[None, :], dtype=buffer_rows.dtype)
    picked_rows = jnp.einsum(
        "se,ecd->scd", chosen, padded, preferred_element_type=jnp.float32
    ).astype(buffer_rows.dtype)
    return picked_rows.reshape(devices, span_count, CAP, MODEL_WIDTH)


def merge_entries(returned, combine_table):
    flat_rows = returned.reshape(returned.shape[0] * returned.shape[1], CAP * MODEL_WIDTH)
    summed = jnp.dot(
        jnp.asarray(combine_table),
        flat_rows,
        precision=PRECISE_ARITHMETIC,
        preferred_element_type=jnp.float32,
    )
    return summed.reshape(E, CAP, MODEL_WIDTH)


def on_device(
    layer_input,
    cotangent,
    sequence_ids,
    expert_ids,
    attention_gain,
    qkv_weight,
    output_weight,
    moe_gain,
    router,
    gate_up,
    down_proj,
):
    sequence_length = layer_input.shape[0]
    shard_rows = gate_up.shape[0]
    query_group_count = QUERY_HEADS // KEY_VALUE_HEADS
    query_feature_width = QUERY_HEADS * HEAD_WIDTH
    key_feature_width = KEY_VALUE_HEADS * HEAD_WIDTH
    rows_per_block = min(512, sequence_length)
    devices = lax.axis_size("fsdp")
    dense_set = (
        lax.all_gather(attention_gain, "fsdp", axis=0, tiled=True),
        lax.all_gather(qkv_weight, "fsdp", axis=0, tiled=True),
        lax.all_gather(output_weight, "fsdp", axis=0, tiled=True),
        lax.all_gather(moe_gain, "fsdp", axis=0, tiled=True),
        lax.all_gather(router, "fsdp", axis=0, tiled=True),
    )
    gain_one, qkv_full, out_full, gain_two, router_full = dense_set
    width_owned, span_count, send_table, combine_table = owner_tables(devices)
    gate_cols = jnp.transpose(gate_up.reshape(shard_rows, E, 2, F), (0, 2, 1, 3)).reshape(
        shard_rows, 2, E * F
    )
    down_cols = down_proj.reshape(shard_rows, 1, E * F)
    owned_weights = lax.all_to_all(
        jnp.concatenate([gate_cols, down_cols], axis=1),
        "fsdp",
        split_axis=2,
        concat_axis=0,
        tiled=True,
    )
    owned_gate_up = owned_weights[:, :2, :]
    owned_down = owned_weights[:, 2, :]
    owner_index = lax.axis_index("fsdp")
    owned_start = owner_index * width_owned
    owned_columns = owned_start + jnp.arange(width_owned, dtype=jnp.int32)
    slot_of = owned_columns // F - owned_start // F
    column_mask = (slot_of[None, :] == jnp.arange(span_count, dtype=jnp.int32)[:, None]).astype(
        jnp.float32
    )
    inputs = layer_input.astype(jnp.float32)
    scale_one = norm_scale(inputs)
    normed_one = (inputs * scale_one * gain_one.astype(jnp.float32)).astype(jnp.bfloat16)
    joined_projection = jnp.dot(normed_one, qkv_full, preferred_element_type=jnp.float32)
    places = positions(sequence_ids)
    cosine_lookup, sine_lookup = rope_tables(places, HEAD_WIDTH)
    query_rows = apply_rotary(
        joined_projection[:, :query_feature_width].reshape(
            sequence_length, QUERY_HEADS, HEAD_WIDTH
        ),
        cosine_lookup,
        sine_lookup,
    ).astype(jnp.bfloat16)
    query_rows = query_rows.reshape(sequence_length, KEY_VALUE_HEADS, query_group_count, HEAD_WIDTH)
    rotated_keys = apply_rotary(
        joined_projection[:, query_feature_width : query_feature_width + key_feature_width].reshape(
            sequence_length, KEY_VALUE_HEADS, HEAD_WIDTH
        ),
        cosine_lookup,
        sine_lookup,
    ).astype(jnp.bfloat16)
    value_inputs = (
        joined_projection[:, query_feature_width + key_feature_width :]
        .reshape(sequence_length, KEY_VALUE_HEADS, HEAD_WIDTH)
        .astype(jnp.bfloat16)
    )
    token_index = jnp.arange(sequence_length, dtype=jnp.int32)

    def block_scores(offset):
        scores = (
            jnp.einsum(
                "qkgd,tkd->kgqt", query_rows, rotated_keys, preferred_element_type=jnp.float32
            )
            * ATTN_SCALE
        )
        allowed = (
            sequence_ids[offset : offset + rows_per_block, None] == sequence_ids[None, :]
        ) & (token_index[None, :] <= token_index[offset : offset + rows_per_block, None])
        return jnp.where(allowed, scores, -jnp.inf)

    offset = 0
    scores = block_scores(offset)
    row_peak = jnp.max(scores, axis=-1, keepdims=True)
    log_total = row_peak + jnp.log(jnp.sum(jnp.exp(scores - row_peak), axis=-1, keepdims=True))
    probs_half = jnp.exp(scores - log_total).astype(jnp.bfloat16)
    mixed_heads = jnp.einsum(
        "kgqt,tkd->qkgd", probs_half, value_inputs, preferred_element_type=jnp.float32
    )
    attention_output_list = mixed_heads.reshape(rows_per_block, query_feature_width).astype(
        jnp.bfloat16
    )
    total_list = [log_total]
    branch = jnp.dot(attention_output_list, out_full, preferred_element_type=jnp.float32)
    middle = inputs + RESIDUAL_SCALE * branch
    scale_two = norm_scale(middle)
    normed_two = (middle * scale_two * gain_two.astype(jnp.float32)).astype(jnp.bfloat16)
    logits = jnp.dot(normed_two, router_full, preferred_element_type=jnp.float32)
    gate_probs = jax.nn.softmax(logits, axis=-1)
    picked = (expert_ids[:, :, None] == jnp.arange(E, dtype=jnp.int32)[None, None, :]).astype(
        jnp.float32
    )
    route_weight = jnp.einsum("tke,te->tk", picked, gate_probs, precision=PRECISE_ARITHMETIC)
    slot_rows = expert_slots(expert_ids, E, CAP)
    received_storage = (
        jnp.zeros((E * CAP, MODEL_WIDTH), jnp.bfloat16)
        .at[slot_rows]
        .set(jnp.repeat(normed_two, TOP, axis=0))
        .reshape(E, CAP, MODEL_WIDTH)
    )
    send_in = dispatch_rows(received_storage, send_table, devices, span_count)
    pre_cols = jnp.einsum(
        "nrkd,dgw->nrkgw",
        lax.all_to_all(send_in, "fsdp", split_axis=0, concat_axis=0, tiled=True),
        owned_gate_up,
        preferred_element_type=jnp.float32,
    )
    pre_cols = pre_cols * column_mask[None, :, None, None, :]
    gate_cols_pre = pre_cols[..., 0, :]
    up_cols_pre = pre_cols[..., 1, :]
    acted = (gate_cols_pre * jax.nn.sigmoid(gate_cols_pre) * up_cols_pre).astype(jnp.bfloat16)
    partial_out = jnp.einsum("nrkw,dw->nrkd", acted, owned_down, preferred_element_type=jnp.float32)
    returned_out = lax.all_to_all(partial_out, "fsdp", split_axis=0, concat_axis=0, tiled=True)
    buffer_out = merge_entries(returned_out, combine_table)
    routed_out = buffer_out.reshape(E * CAP, MODEL_WIDTH)[slot_rows].reshape(
        sequence_length, TOP, MODEL_WIDTH
    )
    combined = jnp.einsum("tk,tkd->td", route_weight, routed_out, precision=PRECISE_ARITHMETIC)
    layer_output = (middle + RESIDUAL_SCALE * combined).astype(jnp.bfloat16)
    upstream = cotangent.astype(jnp.float32)
    grad_mix = RESIDUAL_SCALE * upstream
    grad_weight = jnp.einsum("td,tkd->tk", grad_mix, routed_out, precision=PRECISE_ARITHMETIC)
    grad_rows = (
        (route_weight[:, :, None] * grad_mix[:, None, :])
        .astype(jnp.bfloat16)
        .reshape(sequence_length * TOP, MODEL_WIDTH)
    )
    buffer_grad = (
        jnp.zeros((E * CAP, MODEL_WIDTH), jnp.bfloat16)
        .at[slot_rows]
        .set(grad_rows)
        .reshape(E, CAP, MODEL_WIDTH)
    )
    gain_one_back, qkv_back, out_back, gain_two_back, router_back = dense_set
    send_grad = dispatch_rows(buffer_grad, send_table, devices, span_count)
    rows_in = lax.all_to_all(send_in, "fsdp", split_axis=0, concat_axis=0, tiled=True)
    rows_grad = lax.all_to_all(send_grad, "fsdp", split_axis=0, concat_axis=0, tiled=True)
    pre_cols = jnp.einsum(
        "nrkd,dgw->nrkgw", rows_in, owned_gate_up, preferred_element_type=jnp.float32
    )
    pre_cols = pre_cols * column_mask[None, :, None, None, :]
    gate_cols_pre = pre_cols[..., 0, :]
    up_cols_pre = pre_cols[..., 1, :]
    sigmoid_cols = jax.nn.sigmoid(gate_cols_pre)
    silu_cols = gate_cols_pre * sigmoid_cols
    acted = (silu_cols * up_cols_pre).astype(jnp.bfloat16)
    grad_act_cols = jnp.einsum(
        "nrkd,dw->nrkw", rows_grad, owned_down, preferred_element_type=jnp.float32
    )
    grad_gate_cols = (
        grad_act_cols * up_cols_pre * sigmoid_cols * (1.0 + gate_cols_pre * (1.0 - sigmoid_cols))
    )
    grad_up_cols = grad_act_cols * silu_cols
    grad_pair = jnp.stack([grad_gate_cols, grad_up_cols], axis=3).astype(jnp.bfloat16)
    partial_back = jnp.einsum(
        "nrkgw,dgw->nrkd", grad_pair, owned_gate_up, preferred_element_type=jnp.float32
    )
    returned_back = lax.all_to_all(partial_back, "fsdp", split_axis=0, concat_axis=0, tiled=True)
    results = (returned_back, rows_in, rows_grad, grad_pair, acted)
    returned_back, rows_in_all, rows_grad_all, grad_pair_all, acted_all = results
    backward_buffer = merge_entries(returned_back, combine_table)
    owned_gate_up_grad = jnp.einsum(
        "nrkd,nrkgw->dgw", rows_in_all, grad_pair_all, preferred_element_type=jnp.float32
    )
    owned_down_grad = jnp.einsum(
        "nrkd,nrkw->dw", rows_grad_all, acted_all, preferred_element_type=jnp.float32
    )
    owned_grads = jnp.concatenate([owned_gate_up_grad, owned_down_grad[:, None, :]], axis=1)
    relaid = lax.all_to_all(owned_grads, "fsdp", split_axis=0, concat_axis=2, tiled=True)
    gate_up_grad = jnp.transpose(
        relaid[:, :2, :].reshape(shard_rows, 2, E, F), (0, 2, 1, 3)
    ).reshape(shard_rows, E, 2 * F)
    down_grad = relaid[:, 2, :].reshape(shard_rows, E, F)
    grad_normed = jnp.sum(
        backward_buffer.reshape(E * CAP, MODEL_WIDTH)[slot_rows].reshape(
            sequence_length, TOP, MODEL_WIDTH
        ),
        axis=1,
    )
    grad_gates = jnp.einsum("tk,tke->te", grad_weight, picked, precision=PRECISE_ARITHMETIC)
    grad_logits = gate_probs * (
        grad_gates - jnp.sum(gate_probs * grad_gates, axis=-1, keepdims=True)
    )
    grad_normed = grad_normed + jnp.einsum(
        "te,de->td", grad_logits, router_back.astype(jnp.float32), precision=PRECISE_ARITHMETIC
    )
    router_part = jnp.einsum(
        "td,te->de", normed_two.astype(jnp.float32), grad_logits, precision=PRECISE_ARITHMETIC
    )
    grad_middle, gain_two_part = norm_back(middle, gain_two_back, scale_two, grad_normed)
    grad_middle = grad_middle + upstream
    grad_branch = (RESIDUAL_SCALE * grad_middle).astype(jnp.bfloat16)
    out_part = jnp.einsum(
        "tq,td->qd", attention_output_list, grad_branch, preferred_element_type=jnp.float32
    )
    attention_output_gradient = jnp.einsum(
        "td,qd->tq", grad_branch, out_back, preferred_element_type=jnp.float32
    ).astype(jnp.bfloat16)
    value_gradient = jnp.zeros((sequence_length, KEY_VALUE_HEADS, HEAD_WIDTH), jnp.float32)
    key_gradient = jnp.zeros((sequence_length, KEY_VALUE_HEADS, HEAD_WIDTH), jnp.float32)
    query_grads = []
    for block_number, offset in enumerate(range(0, sequence_length, rows_per_block)):
        scores = block_scores(offset)
        attn_probs = jnp.exp(scores - total_list[block_number])
        block_gradient = attention_output_gradient.reshape(
            rows_per_block, KEY_VALUE_HEADS, query_group_count, HEAD_WIDTH
        )
        attention_output_block = attention_output_list.reshape(
            rows_per_block, KEY_VALUE_HEADS, query_group_count, HEAD_WIDTH
        )
        row_delta = jnp.sum(
            block_gradient.astype(jnp.float32) * attention_output_block.astype(jnp.float32), axis=-1
        )
        row_delta = jnp.transpose(row_delta, (1, 2, 0))[..., None]
        value_gradient = jnp.einsum(
            "kgqt,qkgd->tkd",
            attn_probs.astype(jnp.bfloat16),
            block_gradient,
            preferred_element_type=jnp.float32,
        )
        grad_probs = jnp.einsum(
            "qkgd,tkd->kgqt", block_gradient, value_inputs, preferred_element_type=jnp.float32
        )
        grad_scores = (attn_probs * (grad_probs - row_delta) * ATTN_SCALE).astype(jnp.bfloat16)
        query_grads.append(
            jnp.einsum(
                "kgqt,tkd->qkgd", grad_scores, rotated_keys, preferred_element_type=jnp.float32
            )
        )
        key_gradient = jnp.einsum(
            "kgqt,qkgd->tkd", grad_scores, query_rows, preferred_element_type=jnp.float32
        )
    grad_queries = query_grads[0].reshape(sequence_length, QUERY_HEADS, HEAD_WIDTH)
    grad_joined = jnp.concatenate(
        [
            rotate_back(grad_queries, cosine_lookup, sine_lookup).reshape(
                sequence_length, query_feature_width
            ),
            rotate_back(key_gradient, cosine_lookup, sine_lookup).reshape(
                sequence_length, key_feature_width
            ),
            value_gradient.reshape(sequence_length, key_feature_width),
        ],
        axis=-1,
    ).astype(jnp.bfloat16)
    qkv_part = jnp.einsum("td,tm->dm", normed_one, grad_joined, preferred_element_type=jnp.float32)
    grad_normed_one = jnp.einsum(
        "tm,dm->td", grad_joined, qkv_back, preferred_element_type=jnp.float32
    )
    grad_inputs, gain_one_part = norm_back(inputs, gain_one_back, scale_one, grad_normed_one)
    input_grad = (grad_inputs + grad_middle).astype(jnp.bfloat16)
    dense_grads = (
        lax.psum_scatter(gain_one_part, "fsdp", scatter_dimension=0, tiled=True),
        lax.psum_scatter(qkv_part, "fsdp", scatter_dimension=0, tiled=True),
        lax.psum_scatter(out_part, "fsdp", scatter_dimension=0, tiled=True),
        lax.psum_scatter(gain_two_part, "fsdp", scatter_dimension=0, tiled=True),
        lax.psum_scatter(router_part, "fsdp", scatter_dimension=0, tiled=True),
    )
    return (
        layer_output,
        input_grad,
        dense_grads[0],
        dense_grads[1],
        dense_grads[2],
        dense_grads[3],
        dense_grads[4],
        gate_up_grad,
        down_grad,
    )


MESH = pl.DeviceIdType.MESH
DEVICES = 32
TURNS = tuple(sorted(range(1, DEVICES), key=lambda k: (k % 8 * 5 % 8, k)))

def place():
    me = lax.axis_index("fsdp")
    return me // 8, lax.rem(me // 4, 2), lax.rem(me // 2, 2), lax.rem(me, 2)

def dev(z, y, x, c):
    return ((z * 2 + y) * 2 + x) * 2 + c

def z_order(z, q):
    table = ((0, 1, 2, 3), (1, 0, 2, 3), (2, 3, 1, 0), (3, 2, 1, 0))
    v = jnp.int32(table[0][q])
    for k in range(1, 4):
        v = jnp.where(z == k, table[k][q], v)
    return v

def greet(z, near, up, down):
    barrier = pltpu.get_barrier_semaphore()
    for d in near:
        pl.semaphore_signal(barrier, inc=1, device_id=(d,), device_id_type=MESH)
    @pl.when(z < 3)
    def _():
        pl.semaphore_signal(barrier, inc=1, device_id=(up,), device_id_type=MESH)
    @pl.when(z > 0)
    def _():
        pl.semaphore_signal(barrier, inc=1, device_id=(down,), device_id_type=MESH)
    pl.semaphore_wait(barrier, len(near) + jnp.where(z < 3, 1, 0) + jnp.where(z > 0, 1, 0))

def greet_all():
    me = lax.axis_index("fsdp")
    barrier = pltpu.get_barrier_semaphore()
    for k in range(1, DEVICES):
        pl.semaphore_signal(barrier, inc=1, device_id=(lax.rem(me + k, DEVICES),), device_id_type=MESH)
    pl.semaphore_wait(barrier, DEVICES - 1)

def rc(src, dst, ss, rs, to):
    return pltpu.make_async_remote_copy(src_ref=src, dst_ref=dst, send_sem=ss, recv_sem=rs, device_id=(to,), device_id_type=MESH)

class Direct:
    def __init__(self, pieces, refs, sems):
        self.pieces, self.refs, (self.ss, self.rs, self.ls) = pieces, refs, sems
        self.me = lax.axis_index("fsdp")

    def own(self):
        self.local = [pltpu.make_async_copy(a, b, self.ls.at[i]) for i, (a, b) in enumerate(self.pieces(self.me, self.me, self.refs))]
        for l in self.local:
            l.start()

    def start(self, turns):
        for k in turns:
            to = lax.rem(self.me + k, DEVICES)
            for i, (a, b) in enumerate(self.pieces(self.me, to, self.refs)):
                rc(a, b, self.ss.at[k, i], self.rs.at[k, i], to).start()

    def finish(self):
        for k in TURNS:
            src = lax.rem(self.me + DEVICES - k, DEVICES)
            for i, (a, b) in enumerate(self.pieces(src, self.me, self.refs)):
                rc(a, b, self.ss.at[k, i], self.rs.at[k, i], src).wait_recv()
        for k in TURNS:
            to = lax.rem(self.me + k, DEVICES)
            for i, (a, b) in enumerate(self.pieces(self.me, to, self.refs)):
                rc(a, b, self.ss.at[k, i], self.rs.at[k, i], to).wait_send()
        for l in self.local:
            l.wait()

    @staticmethod
    def scratch(count):
        dma = pltpu.SemaphoreType.DMA
        return [dma((DEVICES, count)), dma((DEVICES, count)), dma((count,))]

def gather_kernel(parts, count, extra, *refs):
    pieces, n_in, n_out, batches = extra or (None, 0, 0, ())
    shards, refs = refs[:count], refs[count:]
    extra_in, refs = refs[:n_in], refs[n_in:]
    outs, refs = refs[:count], refs[count:]
    extra_out, refs = refs[:n_out], refs[n_out:]
    (local_sem, zs, zs2, zr, fs, fr, s1s, s1r, s2s, s2r, cs, cr), sems = refs[:12], refs[12:]
    z, y, x, c = place()
    sib, xn, yn = dev(z, y, x, 1 - c), dev(z, y, 1 - x, c), dev(z, 1 - y, x, c)
    up, down = dev(z + 1, y, x, c), dev(z - 1, y, x, c)
    if extra:
        greet_all()
        direct = Direct(pieces, extra_in + extra_out, sems)
    else:
        greet(z, (sib, xn, yn), up, down)

    def at(p, d):
        a, c0, w, _ = parts[p]
        rows = shards[a].shape[0]
        return outs[a].at[pl.ds(pl.multiple_of(d * rows, rows), rows), pl.ds(c0, w)]

    def own(p):
        a, c0, w, _ = parts[p]
        return shards[a].at[:, pl.ds(c0, w)]

    me = dev(z, y, x, c)
    P = len(parts)
    zq = [z_order(z, q) for q in range(4)]
    sends = []
    def go(copy):
        copy.start()
        sends.append(copy)

    def stage1(q):
        for p in range(P):
            first, second = (xn, yn) if parts[p][3] == 0 else (yn, xn)
            here = at(p, dev(zq[q], y, x, c))
            if q == 0:
                src = own(p)
                @pl.when(z < 3)
                def _():
                    rc(src, here, zs.at[0, p], zr.at[z, p], up).start()
                @pl.when(z > 0)
                def _():
                    rc(src, here, zs2.at[p], zr.at[z, p], down).start()
            else:
                src = here
                rc(here, here, zs.at[q, p], zr.at[zq[q], p], up).wait_recv()
                @pl.when((zq[q] < z) & (z < 3))
                def _():
                    rc(src, here, zs.at[q, p], zr.at[zq[q], p], up).start()
                @pl.when((zq[q] > z) & (z > 0))
                def _():
                    rc(src, here, zs.at[q, p], zr.at[zq[q], p], down).start()
            go(rc(src, here, fs.at[q, p], fr.at[q, p], first))
            go(rc(src, here, s1s.at[q, p], s1r.at[q, p], second))
            go(rc(src, here, cs.at[0, q, p], cr.at[0, q, p], sib))

    def spot(p, q, k, core):
        flip_x, flip_y = ((0, 0), (1, 0), (0, 1), (1, 1))[k] if parts[p][3] == 0 else ((0, 0), (0, 1), (1, 0), (1, 1))[k]
        return at(p, dev(zq[q], 1 - y if flip_y else y, 1 - x if flip_x else x, core))

    def stage2(q):
        for p in range(P):
            second = yn if parts[p][3] == 0 else xn
            there = spot(p, q, 1, c)
            rc(there, there, fs.at[q, p], fr.at[q, p], second).wait_recv()
            go(rc(there, there, s2s.at[q, p], s2r.at[q, p], second))
            go(rc(there, there, cs.at[1, q, p], cr.at[1, q, p], sib))

    def stage3(q):
        for k, (ss, rs) in ((2, (s1s, s1r)), (3, (s2s, s2r))):
            for p in range(P):
                there = spot(p, q, k, c)
                rc(there, there, ss.at[q, p], rs.at[q, p], sib).wait_recv()
                go(rc(there, there, cs.at[k, q, p], cr.at[k, q, p], sib))

    locals_ = []
    for step, (f, q) in enumerate(((1, 0), (1, 1), (2, 0), (1, 2), (2, 1), (3, 0), (1, 3), (2, 2), (3, 1), (2, 3), (3, 2), (3, 3))):
        (stage1, stage2, stage3)[f - 1](q)
        if step == 0:
            for a in range(count):
                rows = shards[a].shape[0]
                l = pltpu.make_async_copy(shards[a], outs[a].at[pl.ds(pl.multiple_of(me * rows, rows), rows)], local_sem.at[a])
                l.start()
                locals_.append(l)
            if extra:
                direct.own()
        if extra and step < len(batches):
            lo = sum(batches[:step])
            direct.start(TURNS[lo:lo + batches[step]])
    for q in range(4):
        for k in range(4):
            for p in range(P):
                there = spot(p, q, k, 1 - c)
                rc(there, there, cs.at[k, q, p], cr.at[k, q, p], sib).wait_recv()
    for copy in sends:
        copy.wait_send()
    for p in range(P):
        here = at(p, me)
        @pl.when(z < 3)
        def _():
            rc(here, here, zs.at[0, p], zr.at[z, p], up).wait_send()
        @pl.when(z > 0)
        def _():
            rc(here, here, zs2.at[p], zr.at[z, p], down).wait_send()
        for q in range(1, 4):
            @pl.when(((zq[q] < z) & (z < 3)) | ((zq[q] > z) & (z > 0)))
            def _():
                rc(here, here, zs.at[q, p], zr.at[zq[q], p], up).wait_send()
    for l in locals_:
        l.wait()
    if extra:
        direct.finish()

def gather(arrays, parts, collective_id, extra=None, extra_in=(), extra_out=()):
    k, P = len(arrays), len(parts)
    dma = pltpu.SemaphoreType.DMA
    if extra:
        pieces, count, batches = extra
        extra = (pieces, len(extra_in), len(extra_out), batches)
    return pl.pallas_call(
        functools.partial(gather_kernel, parts, k, extra),
        out_shape=[jax.ShapeDtypeStruct((DEVICES * a.shape[0],) + a.shape[1:], a.dtype) for a in arrays] + list(extra_out),
        in_specs=[pl.BlockSpec(memory_space=pl.ANY)] * (k + len(extra_in)),
        out_specs=[pl.BlockSpec(memory_space=pl.ANY)] * (k + len(extra_out)),
        scratch_shapes=[dma((k,)), dma((4, P)), dma((P,))] + [dma((4, P))] * 7 + [dma((4, 4, P))] * 2 + (Direct.scratch(count) if extra else []),
        compiler_params=pltpu.CompilerParams(collective_id=collective_id, has_side_effects=True),
    )(*arrays, *extra_in)


def scatter_kernel(parts, count, rows, extra, *refs):
    pieces, n_in, n_out, batches = extra or (None, 0, 0, ())
    fulls, refs = refs[:count], refs[count:]
    extra_in, refs = refs[:n_in], refs[n_in:]
    outs, refs = refs[:count], refs[count:]
    extra_out, refs = refs[:n_out], refs[n_out:]
    held, r0, r1, r2, r3 = (refs[i * count:(i + 1) * count] for i in range(5))
    refs = refs[5 * count:]
    (ls, s0, e0, s1, e1, s2, e2, s3, e3), sems = refs[:9], refs[9:]
    z, y, x, c = place()
    sib, xn, yn = dev(z, y, x, 1 - c), dev(z, y, 1 - x, c), dev(z, 1 - y, x, c)
    up, down = dev(z + 1, y, x, c), dev(z - 1, y, x, c)
    if extra:
        greet_all()
        direct = Direct(pieces, extra_in + extra_out, sems)
    else:
        greet(z, (sib, xn, yn), up, down)

    P = len(parts)
    zq = [z_order(z, q) for q in range(4)]
    sends = []
    def go(copy):
        copy.start()
        sends.append(copy)
    def cut(p):
        return pl.ds(parts[p][1], parts[p][2])
    def spot(p, k):
        if parts[p][3] == 0:
            return ((1 - y, 1 - x), (1 - y, x), (y, 1 - x), (y, x))[k]
        return ((1 - y, 1 - x), (y, 1 - x), (1 - y, x), (y, x))[k]
    def slot(q, yy, xx):
        return (yy * 2 + xx) * 4 + zq[q]
    def source(p, q, k, core):
        a = parts[p][0]
        yy, xx = spot(p, k)
        d = dev(zq[q], yy, xx, core)
        return fulls[a].at[pl.ds(pl.multiple_of(d * rows[a], rows[a]), rows[a]), cut(p)]

    loads = {}
    for q in (3, 2, 1, 0):
        for k in range(4):
            for p in range(P):
                a = parts[p][0]
                s = slot(q, *spot(p, k))
                go(rc(source(p, q, k, 1 - c), r0[a].at[s, :, cut(p)], s0.at[q, k, p], e0.at[q, k, p], sib))
                l = pltpu.make_async_copy(source(p, q, k, c), held[a].at[s, :, cut(p)], ls.at[q, k, p])
                l.start()
                loads[q, k, p] = l
    if extra:
        direct.own()

    STEP = 16
    def chunks(a, body):
        def one(i, carry):
            body(pl.ds(pl.multiple_of(i * STEP, STEP), STEP))
            return carry
        lax.fori_loop(0, rows[a] // STEP, one, 0)

    def add(p, s, src, s_src):
        a, c0, w, _ = parts[p]
        dst = held[a]
        def body(r):
            v = dst[s, r, c0:c0 + w].astype(jnp.float32) + src[s_src, r, c0:c0 + w].astype(jnp.float32)
            dst[s, r, c0:c0 + w] = v.astype(dst.dtype)
        chunks(a, body)

    def stage1(q):
        for k in range(4):
            for p in range(P):
                a = parts[p][0]
                first = yn if parts[p][3] == 0 else xn
                s = slot(q, *spot(p, k))
                here = held[a].at[s, :, cut(p)]
                rc(here, r0[a].at[s, :, cut(p)], s0.at[q, k, p], e0.at[q, k, p], sib).wait_recv()
                loads[q, k, p].wait()
                add(p, s, r0[a], s)
                if k < 2:
                    go(rc(here, r1[a].at[q * 2 + k, :, cut(p)], s1.at[q, k, p], e1.at[q, k, p], first))

    def stage2(q):
        for k in range(2):
            for p in range(P):
                a = parts[p][0]
                second = xn if parts[p][3] == 0 else yn
                s = slot(q, *spot(p, k + 2))
                here = held[a].at[s, :, cut(p)]
                rc(here, r1[a].at[q * 2 + k, :, cut(p)], s1.at[q, k, p], e1.at[q, k, p], sib).wait_recv()
                add(p, s, r1[a], q * 2 + k)
                if k == 0:
                    go(rc(here, r2[a].at[q, :, cut(p)], s2.at[q, p], e2.at[q, p], second))

    def stage3(q):
        for p in range(P):
            a, c0, w, _ = parts[p]
            s = slot(q, y, x)
            here = held[a].at[s, :, cut(p)]
            rc(here, r2[a].at[q, :, cut(p)], s2.at[q, p], e2.at[q, p], sib).wait_recv()
            add(p, s, r2[a], q)
            if q > 0:
                @pl.when((zq[q] > z) & (z > 0) | (zq[q] < z) & (z < 3))
                def _():
                    land = r3[a].at[zq[q], :, cut(p)]
                    rc(here, land, s3.at[q, p], e3.at[zq[q], p], sib).wait_recv()
                    add(p, s, r3[a], zq[q])
                @pl.when(zq[q] > z)
                def _():
                    rc(here, r3[a].at[zq[q], :, cut(p)], s3.at[q, p], e3.at[zq[q], p], up).start()
                @pl.when((zq[q] < z) & (zq[q] == z - 1))
                def _():
                    rc(here, r3[a].at[4, :, cut(p)], s3.at[q, p], e3.at[4, p], down).start()
                @pl.when(zq[q] < z - 1)
                def _():
                    rc(here, r3[a].at[zq[q], :, cut(p)], s3.at[q, p], e3.at[zq[q], p], down).start()
            else:
                def first_sum(r):
                    outs[a][r, c0:c0 + w] = held[a][s, r, c0:c0 + w].astype(jnp.float32)
                chunks(a, first_sum)
                for cond, where in ((z > 0, z), (z < 3, 4)):
                    @pl.when(cond)
                    def _():
                        rc(here, r3[a].at[where, :, cut(p)], s3.at[q, p], e3.at[where, p], sib).wait_recv()
                        def more(r):
                            outs[a][r, c0:c0 + w] += r3[a][where, r, c0:c0 + w].astype(jnp.float32)
                        chunks(a, more)

    for step, (f, q) in enumerate(((1, 3), (1, 2), (2, 3), (1, 1), (2, 2), (3, 3), (1, 0), (2, 1), (3, 2), (2, 0), (3, 1), (3, 0))):
        (stage1, stage2, stage3)[f - 1](q)
        if extra and step < len(batches):
            lo = sum(batches[:step])
            direct.start(TURNS[lo:lo + batches[step]])
    for copy in sends:
        copy.wait_send()
    for q in range(1, 4):
        for p in range(P):
            a = parts[p][0]
            here = held[a].at[slot(q, y, x), :, cut(p)]
            rc(here, here, s3.at[q, p], e3.at[0, p], sib).wait_send()
    if extra:
        direct.finish()

def scatter(arrays, parts, collective_id, extra=None, extra_in=(), extra_out=()):
    k, P = len(arrays), len(parts)
    dma = pltpu.SemaphoreType.DMA
    rows = [a.shape[0] // DEVICES for a in arrays]
    if extra:
        pieces, number, batches = extra
        extra = (pieces, len(extra_in), len(extra_out), batches)
    spaces = []
    for cnt in (16, 16, 8, 4, 5):
        spaces += [pltpu.VMEM((cnt, r, a.shape[1]), a.dtype) for r, a in zip(rows, arrays)]
    hbm, vmem = pl.BlockSpec(memory_space=pl.ANY), pl.BlockSpec(memory_space=pltpu.VMEM)
    return pl.pallas_call(
        functools.partial(scatter_kernel, parts, k, rows, extra),
        out_shape=[jax.ShapeDtypeStruct((r, a.shape[1]), jnp.float32) for r, a in zip(rows, arrays)] + list(extra_out),
        in_specs=[hbm] * (k + len(extra_in)),
        out_specs=[vmem] * k + [hbm] * len(extra_out),
        scratch_shapes=spaces + [dma((4, 4, P))] * 3 + [dma((4, 2, P))] * 2 + [dma((4, P))] * 3 + [dma((5, P))] + (Direct.scratch(number) if extra else []),
        compiler_params=pltpu.CompilerParams(collective_id=collective_id, has_side_effects=True, vmem_limit_bytes=60 * 2**20),
    )(*arrays, *extra_in)


D = MODEL_WIDTH
SRC = 8
STEPS = 4
M = SRC * CAP
F32, BF16 = jnp.float32, jnp.bfloat16

def nt(a, b):
    return lax.dot_general(a, b, (((1,), (1,)), ((), ())), preferred_element_type=F32)
def nn(a, b):
    return lax.dot_general(a, b, (((1,), (0,)), ((), ())), preferred_element_type=F32)
def tn(a, b):
    return lax.dot_general(a, b, (((0,), (0,)), ((), ())), preferred_element_type=F32)

QUARTER, DOWN_WHOLE, DOWN_QUARTER, OWN_WIDTH = 0, 256, 768, 896

def expert_kernel(own_ref, t_ref, c_ref, pick_ref, router_ref, wf_ref, wo_ref, out_ref, gin_ref, gg_ref, dwf_ref, dwo_ref,
                  x_ref, g_ref, rw_ref, act_ref, dgu_ref, actq_ref, dguq_ref, ow_ref, gi_ref):
    i = pl.program_id(0)
    mine = (own_ref[0], own_ref[1])
    logits = nt(router_ref[...], t_ref[...])
    row = lax.broadcasted_iota(jnp.int32, logits.shape, 0)
    logits = jnp.where(row < E, logits, -jnp.inf)
    e = jnp.exp(logits - jnp.max(logits, axis=0, keepdims=True))
    probs = e / jnp.sum(e, axis=0, keepdims=True)
    mineprob = [jnp.sum(jnp.where(row == m, probs, 0.0), axis=0, keepdims=True) for m in mine]
    at = pl.ds(pl.multiple_of(i * M, M), M)
    for s in range(SRC):
        pick = pick_ref[s * 64:s * 64 + 64, :]
        xs = nn(pick, t_ref[s * 128:s * 128 + 128, :]).astype(BF16)
        gs = nn(pick, c_ref[s * 128:s * 128 + 128, :]).astype(BF16)
        wide = pick.astype(F32)
        for k in range(2):
            to = pl.ds(pl.multiple_of(i * M + s * CAP, CAP), CAP)
            x_ref[k, to, :] = xs[k * 32:k * 32 + 32]
            g_ref[k, to, :] = gs[k * 32:k * 32 + 32]
            rw_ref[k, s * CAP:s * CAP + CAP, :] = jnp.broadcast_to(jnp.sum(wide[k * 32:k * 32 + 32] * mineprob[k][:, s * 128:(s + 1) * 128], axis=1, keepdims=True), (CAP, 128))
    gws = []
    sets = (
        (act_ref, dgu_ref, 512, wf_ref[...], wo_ref[:, DOWN_WHOLE:DOWN_WHOLE + 512]),
        (actq_ref, dguq_ref, 128, wo_ref[:, QUARTER:QUARTER + 256], wo_ref[:, DOWN_QUARTER:DOWN_QUARTER + 128]),
    )
    for k, (acts, dgus, w, w_gu, w_d) in enumerate(sets):
        pre = nn(x_ref[k, at, :], w_gu)
        gate, up = pre[:, :w], pre[:, w:]
        sig = jax.nn.sigmoid(gate)
        silu = gate * sig
        act = silu * up
        share = rw_ref[k, :, 0:1] * RESIDUAL_SCALE
        scaled = (share * act).astype(BF16)
        acts[at, :] = scaled
        da = nn(g_ref[k, at, :], w_d)
        gws.append(RESIDUAL_SCALE * jnp.sum(act.astype(BF16).astype(F32) * da, axis=1, keepdims=True))
        ow_ref[k] = nt(scaled, w_d).astype(BF16)
        da = share * da
        dgu = jnp.concatenate([(da * up * sig * (1.0 + gate * (1.0 - sig))).astype(BF16), (da * silu).astype(BF16)], axis=1)
        dgus[at, :] = dgu
        gi_ref[k] = nt(dgu, w_gu).astype(BF16)
    for s in range(SRC):
        r = slice(s * CAP, s * CAP + CAP)
        pick = pick_ref[s * 64:s * 64 + 64, :]
        to = slice(s * 128, s * 128 + 128)
        out_ref[to, :] = tn(pick, jnp.concatenate([ow_ref[0, r, :], ow_ref[1, r, :]], axis=0)).astype(BF16)
        gin_ref[to, :] = tn(pick, jnp.concatenate([gi_ref[0, r, :], gi_ref[1, r, :]], axis=0)).astype(BF16)
        wide = pick.astype(F32)
        for k in range(2):
            gg_ref[s, k:k + 1, :] = jnp.sum(wide[k * 32:k * 32 + 32] * gws[k][r], axis=0, keepdims=True)
        gg_ref[s, 2:8, :] = jnp.zeros((6, 128), F32)

    @pl.when(i == STEPS - 1)
    def _():
        def body(j, carry):
            c = pl.ds(pl.multiple_of(j * 256, 256), 256)
            dwf_ref[c, :] = tn(x_ref[0, :, c], dgu_ref[...]).astype(BF16)
            dwo_ref[c, QUARTER:QUARTER + 256] = tn(x_ref[1, :, c], dguq_ref[...]).astype(BF16)
            dwo_ref[c, DOWN_WHOLE:DOWN_WHOLE + 512] = tn(g_ref[0, :, c], act_ref[...]).astype(BF16)
            dwo_ref[c, DOWN_QUARTER:DOWN_QUARTER + 128] = tn(g_ref[1, :, c], actq_ref[...]).astype(BF16)
            return carry
        lax.fori_loop(0, D // 256, body, 0)

def experts(owned, tokens, cot, picks, router_t, wf, wo):
    R = SRC * 128
    once = lambda shape: pl.BlockSpec(shape, lambda i: (0, 0), pipeline_mode=pl.Buffered(1))
    rows = pl.BlockSpec((R, D), lambda i: (i, 0))
    vmem = lambda *shape, dtype=BF16: pltpu.VMEM(shape, dtype)
    return pl.pallas_call(
        expert_kernel,
        grid=(STEPS,),
        in_specs=[
            pl.BlockSpec(memory_space=pltpu.SMEM), rows, rows, pl.BlockSpec((SRC * 64, 128), lambda i: (i, 0)),
            once((64, D)), once((D, 2 * F)), once((D, OWN_WIDTH)),
        ],
        out_specs=[rows, rows, pl.BlockSpec((SRC, 8, 128), lambda i: (i, 0, 0)), once((D, 2 * F)), once((D, OWN_WIDTH))],
        out_shape=[
            jax.ShapeDtypeStruct((4096, D), BF16), jax.ShapeDtypeStruct((4096, D), BF16), jax.ShapeDtypeStruct((32, 8, 128), F32),
            jax.ShapeDtypeStruct((D, 2 * F), BF16), jax.ShapeDtypeStruct((D, OWN_WIDTH), BF16),
        ],
        scratch_shapes=[
            vmem(2, 1024, D), vmem(2, 1024, D), vmem(2, M, 128, dtype=F32),
            vmem(1024, 512), vmem(1024, 1024), vmem(1024, 128), vmem(1024, 256), vmem(2, M, D), vmem(2, M, D),
        ],
        compiler_params=pltpu.CompilerParams(vmem_limit_bytes=62 * 2**20),
        cost_estimate=pl.CostEstimate(flops=22 * 10**9, bytes_accessed=62 * 10**6, transcendentals=0),
    )(owned, tokens, cot, picks, router_t, wf, wo)


TOKEN_HALVES = ((0, 0, 768, 0), (0, 768, 768, 1))
GATHER_FIRST = ((0, 0, 1280, 0), (0, 1280, 1280, 1), (1, 0, 768, 0), (1, 768, 768, 1), (2, 0, 128, 1), (3, 0, 128, 0), (4, 0, 768, 0), (4, 768, 768, 1))
SCATTER_LAST = ((0, 0, 1280, 0), (0, 1280, 1280, 1), (1, 0, 768, 0), (1, 768, 768, 1), (2, 0, 128, 0), (3, 0, 768, 0), (3, 768, 768, 1))
OUT_BATCHES = (2, 2, 2, 3, 3, 3, 4, 4, 4, 4)
BACK_BATCHES = (3, 3, 3, 3, 3, 3, 3, 3, 3, 4)


def lanes(start):
    return pl.ds(pl.multiple_of(start, 128), 128)


def weights_out(src, dst, refs):
    g_ref, d_ref, wo_ref = refs
    group, quarter = dst // 4, lax.rem(dst, 4) * 128
    rows = pl.ds(pl.multiple_of(src * 48, 48), 48)
    fifth = group * 5 + 4
    return (
        (g_ref.at[fifth, :, lanes(quarter)], wo_ref.at[rows, pl.ds(QUARTER, 128)]),
        (g_ref.at[fifth, :, lanes(F + quarter)], wo_ref.at[rows, pl.ds(QUARTER + 128, 128)]),
        (d_ref.at[group * 5 + lax.rem(dst, 4)], wo_ref.at[rows, pl.ds(DOWN_WHOLE, F)]),
        (d_ref.at[fifth, :, lanes(quarter)], wo_ref.at[rows, pl.ds(DOWN_QUARTER, 128)]),
    )


def grads_back(src, dst, refs):
    dwo_ref, gates_ref, g_ref, d_ref, all_gates_ref = refs
    group, quarter = src // 4, lax.rem(src, 4) * 128
    rows = pl.ds(pl.multiple_of(dst * 48, 48), 48)
    return (
        (dwo_ref.at[rows, pl.ds(QUARTER, 128)], g_ref.at[group, :, lanes(quarter)]),
        (dwo_ref.at[rows, pl.ds(QUARTER + 128, 128)], g_ref.at[group, :, lanes(F + quarter)]),
        (dwo_ref.at[rows, pl.ds(DOWN_WHOLE, F)], d_ref.at[group * 5 + lax.rem(src, 4)]),
        (dwo_ref.at[rows, pl.ds(DOWN_QUARTER, 128)], d_ref.at[group * 5 + 4, :, lanes(quarter)]),
        (gates_ref.at[dst], all_gates_ref.at[src]),
    )


def fast(
    layer_input, cotangent, sequence_ids, expert_ids, attention_gain, qkv_weight, output_weight, moe_gain, router, gate_up, down_proj
):
    n, own_rows, T = 32, gate_up.shape[0], layer_input.shape[0]
    group = QUERY_HEADS // KEY_VALUE_HEADS
    q_width, k_width = QUERY_HEADS * HEAD_WIDTH, KEY_VALUE_HEADS * HEAD_WIDTH
    me = lax.axis_index("fsdp")
    small = jnp.concatenate(
        [router, attention_gain[:, None], moe_gain[:, None], jnp.zeros((own_rows, 86), BF16)], axis=1
    )
    gu = jnp.transpose(gate_up, (1, 0, 2))
    dp = jnp.transpose(down_proj, (1, 0, 2))
    qkv_full, out_full, small_full, ids_all, cots, wo = gather(
        [qkv_weight, output_weight, small, expert_ids.T, cotangent],
        GATHER_FIRST,
        0,
        (weights_out, 4, OUT_BATCHES),
        (gu, dp),
        (jax.ShapeDtypeStruct((D, OWN_WIDTH), BF16),),
    )
    router_full, gain_one, gain_two = small_full[:, :E], small_full[:, E].astype(F32), small_full[:, E + 1].astype(F32)
    whole = gu.reshape(8, 5, own_rows, 2 * F)[:, :4].reshape(n, own_rows, 2 * F)
    whole, qkv_full = lax.optimization_barrier((whole, qkv_full))
    wf = lax.all_to_all(whole, "fsdp", split_axis=0, concat_axis=0, tiled=True).reshape(D, 2 * F)

    inputs = layer_input.astype(F32)
    scale_one = norm_scale(inputs)
    normed_one = (inputs * scale_one * gain_one).astype(BF16)
    joined = jnp.dot(normed_one, qkv_full, preferred_element_type=F32)
    cosine, sine = rope_tables(positions(sequence_ids), HEAD_WIDTH)
    queries = apply_rotary(joined[:, :q_width].reshape(T, QUERY_HEADS, HEAD_WIDTH), cosine, sine).astype(BF16)
    queries = queries.reshape(T, KEY_VALUE_HEADS, group, HEAD_WIDTH)
    keys = apply_rotary(joined[:, q_width : q_width + k_width].reshape(T, KEY_VALUE_HEADS, HEAD_WIDTH), cosine, sine).astype(BF16)
    values = joined[:, q_width + k_width :].reshape(T, KEY_VALUE_HEADS, HEAD_WIDTH).astype(BF16)
    place_in = jnp.arange(T, dtype=jnp.int32)
    allowed = (sequence_ids[:, None] == sequence_ids[None, :]) & (place_in[None, :] <= place_in[:, None])
    scores = jnp.einsum("qkgd,tkd->kgqt", queries, keys, preferred_element_type=F32) * ATTN_SCALE
    scores = jnp.where(allowed, scores, -jnp.inf)
    peak = jnp.max(scores, axis=-1, keepdims=True)
    log_total = peak + jnp.log(jnp.sum(jnp.exp(scores - peak), axis=-1, keepdims=True))
    probs = jnp.exp(scores - log_total)
    probs_half = probs.astype(BF16)
    attended = jnp.einsum("kgqt,tkd->qkgd", probs_half, values, preferred_element_type=F32).reshape(T, q_width).astype(BF16)
    middle = inputs + RESIDUAL_SCALE * jnp.dot(attended, out_full, preferred_element_type=F32)
    scale_two = norm_scale(middle)
    normed_two = (middle * scale_two * gain_two).astype(BF16)

    [tokens] = gather([normed_two], TOKEN_HALVES, 1)
    owned = jnp.stack([(me // 4) * 5 + lax.rem(me, 4), (me // 4) * 5 + 4])
    named = jnp.any(ids_all.reshape(n, TOP, T)[:, :, None, :] == owned[None, None, :, None], axis=1)
    before = (place_in[:, None] < place_in[None, :]).astype(BF16)
    ranks = jnp.dot(named.astype(BF16).reshape(2 * n, T), before, preferred_element_type=F32).reshape(n, 2, 1, T)
    picks = ((ranks == jnp.arange(CAP, dtype=F32)[:, None]) & named[:, :, None, :]).astype(BF16).reshape(n * 64, T)
    router_t = jnp.pad(router_full.T, ((0, 64 - E), (0, 0)))
    out_part, gin_part, gg, dwf, dwo = experts(owned, tokens, cots, picks, router_t, wf, wo)
    gin, grad_fifth, grad_down, gg_all = scatter(
        [gin_part],
        TOKEN_HALVES,
        2,
        (grads_back, 5, BACK_BATCHES),
        (dwo, gg),
        (jax.ShapeDtypeStruct((8, own_rows, 2 * F), BF16), jax.ShapeDtypeStruct((E, own_rows, F), BF16), jax.ShapeDtypeStruct((n, 8, T), F32)),
    )
    gg_all = gg_all.reshape(8, 4, 8, T)
    grad_gates = jnp.concatenate([gg_all[:, :, 0], jnp.sum(gg_all[:, :, 1], axis=1, keepdims=True)], axis=1).reshape(E, T).T
    dwf, gin = lax.optimization_barrier((dwf, gin))
    grad_whole = lax.all_to_all(dwf.reshape(n, own_rows, 2 * F), "fsdp", split_axis=0, concat_axis=0, tiled=True)

    upstream = cotangent.astype(F32)
    logits = jnp.dot(normed_two, router_full, preferred_element_type=F32)
    gate_probs = jax.nn.softmax(logits, axis=-1)
    grad_logits = gate_probs * (grad_gates - jnp.sum(gate_probs * grad_gates, axis=-1, keepdims=True))
    grad_normed = gin + jnp.einsum("te,de->td", grad_logits, router_full.astype(F32), precision=PRECISE_ARITHMETIC)
    router_part = jnp.einsum("td,te->de", normed_two.astype(F32), grad_logits, precision=PRECISE_ARITHMETIC)
    grad_middle, gain_two_part = norm_back(middle, gain_two, scale_two, grad_normed)
    grad_middle = grad_middle + upstream
    grad_branch = (RESIDUAL_SCALE * grad_middle).astype(BF16)

    out_grad_part = jnp.einsum("tq,td->qd", attended, grad_branch, preferred_element_type=F32)
    grad_attended = jnp.einsum("td,qd->tq", grad_branch, out_full, preferred_element_type=F32).astype(BF16)
    grad_heads = grad_attended.reshape(T, KEY_VALUE_HEADS, group, HEAD_WIDTH)
    row_delta = jnp.sum(grad_heads.astype(F32) * attended.reshape(grad_heads.shape).astype(F32), axis=-1)
    row_delta = jnp.transpose(row_delta, (1, 2, 0))[..., None]
    grad_values = jnp.einsum("kgqt,qkgd->tkd", probs_half, grad_heads, preferred_element_type=F32)
    grad_probs = jnp.einsum("qkgd,tkd->kgqt", grad_heads, values, preferred_element_type=F32)
    grad_scores = (probs * (grad_probs - row_delta) * ATTN_SCALE).astype(BF16)
    grad_queries = jnp.einsum("kgqt,tkd->qkgd", grad_scores, keys, preferred_element_type=F32)
    grad_keys = jnp.einsum("kgqt,qkgd->tkd", grad_scores, queries, preferred_element_type=F32)
    grad_joined = jnp.concatenate(
        [
            rotate_back(grad_queries.reshape(T, QUERY_HEADS, HEAD_WIDTH), cosine, sine).reshape(T, q_width),
            rotate_back(grad_keys, cosine, sine).reshape(T, k_width),
            grad_values.reshape(T, k_width),
        ],
        axis=-1,
    ).astype(BF16)
    qkv_part = jnp.einsum("td,tm->dm", normed_one, grad_joined, preferred_element_type=F32)
    grad_normed_one = jnp.einsum("tm,dm->td", grad_joined, qkv_full, preferred_element_type=F32)
    grad_inputs, gain_one_part = norm_back(inputs, gain_one, scale_one, grad_normed_one)
    input_grad = (grad_inputs + grad_middle).astype(BF16)

    small_part = jnp.concatenate(
        [router_part, gain_one_part[:, None], gain_two_part[:, None], jnp.zeros((D, 86), F32)], axis=1
    ).astype(BF16)
    qkv_grad, out_grad, small_grad, combined = scatter(
        [qkv_part.astype(BF16), out_grad_part.astype(BF16), small_part, out_part], SCATTER_LAST, 3
    )
    layer_output = (middle + combined).astype(BF16)

    grad_gu = jnp.concatenate([grad_whole.reshape(8, 4, own_rows, 2 * F), grad_fifth[:, None]], axis=1)
    gate_up_grad = jnp.transpose(grad_gu.reshape(E, own_rows, 2 * F), (1, 0, 2)).astype(F32)
    down_grad = jnp.transpose(grad_down, (1, 0, 2)).astype(F32)
    return (
        layer_output,
        input_grad,
        small_grad[:, E],
        qkv_grad,
        out_grad,
        small_grad[:, E + 1],
        small_grad[:, :E],
        gate_up_grad,
        down_grad,
    )


def solution(mesh):
    rows, flat, cube = P("fsdp", None), P("fsdp"), P("fsdp", None, None)
    return jax.shard_map(
        fast if mesh.shape["fsdp"] == 32 else on_device,
        mesh=mesh,
        in_specs=(rows, rows, flat, rows, flat, rows, rows, flat, rows, cube, cube),
        out_specs=(rows, rows, flat, rows, rows, flat, rows, cube, cube),
        check_vma=False,
    )
```

```python
import functools
import math
import jax
import jax.numpy as jnp
import numpy as np
from jax import lax
from jax.experimental import pallas as pl
from jax.experimental.pallas import tpu as pltpu
from jax.sharding import PartitionSpec as P

MODEL_WIDTH = 1536
QUERY_HEADS = 24
KEY_VALUE_HEADS = 8
HEAD_WIDTH = 64
E = 40
F = 512
TOP = 8
CAP = 32


EPSILON = 1e-06
ATTN_SCALE = 0.015625
RESIDUAL_SCALE = 0.22
ROPE_BASE = 10000.0
PRECISE_ARITHMETIC = lax.Precision.HIGHEST


def positions(sequence_ids):
    sequence_length = sequence_ids.shape[0]
    places = jnp.arange(sequence_length, dtype=jnp.int32)
    same = (sequence_ids[:, None] == sequence_ids[None, :]) & (places[None, :] < places[:, None])
    return jnp.sum(same.astype(jnp.int32), axis=1, dtype=jnp.int32)


def rope_tables(places, head_size):
    half_size = head_size // 2
    exponents = jnp.arange(half_size, dtype=jnp.float32) * (2.0 / head_size)
    inverse = jnp.exp(exponents * -math.log(ROPE_BASE))
    angles = places.astype(jnp.float32)[:, None] * inverse[None, :]
    return (jnp.cos(angles), jnp.sin(angles))


def apply_rotary(tensor, cosine_lookup, sine_lookup):
    half_size = tensor.shape[-1] // 2
    first_half = tensor[..., :half_size]
    second_half = tensor[..., half_size:]
    cosine_rows = cosine_lookup[:, None, :]
    sine_rows = sine_lookup[:, None, :]
    return jnp.concatenate(
        [
            first_half * cosine_rows - second_half * sine_rows,
            second_half * cosine_rows + first_half * sine_rows,
        ],
        axis=-1,
    )


def rotate_back(tensor, cosine_lookup, sine_lookup):
    half_size = tensor.shape[-1] // 2
    first_half = tensor[..., :half_size]
    second_half = tensor[..., half_size:]
    cosine_rows = cosine_lookup[:, None, :]
    sine_rows = sine_lookup[:, None, :]
    return jnp.concatenate(
        [
            first_half * cosine_rows + second_half * sine_rows,
            second_half * cosine_rows - first_half * sine_rows,
        ],
        axis=-1,
    )


def norm_scale(hidden_state):
    return lax.rsqrt(jnp.mean(hidden_state * hidden_state, axis=-1, keepdims=True) + EPSILON)


def norm_back(hidden_state, gain_vector, scale_rows, upstream):
    weighted = upstream * gain_vector.astype(jnp.float32)
    inner_mean = jnp.mean(weighted * hidden_state, axis=-1, keepdims=True)
    grad_hidden = scale_rows * weighted - hidden_state * scale_rows**3 * inner_mean
    grad_gain = jnp.sum(upstream * hidden_state * scale_rows, axis=0)
    return (grad_hidden, grad_gain)


def expert_slots(expert_ids, experts, capacity):
    rows = expert_ids.shape[0]
    picked = expert_ids[:, :, None] == jnp.arange(experts, dtype=jnp.int32)[None, None, :]
    named = jnp.any(picked, axis=1).astype(jnp.bfloat16)
    places = jnp.arange(rows, dtype=jnp.int32)
    before = (places[None, :] < places[:, None]).astype(jnp.bfloat16)
    ranks = jnp.dot(before, named, preferred_element_type=jnp.float32)
    ranks = jnp.sum(jnp.where(picked, ranks[:, None, :], 0.0), axis=-1).astype(jnp.int32)
    return (expert_ids * capacity + ranks).reshape(-1)


def owner_tables(devices):
    width_owned = E * F // devices
    span_count = (F + width_owned - 2) // F + 1
    first_expert = np.arange(devices) * width_owned // F
    send_table = np.minimum(first_expert[:, None] + np.arange(span_count)[None, :], E).reshape(-1)
    combine_table = (send_table[None, :] == np.arange(E)[:, None]).astype(np.float32)
    return (width_owned, span_count, send_table, combine_table)


def dispatch_rows(buffer_rows, send_table, devices, span_count):
    padded = jnp.concatenate(
        [buffer_rows, jnp.zeros((1, CAP, MODEL_WIDTH), buffer_rows.dtype)], axis=0
    )
    chosen = jnp.asarray(send_table[:, None] == np.arange(E + 1)[None, :], dtype=buffer_rows.dtype)
    picked_rows = jnp.einsum(
        "se,ecd->scd", chosen, padded, preferred_element_type=jnp.float32
    ).astype(buffer_rows.dtype)
    return picked_rows.reshape(devices, span_count, CAP, MODEL_WIDTH)


def merge_entries(returned, combine_table):
    flat_rows = returned.reshape(returned.shape[0] * returned.shape[1], CAP * MODEL_WIDTH)
    summed = jnp.dot(
        jnp.asarray(combine_table),
        flat_rows,
        precision=PRECISE_ARITHMETIC,
        preferred_element_type=jnp.float32,
    )
    return summed.reshape(E, CAP, MODEL_WIDTH)


def on_device(
    layer_input,
    cotangent,
    sequence_ids,
    expert_ids,
    attention_gain,
    qkv_weight,
    output_weight,
    moe_gain,
    router,
    gate_up,
    down_proj,
):
    sequence_length = layer_input.shape[0]
    shard_rows = gate_up.shape[0]
    query_group_count = QUERY_HEADS // KEY_VALUE_HEADS
    query_feature_width = QUERY_HEADS * HEAD_WIDTH
    key_feature_width = KEY_VALUE_HEADS * HEAD_WIDTH
    rows_per_block = min(512, sequence_length)
    devices = lax.axis_size("fsdp")
    dense_set = (
        lax.all_gather(attention_gain, "fsdp", axis=0, tiled=True),
        lax.all_gather(qkv_weight, "fsdp", axis=0, tiled=True),
        lax.all_gather(output_weight, "fsdp", axis=0, tiled=True),
        lax.all_gather(moe_gain, "fsdp", axis=0, tiled=True),
        lax.all_gather(router, "fsdp", axis=0, tiled=True),
    )
    gain_one, qkv_full, out_full, gain_two, router_full = dense_set
    width_owned, span_count, send_table, combine_table = owner_tables(devices)
    gate_cols = jnp.transpose(gate_up.reshape(shard_rows, E, 2, F), (0, 2, 1, 3)).reshape(
        shard_rows, 2, E * F
    )
    down_cols = down_proj.reshape(shard_rows, 1, E * F)
    owned_weights = lax.all_to_all(
        jnp.concatenate([gate_cols, down_cols], axis=1),
        "fsdp",
        split_axis=2,
        concat_axis=0,
        tiled=True,
    )
    owned_gate_up = owned_weights[:, :2, :]
    owned_down = owned_weights[:, 2, :]
    owner_index = lax.axis_index("fsdp")
    owned_start = owner_index * width_owned
    owned_columns = owned_start + jnp.arange(width_owned, dtype=jnp.int32)
    slot_of = owned_columns // F - owned_start // F
    column_mask = (slot_of[None, :] == jnp.arange(span_count, dtype=jnp.int32)[:, None]).astype(
        jnp.float32
    )
    inputs = layer_input.astype(jnp.float32)
    scale_one = norm_scale(inputs)
    normed_one = (inputs * scale_one * gain_one.astype(jnp.float32)).astype(jnp.bfloat16)
    joined_projection = jnp.dot(normed_one, qkv_full, preferred_element_type=jnp.float32)
    places = positions(sequence_ids)
    cosine_lookup, sine_lookup = rope_tables(places, HEAD_WIDTH)
    query_rows = apply_rotary(
        joined_projection[:, :query_feature_width].reshape(
            sequence_length, QUERY_HEADS, HEAD_WIDTH
        ),
        cosine_lookup,
        sine_lookup,
    ).astype(jnp.bfloat16)
    query_rows = query_rows.reshape(sequence_length, KEY_VALUE_HEADS, query_group_count, HEAD_WIDTH)
    rotated_keys = apply_rotary(
        joined_projection[:, query_feature_width : query_feature_width + key_feature_width].reshape(
            sequence_length, KEY_VALUE_HEADS, HEAD_WIDTH
        ),
        cosine_lookup,
        sine_lookup,
    ).astype(jnp.bfloat16)
    value_inputs = (
        joined_projection[:, query_feature_width + key_feature_width :]
        .reshape(sequence_length, KEY_VALUE_HEADS, HEAD_WIDTH)
        .astype(jnp.bfloat16)
    )
    token_index = jnp.arange(sequence_length, dtype=jnp.int32)

    def block_scores(offset):
        scores = (
            jnp.einsum(
                "qkgd,tkd->kgqt", query_rows, rotated_keys, preferred_element_type=jnp.float32
            )
            * ATTN_SCALE
        )
        allowed = (
            sequence_ids[offset : offset + rows_per_block, None] == sequence_ids[None, :]
        ) & (token_index[None, :] <= token_index[offset : offset + rows_per_block, None])
        return jnp.where(allowed, scores, -jnp.inf)

    offset = 0
    scores = block_scores(offset)
    row_peak = jnp.max(scores, axis=-1, keepdims=True)
    log_total = row_peak + jnp.log(jnp.sum(jnp.exp(scores - row_peak), axis=-1, keepdims=True))
    probs_half = jnp.exp(scores - log_total).astype(jnp.bfloat16)
    mixed_heads = jnp.einsum(
        "kgqt,tkd->qkgd", probs_half, value_inputs, preferred_element_type=jnp.float32
    )
    attention_output_list = mixed_heads.reshape(rows_per_block, query_feature_width).astype(
        jnp.bfloat16
    )
    total_list = [log_total]
    branch = jnp.dot(attention_output_list, out_full, preferred_element_type=jnp.float32)
    middle = inputs + RESIDUAL_SCALE * branch
    scale_two = norm_scale(middle)
    normed_two = (middle * scale_two * gain_two.astype(jnp.float32)).astype(jnp.bfloat16)
    logits = jnp.dot(normed_two, router_full, preferred_element_type=jnp.float32)
    gate_probs = jax.nn.softmax(logits, axis=-1)
    picked = (expert_ids[:, :, None] == jnp.arange(E, dtype=jnp.int32)[None, None, :]).astype(
        jnp.float32
    )
    route_weight = jnp.einsum("tke,te->tk", picked, gate_probs, precision=PRECISE_ARITHMETIC)
    slot_rows = expert_slots(expert_ids, E, CAP)
    received_storage = (
        jnp.zeros((E * CAP, MODEL_WIDTH), jnp.bfloat16)
        .at[slot_rows]
        .set(jnp.repeat(normed_two, TOP, axis=0))
        .reshape(E, CAP, MODEL_WIDTH)
    )
    send_in = dispatch_rows(received_storage, send_table, devices, span_count)
    pre_cols = jnp.einsum(
        "nrkd,dgw->nrkgw",
        lax.all_to_all(send_in, "fsdp", split_axis=0, concat_axis=0, tiled=True),
        owned_gate_up,
        preferred_element_type=jnp.float32,
    )
    pre_cols = pre_cols * column_mask[None, :, None, None, :]
    gate_cols_pre = pre_cols[..., 0, :]
    up_cols_pre = pre_cols[..., 1, :]
    acted = (gate_cols_pre * jax.nn.sigmoid(gate_cols_pre) * up_cols_pre).astype(jnp.bfloat16)
    partial_out = jnp.einsum("nrkw,dw->nrkd", acted, owned_down, preferred_element_type=jnp.float32)
    returned_out = lax.all_to_all(partial_out, "fsdp", split_axis=0, concat_axis=0, tiled=True)
    buffer_out = merge_entries(returned_out, combine_table)
    routed_out = buffer_out.reshape(E * CAP, MODEL_WIDTH)[slot_rows].reshape(
        sequence_length, TOP, MODEL_WIDTH
    )
    combined = jnp.einsum("tk,tkd->td", route_weight, routed_out, precision=PRECISE_ARITHMETIC)
    layer_output = (middle + RESIDUAL_SCALE * combined).astype(jnp.bfloat16)
    upstream = cotangent.astype(jnp.float32)
    grad_mix = RESIDUAL_SCALE * upstream
    grad_weight = jnp.einsum("td,tkd->tk", grad_mix, routed_out, precision=PRECISE_ARITHMETIC)
    grad_rows = (
        (route_weight[:, :, None] * grad_mix[:, None, :])
        .astype(jnp.bfloat16)
        .reshape(sequence_length * TOP, MODEL_WIDTH)
    )
    buffer_grad = (
        jnp.zeros((E * CAP, MODEL_WIDTH), jnp.bfloat16)
        .at[slot_rows]
        .set(grad_rows)
        .reshape(E, CAP, MODEL_WIDTH)
    )
    gain_one_back, qkv_back, out_back, gain_two_back, router_back = dense_set
    send_grad = dispatch_rows(buffer_grad, send_table, devices, span_count)
    rows_in = lax.all_to_all(send_in, "fsdp", split_axis=0, concat_axis=0, tiled=True)
    rows_grad = lax.all_to_all(send_grad, "fsdp", split_axis=0, concat_axis=0, tiled=True)
    pre_cols = jnp.einsum(
        "nrkd,dgw->nrkgw", rows_in, owned_gate_up, preferred_element_type=jnp.float32
    )
    pre_cols = pre_cols * column_mask[None, :, None, None, :]
    gate_cols_pre = pre_cols[..., 0, :]
    up_cols_pre = pre_cols[..., 1, :]
    sigmoid_cols = jax.nn.sigmoid(gate_cols_pre)
    silu_cols = gate_cols_pre * sigmoid_cols
    acted = (silu_cols * up_cols_pre).astype(jnp.bfloat16)
    grad_act_cols = jnp.einsum(
        "nrkd,dw->nrkw", rows_grad, owned_down, preferred_element_type=jnp.float32
    )
    grad_gate_cols = (
        grad_act_cols * up_cols_pre * sigmoid_cols * (1.0 + gate_cols_pre * (1.0 - sigmoid_cols))
    )
    grad_up_cols = grad_act_cols * silu_cols
    grad_pair = jnp.stack([grad_gate_cols, grad_up_cols], axis=3).astype(jnp.bfloat16)
    partial_back = jnp.einsum(
        "nrkgw,dgw->nrkd", grad_pair, owned_gate_up, preferred_element_type=jnp.float32
    )
    returned_back = lax.all_to_all(partial_back, "fsdp", split_axis=0, concat_axis=0, tiled=True)
    results = (returned_back, rows_in, rows_grad, grad_pair, acted)
    returned_back, rows_in_all, rows_grad_all, grad_pair_all, acted_all = results
    backward_buffer = merge_entries(returned_back, combine_table)
    owned_gate_up_grad = jnp.einsum(
        "nrkd,nrkgw->dgw", rows_in_all, grad_pair_all, preferred_element_type=jnp.float32
    )
    owned_down_grad = jnp.einsum(
        "nrkd,nrkw->dw", rows_grad_all, acted_all, preferred_element_type=jnp.float32
    )
    owned_grads = jnp.concatenate([owned_gate_up_grad, owned_down_grad[:, None, :]], axis=1)
    relaid = lax.all_to_all(owned_grads, "fsdp", split_axis=0, concat_axis=2, tiled=True)
    gate_up_grad = jnp.transpose(
        relaid[:, :2, :].reshape(shard_rows, 2, E, F), (0, 2, 1, 3)
    ).reshape(shard_rows, E, 2 * F)
    down_grad = relaid[:, 2, :].reshape(shard_rows, E, F)
    grad_normed = jnp.sum(
        backward_buffer.reshape(E * CAP, MODEL_WIDTH)[slot_rows].reshape(
            sequence_length, TOP, MODEL_WIDTH
        ),
        axis=1,
    )
    grad_gates = jnp.einsum("tk,tke->te", grad_weight, picked, precision=PRECISE_ARITHMETIC)
    grad_logits = gate_probs * (
        grad_gates - jnp.sum(gate_probs * grad_gates, axis=-1, keepdims=True)
    )
    grad_normed = grad_normed + jnp.einsum(
        "te,de->td", grad_logits, router_back.astype(jnp.float32), precision=PRECISE_ARITHMETIC
    )
    router_part = jnp.einsum(
        "td,te->de", normed_two.astype(jnp.float32), grad_logits, precision=PRECISE_ARITHMETIC
    )
    grad_middle, gain_two_part = norm_back(middle, gain_two_back, scale_two, grad_normed)
    grad_middle = grad_middle + upstream
    grad_branch = (RESIDUAL_SCALE * grad_middle).astype(jnp.bfloat16)
    out_part = jnp.einsum(
        "tq,td->qd", attention_output_list, grad_branch, preferred_element_type=jnp.float32
    )
    attention_output_gradient = jnp.einsum(
        "td,qd->tq", grad_branch, out_back, preferred_element_type=jnp.float32
    ).astype(jnp.bfloat16)
    value_gradient = jnp.zeros((sequence_length, KEY_VALUE_HEADS, HEAD_WIDTH), jnp.float32)
    key_gradient = jnp.zeros((sequence_length, KEY_VALUE_HEADS, HEAD_WIDTH), jnp.float32)
    query_grads = []
    for block_number, offset in enumerate(range(0, sequence_length, rows_per_block)):
        scores = block_scores(offset)
        attn_probs = jnp.exp(scores - total_list[block_number])
        block_gradient = attention_output_gradient.reshape(
            rows_per_block, KEY_VALUE_HEADS, query_group_count, HEAD_WIDTH
        )
        attention_output_block = attention_output_list.reshape(
            rows_per_block, KEY_VALUE_HEADS, query_group_count, HEAD_WIDTH
        )
        row_delta = jnp.sum(
            block_gradient.astype(jnp.float32) * attention_output_block.astype(jnp.float32), axis=-1
        )
        row_delta = jnp.transpose(row_delta, (1, 2, 0))[..., None]
        value_gradient = jnp.einsum(
            "kgqt,qkgd->tkd",
            attn_probs.astype(jnp.bfloat16),
            block_gradient,
            preferred_element_type=jnp.float32,
        )
        grad_probs = jnp.einsum(
            "qkgd,tkd->kgqt", block_gradient, value_inputs, preferred_element_type=jnp.float32
        )
        grad_scores = (attn_probs * (grad_probs - row_delta) * ATTN_SCALE).astype(jnp.bfloat16)
        query_grads.append(
            jnp.einsum(
                "kgqt,tkd->qkgd", grad_scores, rotated_keys, preferred_element_type=jnp.float32
            )
        )
        key_gradient = jnp.einsum(
            "kgqt,qkgd->tkd", grad_scores, query_rows, preferred_element_type=jnp.float32
        )
    grad_queries = query_grads[0].reshape(sequence_length, QUERY_HEADS, HEAD_WIDTH)
    grad_joined = jnp.concatenate(
        [
            rotate_back(grad_queries, cosine_lookup, sine_lookup).reshape(
                sequence_length, query_feature_width
            ),
            rotate_back(key_gradient, cosine_lookup, sine_lookup).reshape(
                sequence_length, key_feature_width
            ),
            value_gradient.reshape(sequence_length, key_feature_width),
        ],
        axis=-1,
    ).astype(jnp.bfloat16)
    qkv_part = jnp.einsum("td,tm->dm", normed_one, grad_joined, preferred_element_type=jnp.float32)
    grad_normed_one = jnp.einsum(
        "tm,dm->td", grad_joined, qkv_back, preferred_element_type=jnp.float32
    )
    grad_inputs, gain_one_part = norm_back(inputs, gain_one_back, scale_one, grad_normed_one)
    input_grad = (grad_inputs + grad_middle).astype(jnp.bfloat16)
    dense_grads = (
        lax.psum_scatter(gain_one_part, "fsdp", scatter_dimension=0, tiled=True),
        lax.psum_scatter(qkv_part, "fsdp", scatter_dimension=0, tiled=True),
        lax.psum_scatter(out_part, "fsdp", scatter_dimension=0, tiled=True),
        lax.psum_scatter(gain_two_part, "fsdp", scatter_dimension=0, tiled=True),
        lax.psum_scatter(router_part, "fsdp", scatter_dimension=0, tiled=True),
    )
    return (
        layer_output,
        input_grad,
        dense_grads[0],
        dense_grads[1],
        dense_grads[2],
        dense_grads[3],
        dense_grads[4],
        gate_up_grad,
        down_grad,
    )


D = MODEL_WIDTH
SRC = 8
STEPS = 4
M = SRC * CAP
F32, BF16 = jnp.float32, jnp.bfloat16

def nt(a, b):
    return lax.dot_general(a, b, (((1,), (1,)), ((), ())), preferred_element_type=F32)
def nn(a, b):
    return lax.dot_general(a, b, (((1,), (0,)), ((), ())), preferred_element_type=F32)
def tn(a, b):
    return lax.dot_general(a, b, (((0,), (0,)), ((), ())), preferred_element_type=F32)

QUARTER, DOWN_WHOLE, DOWN_QUARTER, OWN_WIDTH = 0, 256, 768, 896

def expert_kernel(own_ref, t_ref, c_ref, pick_ref, router_ref, wf_ref, wo_ref, out_ref, gin_ref, gg_ref, dwf_ref, dwo_ref,
                  x_ref, g_ref, rw_ref, act_ref, dgu_ref, actq_ref, dguq_ref, ow_ref, gi_ref):
    i = pl.program_id(0)
    mine = (own_ref[0], own_ref[1])
    logits = nt(router_ref[...], t_ref[...])
    row = lax.broadcasted_iota(jnp.int32, logits.shape, 0)
    logits = jnp.where(row < E, logits, -jnp.inf)
    e = jnp.exp(logits - jnp.max(logits, axis=0, keepdims=True))
    probs = e / jnp.sum(e, axis=0, keepdims=True)
    mineprob = [jnp.sum(jnp.where(row == m, probs, 0.0), axis=0, keepdims=True) for m in mine]
    at = pl.ds(pl.multiple_of(i * M, M), M)
    for s in range(SRC):
        pick = pick_ref[s * 64:s * 64 + 64, :]
        xs = nn(pick, t_ref[s * 128:s * 128 + 128, :]).astype(BF16)
        gs = nn(pick, c_ref[s * 128:s * 128 + 128, :]).astype(BF16)
        wide = pick.astype(F32)
        for k in range(2):
            to = pl.ds(pl.multiple_of(i * M + s * CAP, CAP), CAP)
            x_ref[k, to, :] = xs[k * 32:k * 32 + 32]
            g_ref[k, to, :] = gs[k * 32:k * 32 + 32]
            rw_ref[k, s * CAP:s * CAP + CAP, :] = jnp.broadcast_to(jnp.sum(wide[k * 32:k * 32 + 32] * mineprob[k][:, s * 128:(s + 1) * 128], axis=1, keepdims=True), (CAP, 128))
    gws = []
    sets = (
        (act_ref, dgu_ref, 512, wf_ref[...], wo_ref[:, DOWN_WHOLE:DOWN_WHOLE + 512]),
        (actq_ref, dguq_ref, 128, wo_ref[:, QUARTER:QUARTER + 256], wo_ref[:, DOWN_QUARTER:DOWN_QUARTER + 128]),
    )
    for k, (acts, dgus, w, w_gu, w_d) in enumerate(sets):
        pre = nn(x_ref[k, at, :], w_gu)
        gate, up = pre[:, :w], pre[:, w:]
        sig = jax.nn.sigmoid(gate)
        silu = gate * sig
        act = silu * up
        share = rw_ref[k, :, 0:1] * RESIDUAL_SCALE
        scaled = (share * act).astype(BF16)
        acts[at, :] = scaled
        da = nn(g_ref[k, at, :], w_d)
        gws.append(RESIDUAL_SCALE * jnp.sum(act.astype(BF16).astype(F32) * da, axis=1, keepdims=True))
        ow_ref[k] = nt(scaled, w_d).astype(BF16)
        da = share * da
        dgu = jnp.concatenate([(da * up * sig * (1.0 + gate * (1.0 - sig))).astype(BF16), (da * silu).astype(BF16)], axis=1)
        dgus[at, :] = dgu
        gi_ref[k] = nt(dgu, w_gu).astype(BF16)
    for s in range(SRC):
        r = slice(s * CAP, s * CAP + CAP)
        pick = pick_ref[s * 64:s * 64 + 64, :]
        to = slice(s * 128, s * 128 + 128)
        out_ref[to, :] = tn(pick, jnp.concatenate([ow_ref[0, r, :], ow_ref[1, r, :]], axis=0)).astype(BF16)
        gin_ref[to, :] = tn(pick, jnp.concatenate([gi_ref[0, r, :], gi_ref[1, r, :]], axis=0)).astype(BF16)
        wide = pick.astype(F32)
        for k in range(2):
            gg_ref[s, k:k + 1, :] = jnp.sum(wide[k * 32:k * 32 + 32] * gws[k][r], axis=0, keepdims=True)
        gg_ref[s, 2:8, :] = jnp.zeros((6, 128), F32)

    @pl.when(i == STEPS - 1)
    def _():
        def body(j, carry):
            c = pl.ds(pl.multiple_of(j * 256, 256), 256)
            dwf_ref[c, :] = tn(x_ref[0, :, c], dgu_ref[...]).astype(BF16)
            dwo_ref[c, QUARTER:QUARTER + 256] = tn(x_ref[1, :, c], dguq_ref[...]).astype(BF16)
            dwo_ref[c, DOWN_WHOLE:DOWN_WHOLE + 512] = tn(g_ref[0, :, c], act_ref[...]).astype(BF16)
            dwo_ref[c, DOWN_QUARTER:DOWN_QUARTER + 128] = tn(g_ref[1, :, c], actq_ref[...]).astype(BF16)
            return carry
        lax.fori_loop(0, D // 256, body, 0)

def experts(owned, tokens, cot, picks, router_t, wf, wo):
    R = SRC * 128
    once = lambda shape: pl.BlockSpec(shape, lambda i: (0, 0), pipeline_mode=pl.Buffered(1))
    rows = pl.BlockSpec((R, D), lambda i: (i, 0))
    vmem = lambda *shape, dtype=BF16: pltpu.VMEM(shape, dtype)
    return pl.pallas_call(
        expert_kernel,
        grid=(STEPS,),
        in_specs=[
            pl.BlockSpec(memory_space=pltpu.SMEM), rows, rows, pl.BlockSpec((SRC * 64, 128), lambda i: (i, 0)),
            once((64, D)), once((D, 2 * F)), once((D, OWN_WIDTH)),
        ],
        out_specs=[rows, rows, pl.BlockSpec((SRC, 8, 128), lambda i: (i, 0, 0)), once((D, 2 * F)), once((D, OWN_WIDTH))],
        out_shape=[
            jax.ShapeDtypeStruct((4096, D), BF16), jax.ShapeDtypeStruct((4096, D), BF16), jax.ShapeDtypeStruct((32, 8, 128), F32),
            jax.ShapeDtypeStruct((D, 2 * F), BF16), jax.ShapeDtypeStruct((D, OWN_WIDTH), BF16),
        ],
        scratch_shapes=[
            vmem(2, 1024, D), vmem(2, 1024, D), vmem(2, M, 128, dtype=F32),
            vmem(1024, 512), vmem(1024, 1024), vmem(1024, 128), vmem(1024, 256), vmem(2, M, D), vmem(2, M, D),
        ],
        compiler_params=pltpu.CompilerParams(vmem_limit_bytes=62 * 2**20),
        cost_estimate=pl.CostEstimate(flops=22 * 10**9, bytes_accessed=62 * 10**6, transcendentals=0),
    )(owned, tokens, cot, picks, router_t, wf, wo)


MESH = pl.DeviceIdType.MESH
DEVICES = 32
TURNS = tuple(sorted(range(1, DEVICES), key=lambda k: (k % 8 * 5 % 8, k)))
DMA = pltpu.SemaphoreType.DMA


def dev(z, y, x, c):
    return ((z * 2 + y) * 2 + x) * 2 + c


class Place:
    def __init__(self):
        me = lax.axis_index("fsdp")
        self.me = me
        z, y, x, c = me // 8, lax.rem(me // 4, 2), lax.rem(me // 2, 2), lax.rem(me, 2)
        self.z, self.y, self.x, self.c = z, y, x, c
        self.sib, self.xn, self.yn = dev(z, y, x, 1 - c), dev(z, y, 1 - x, c), dev(z, 1 - y, x, c)
        self.up, self.down = dev(z + 1, y, x, c), dev(z - 1, y, x, c)
        table = ((0, 1, 2, 3), (1, 0, 2, 3), (2, 3, 1, 0), (3, 2, 1, 0))
        self.zq = []
        for q in range(4):
            v = jnp.int32(table[0][q])
            for k in range(1, 4):
                v = jnp.where(z == k, table[k][q], v)
            self.zq.append(v)


def greet_all():
    me = lax.axis_index("fsdp")
    barrier = pltpu.get_barrier_semaphore()
    for k in range(1, DEVICES):
        pl.semaphore_signal(barrier, inc=1, device_id=(lax.rem(me + k, DEVICES),), device_id_type=MESH)
    pl.semaphore_wait(barrier, DEVICES - 1)


def rc(src, dst, ss, rs, to):
    return pltpu.make_async_remote_copy(src_ref=src, dst_ref=dst, send_sem=ss, recv_sem=rs, device_id=(to,), device_id_type=MESH)


class Direct:
    def __init__(self, pieces, refs, sems):
        self.pieces, self.refs, (self.ss, self.rs, self.ls) = pieces, refs, sems
        self.me = lax.axis_index("fsdp")
        self.left = list(TURNS)

    @staticmethod
    def scratch(count):
        return [DMA((DEVICES, count)), DMA((DEVICES, count)), DMA((count,))]

    def own(self):
        self.local = [pltpu.make_async_copy(a, b, self.ls.at[i]) for i, (a, b) in enumerate(self.pieces(self.me, self.me, self.refs))]
        for l in self.local:
            l.start()

    def start(self, number):
        turns, self.left = self.left[:number], self.left[number:]
        for k in turns:
            to = lax.rem(self.me + k, DEVICES)
            for i, (a, b) in enumerate(self.pieces(self.me, to, self.refs)):
                rc(a, b, self.ss.at[k, i], self.rs.at[k, i], to).start()

    def finish(self):
        self.start(DEVICES)
        for k in TURNS:
            src = lax.rem(self.me + DEVICES - k, DEVICES)
            for i, (a, b) in enumerate(self.pieces(src, self.me, self.refs)):
                rc(a, b, self.ss.at[k, i], self.rs.at[k, i], src).wait_recv()
        for k in TURNS:
            to = lax.rem(self.me + k, DEVICES)
            for i, (a, b) in enumerate(self.pieces(self.me, to, self.refs)):
                rc(a, b, self.ss.at[k, i], self.rs.at[k, i], to).wait_send()
        for l in self.local:
            l.wait()


class Gather:
    ORDER = ((1, 0), (1, 1), (2, 0), (1, 2), (2, 1), (3, 0), (1, 3), (2, 2), (3, 1), (2, 3), (3, 2), (3, 3))

    def __init__(self, p, parts, shards, outs, sems):
        self.p, self.parts, self.shards, self.outs, self.sems = p, parts, shards, outs, sems
        self.P, self.sends, self.locals = len(parts), [], []
        self.left = list(self.ORDER)

    @staticmethod
    def scratch(arrays, parts):
        P = len(parts)
        return [DMA((arrays,)), DMA((4, P)), DMA((P,))] + [DMA((4, P))] * 7 + [DMA((4, 4, P))] * 2

    def at(self, i, d):
        a, c0, w, _ = self.parts[i]
        rows = self.shards[a].shape[0]
        return self.outs[a].at[pl.ds(pl.multiple_of(d * rows, rows), rows), pl.ds(c0, w)]

    def spot(self, i, q, k, core):
        p = self.p
        flip_x, flip_y = ((0, 0), (1, 0), (0, 1), (1, 1))[k] if self.parts[i][3] == 0 else ((0, 0), (0, 1), (1, 0), (1, 1))[k]
        return self.at(i, dev(p.zq[q], 1 - p.y if flip_y else p.y, 1 - p.x if flip_x else p.x, core))

    def go(self, copy):
        copy.start()
        self.sends.append(copy)

    def step(self, number=1):
        for f, q in self.left[:number]:
            (self.stage1, self.stage2, self.stage3)[f - 1](q)
        self.left = self.left[number:]

    def stage1(self, q):
        p = self.p
        _, zs, zs2, zr, fs, fr, s1s, s1r, s2s, s2r, cs, cr = self.sems
        for i in range(self.P):
            a, c0, w, mode = self.parts[i]
            first, second = (p.xn, p.yn) if mode == 0 else (p.yn, p.xn)
            here = self.spot(i, q, 0, p.c)
            if q == 0:
                src = self.shards[a].at[:, pl.ds(c0, w)]

                @pl.when(p.z < 3)
                def _():
                    rc(src, here, zs.at[0, i], zr.at[p.z, i], p.up).start()

                @pl.when(p.z > 0)
                def _():
                    rc(src, here, zs2.at[i], zr.at[p.z, i], p.down).start()
            else:
                src, zq = here, p.zq[q]
                rc(here, here, zs.at[q, i], zr.at[zq, i], p.up).wait_recv()

                @pl.when((zq < p.z) & (p.z < 3))
                def _():
                    rc(src, here, zs.at[q, i], zr.at[zq, i], p.up).start()

                @pl.when((zq > p.z) & (p.z > 0))
                def _():
                    rc(src, here, zs.at[q, i], zr.at[zq, i], p.down).start()
            self.go(rc(src, here, fs.at[q, i], fr.at[q, i], first))
            self.go(rc(src, here, s1s.at[q, i], s1r.at[q, i], second))
            self.go(rc(src, here, cs.at[0, q, i], cr.at[0, q, i], p.sib))
        if q == 0:
            for a, (shard, out) in enumerate(zip(self.shards, self.outs)):
                rows = shard.shape[0]
                l = pltpu.make_async_copy(shard, out.at[pl.ds(pl.multiple_of(p.me * rows, rows), rows)], self.sems[0].at[a])
                l.start()
                self.locals.append(l)

    def stage2(self, q):
        p = self.p
        fs, fr, s2s, s2r, cs, cr = self.sems[4:6] + self.sems[8:12]
        for i in range(self.P):
            second = p.yn if self.parts[i][3] == 0 else p.xn
            there = self.spot(i, q, 1, p.c)
            rc(there, there, fs.at[q, i], fr.at[q, i], second).wait_recv()
            self.go(rc(there, there, s2s.at[q, i], s2r.at[q, i], second))
            self.go(rc(there, there, cs.at[1, q, i], cr.at[1, q, i], p.sib))

    def stage3(self, q):
        p = self.p
        cs, cr = self.sems[10:12]
        for k, (ss, rs) in ((2, self.sems[6:8]), (3, self.sems[8:10])):
            for i in range(self.P):
                there = self.spot(i, q, k, p.c)
                rc(there, there, ss.at[q, i], rs.at[q, i], p.sib).wait_recv()
                self.go(rc(there, there, cs.at[k, q, i], cr.at[k, q, i], p.sib))

    def arrived(self):
        self.step(12)
        cs, cr = self.sems[10:12]
        for q in range(4):
            for k in range(4):
                for i in range(self.P):
                    there = self.spot(i, q, k, 1 - self.p.c)
                    rc(there, there, cs.at[k, q, i], cr.at[k, q, i], self.p.sib).wait_recv()
        for l in self.locals:
            l.wait()

    def finish(self):
        p = self.p
        zs, zs2, zr = self.sems[1:4]
        for copy in self.sends:
            copy.wait_send()
        for i in range(self.P):
            here = self.at(i, p.me)

            @pl.when(p.z < 3)
            def _():
                rc(here, here, zs.at[0, i], zr.at[p.z, i], p.up).wait_send()

            @pl.when(p.z > 0)
            def _():
                rc(here, here, zs2.at[i], zr.at[p.z, i], p.down).wait_send()

            for q in range(1, 4):
                zq = p.zq[q]

                @pl.when(((zq < p.z) & (p.z < 3)) | ((zq > p.z) & (p.z > 0)))
                def _():
                    rc(here, here, zs.at[q, i], zr.at[zq, i], p.up).wait_send()


class Scatter:
    ORDER = ((1, 3), (1, 2), (2, 3), (1, 1), (2, 2), (3, 3), (1, 0), (2, 1), (3, 2), (2, 0), (3, 1), (3, 0))
    STEP = 16

    def __init__(self, p, parts, fulls, outs, spaces, sems, in_place=False):
        self.p, self.parts, self.fulls, self.outs, self.sems, self.in_place = p, parts, fulls, outs, sems, in_place
        count = len(fulls)
        if in_place:
            spaces = (None,) * count + tuple(spaces)
        self.held, self.r0, self.r1, self.r2, self.r3 = (spaces[i * count : (i + 1) * count] for i in range(5))
        self.rows = [f.shape[0] // DEVICES for f in fulls]
        self.P, self.sends, self.loads = len(parts), [], {}
        self.left = list(self.ORDER)

    @staticmethod
    def scratch(arrays, parts, in_place=False):
        P = len(parts)
        spaces = []
        for cnt in (16, 8, 4, 5) if in_place else (16, 16, 8, 4, 5):
            spaces += [pltpu.VMEM((cnt, a.shape[0] // DEVICES, a.shape[1]), a.dtype) for a in arrays]
        return spaces, [DMA((4, 4, P))] * 3 + [DMA((4, 2, P))] * 2 + [DMA((4, P))] * 3 + [DMA((5, P))]

    def go(self, copy):
        copy.start()
        self.sends.append(copy)

    def cut(self, i):
        return pl.ds(self.parts[i][1], self.parts[i][2])

    def spot(self, i, k):
        x, y = self.p.x, self.p.y
        if self.parts[i][3] == 0:
            return ((1 - y, 1 - x), (1 - y, x), (y, 1 - x), (y, x))[k]
        return ((1 - y, 1 - x), (y, 1 - x), (1 - y, x), (y, x))[k]

    def slot(self, q, yy, xx):
        return (yy * 2 + xx) * 4 + self.p.zq[q]

    def hold(self, a, q, yy, xx):
        if self.in_place:
            start = dev(self.p.zq[q], yy, xx, self.p.c) * self.rows[a]
            return self.fulls[a].at[pl.ds(pl.multiple_of(start, self.rows[a]), self.rows[a])]
        return self.held[a].at[self.slot(q, yy, xx)]

    def source(self, i, q, k, core):
        a = self.parts[i][0]
        d = dev(self.p.zq[q], *self.spot(i, k), core)
        return self.fulls[a].at[pl.ds(pl.multiple_of(d * self.rows[a], self.rows[a]), self.rows[a]), self.cut(i)]

    def begin(self, only=None):
        ls, s0, e0 = self.sems[:3]
        for q in (3, 2, 1, 0):
            for k in range(4):
                for i in range(self.P):
                    a = self.parts[i][0]
                    if only is not None and a not in only:
                        continue
                    s = self.slot(q, *self.spot(i, k))
                    self.go(rc(self.source(i, q, k, 1 - self.p.c), self.r0[a].at[s, :, self.cut(i)], s0.at[q, k, i], e0.at[q, k, i], self.p.sib))
                    if not self.in_place:
                        l = pltpu.make_async_copy(self.source(i, q, k, self.p.c), self.held[a].at[s, :, self.cut(i)], ls.at[q, k, i])
                        l.start()
                        self.loads[q, k, i] = l

    def step(self, number=1):
        for f, q in self.left[:number]:
            (self.stage1, self.stage2, self.stage3)[f - 1](q)
        self.left = self.left[number:]

    def chunks(self, a, body):
        def one(n, carry):
            body(pl.ds(pl.multiple_of(n * self.STEP, self.STEP), self.STEP))
            return carry

        lax.fori_loop(0, self.rows[a] // self.STEP, one, 0)

    def add(self, i, dst, src, s_src):
        a, c0, w, _ = self.parts[i]

        def body(r):
            v = dst[r, c0 : c0 + w].astype(F32) + src[s_src, r, c0 : c0 + w].astype(F32)
            dst[r, c0 : c0 + w] = v.astype(dst.dtype)

        self.chunks(a, body)

    def stage1(self, q):
        p = self.p
        _, s0, e0, s1, e1 = self.sems[:5]
        for k in range(4):
            for i in range(self.P):
                a = self.parts[i][0]
                first = p.yn if self.parts[i][3] == 0 else p.xn
                s = self.slot(q, *self.spot(i, k))
                sums = self.hold(a, q, *self.spot(i, k))
                here = sums.at[:, self.cut(i)]
                rc(here, self.r0[a].at[s, :, self.cut(i)], s0.at[q, k, i], e0.at[q, k, i], p.sib).wait_recv()
                if not self.in_place:
                    self.loads[q, k, i].wait()
                self.add(i, sums, self.r0[a], s)
                if k < 2:
                    self.go(rc(here, self.r1[a].at[q * 2 + k, :, self.cut(i)], s1.at[q, k, i], e1.at[q, k, i], first))

    def stage2(self, q):
        p = self.p
        s1, e1, s2, e2 = self.sems[3:7]
        for k in range(2):
            for i in range(self.P):
                a = self.parts[i][0]
                second = p.xn if self.parts[i][3] == 0 else p.yn
                sums = self.hold(a, q, *self.spot(i, k + 2))
                here = sums.at[:, self.cut(i)]
                rc(here, self.r1[a].at[q * 2 + k, :, self.cut(i)], s1.at[q, k, i], e1.at[q, k, i], p.sib).wait_recv()
                self.add(i, sums, self.r1[a], q * 2 + k)
                if k == 0:
                    self.go(rc(here, self.r2[a].at[q, :, self.cut(i)], s2.at[q, i], e2.at[q, i], second))

    def stage3(self, q):
        p = self.p
        s2, e2, s3, e3 = self.sems[5:9]
        zq, z = p.zq[q], p.z
        for i in range(self.P):
            a, c0, w, _ = self.parts[i]
            r3, out, sums = self.r3[a], self.outs[a], self.hold(a, q, p.y, p.x)
            here = sums.at[:, self.cut(i)]
            rc(here, self.r2[a].at[q, :, self.cut(i)], s2.at[q, i], e2.at[q, i], p.sib).wait_recv()
            self.add(i, sums, self.r2[a], q)
            if q > 0:

                @pl.when((zq > z) & (z > 0) | (zq < z) & (z < 3))
                def _():
                    rc(here, r3.at[zq, :, self.cut(i)], s3.at[q, i], e3.at[zq, i], p.sib).wait_recv()
                    self.add(i, sums, r3, zq)

                @pl.when(zq > z)
                def _():
                    rc(here, r3.at[zq, :, self.cut(i)], s3.at[q, i], e3.at[zq, i], p.up).start()

                @pl.when((zq < z) & (zq == z - 1))
                def _():
                    rc(here, r3.at[4, :, self.cut(i)], s3.at[q, i], e3.at[4, i], p.down).start()

                @pl.when(zq < z - 1)
                def _():
                    rc(here, r3.at[zq, :, self.cut(i)], s3.at[q, i], e3.at[zq, i], p.down).start()
            else:

                def first_sum(r):
                    out[r, c0 : c0 + w] = sums[r, c0 : c0 + w].astype(F32)

                self.chunks(a, first_sum)
                for cond, where in ((z > 0, z), (z < 3, 4)):

                    @pl.when(cond)
                    def _():
                        rc(here, r3.at[where, :, self.cut(i)], s3.at[q, i], e3.at[where, i], p.sib).wait_recv()

                        def more(r):
                            out[r, c0 : c0 + w] += r3[where, r, c0 : c0 + w].astype(F32)

                        self.chunks(a, more)

    def finish(self):
        p = self.p
        s3, e3 = self.sems[7:9]
        for copy in self.sends:
            copy.wait_send()
        for q in range(1, 4):
            for i in range(self.P):
                here = self.hold(self.parts[i][0], q, p.y, p.x).at[:, self.cut(i)]
                rc(here, here, s3.at[q, i], e3.at[0, i], p.sib).wait_send()


HBM = pl.BlockSpec(memory_space=pl.ANY)
VMEM = pl.BlockSpec(memory_space=pltpu.VMEM)


def like(*shape, dtype=None):
    return jax.ShapeDtypeStruct(shape, dtype or jnp.bfloat16)


def cut_up(refs, *counts):
    out, i = [], 0
    for c in counts:
        out.append(refs[i : i + c])
        i += c
    return out + [refs[i:]]


GROUP = QUERY_HEADS // KEY_VALUE_HEADS
Q_WIDTH, K_WIDTH = QUERY_HEADS * HEAD_WIDTH, KEY_VALUE_HEADS * HEAD_WIDTH
TOK = 128


def partner(v):
    lane = lax.broadcasted_iota(jnp.int32, v.shape, 1) % HEAD_WIDTH
    return jnp.where(lane < HEAD_WIDTH // 2, pltpu.roll(v, 96, 1), pltpu.roll(v, 32, 1))


def attention_forward(x_ref, cos_ref, sin_ref, bias_ref, qkv_ref, out_ref, small_ref, r):
    def norm_one():
        r.small_t[...] = nt(jnp.eye(TOK, dtype=BF16), small_ref[...])
        x = x_ref[...].astype(F32)
        r.n1[...] = (x * norm_scale(x) * r.small_t[E : E + 1, :]).astype(BF16)

    def project(t):
        def run():
            tile = nn(r.n1[...], qkv_ref[:, t * 512 : t * 512 + 512])
            for b in range(4):
                col = t * 512 + b * 128
                v = tile[:, b * 128 : b * 128 + 128]
                if col < Q_WIDTH + K_WIDTH:
                    v = v * cos_ref[...] + partner(v) * sin_ref[...]
                v = v.astype(BF16)
                for half in range(2):
                    piece = v[:, half * 64 : half * 64 + 64]
                    head = col // 64 + half
                    if col < Q_WIDTH:
                        r.q[head // GROUP, head % GROUP * TOK : head % GROUP * TOK + TOK, :] = piece
                    elif col < Q_WIDTH + K_WIDTH:
                        r.k[head - QUERY_HEADS] = piece
                    else:
                        r.v[head - QUERY_HEADS - KEY_VALUE_HEADS] = piece

        return run

    def attend(j):
        def run():
            s = nt(r.q[j], r.k[j]) * ATTN_SCALE
            s = s + jnp.concatenate([bias_ref[...]] * GROUP, axis=0)
            e = jnp.exp(s - jnp.max(s, axis=1, keepdims=True))
            probs = e / jnp.sum(e, axis=1, keepdims=True)
            r.probs[j] = probs
            o = nn(probs.astype(BF16), r.v[j]).astype(BF16)
            for g in range(GROUP):
                h = j * GROUP + g
                r.att[:, h * 64 : h * 64 + 64] = o[g * TOK : g * TOK + TOK]

        return run

    def output(t):
        def run():
            c = slice(t * 512, t * 512 + 512)
            r.middle[:, c] = x_ref[:, c].astype(F32) + RESIDUAL_SCALE * nn(r.att[...], out_ref[:, c])

        return run

    def norm_two():
        m = r.middle[...]
        r.n2[...] = (m * norm_scale(m) * r.small_t[E + 1 : E + 2, :]).astype(BF16)

    return (
        [norm_one]
        + [project(t) for t in range((Q_WIDTH + 2 * K_WIDTH) // 512)]
        + [attend(j) for j in range(KEY_VALUE_HEADS)]
        + [output(t) for t in range(D // 512)]
        + [norm_two]
    )


def split_dot(form, a, b):
    one = b.astype(BF16)
    rest = b - one.astype(F32)
    two = rest.astype(BF16)
    three = (rest - two.astype(F32)).astype(BF16)
    return form(a, one) + form(a, two) + form(a, three)


def norm_back_rows(hidden, gain, upstream):
    scale = norm_scale(hidden)
    weighted = upstream * gain
    inner = jnp.mean(weighted * hidden, axis=-1, keepdims=True)
    return scale * weighted - hidden * scale**3 * inner, upstream * hidden * scale


def attention_backward(x_ref, cot_ref, gin_ref, gates_ref, cos_ref, sin_ref, qkv_ref, out_ref, r, put_qkv, put_out, put_small):
    def router():
        m = r.middle[...]
        logits = nt(r.small_t[:64, :].astype(BF16), r.n2[...])
        row = lax.broadcasted_iota(jnp.int32, logits.shape, 0)
        logits = jnp.where(row < E, logits, -jnp.inf)
        e = jnp.exp(logits - jnp.max(logits, axis=0, keepdims=True))
        probs = e / jnp.sum(e, axis=0, keepdims=True)
        gates = gates_ref[...]
        gl = probs * (gates - jnp.sum(probs * gates, axis=0, keepdims=True))
        gl = jnp.where(row < E, gl, 0.0)
        gl = jnp.concatenate([gl, jnp.zeros((64, TOK), F32)], axis=0).T
        r.gl[...] = gl
        back = nn(gl.astype(BF16), r.small_t[...].astype(BF16))
        low = gl - gl.astype(BF16).astype(F32)
        back = back + nn(low.astype(BF16), r.small_t[...].astype(BF16))
        low = low - low.astype(BF16).astype(F32)
        back = back + nn(low.astype(BF16), r.small_t[...].astype(BF16))
        up = gin_ref[...] + back
        gm, gain_rows = norm_back_rows(m, r.small_t[E + 1 : E + 2, :], up)
        gm = gm + cot_ref[...].astype(F32)
        r.gm[...] = gm
        r.gain2[...] = gain_rows
        r.branch[...] = (RESIDUAL_SCALE * gm).astype(BF16)

    def attended(t):
        def run():
            c = slice(t * 512, t * 512 + 512)
            r.ga[:, c] = nt(r.branch[...], out_ref[c, :]).astype(BF16)

        return run

    def out_part(t):
        def run():
            put_out(t, tn(r.att[:, t * 256 : t * 256 + 256], r.branch[...]).astype(BF16))

        return run

    def head(j):
        def run():
            cols = [slice((j * GROUP + g) * 64, (j * GROUP + g) * 64 + 64) for g in range(GROUP)]
            ga = jnp.concatenate([r.ga[:, c] for c in cols], axis=0)
            at = jnp.concatenate([r.att[:, c] for c in cols], axis=0)
            delta = jnp.sum(ga.astype(F32) * at.astype(F32), axis=1, keepdims=True)
            probs = r.probs[j]
            ds = (probs * (nt(ga, r.v[j]) - delta) * ATTN_SCALE).astype(BF16)
            gq = nn(ds, r.k[j])
            for g, c in enumerate(cols):
                r.gjf[:, c] = gq[g * TOK : g * TOK + TOK]
            r.gjf[:, Q_WIDTH + j * 64 : Q_WIDTH + j * 64 + 64] = tn(ds, r.q[j])
            r.gjf[:, Q_WIDTH + K_WIDTH + j * 64 : Q_WIDTH + K_WIDTH + j * 64 + 64] = tn(probs.astype(BF16), ga)

        return run

    def rotate():
        for col in range(0, Q_WIDTH + 2 * K_WIDTH, 128):
            v = r.gjf[:, col : col + 128]
            if col < Q_WIDTH + K_WIDTH:
                v = v * cos_ref[...] - partner(v) * sin_ref[...]
            r.gj[:, col : col + 128] = v.astype(BF16)

    def qkv_part(t):
        def run():
            put_qkv(t, tn(r.n1[:, t * 256 : t * 256 + 256], r.gj[...]).astype(BF16))

        return run

    def into_normed(t):
        def run():
            c = slice(t * 256, t * 256 + 256)
            r.gn[:, c] = nt(r.gj[...], qkv_ref[c, :])

        return run

    def input_back():
        x = x_ref[...].astype(F32)
        gx, gain_rows = norm_back_rows(x, r.small_t[E : E + 1, :], r.gn[...])
        r.input_grad[...] = (gx + r.gm[...]).astype(BF16)
        lane = lax.broadcasted_iota(jnp.int32, (TOK, TOK), 1)
        small = split_dot(tn, r.n2[...], r.gl[...])
        for rows, at in ((gain_rows, E), (r.gain2[...], E + 1)):
            ones = jnp.where(lane == at, 1.0, 0.0).astype(BF16)
            hi = rows.astype(BF16)
            lo = (rows - hi.astype(F32)).astype(BF16)
            small = small + tn(hi, ones) + tn(lo, ones)
        put_small(small.astype(BF16))

    first = [router] + [attended(t) for t in range(3)] + [out_part(t) for t in range(6)]
    heads = [head(j) for j in range(KEY_VALUE_HEADS)] + [rotate]
    last = [into_normed(t) for t in range(6)] + [input_back] + [qkv_part(t) for t in range(6)]
    return first, heads, last


class Results:
    pass


ATT_NAMES = ("small_t", "n1", "q", "k", "v", "probs", "att", "middle", "n2")
ATT_SHAPES = (
    ((TOK, D), F32),
    ((TOK, D), BF16),
    ((KEY_VALUE_HEADS, GROUP * TOK, HEAD_WIDTH), BF16),
    ((KEY_VALUE_HEADS, TOK, HEAD_WIDTH), BF16),
    ((KEY_VALUE_HEADS, TOK, HEAD_WIDTH), BF16),
    ((KEY_VALUE_HEADS, GROUP * TOK, TOK), F32),
    ((TOK, Q_WIDTH), BF16),
    ((TOK, D), F32),
    ((TOK, D), BF16),
)
ROW_HALVES = ((0, 0, 768, 0), (0, 768, 768, 1))
DENSE_PARTS = ((0, 0, 1280, 0), (0, 1280, 1280, 1), (1, 0, 768, 0), (1, 768, 768, 1), (2, 0, 128, 1))
FIRST_PARTS = DENSE_PARTS + ((3, 0, 128, 0),)


def lanes(start):
    return pl.ds(pl.multiple_of(start, 128), 128)


def weights_out(src, dst, refs):
    g_ref, d_ref, wf_ref, wo_ref = refs
    group, own, quarter = dst // 4, lax.rem(dst, 4), lax.rem(dst, 4) * 128
    rows = pl.ds(pl.multiple_of(src * 48, 48), 48)
    fifth = group * 5 + 4
    return (
        (g_ref.at[fifth, :, lanes(quarter)], wo_ref.at[rows, pl.ds(QUARTER, 128)]),
        (g_ref.at[fifth, :, lanes(F + quarter)], wo_ref.at[rows, pl.ds(QUARTER + 128, 128)]),
        (d_ref.at[group * 5 + own], wo_ref.at[rows, pl.ds(DOWN_WHOLE, F)]),
        (d_ref.at[fifth, :, lanes(quarter)], wo_ref.at[rows, pl.ds(DOWN_QUARTER, 128)]),
        (g_ref.at[group * 5 + own], wf_ref.at[rows]),
    )


def down_back(src, dst, refs):
    dwo_ref, gates_ref, d_ref, all_gates_ref = refs
    group, quarter = src // 4, lax.rem(src, 4) * 128
    rows = pl.ds(pl.multiple_of(dst * 48, 48), 48)
    return (
        (gates_ref.at[dst], all_gates_ref.at[src]),
        (dwo_ref.at[rows, pl.ds(DOWN_WHOLE, F)], d_ref.at[group * 5 + lax.rem(src, 4)]),
        (dwo_ref.at[rows, pl.ds(DOWN_QUARTER, 128)], d_ref.at[group * 5 + 4, :, lanes(quarter)]),
    )


def gate_up_back(src, dst, refs):
    dwf_ref, dwo_ref, g_ref = refs
    group, quarter = src // 4, lax.rem(src, 4) * 128
    rows = pl.ds(pl.multiple_of(dst * 48, 48), 48)
    return (
        (dwo_ref.at[rows, pl.ds(QUARTER, 128)], g_ref.at[group * 5 + 4, :, lanes(quarter)]),
        (dwo_ref.at[rows, pl.ds(QUARTER + 128, 128)], g_ref.at[group * 5 + 4, :, lanes(F + quarter)]),
        (dwf_ref.at[rows], g_ref.at[group * 5 + lax.rem(src, 4)]),
    )


def first_kernel(*refs):
    (x, cos, sin, bias), dense, (cot,), experts_in, dense_out, (cots, tokens, wf, wo), results, weights, (load_sem,), refs = cut_up(
        refs, 4, 4, 1, 2, 4, 4, 9, 3, 1
    )
    sems1, sems2, sems3, direct_sems, _ = cut_up(refs, 12, 12, 12, 3)
    greet_all()
    p = Place()
    r = Results()
    for name, ref in zip(ATT_NAMES, results):
        setattr(r, name, ref)
    g1 = Gather(p, FIRST_PARTS, dense, dense_out, sems1)
    g2 = Gather(p, ROW_HALVES, [cot], [cots], sems2)
    g3 = Gather(p, ROW_HALVES, [r.n2], [tokens], sems3)
    direct = Direct(weights_out, tuple(experts_in) + (wf, wo), direct_sems)
    g1.step()
    direct.own()
    for n in FIRST_BATCHES:
        g1.step()
        direct.start(n)
    g2.step(2)
    g1.arrived()
    loads = [pltpu.make_async_copy(a, b, load_sem.at[i]) for i, (a, b) in enumerate(zip(dense_out[:3], weights))]
    for l in loads:
        l.start()
    g2.step(2)
    for l in loads:
        l.wait()
    for i, chunk in enumerate(attention_forward(x, cos, sin, bias, *weights, r)):
        chunk()
        if i % 2 == 1:
            g2.step()
            direct.start(SECOND_BATCH)
    g3.step(2)
    direct.start(SECOND_BATCH)
    g2.arrived()
    g3.step(2)
    direct.start(DEVICES)
    g3.arrived()
    for g in (g1, g2, g3):
        g.finish()
    direct.finish()


FIRST_BATCHES = (1, 1, 1, 1, 1, 1, 1, 1, 1, 1)
SECOND_BATCH = 2


def first(x, cos, sin, bias, dense, cot, gu, dp):
    wide = lambda a: like(DEVICES * a.shape[0], a.shape[1], dtype=a.dtype)
    dense_full = [wide(a) for a in dense]
    return pl.pallas_call(
        first_kernel,
        in_specs=[VMEM] * 4 + [HBM] * 7,
        out_specs=[HBM] * 8 + [VMEM] * 9,
        out_shape=dense_full + [wide(cot), wide(cot), like(D, 2 * F), like(D, OWN_WIDTH)] + [like(*s, dtype=t) for s, t in ATT_SHAPES],
        scratch_shapes=[pltpu.VMEM(a.shape, a.dtype) for a in dense_full[:3]]
        + [DMA((3,))]
        + Gather.scratch(4, FIRST_PARTS)
        + Gather.scratch(1, ROW_HALVES) * 2
        + Direct.scratch(5),
        compiler_params=pltpu.CompilerParams(collective_id=0, has_side_effects=True, vmem_limit_bytes=60 * 2**20),
    )(x, cos, sin, bias, *dense, cot, gu, dp)


def middle_kernel(*refs):
    (gin_part, dwo, gates), (gin, grad_down, all_gates), spaces, sems, direct_sems, _ = cut_up(refs, 3, 3, 5, 9, 3)
    greet_all()
    p = Place()
    s = Scatter(p, ROW_HALVES, [gin_part], [gin], spaces, sems)
    direct = Direct(down_back, (dwo, gates, grad_down, all_gates), direct_sems)
    s.begin()
    direct.own()
    for n in MIDDLE_BATCHES:
        s.step()
        direct.start(n)
    s.step(12)
    direct.start(DEVICES)
    s.finish()
    direct.finish()


MIDDLE_BATCHES = (3, 3, 3, 3, 3, 3, 3, 3, 3, 4)


def middle(gin_part, dwo, gates):
    spaces, sems = Scatter.scratch([gin_part], ROW_HALVES)
    return pl.pallas_call(
        middle_kernel,
        in_specs=[HBM] * 3,
        out_specs=[VMEM] + [HBM] * 2,
        out_shape=[like(TOK, D, dtype=F32), like(E, D // DEVICES, F), like(DEVICES, 8, TOK, dtype=F32)],
        scratch_shapes=spaces + sems + Direct.scratch(3),
        compiler_params=pltpu.CompilerParams(collective_id=1, has_side_effects=True, vmem_limit_bytes=60 * 2**20),
    )(gin_part, dwo, gates)


WORK = (
    ("gl", (TOK, TOK), F32),
    ("gm", (TOK, D), F32),
    ("gain2", (TOK, D), F32),
    ("branch", (TOK, D), BF16),
    ("ga", (TOK, D), BF16),
    ("gjf", (TOK, Q_WIDTH + 2 * K_WIDTH), F32),
    ("gj", (TOK, Q_WIDTH + 2 * K_WIDTH), BF16),
    ("gn", (TOK, D), F32),
)


def last_kernel(*refs):
    (x, cot, gin, gates, cos, sin), results, (qkv_full, out_full, out_part, dwf, dwo), outs, work, weights, (small_src, load_sem), refs = cut_up(
        refs, 6, 9, 5, 6, len(WORK), 2, 2
    )
    input_grad, combined, qkv_grad, out_grad, small_grad, grad_gu = outs
    spaces1, sems1, spaces2, sems2, direct_sems, _ = cut_up(refs, 5, 9, 12, 9, 3)
    greet_all()
    p = Place()
    r = Results()
    for name, ref in zip(ATT_NAMES + tuple(w[0] for w in WORK), tuple(results) + tuple(work)):
        setattr(r, name, ref)
    r.input_grad = input_grad
    qkv_ref, out_ref = weights
    s1 = Scatter(p, ROW_HALVES, [out_part], [combined], spaces1, sems1)
    s2 = Scatter(p, DENSE_PARTS, [qkv_ref, out_ref, small_src], [qkv_grad, out_grad, small_grad], spaces2, sems2, in_place=True)
    direct = Direct(gate_up_back, (dwf, dwo, grad_gu), direct_sems)
    s1.begin()
    loads = [pltpu.make_async_copy(a, b, load_sem.at[i]) for i, (a, b) in enumerate(((out_full, out_ref), (qkv_full, qkv_ref)))]
    for l in loads:
        l.start()
    direct.own()
    direct.start(2)

    def put_qkv(t, value):
        qkv_ref[t * 256 : t * 256 + 256, :] = value

    def put_out(t, value):
        out_ref[t * 256 : t * 256 + 256, :] = value

    def put_small(value):
        small_src[...] = value

    begin, heads, end = attention_backward(x, cot, gin, gates, cos, sin, qkv_ref, out_ref, r, put_qkv, put_out, put_small)
    for l in loads:
        l.wait()
    for i, chunk in enumerate(begin + heads + end):
        chunk()
        if i % 3 == 2:
            s1.step()
            direct.start(2)
    s2.begin()
    s1.step(12)
    while s2.left:
        s2.step()
        direct.start(2)
    direct.start(DEVICES)
    s1.finish()
    s2.finish()
    direct.finish()


def last(x, cot, gin, gates, cos, sin, results, qkv_full, out_full, out_part, dwf, dwo):
    small = like(D, TOK)
    spaces1, sems1 = Scatter.scratch([out_part], ROW_HALVES)
    spaces2, sems2 = Scatter.scratch([qkv_full, out_full, small], DENSE_PARTS, in_place=True)
    own = D // DEVICES
    return pl.pallas_call(
        last_kernel,
        in_specs=[VMEM] * 15 + [HBM] * 5,
        out_specs=[VMEM] * 5 + [HBM],
        out_shape=[
            like(TOK, D), like(TOK, D, dtype=F32), like(own, qkv_full.shape[1], dtype=F32), like(own, D, dtype=F32),
            like(own, TOK, dtype=F32), like(E, own, 2 * F),
        ],
        scratch_shapes=[pltpu.VMEM(s, t) for _, s, t in WORK]
        + [pltpu.VMEM(qkv_full.shape, BF16), pltpu.VMEM(out_full.shape, BF16), pltpu.VMEM(small.shape, BF16), DMA((2,))]
        + spaces1 + sems1 + spaces2 + sems2
        + Direct.scratch(3),
        compiler_params=pltpu.CompilerParams(collective_id=2, has_side_effects=True, vmem_limit_bytes=63 * 2**20),
    )(x, cot, gin, gates, cos, sin, *results, qkv_full, out_full, out_part, dwf, dwo)


def fast(
    layer_input, cotangent, sequence_ids, expert_ids, attention_gain, qkv_weight, output_weight, moe_gain, router, gate_up, down_proj
):
    n, own_rows, T = DEVICES, gate_up.shape[0], layer_input.shape[0]
    me = lax.axis_index("fsdp")
    small = jnp.concatenate(
        [router, attention_gain[:, None], moe_gain[:, None], jnp.zeros((own_rows, 86), BF16)], axis=1
    )
    cosine, sine = rope_tables(positions(sequence_ids), HEAD_WIDTH)
    cos = jnp.concatenate([cosine] * 4, axis=1)
    sin = jnp.concatenate([-sine, sine] * 2, axis=1)
    place_in = jnp.arange(T, dtype=jnp.int32)
    allowed = (sequence_ids[:, None] == sequence_ids[None, :]) & (place_in[None, :] <= place_in[:, None])
    bias = jnp.where(allowed, 0.0, -jnp.inf).astype(F32)

    qkv_full, out_full, small_full, ids_all, cots, tokens, wf, wo, *results = first(
        layer_input, cos, sin, bias, [qkv_weight, output_weight, small, expert_ids.T], cotangent,
        jnp.transpose(gate_up, (1, 0, 2)), jnp.transpose(down_proj, (1, 0, 2)),
    )

    owned = jnp.stack([(me // 4) * 5 + lax.rem(me, 4), (me // 4) * 5 + 4])
    named = jnp.any(ids_all.reshape(n, TOP, T)[:, :, None, :] == owned[None, None, :, None], axis=1)
    before = (place_in[:, None] < place_in[None, :]).astype(BF16)
    ranks = jnp.dot(named.astype(BF16).reshape(2 * n, T), before, preferred_element_type=F32).reshape(n, 2, 1, T)
    picks = ((ranks == jnp.arange(CAP, dtype=F32)[:, None]) & named[:, :, None, :]).astype(BF16).reshape(n * 64, T)
    router_t = results[0][:64].astype(BF16)
    out_part, gin_part, gates, dwf, dwo = experts(owned, tokens, cots, picks, router_t, wf, wo)

    gin, grad_down, gates = middle(gin_part, dwo, gates)
    gates = gates.reshape(8, 4, 8, T)
    gates = jnp.concatenate([gates[:, :, 0], jnp.sum(gates[:, :, 1], axis=1, keepdims=True)], axis=1).reshape(E, T)
    gates = jnp.pad(gates, ((0, 64 - E), (0, 0)))
    input_grad, combined, qkv_grad, out_grad, small_grad, grad_gu = last(
        layer_input, cotangent, gin, gates, cos, sin, results, qkv_full, out_full, out_part, dwf, dwo
    )
    layer_output = (results[ATT_NAMES.index("middle")] + combined).astype(BF16)
    gate_up_grad = jnp.transpose(grad_gu, (1, 0, 2)).astype(F32)
    down_grad = jnp.transpose(grad_down, (1, 0, 2)).astype(F32)
    return (
        layer_output,
        input_grad,
        small_grad[:, E],
        qkv_grad,
        out_grad,
        small_grad[:, E + 1],
        small_grad[:, :E],
        gate_up_grad,
        down_grad,
    )


def solution(mesh):
    rows, flat, cube = P("fsdp", None), P("fsdp"), P("fsdp", None, None)
    return jax.shard_map(
        fast if mesh.shape["fsdp"] == 32 else on_device,
        mesh=mesh,
        in_specs=(rows, rows, flat, rows, flat, rows, rows, flat, rows, cube, cube),
        out_specs=(rows, rows, flat, rows, rows, flat, rows, cube, cube),
        check_vma=False,
    )
```

```python
import functools
import math
import jax
import jax.numpy as jnp
import numpy as np
from jax import lax
from jax.experimental import pallas as pl
from jax.experimental.pallas import tpu as pltpu
from jax.sharding import PartitionSpec as P

MODEL_WIDTH = 1536
QUERY_HEADS = 24
KEY_VALUE_HEADS = 8
HEAD_WIDTH = 64
E = 40
F = 512
TOP = 8
CAP = 32


EPSILON = 1e-06
ATTN_SCALE = 0.015625
RESIDUAL_SCALE = 0.22
ROPE_BASE = 10000.0
PRECISE_ARITHMETIC = lax.Precision.HIGHEST


def positions(sequence_ids):
    sequence_length = sequence_ids.shape[0]
    places = jnp.arange(sequence_length, dtype=jnp.int32)
    same = (sequence_ids[:, None] == sequence_ids[None, :]) & (places[None, :] < places[:, None])
    return jnp.sum(same.astype(jnp.int32), axis=1, dtype=jnp.int32)


def rope_tables(places, head_size):
    half_size = head_size // 2
    exponents = jnp.arange(half_size, dtype=jnp.float32) * (2.0 / head_size)
    inverse = jnp.exp(exponents * -math.log(ROPE_BASE))
    angles = places.astype(jnp.float32)[:, None] * inverse[None, :]
    return (jnp.cos(angles), jnp.sin(angles))


def apply_rotary(tensor, cosine_lookup, sine_lookup):
    half_size = tensor.shape[-1] // 2
    first_half = tensor[..., :half_size]
    second_half = tensor[..., half_size:]
    cosine_rows = cosine_lookup[:, None, :]
    sine_rows = sine_lookup[:, None, :]
    return jnp.concatenate(
        [
            first_half * cosine_rows - second_half * sine_rows,
            second_half * cosine_rows + first_half * sine_rows,
        ],
        axis=-1,
    )


def rotate_back(tensor, cosine_lookup, sine_lookup):
    half_size = tensor.shape[-1] // 2
    first_half = tensor[..., :half_size]
    second_half = tensor[..., half_size:]
    cosine_rows = cosine_lookup[:, None, :]
    sine_rows = sine_lookup[:, None, :]
    return jnp.concatenate(
        [
            first_half * cosine_rows + second_half * sine_rows,
            second_half * cosine_rows - first_half * sine_rows,
        ],
        axis=-1,
    )


def norm_scale(hidden_state):
    return lax.rsqrt(jnp.mean(hidden_state * hidden_state, axis=-1, keepdims=True) + EPSILON)


def norm_back(hidden_state, gain_vector, scale_rows, upstream):
    weighted = upstream * gain_vector.astype(jnp.float32)
    inner_mean = jnp.mean(weighted * hidden_state, axis=-1, keepdims=True)
    grad_hidden = scale_rows * weighted - hidden_state * scale_rows**3 * inner_mean
    grad_gain = jnp.sum(upstream * hidden_state * scale_rows, axis=0)
    return (grad_hidden, grad_gain)


def expert_slots(expert_ids, experts, capacity):
    rows = expert_ids.shape[0]
    picked = expert_ids[:, :, None] == jnp.arange(experts, dtype=jnp.int32)[None, None, :]
    named = jnp.any(picked, axis=1).astype(jnp.bfloat16)
    places = jnp.arange(rows, dtype=jnp.int32)
    before = (places[None, :] < places[:, None]).astype(jnp.bfloat16)
    ranks = jnp.dot(before, named, preferred_element_type=jnp.float32)
    ranks = jnp.sum(jnp.where(picked, ranks[:, None, :], 0.0), axis=-1).astype(jnp.int32)
    return (expert_ids * capacity + ranks).reshape(-1)


def owner_tables(devices):
    width_owned = E * F // devices
    span_count = (F + width_owned - 2) // F + 1
    first_expert = np.arange(devices) * width_owned // F
    send_table = np.minimum(first_expert[:, None] + np.arange(span_count)[None, :], E).reshape(-1)
    combine_table = (send_table[None, :] == np.arange(E)[:, None]).astype(np.float32)
    return (width_owned, span_count, send_table, combine_table)


def dispatch_rows(buffer_rows, send_table, devices, span_count):
    padded = jnp.concatenate(
        [buffer_rows, jnp.zeros((1, CAP, MODEL_WIDTH), buffer_rows.dtype)], axis=0
    )
    chosen = jnp.asarray(send_table[:, None] == np.arange(E + 1)[None, :], dtype=buffer_rows.dtype)
    picked_rows = jnp.einsum(
        "se,ecd->scd", chosen, padded, preferred_element_type=jnp.float32
    ).astype(buffer_rows.dtype)
    return picked_rows.reshape(devices, span_count, CAP, MODEL_WIDTH)


def merge_entries(returned, combine_table):
    flat_rows = returned.reshape(returned.shape[0] * returned.shape[1], CAP * MODEL_WIDTH)
    summed = jnp.dot(
        jnp.asarray(combine_table),
        flat_rows,
        precision=PRECISE_ARITHMETIC,
        preferred_element_type=jnp.float32,
    )
    return summed.reshape(E, CAP, MODEL_WIDTH)


def on_device(
    layer_input,
    cotangent,
    sequence_ids,
    expert_ids,
    attention_gain,
    qkv_weight,
    output_weight,
    moe_gain,
    router,
    gate_up,
    down_proj,
):
    sequence_length = layer_input.shape[0]
    shard_rows = gate_up.shape[0]
    query_group_count = QUERY_HEADS // KEY_VALUE_HEADS
    query_feature_width = QUERY_HEADS * HEAD_WIDTH
    key_feature_width = KEY_VALUE_HEADS * HEAD_WIDTH
    rows_per_block = min(512, sequence_length)
    devices = lax.axis_size("fsdp")
    dense_set = (
        lax.all_gather(attention_gain, "fsdp", axis=0, tiled=True),
        lax.all_gather(qkv_weight, "fsdp", axis=0, tiled=True),
        lax.all_gather(output_weight, "fsdp", axis=0, tiled=True),
        lax.all_gather(moe_gain, "fsdp", axis=0, tiled=True),
        lax.all_gather(router, "fsdp", axis=0, tiled=True),
    )
    gain_one, qkv_full, out_full, gain_two, router_full = dense_set
    width_owned, span_count, send_table, combine_table = owner_tables(devices)
    gate_cols = jnp.transpose(gate_up.reshape(shard_rows, E, 2, F), (0, 2, 1, 3)).reshape(
        shard_rows, 2, E * F
    )
    down_cols = down_proj.reshape(shard_rows, 1, E * F)
    owned_weights = lax.all_to_all(
        jnp.concatenate([gate_cols, down_cols], axis=1),
        "fsdp",
        split_axis=2,
        concat_axis=0,
        tiled=True,
    )
    owned_gate_up = owned_weights[:, :2, :]
    owned_down = owned_weights[:, 2, :]
    owner_index = lax.axis_index("fsdp")
    owned_start = owner_index * width_owned
    owned_columns = owned_start + jnp.arange(width_owned, dtype=jnp.int32)
    slot_of = owned_columns // F - owned_start // F
    column_mask = (slot_of[None, :] == jnp.arange(span_count, dtype=jnp.int32)[:, None]).astype(
        jnp.float32
    )
    inputs = layer_input.astype(jnp.float32)
    scale_one = norm_scale(inputs)
    normed_one = (inputs * scale_one * gain_one.astype(jnp.float32)).astype(jnp.bfloat16)
    joined_projection = jnp.dot(normed_one, qkv_full, preferred_element_type=jnp.float32)
    places = positions(sequence_ids)
    cosine_lookup, sine_lookup = rope_tables(places, HEAD_WIDTH)
    query_rows = apply_rotary(
        joined_projection[:, :query_feature_width].reshape(
            sequence_length, QUERY_HEADS, HEAD_WIDTH
        ),
        cosine_lookup,
        sine_lookup,
    ).astype(jnp.bfloat16)
    query_rows = query_rows.reshape(sequence_length, KEY_VALUE_HEADS, query_group_count, HEAD_WIDTH)
    rotated_keys = apply_rotary(
        joined_projection[:, query_feature_width : query_feature_width + key_feature_width].reshape(
            sequence_length, KEY_VALUE_HEADS, HEAD_WIDTH
        ),
        cosine_lookup,
        sine_lookup,
    ).astype(jnp.bfloat16)
    value_inputs = (
        joined_projection[:, query_feature_width + key_feature_width :]
        .reshape(sequence_length, KEY_VALUE_HEADS, HEAD_WIDTH)
        .astype(jnp.bfloat16)
    )
    token_index = jnp.arange(sequence_length, dtype=jnp.int32)

    def block_scores(offset):
        scores = (
            jnp.einsum(
                "qkgd,tkd->kgqt", query_rows, rotated_keys, preferred_element_type=jnp.float32
            )
            * ATTN_SCALE
        )
        allowed = (
            sequence_ids[offset : offset + rows_per_block, None] == sequence_ids[None, :]
        ) & (token_index[None, :] <= token_index[offset : offset + rows_per_block, None])
        return jnp.where(allowed, scores, -jnp.inf)

    offset = 0
    scores = block_scores(offset)
    row_peak = jnp.max(scores, axis=-1, keepdims=True)
    log_total = row_peak + jnp.log(jnp.sum(jnp.exp(scores - row_peak), axis=-1, keepdims=True))
    probs_half = jnp.exp(scores - log_total).astype(jnp.bfloat16)
    mixed_heads = jnp.einsum(
        "kgqt,tkd->qkgd", probs_half, value_inputs, preferred_element_type=jnp.float32
    )
    attention_output_list = mixed_heads.reshape(rows_per_block, query_feature_width).astype(
        jnp.bfloat16
    )
    total_list = [log_total]
    branch = jnp.dot(attention_output_list, out_full, preferred_element_type=jnp.float32)
    middle = inputs + RESIDUAL_SCALE * branch
    scale_two = norm_scale(middle)
    normed_two = (middle * scale_two * gain_two.astype(jnp.float32)).astype(jnp.bfloat16)
    logits = jnp.dot(normed_two, router_full, preferred_element_type=jnp.float32)
    gate_probs = jax.nn.softmax(logits, axis=-1)
    picked = (expert_ids[:, :, None] == jnp.arange(E, dtype=jnp.int32)[None, None, :]).astype(
        jnp.float32
    )
    route_weight = jnp.einsum("tke,te->tk", picked, gate_probs, precision=PRECISE_ARITHMETIC)
    slot_rows = expert_slots(expert_ids, E, CAP)
    received_storage = (
        jnp.zeros((E * CAP, MODEL_WIDTH), jnp.bfloat16)
        .at[slot_rows]
        .set(jnp.repeat(normed_two, TOP, axis=0))
        .reshape(E, CAP, MODEL_WIDTH)
    )
    send_in = dispatch_rows(received_storage, send_table, devices, span_count)
    pre_cols = jnp.einsum(
        "nrkd,dgw->nrkgw",
        lax.all_to_all(send_in, "fsdp", split_axis=0, concat_axis=0, tiled=True),
        owned_gate_up,
        preferred_element_type=jnp.float32,
    )
    pre_cols = pre_cols * column_mask[None, :, None, None, :]
    gate_cols_pre = pre_cols[..., 0, :]
    up_cols_pre = pre_cols[..., 1, :]
    acted = (gate_cols_pre * jax.nn.sigmoid(gate_cols_pre) * up_cols_pre).astype(jnp.bfloat16)
    partial_out = jnp.einsum("nrkw,dw->nrkd", acted, owned_down, preferred_element_type=jnp.float32)
    returned_out = lax.all_to_all(partial_out, "fsdp", split_axis=0, concat_axis=0, tiled=True)
    buffer_out = merge_entries(returned_out, combine_table)
    routed_out = buffer_out.reshape(E * CAP, MODEL_WIDTH)[slot_rows].reshape(
        sequence_length, TOP, MODEL_WIDTH
    )
    combined = jnp.einsum("tk,tkd->td", route_weight, routed_out, precision=PRECISE_ARITHMETIC)
    layer_output = (middle + RESIDUAL_SCALE * combined).astype(jnp.bfloat16)
    upstream = cotangent.astype(jnp.float32)
    grad_mix = RESIDUAL_SCALE * upstream
    grad_weight = jnp.einsum("td,tkd->tk", grad_mix, routed_out, precision=PRECISE_ARITHMETIC)
    grad_rows = (
        (route_weight[:, :, None] * grad_mix[:, None, :])
        .astype(jnp.bfloat16)
        .reshape(sequence_length * TOP, MODEL_WIDTH)
    )
    buffer_grad = (
        jnp.zeros((E * CAP, MODEL_WIDTH), jnp.bfloat16)
        .at[slot_rows]
        .set(grad_rows)
        .reshape(E, CAP, MODEL_WIDTH)
    )
    gain_one_back, qkv_back, out_back, gain_two_back, router_back = dense_set
    send_grad = dispatch_rows(buffer_grad, send_table, devices, span_count)
    rows_in = lax.all_to_all(send_in, "fsdp", split_axis=0, concat_axis=0, tiled=True)
    rows_grad = lax.all_to_all(send_grad, "fsdp", split_axis=0, concat_axis=0, tiled=True)
    pre_cols = jnp.einsum(
        "nrkd,dgw->nrkgw", rows_in, owned_gate_up, preferred_element_type=jnp.float32
    )
    pre_cols = pre_cols * column_mask[None, :, None, None, :]
    gate_cols_pre = pre_cols[..., 0, :]
    up_cols_pre = pre_cols[..., 1, :]
    sigmoid_cols = jax.nn.sigmoid(gate_cols_pre)
    silu_cols = gate_cols_pre * sigmoid_cols
    acted = (silu_cols * up_cols_pre).astype(jnp.bfloat16)
    grad_act_cols = jnp.einsum(
        "nrkd,dw->nrkw", rows_grad, owned_down, preferred_element_type=jnp.float32
    )
    grad_gate_cols = (
        grad_act_cols * up_cols_pre * sigmoid_cols * (1.0 + gate_cols_pre * (1.0 - sigmoid_cols))
    )
    grad_up_cols = grad_act_cols * silu_cols
    grad_pair = jnp.stack([grad_gate_cols, grad_up_cols], axis=3).astype(jnp.bfloat16)
    partial_back = jnp.einsum(
        "nrkgw,dgw->nrkd", grad_pair, owned_gate_up, preferred_element_type=jnp.float32
    )
    returned_back = lax.all_to_all(partial_back, "fsdp", split_axis=0, concat_axis=0, tiled=True)
    results = (returned_back, rows_in, rows_grad, grad_pair, acted)
    returned_back, rows_in_all, rows_grad_all, grad_pair_all, acted_all = results
    backward_buffer = merge_entries(returned_back, combine_table)
    owned_gate_up_grad = jnp.einsum(
        "nrkd,nrkgw->dgw", rows_in_all, grad_pair_all, preferred_element_type=jnp.float32
    )
    owned_down_grad = jnp.einsum(
        "nrkd,nrkw->dw", rows_grad_all, acted_all, preferred_element_type=jnp.float32
    )
    owned_grads = jnp.concatenate([owned_gate_up_grad, owned_down_grad[:, None, :]], axis=1)
    relaid = lax.all_to_all(owned_grads, "fsdp", split_axis=0, concat_axis=2, tiled=True)
    gate_up_grad = jnp.transpose(
        relaid[:, :2, :].reshape(shard_rows, 2, E, F), (0, 2, 1, 3)
    ).reshape(shard_rows, E, 2 * F)
    down_grad = relaid[:, 2, :].reshape(shard_rows, E, F)
    grad_normed = jnp.sum(
        backward_buffer.reshape(E * CAP, MODEL_WIDTH)[slot_rows].reshape(
            sequence_length, TOP, MODEL_WIDTH
        ),
        axis=1,
    )
    grad_gates = jnp.einsum("tk,tke->te", grad_weight, picked, precision=PRECISE_ARITHMETIC)
    grad_logits = gate_probs * (
        grad_gates - jnp.sum(gate_probs * grad_gates, axis=-1, keepdims=True)
    )
    grad_normed = grad_normed + jnp.einsum(
        "te,de->td", grad_logits, router_back.astype(jnp.float32), precision=PRECISE_ARITHMETIC
    )
    router_part = jnp.einsum(
        "td,te->de", normed_two.astype(jnp.float32), grad_logits, precision=PRECISE_ARITHMETIC
    )
    grad_middle, gain_two_part = norm_back(middle, gain_two_back, scale_two, grad_normed)
    grad_middle = grad_middle + upstream
    grad_branch = (RESIDUAL_SCALE * grad_middle).astype(jnp.bfloat16)
    out_part = jnp.einsum(
        "tq,td->qd", attention_output_list, grad_branch, preferred_element_type=jnp.float32
    )
    attention_output_gradient = jnp.einsum(
        "td,qd->tq", grad_branch, out_back, preferred_element_type=jnp.float32
    ).astype(jnp.bfloat16)
    value_gradient = jnp.zeros((sequence_length, KEY_VALUE_HEADS, HEAD_WIDTH), jnp.float32)
    key_gradient = jnp.zeros((sequence_length, KEY_VALUE_HEADS, HEAD_WIDTH), jnp.float32)
    query_grads = []
    for block_number, offset in enumerate(range(0, sequence_length, rows_per_block)):
        scores = block_scores(offset)
        attn_probs = jnp.exp(scores - total_list[block_number])
        block_gradient = attention_output_gradient.reshape(
            rows_per_block, KEY_VALUE_HEADS, query_group_count, HEAD_WIDTH
        )
        attention_output_block = attention_output_list.reshape(
            rows_per_block, KEY_VALUE_HEADS, query_group_count, HEAD_WIDTH
        )
        row_delta = jnp.sum(
            block_gradient.astype(jnp.float32) * attention_output_block.astype(jnp.float32), axis=-1
        )
        row_delta = jnp.transpose(row_delta, (1, 2, 0))[..., None]
        value_gradient = jnp.einsum(
            "kgqt,qkgd->tkd",
            attn_probs.astype(jnp.bfloat16),
            block_gradient,
            preferred_element_type=jnp.float32,
        )
        grad_probs = jnp.einsum(
            "qkgd,tkd->kgqt", block_gradient, value_inputs, preferred_element_type=jnp.float32
        )
        grad_scores = (attn_probs * (grad_probs - row_delta) * ATTN_SCALE).astype(jnp.bfloat16)
        query_grads.append(
            jnp.einsum(
                "kgqt,tkd->qkgd", grad_scores, rotated_keys, preferred_element_type=jnp.float32
            )
        )
        key_gradient = jnp.einsum(
            "kgqt,qkgd->tkd", grad_scores, query_rows, preferred_element_type=jnp.float32
        )
    grad_queries = query_grads[0].reshape(sequence_length, QUERY_HEADS, HEAD_WIDTH)
    grad_joined = jnp.concatenate(
        [
            rotate_back(grad_queries, cosine_lookup, sine_lookup).reshape(
                sequence_length, query_feature_width
            ),
            rotate_back(key_gradient, cosine_lookup, sine_lookup).reshape(
                sequence_length, key_feature_width
            ),
            value_gradient.reshape(sequence_length, key_feature_width),
        ],
        axis=-1,
    ).astype(jnp.bfloat16)
    qkv_part = jnp.einsum("td,tm->dm", normed_one, grad_joined, preferred_element_type=jnp.float32)
    grad_normed_one = jnp.einsum(
        "tm,dm->td", grad_joined, qkv_back, preferred_element_type=jnp.float32
    )
    grad_inputs, gain_one_part = norm_back(inputs, gain_one_back, scale_one, grad_normed_one)
    input_grad = (grad_inputs + grad_middle).astype(jnp.bfloat16)
    dense_grads = (
        lax.psum_scatter(gain_one_part, "fsdp", scatter_dimension=0, tiled=True),
        lax.psum_scatter(qkv_part, "fsdp", scatter_dimension=0, tiled=True),
        lax.psum_scatter(out_part, "fsdp", scatter_dimension=0, tiled=True),
        lax.psum_scatter(gain_two_part, "fsdp", scatter_dimension=0, tiled=True),
        lax.psum_scatter(router_part, "fsdp", scatter_dimension=0, tiled=True),
    )
    return (
        layer_output,
        input_grad,
        dense_grads[0],
        dense_grads[1],
        dense_grads[2],
        dense_grads[3],
        dense_grads[4],
        gate_up_grad,
        down_grad,
    )


D = MODEL_WIDTH
SRC = 8
STEPS = 4
M = SRC * CAP
F32, BF16 = jnp.float32, jnp.bfloat16

def nt(a, b):
    return lax.dot_general(a, b, (((1,), (1,)), ((), ())), preferred_element_type=F32)
def nn(a, b):
    return lax.dot_general(a, b, (((1,), (0,)), ((), ())), preferred_element_type=F32)
def tn(a, b):
    return lax.dot_general(a, b, (((0,), (0,)), ((), ())), preferred_element_type=F32)

QUARTER, DOWN_WHOLE, DOWN_QUARTER, OWN_WIDTH = 0, 256, 768, 896

class Experts:
    NAMES = ("x", "c", "rw", "gw", "act", "dgu", "actq", "dguq", "ow", "gi")

    @staticmethod
    def scratch():
        R = STEPS * M
        return [
            pltpu.VMEM((2, R, D), BF16), pltpu.VMEM((2, R, D), BF16), pltpu.VMEM((2, M, 128), F32), pltpu.VMEM((2, M, 128), F32),
            pltpu.VMEM((R, F), BF16), pltpu.VMEM((R, 2 * F), BF16), pltpu.VMEM((R, 128), BF16), pltpu.VMEM((R, 256), BF16),
            pltpu.VMEM((2, M, D), BF16), pltpu.VMEM((2, M, D), BF16),
        ]

    def __init__(self, refs, wf_ref, wo_ref, pick_ref, prob_ref, gates_ref):
        for name, ref in zip(self.NAMES, refs):
            setattr(self, name, ref)
        self.wf, self.wo, self.pick, self.prob, self.gates = wf_ref, wo_ref, pick_ref, prob_ref, gates_ref

    def picks(self, plane, s):
        return self.pick[pl.ds(pl.multiple_of(plane * (SRC * 64) + s * 64, 64), 64), :]

    def load(self, step, plane, t_ref, c_ref):
        def one(s):
            pick = self.picks(plane, s)
            block = pl.ds(pl.multiple_of(s * 128, 128), 128)
            xs = nn(pick, t_ref[block, :]).astype(BF16)
            cs = nn(pick, c_ref[block, :]).astype(BF16)
            share = pick.astype(F32) * self.prob[pl.ds(pl.multiple_of(plane * (SRC * 64) + s * 64, 64), 64), :]
            share = jnp.sum(share, axis=1, keepdims=True) * RESIDUAL_SCALE
            here = pl.ds(pl.multiple_of(s * CAP, CAP), CAP)
            to = pl.ds(pl.multiple_of(step * M + s * CAP, CAP), CAP)
            for k in range(2):
                self.x[k, to, :] = xs[k * CAP:k * CAP + CAP]
                self.c[k, to, :] = cs[k * CAP:k * CAP + CAP]
                self.rw[k, here, :] = jnp.broadcast_to(share[k * CAP:k * CAP + CAP], (CAP, 128))
        for s in range(SRC):
            one(s)

    def run(self, step):
        at = slice(step * M, step * M + M)
        sets = (
            (self.act, self.dgu, 512, lambda: self.wf[...], DOWN_WHOLE),
            (self.actq, self.dguq, 128, lambda: self.wo[:, QUARTER:QUARTER + 256], DOWN_QUARTER),
        )
        for k, (acts, dgus, w, w_gu, d0) in enumerate(sets):
            pre = nn(self.x[k, at, :], w_gu())
            gate, up = pre[:, :w], pre[:, w:]
            sig = jax.nn.sigmoid(gate)
            silu = gate * sig
            act = silu * up
            share = self.rw[k, :, 0:1]
            scaled = (share * act).astype(BF16)
            acts[at, :] = scaled
            da = nn(self.c[k, at, :], self.wo[:, d0:d0 + w])
            gw = RESIDUAL_SCALE * jnp.sum(act.astype(BF16).astype(F32) * da, axis=1, keepdims=True)
            self.gw[k] = jnp.broadcast_to(gw, (M, 128))
            self.ow[k] = nt(scaled, self.wo[:, d0:d0 + w]).astype(BF16)
            da = share * da
            dgus[at, :w] = (da * up * sig * (1.0 + gate * (1.0 - sig))).astype(BF16)
            dgus[at, w:] = (da * silu).astype(BF16)
            self.gi[k] = nt(dgus[at, :], w_gu()).astype(BF16)

    def give(self, plane, out_ref, gin_ref):
        def one(s):
            r = pl.ds(pl.multiple_of(s * CAP, CAP), CAP)
            pick = self.picks(plane, s)
            to = pl.ds(pl.multiple_of(s * 128, 128), 128)
            out_ref[to, :] = tn(pick, jnp.concatenate([self.ow[0, r, :], self.ow[1, r, :]], axis=0)).astype(BF16)
            gin_ref[to, :] = tn(pick, jnp.concatenate([self.gi[0, r, :], self.gi[1, r, :]], axis=0)).astype(BF16)
            wide = pick.astype(F32)
            rows = [jnp.sum(wide[k * CAP:k * CAP + CAP] * self.gw[k, r, :], axis=0, keepdims=True) for k in range(2)]
            self.gates[plane * SRC + s] = jnp.concatenate(rows + [jnp.zeros((6, 128), F32)], axis=0)
        for s in range(SRC):
            one(s)

    def own_grads(self, j, ref):
        c = slice(j * 256, j * 256 + 256)
        ref[:, QUARTER:QUARTER + 256] = tn(self.x[1, :, c], self.dguq[...]).astype(BF16)
        ref[:, DOWN_WHOLE:DOWN_WHOLE + 512] = tn(self.c[0, :, c], self.act[...]).astype(BF16)
        ref[:, DOWN_QUARTER:DOWN_QUARTER + 128] = tn(self.c[1, :, c], self.actq[...]).astype(BF16)

    def whole_grads(self, j, ref):
        ref[...] = tn(self.x[0, :, j * 256:j * 256 + 256], self.dgu[...]).astype(BF16)


MESH = pl.DeviceIdType.MESH
DEVICES = 32
TURNS = tuple(sorted(range(1, DEVICES), key=lambda k: (k % 8 * 5 % 8, k)))
DMA = pltpu.SemaphoreType.DMA


def dev(z, y, x, c):
    return ((z * 2 + y) * 2 + x) * 2 + c


class Place:
    def __init__(self):
        me = lax.axis_index("fsdp")
        self.me = me
        z, y, x, c = me // 8, lax.rem(me // 4, 2), lax.rem(me // 2, 2), lax.rem(me, 2)
        self.z, self.y, self.x, self.c = z, y, x, c
        self.sib, self.xn, self.yn = dev(z, y, x, 1 - c), dev(z, y, 1 - x, c), dev(z, 1 - y, x, c)
        self.up, self.down = dev(z + 1, y, x, c), dev(z - 1, y, x, c)
        table = ((0, 1, 2, 3), (1, 0, 2, 3), (2, 3, 1, 0), (3, 2, 1, 0))
        self.zq = []
        for q in range(4):
            v = jnp.int32(table[0][q])
            for k in range(1, 4):
                v = jnp.where(z == k, table[k][q], v)
            self.zq.append(v)


def greet_all():
    me = lax.axis_index("fsdp")
    barrier = pltpu.get_barrier_semaphore()
    for k in range(1, DEVICES):
        pl.semaphore_signal(barrier, inc=1, device_id=(lax.rem(me + k, DEVICES),), device_id_type=MESH)
    pl.semaphore_wait(barrier, DEVICES - 1)


def rc(src, dst, ss, rs, to):
    return pltpu.make_async_remote_copy(src_ref=src, dst_ref=dst, send_sem=ss, recv_sem=rs, device_id=(to,), device_id_type=MESH)


class Direct:
    def __init__(self, pieces, refs, sems):
        self.pieces, self.refs, (self.ss, self.rs, self.ls) = pieces, refs, sems
        self.me = lax.axis_index("fsdp")
        self.left = list(TURNS)

    @staticmethod
    def scratch(count):
        return [DMA((DEVICES, count)), DMA((DEVICES, count)), DMA((count,))]

    def own(self):
        self.local = [pltpu.make_async_copy(a, b, self.ls.at[i]) for i, (a, b) in enumerate(self.pieces(self.me, self.me, self.refs))]
        for l in self.local:
            l.start()

    def start(self, number):
        turns, self.left = self.left[:number], self.left[number:]
        for k in turns:
            to = lax.rem(self.me + k, DEVICES)
            for i, (a, b) in enumerate(self.pieces(self.me, to, self.refs)):
                rc(a, b, self.ss.at[k, i], self.rs.at[k, i], to).start()

    def finish(self):
        self.start(DEVICES)
        for k in TURNS:
            src = lax.rem(self.me + DEVICES - k, DEVICES)
            for i, (a, b) in enumerate(self.pieces(src, self.me, self.refs)):
                rc(a, b, self.ss.at[k, i], self.rs.at[k, i], src).wait_recv()
        for k in TURNS:
            to = lax.rem(self.me + k, DEVICES)
            for i, (a, b) in enumerate(self.pieces(self.me, to, self.refs)):
                rc(a, b, self.ss.at[k, i], self.rs.at[k, i], to).wait_send()
        for l in self.local:
            l.wait()


class Gather:
    ORDER = ((1, 0), (1, 1), (2, 0), (1, 2), (2, 1), (3, 0), (1, 3), (2, 2), (3, 1), (2, 3), (3, 2), (3, 3))

    def __init__(self, p, parts, shards, outs, sems):
        self.p, self.parts, self.shards, self.outs, self.sems = p, parts, shards, outs, sems
        self.P, self.sends, self.locals = len(parts), [], []
        self.left = list(self.ORDER)

    @staticmethod
    def scratch(arrays, parts):
        P = len(parts)
        return [DMA((arrays,)), DMA((4, P)), DMA((P,))] + [DMA((4, P))] * 7 + [DMA((4, 4, P))] * 2

    def at(self, i, d):
        a, c0, w, _ = self.parts[i]
        rows = self.shards[a].shape[0]
        return self.outs[a].at[pl.ds(pl.multiple_of(d * rows, rows), rows), pl.ds(c0, w)]

    def spot(self, i, q, k, core):
        p = self.p
        flip_x, flip_y = ((0, 0), (1, 0), (0, 1), (1, 1))[k] if self.parts[i][3] == 0 else ((0, 0), (0, 1), (1, 0), (1, 1))[k]
        return self.at(i, dev(p.zq[q], 1 - p.y if flip_y else p.y, 1 - p.x if flip_x else p.x, core))

    def go(self, copy):
        copy.start()
        self.sends.append(copy)

    def step(self, number=1):
        for f, q in self.left[:number]:
            (self.stage1, self.stage2, self.stage3)[f - 1](q)
        self.left = self.left[number:]

    def stage1(self, q):
        p = self.p
        _, zs, zs2, zr, fs, fr, s1s, s1r, s2s, s2r, cs, cr = self.sems
        for i in range(self.P):
            a, c0, w, mode = self.parts[i]
            first, second = (p.xn, p.yn) if mode == 0 else (p.yn, p.xn)
            here = self.spot(i, q, 0, p.c)
            if q == 0:
                src = self.shards[a].at[:, pl.ds(c0, w)]

                @pl.when(p.z < 3)
                def _():
                    rc(src, here, zs.at[0, i], zr.at[p.z, i], p.up).start()

                @pl.when(p.z > 0)
                def _():
                    rc(src, here, zs2.at[i], zr.at[p.z, i], p.down).start()
            else:
                src, zq = here, p.zq[q]
                rc(here, here, zs.at[q, i], zr.at[zq, i], p.up).wait_recv()

                @pl.when((zq < p.z) & (p.z < 3))
                def _():
                    rc(src, here, zs.at[q, i], zr.at[zq, i], p.up).start()

                @pl.when((zq > p.z) & (p.z > 0))
                def _():
                    rc(src, here, zs.at[q, i], zr.at[zq, i], p.down).start()
            self.go(rc(src, here, fs.at[q, i], fr.at[q, i], first))
            self.go(rc(src, here, s1s.at[q, i], s1r.at[q, i], second))
            self.go(rc(src, here, cs.at[0, q, i], cr.at[0, q, i], p.sib))
        if q == 0:
            for a, (shard, out) in enumerate(zip(self.shards, self.outs)):
                rows = shard.shape[0]
                l = pltpu.make_async_copy(shard, out.at[pl.ds(pl.multiple_of(p.me * rows, rows), rows)], self.sems[0].at[a])
                l.start()
                self.locals.append(l)

    def stage2(self, q):
        p = self.p
        fs, fr, s2s, s2r, cs, cr = self.sems[4:6] + self.sems[8:12]
        for i in range(self.P):
            second = p.yn if self.parts[i][3] == 0 else p.xn
            there = self.spot(i, q, 1, p.c)
            rc(there, there, fs.at[q, i], fr.at[q, i], second).wait_recv()
            self.go(rc(there, there, s2s.at[q, i], s2r.at[q, i], second))
            self.go(rc(there, there, cs.at[1, q, i], cr.at[1, q, i], p.sib))

    def stage3(self, q):
        p = self.p
        cs, cr = self.sems[10:12]
        for k, (ss, rs) in ((2, self.sems[6:8]), (3, self.sems[8:10])):
            for i in range(self.P):
                there = self.spot(i, q, k, p.c)
                rc(there, there, ss.at[q, i], rs.at[q, i], p.sib).wait_recv()
                self.go(rc(there, there, cs.at[k, q, i], cr.at[k, q, i], p.sib))

    def arrived(self):
        self.step(12)
        cs, cr = self.sems[10:12]
        for q in range(4):
            for k in range(4):
                for i in range(self.P):
                    there = self.spot(i, q, k, 1 - self.p.c)
                    rc(there, there, cs.at[k, q, i], cr.at[k, q, i], self.p.sib).wait_recv()
        for l in self.locals:
            l.wait()

    def finish(self):
        p = self.p
        zs, zs2, zr = self.sems[1:4]
        for copy in self.sends:
            copy.wait_send()
        for i in range(self.P):
            here = self.at(i, p.me)

            @pl.when(p.z < 3)
            def _():
                rc(here, here, zs.at[0, i], zr.at[p.z, i], p.up).wait_send()

            @pl.when(p.z > 0)
            def _():
                rc(here, here, zs2.at[i], zr.at[p.z, i], p.down).wait_send()

            for q in range(1, 4):
                zq = p.zq[q]

                @pl.when(((zq < p.z) & (p.z < 3)) | ((zq > p.z) & (p.z > 0)))
                def _():
                    rc(here, here, zs.at[q, i], zr.at[zq, i], p.up).wait_send()


class Scatter:
    ORDER = ((1, 3), (1, 2), (2, 3), (1, 1), (2, 2), (3, 3), (1, 0), (2, 1), (3, 2), (2, 0), (3, 1), (3, 0))
    STEP = 16

    def __init__(self, p, parts, fulls, outs, spaces, sems, in_place=False, by_plane=False):
        self.by_plane, self.reads = by_plane, []
        self.p, self.parts, self.fulls, self.outs, self.sems, self.in_place = p, parts, fulls, outs, sems, in_place
        count = len(fulls)
        if in_place:
            spaces = (None,) * count + tuple(spaces)
        self.held, self.r0, self.r1, self.r2, self.r3 = (spaces[i * count : (i + 1) * count] for i in range(5))
        self.rows = [f.shape[0] // (8 if by_plane else DEVICES) for f in fulls]
        self.P, self.sends = len(parts), []
        self.left = list(self.ORDER)

    def begin_all(self):
        self.reads = self.begin()

    @staticmethod
    def scratch(arrays, parts, in_place=False):
        P = len(parts)
        spaces = []
        for cnt in (16, 8, 4, 5) if in_place else (16, 16, 8, 4, 5):
            spaces += [pltpu.VMEM((cnt, a.shape[0] // DEVICES, a.shape[1]), a.dtype) for a in arrays]
        return spaces, [DMA((4, 4, P))] * 3 + [DMA((4, 2, P))] * 2 + [DMA((4, P))] * 3 + [DMA((5, P))]

    def go(self, copy):
        copy.start()
        self.sends.append(copy)

    def cut(self, i):
        return pl.ds(self.parts[i][1], self.parts[i][2])

    def spot(self, i, k):
        x, y = self.p.x, self.p.y
        if self.parts[i][3] == 0:
            return ((1 - y, 1 - x), (1 - y, x), (y, 1 - x), (y, x))[k]
        return ((1 - y, 1 - x), (y, 1 - x), (1 - y, x), (y, x))[k]

    def slot(self, q, yy, xx):
        return (yy * 2 + xx) * 4 + self.p.zq[q]

    def hold(self, a, q, yy, xx):
        if self.in_place:
            start = dev(self.p.zq[q], yy, xx, self.p.c) * self.rows[a]
            return self.fulls[a].at[pl.ds(pl.multiple_of(start, self.rows[a]), self.rows[a])]
        return self.held[a].at[self.slot(q, yy, xx)]

    def source(self, i, q, k, core):
        a = self.parts[i][0]
        d = dev(0 if self.by_plane else self.p.zq[q], *self.spot(i, k), core)
        return self.fulls[a].at[pl.ds(pl.multiple_of(d * self.rows[a], self.rows[a]), self.rows[a]), self.cut(i)]

    def begin(self, planes=(3, 2, 1, 0)):
        ls, s0, e0 = self.sems[:3]
        made = []
        for q in planes:
            for k in range(4):
                for i in range(self.P):
                    a = self.parts[i][0]
                    s = self.slot(q, *self.spot(i, k))
                    copy = rc(self.source(i, q, k, 1 - self.p.c), self.r0[a].at[s, :, self.cut(i)], s0.at[q, k, i], e0.at[q, k, i], self.p.sib)
                    copy.start()
                    made.append(copy.wait_send)
                    if not self.in_place:
                        l = pltpu.make_async_copy(self.source(i, q, k, self.p.c), self.held[a].at[s, :, self.cut(i)], ls.at[q, k, i])
                        l.start()
                        made.append(l.wait)
        return made

    def step(self, number=1):
        for f, q in self.left[:number]:
            (self.stage1, self.stage2, self.stage3)[f - 1](q)
        self.left = self.left[number:]

    def chunks(self, a, body):
        def one(n, carry):
            body(pl.ds(pl.multiple_of(n * self.STEP, self.STEP), self.STEP))
            return carry

        lax.fori_loop(0, self.rows[a] // self.STEP, one, 0)

    def add(self, i, dst, src, s_src):
        a, c0, w, _ = self.parts[i]

        def body(r):
            v = dst[r, c0 : c0 + w].astype(F32) + src[s_src, r, c0 : c0 + w].astype(F32)
            dst[r, c0 : c0 + w] = v.astype(dst.dtype)

        self.chunks(a, body)

    def stage1(self, q):
        p = self.p
        _, s0, e0, s1, e1 = self.sems[:5]
        for k in range(4):
            for i in range(self.P):
                a = self.parts[i][0]
                first = p.yn if self.parts[i][3] == 0 else p.xn
                s = self.slot(q, *self.spot(i, k))
                sums = self.hold(a, q, *self.spot(i, k))
                here = sums.at[:, self.cut(i)]
                rc(here, self.r0[a].at[s, :, self.cut(i)], s0.at[q, k, i], e0.at[q, k, i], p.sib).wait_recv()
                if self.reads and not self.in_place:
                    self.reads[self.reading(q, k, i) * 2 + 1]()
                self.add(i, sums, self.r0[a], s)
                if k < 2:
                    self.go(rc(here, self.r1[a].at[q * 2 + k, :, self.cut(i)], s1.at[q, k, i], e1.at[q, k, i], first))

    def reading(self, q, k, i):
        return ((3 - q) * 4 + k) * self.P + i

    def stage2(self, q):
        p = self.p
        s1, e1, s2, e2 = self.sems[3:7]
        for k in range(2):
            for i in range(self.P):
                a = self.parts[i][0]
                second = p.xn if self.parts[i][3] == 0 else p.yn
                sums = self.hold(a, q, *self.spot(i, k + 2))
                here = sums.at[:, self.cut(i)]
                rc(here, self.r1[a].at[q * 2 + k, :, self.cut(i)], s1.at[q, k, i], e1.at[q, k, i], p.sib).wait_recv()
                self.add(i, sums, self.r1[a], q * 2 + k)
                if k == 0:
                    self.go(rc(here, self.r2[a].at[q, :, self.cut(i)], s2.at[q, i], e2.at[q, i], second))

    def stage3(self, q):
        p = self.p
        s2, e2, s3, e3 = self.sems[5:9]
        zq, z = p.zq[q], p.z
        for i in range(self.P):
            a, c0, w, _ = self.parts[i]
            r3, out, sums = self.r3[a], self.outs[a], self.hold(a, q, p.y, p.x)
            here = sums.at[:, self.cut(i)]
            rc(here, self.r2[a].at[q, :, self.cut(i)], s2.at[q, i], e2.at[q, i], p.sib).wait_recv()
            self.add(i, sums, self.r2[a], q)
            if q > 0:

                @pl.when((zq > z) & (z > 0) | (zq < z) & (z < 3))
                def _():
                    rc(here, r3.at[zq, :, self.cut(i)], s3.at[q, i], e3.at[zq, i], p.sib).wait_recv()
                    self.add(i, sums, r3, zq)

                @pl.when(zq > z)
                def _():
                    rc(here, r3.at[zq, :, self.cut(i)], s3.at[q, i], e3.at[zq, i], p.up).start()

                @pl.when((zq < z) & (zq == z - 1))
                def _():
                    rc(here, r3.at[4, :, self.cut(i)], s3.at[q, i], e3.at[4, i], p.down).start()

                @pl.when(zq < z - 1)
                def _():
                    rc(here, r3.at[zq, :, self.cut(i)], s3.at[q, i], e3.at[zq, i], p.down).start()
            else:

                def first_sum(r):
                    out[r, c0 : c0 + w] = sums[r, c0 : c0 + w].astype(F32)

                self.chunks(a, first_sum)
                for cond, where in ((z > 0, z), (z < 3, 4)):

                    @pl.when(cond)
                    def _():
                        rc(here, r3.at[where, :, self.cut(i)], s3.at[q, i], e3.at[where, i], p.sib).wait_recv()

                        def more(r):
                            out[r, c0 : c0 + w] += r3[where, r, c0 : c0 + w].astype(F32)

                        self.chunks(a, more)

    def finish(self):
        p = self.p
        s3, e3 = self.sems[7:9]
        for wait in self.reads[:: 1 if self.in_place else 2]:
            wait()
        for copy in self.sends:
            copy.wait_send()
        for q in range(1, 4):
            for i in range(self.P):
                here = self.hold(self.parts[i][0], q, p.y, p.x).at[:, self.cut(i)]
                rc(here, here, s3.at[q, i], e3.at[0, i], p.sib).wait_send()


HBM = pl.BlockSpec(memory_space=pl.ANY)
VMEM = pl.BlockSpec(memory_space=pltpu.VMEM)


def like(*shape, dtype=None):
    return jax.ShapeDtypeStruct(shape, dtype or jnp.bfloat16)


def cut_up(refs, *counts):
    out, i = [], 0
    for c in counts:
        out.append(refs[i : i + c])
        i += c
    return out + [refs[i:]]


GROUP = QUERY_HEADS // KEY_VALUE_HEADS
Q_WIDTH, K_WIDTH = QUERY_HEADS * HEAD_WIDTH, KEY_VALUE_HEADS * HEAD_WIDTH
TOK = 128


def partner(v):
    lane = lax.broadcasted_iota(jnp.int32, v.shape, 1) % HEAD_WIDTH
    return jnp.where(lane < HEAD_WIDTH // 2, pltpu.roll(v, 96, 1), pltpu.roll(v, 32, 1))


def attention_forward(x_ref, cos_ref, sin_ref, bias_ref, qkv_ref, out_ref, small_ref, r):
    def norm_one():
        r.small_t[...] = nt(jnp.eye(TOK, dtype=BF16), small_ref[...])
        x = x_ref[...].astype(F32)
        r.n1[...] = (x * norm_scale(x) * r.small_t[E : E + 1, :]).astype(BF16)

    def project(t):
        def run():
            tile = nn(r.n1[...], qkv_ref[:, t * 512 : t * 512 + 512])
            for b in range(4):
                col = t * 512 + b * 128
                v = tile[:, b * 128 : b * 128 + 128]
                if col < Q_WIDTH + K_WIDTH:
                    v = v * cos_ref[...] + partner(v) * sin_ref[...]
                v = v.astype(BF16)
                for half in range(2):
                    piece = v[:, half * 64 : half * 64 + 64]
                    head = col // 64 + half
                    if col < Q_WIDTH:
                        r.q[head // GROUP, head % GROUP * TOK : head % GROUP * TOK + TOK, :] = piece
                    elif col < Q_WIDTH + K_WIDTH:
                        r.k[head - QUERY_HEADS] = piece
                    else:
                        r.v[head - QUERY_HEADS - KEY_VALUE_HEADS] = piece

        return run

    def attend(j):
        def run():
            s = nt(r.q[j], r.k[j]) * ATTN_SCALE
            s = s + jnp.concatenate([bias_ref[...]] * GROUP, axis=0)
            e = jnp.exp(s - jnp.max(s, axis=1, keepdims=True))
            probs = e / jnp.sum(e, axis=1, keepdims=True)
            r.probs[j] = probs
            o = nn(probs.astype(BF16), r.v[j]).astype(BF16)
            for g in range(GROUP):
                h = j * GROUP + g
                r.att[:, h * 64 : h * 64 + 64] = o[g * TOK : g * TOK + TOK]

        return run

    def output(t):
        def run():
            c = slice(t * 512, t * 512 + 512)
            r.middle[:, c] = x_ref[:, c].astype(F32) + RESIDUAL_SCALE * nn(r.att[...], out_ref[:, c])

        return run

    def norm_two():
        m = r.middle[...]
        r.n2[...] = (m * norm_scale(m) * r.small_t[E + 1 : E + 2, :]).astype(BF16)

    return (
        [norm_one]
        + [project(t) for t in range((Q_WIDTH + 2 * K_WIDTH) // 512)]
        + [attend(j) for j in range(KEY_VALUE_HEADS)]
        + [output(t) for t in range(D // 512)]
        + [norm_two]
    )


def split_dot(form, a, b):
    one = b.astype(BF16)
    rest = b - one.astype(F32)
    two = rest.astype(BF16)
    three = (rest - two.astype(F32)).astype(BF16)
    return form(a, one) + form(a, two) + form(a, three)


def norm_back_rows(hidden, gain, upstream):
    scale = norm_scale(hidden)
    weighted = upstream * gain
    inner = jnp.mean(weighted * hidden, axis=-1, keepdims=True)
    return scale * weighted - hidden * scale**3 * inner, upstream * hidden * scale


def gate_probs(r):
    logits = nt(r.small_t[:64, :].astype(BF16), r.n2[...])
    row = lax.broadcasted_iota(jnp.int32, logits.shape, 0)
    logits = jnp.where(row < E, logits, -jnp.inf)
    e = jnp.exp(logits - jnp.max(logits, axis=0, keepdims=True))
    return e / jnp.sum(e, axis=0, keepdims=True)


def attention_backward(x_ref, cot_ref, gin_ref, gates_ref, cos_ref, sin_ref, qkv_ref, out_ref, r, put_qkv, put_out, put_small):
    def router():
        m = r.middle[...]
        probs = gate_probs(r)
        gates = gates_ref[...]
        gl = probs * (gates - jnp.sum(probs * gates, axis=0, keepdims=True))
        gl = jnp.concatenate([gl, jnp.zeros((64, TOK), F32)], axis=0).T
        r.gl[...] = gl
        back = nn(gl.astype(BF16), r.small_t[...].astype(BF16))
        low = gl - gl.astype(BF16).astype(F32)
        back = back + nn(low.astype(BF16), r.small_t[...].astype(BF16))
        low = low - low.astype(BF16).astype(F32)
        back = back + nn(low.astype(BF16), r.small_t[...].astype(BF16))
        up = gin_ref[...] + back
        gm, gain_rows = norm_back_rows(m, r.small_t[E + 1 : E + 2, :], up)
        gm = gm + cot_ref[...].astype(F32)
        r.gm[...] = gm
        r.gain2[...] = gain_rows
        r.branch[...] = (RESIDUAL_SCALE * gm).astype(BF16)

    def attended(t):
        def run():
            c = slice(t * 512, t * 512 + 512)
            r.ga[:, c] = nt(r.branch[...], out_ref[c, :]).astype(BF16)

        return run

    def out_part(t):
        def run():
            put_out(t, tn(r.att[:, t * 256 : t * 256 + 256], r.branch[...]).astype(BF16))

        return run

    def head(j):
        def run():
            cols = [slice((j * GROUP + g) * 64, (j * GROUP + g) * 64 + 64) for g in range(GROUP)]
            ga = jnp.concatenate([r.ga[:, c] for c in cols], axis=0)
            at = jnp.concatenate([r.att[:, c] for c in cols], axis=0)
            delta = jnp.sum(ga.astype(F32) * at.astype(F32), axis=1, keepdims=True)
            probs = r.probs[j]
            ds = (probs * (nt(ga, r.v[j]) - delta) * ATTN_SCALE).astype(BF16)
            gq = nn(ds, r.k[j])
            for g, c in enumerate(cols):
                r.gjf[:, c] = gq[g * TOK : g * TOK + TOK]
            r.gjf[:, Q_WIDTH + j * 64 : Q_WIDTH + j * 64 + 64] = tn(ds, r.q[j])
            r.gjf[:, Q_WIDTH + K_WIDTH + j * 64 : Q_WIDTH + K_WIDTH + j * 64 + 64] = tn(probs.astype(BF16), ga)

        return run

    def rotate():
        for col in range(0, Q_WIDTH + 2 * K_WIDTH, 128):
            v = r.gjf[:, col : col + 128]
            if col < Q_WIDTH + K_WIDTH:
                v = v * cos_ref[...] - partner(v) * sin_ref[...]
            r.gj[:, col : col + 128] = v.astype(BF16)

    def qkv_part(t):
        def run():
            put_qkv(t, tn(r.n1[:, t * 256 : t * 256 + 256], r.gj[...]).astype(BF16))

        return run

    def into_normed(t):
        def run():
            c = slice(t * 256, t * 256 + 256)
            r.gn[:, c] = nt(r.gj[...], qkv_ref[c, :])

        return run

    def input_back():
        x = x_ref[...].astype(F32)
        gx, gain_rows = norm_back_rows(x, r.small_t[E : E + 1, :], r.gn[...])
        r.input_grad[...] = (gx + r.gm[...]).astype(BF16)
        lane = lax.broadcasted_iota(jnp.int32, (TOK, TOK), 1)
        small = split_dot(tn, r.n2[...], r.gl[...])
        for rows, at in ((gain_rows, E), (r.gain2[...], E + 1)):
            ones = jnp.where(lane == at, 1.0, 0.0).astype(BF16)
            hi = rows.astype(BF16)
            lo = (rows - hi.astype(F32)).astype(BF16)
            small = small + tn(hi, ones) + tn(lo, ones)
        put_small(small.astype(BF16))

    first = [router] + [attended(t) for t in range(3)] + [out_part(t) for t in range(6)]
    heads = [head(j) for j in range(KEY_VALUE_HEADS)] + [rotate]
    last = [into_normed(t) for t in range(6)] + [input_back] + [qkv_part(t) for t in range(6)]
    return first, heads, last


class Results:
    pass


ATT_NAMES = ("small_t", "n1", "q", "k", "v", "probs", "att", "middle", "n2")
ATT_SHAPES = (
    ((TOK, D), F32),
    ((TOK, D), BF16),
    ((KEY_VALUE_HEADS, GROUP * TOK, HEAD_WIDTH), BF16),
    ((KEY_VALUE_HEADS, TOK, HEAD_WIDTH), BF16),
    ((KEY_VALUE_HEADS, TOK, HEAD_WIDTH), BF16),
    ((KEY_VALUE_HEADS, GROUP * TOK, TOK), F32),
    ((TOK, Q_WIDTH), BF16),
    ((TOK, D), F32),
    ((TOK, D), BF16),
)
ROW_HALVES = ((0, 0, 768, 0), (0, 768, 768, 1))
DENSE_PARTS = ((0, 0, 1280, 0), (0, 1280, 1280, 1), (1, 0, 768, 0), (1, 768, 768, 1), (2, 0, 128, 1))
TOKEN_PARTS = ROW_HALVES + ((1, 0, 128, 1),)
FIRST_PARTS = DENSE_PARTS + ((3, 0, 128, 0),)


def lanes(start):
    return pl.ds(pl.multiple_of(start, 128), 128)


def weights_out(src, dst, refs):
    g_ref, d_ref, wf_ref, wo_ref = refs
    group, own, quarter = dst // 4, lax.rem(dst, 4), lax.rem(dst, 4) * 128
    rows = pl.ds(pl.multiple_of(src * 48, 48), 48)
    fifth = group * 5 + 4
    return (
        (g_ref.at[fifth, :, lanes(quarter)], wo_ref.at[rows, pl.ds(QUARTER, 128)]),
        (g_ref.at[fifth, :, lanes(F + quarter)], wo_ref.at[rows, pl.ds(QUARTER + 128, 128)]),
        (d_ref.at[group * 5 + own], wo_ref.at[rows, pl.ds(DOWN_WHOLE, F)]),
        (d_ref.at[fifth, :, lanes(quarter)], wo_ref.at[rows, pl.ds(DOWN_QUARTER, 128)]),
        (g_ref.at[group * 5 + own], wf_ref.at[rows]),
    )


def down_back(src, dst, refs):
    dwo_ref, gates_ref, d_ref, all_gates_ref = refs
    group, quarter = src // 4, lax.rem(src, 4) * 128
    rows = pl.ds(pl.multiple_of(dst * 48, 48), 48)
    return (
        (gates_ref.at[dst], all_gates_ref.at[src]),
        (dwo_ref.at[rows, pl.ds(DOWN_WHOLE, F)], d_ref.at[group * 5 + lax.rem(src, 4)]),
        (dwo_ref.at[rows, pl.ds(DOWN_QUARTER, 128)], d_ref.at[group * 5 + 4, :, lanes(quarter)]),
    )


def gate_up_back(src, dst, refs):
    dwf_ref, dwo_ref, g_ref = refs
    group, quarter = src // 4, lax.rem(src, 4) * 128
    rows = pl.ds(pl.multiple_of(dst * 48, 48), 48)
    return (
        (dwf_ref.at[rows], g_ref.at[group * 5 + lax.rem(src, 4)]),
        (dwo_ref.at[rows, pl.ds(QUARTER, 128)], g_ref.at[group * 5 + 4, :, lanes(quarter)]),
        (dwo_ref.at[rows, pl.ds(QUARTER + 128, 128)], g_ref.at[group * 5 + 4, :, lanes(F + quarter)]),
    )


def route_weights(ids, r, rw):
    probs = gate_probs(r)
    row = lax.broadcasted_iota(jnp.int32, probs.shape, 0)
    for k in range(TOP):
        rw[k : k + 1, :] = jnp.sum(jnp.where(row == ids[k : k + 1, :], probs, 0.0), axis=0, keepdims=True)


def first_kernel(*refs):
    (x, cos, sin, bias, ids), dense, (cot,), experts_in, dense_out, outs, results, weights, (rw, load_sem), refs = cut_up(
        refs, 5, 4, 1, 2, 4, 5, 9, 3, 2
    )
    cots, tokens, shares, wf, wo = outs
    sems1, sems2, sems3, direct_sems, _ = cut_up(refs, 12, 12, 12, 3)
    greet_all()
    p = Place()
    r = Results()
    for name, ref in zip(ATT_NAMES, results):
        setattr(r, name, ref)
    g1 = Gather(p, FIRST_PARTS, dense, dense_out, sems1)
    g2 = Gather(p, ROW_HALVES, [cot], [cots], sems2)
    g3 = Gather(p, TOKEN_PARTS, [r.n2, rw], [tokens, shares], sems3)
    direct = Direct(weights_out, tuple(experts_in) + (wf, wo), direct_sems)
    g1.step()
    direct.own()
    for n in FIRST_BATCHES:
        g1.step()
        direct.start(n)
    g2.step(2)
    direct.start(DEVICES)
    g1.arrived()
    loads = [pltpu.make_async_copy(a, b, load_sem.at[i]) for i, (a, b) in enumerate(zip(dense_out[:3], weights))]
    for l in loads:
        l.start()
    g2.step(2)
    for l in loads:
        l.wait()
    for i, chunk in enumerate(attention_forward(x, cos, sin, bias, *weights, r)):
        chunk()
        if i % 2 == 1:
            g2.step()
    route_weights(ids, r, rw)
    g3.step(2)
    g2.arrived()
    g3.arrived()
    for g in (g1, g2, g3):
        g.finish()
    direct.finish()


FIRST_BATCHES = (1, 1, 1, 1, 1, 1, 1, 1, 1, 1)


def first(x, cos, sin, bias, ids, dense, cot, gu, dp):
    wide = lambda a: like(DEVICES * a.shape[0], a.shape[1], dtype=a.dtype)
    dense_full = [wide(a) for a in dense]
    return pl.pallas_call(
        first_kernel,
        in_specs=[VMEM] * 5 + [HBM] * 7,
        out_specs=[HBM] * 9 + [VMEM] * 9,
        out_shape=dense_full + [wide(cot), wide(cot), like(DEVICES * TOP, TOK, dtype=F32), like(D, 2 * F), like(D, OWN_WIDTH)] + [like(*s, dtype=t) for s, t in ATT_SHAPES],
        scratch_shapes=[pltpu.VMEM(a.shape, a.dtype) for a in dense_full[:3]]
        + [pltpu.VMEM((TOP, TOK), F32), DMA((3,))]
        + Gather.scratch(4, FIRST_PARTS)
        + Gather.scratch(1, ROW_HALVES)
        + Gather.scratch(2, TOKEN_PARTS)
        + Direct.scratch(5),
        compiler_params=pltpu.CompilerParams(collective_id=0, has_side_effects=True, vmem_limit_bytes=60 * 2**20),
    )(x, cos, sin, bias, ids, *dense, cot, gu, dp)


def middle_kernel(*refs):
    (picks, probs), (tokens, cots, wf_in, wo_in), (gin,), outs, blocks, work, refs = cut_up(refs, 2, 4, 1, 5, 9, 10)
    out_part, dwf, dwo, all_gates, grad_down = outs
    t, c, out_block, gin_block, wf, wo, gates, whole, own = blocks
    (weight_sem, load_sem, out_sem, grad_sem), spaces, sems, direct_sems, _ = cut_up(refs, 4, 5, 9, 3)
    greet_all()
    p = Place()
    s = Scatter(p, ROW_HALVES, [gin_block], [gin], spaces, sems, by_plane=True)
    direct = Direct(down_back, (dwo, gates, grad_down, all_gates), direct_sems)
    e = Experts(work, wf, wo, picks, probs, gates)
    R = SRC * TOK

    def plane_rows(q):
        return pl.ds(pl.multiple_of(p.zq[q] * R, R), R)

    def load(q):
        made = [pltpu.make_async_copy(src.at[plane_rows(q)], dst, load_sem.at[i]) for i, (src, dst) in enumerate(((tokens, t), (cots, c)))]
        for l in made:
            l.start()
        return made

    order = (3, 2, 1, 0)
    loads = load(order[0])
    weights = [pltpu.make_async_copy(a, b, weight_sem.at[i]) for i, (a, b) in enumerate(((wf_in, wf), (wo_in, wo)))]
    for l in weights:
        l.start()
    reads, store = [], None
    for step, q in enumerate(order):
        for l in loads:
            l.wait()
        e.load(step, p.zq[q], t, c)
        if step < 3:
            loads = load(order[step + 1])
        if step == 0:
            for l in weights:
                l.wait()
        for wait in reads:
            wait()
        s.step(step)
        e.run(step)
        if store is not None:
            store.wait()
        e.give(p.zq[q], out_block, gin_block)
        reads = s.begin((q,))
        store = pltpu.make_async_copy(out_block, out_part.at[plane_rows(q)], out_sem)
        store.start()
    stores = []
    for n in range(2 * (D // 256)):
        a, j, b = n // (D // 256), n % (D // 256), n % 2
        block, out, make = ((own, dwo, e.own_grads), (whole, dwf, e.whole_grads))[a]
        if j >= 2:
            stores[n - 2].wait()
        make(j, block.at[b])
        l = pltpu.make_async_copy(block.at[b], out.at[pl.ds(j * 256, 256)], grad_sem.at[b, a])
        l.start()
        stores.append(l)
        if j == D // 256 - 1:
            for l in stores[-2:]:
                l.wait()
            if a == 0:
                direct.own()
                direct.start(DEVICES)
        if n == 1:
            for wait in reads:
                wait()
        if n % 2 == 1:
            s.step()
    s.step(12)
    store.wait()
    s.finish()
    direct.finish()


def middle(picks, probs, tokens, cots, wf, wo):
    R = SRC * TOK
    spaces, sems = Scatter.scratch([tokens], ROW_HALVES)
    return pl.pallas_call(
        middle_kernel,
        in_specs=[VMEM] * 2 + [HBM] * 4,
        out_specs=[VMEM] + [HBM] * 5,
        out_shape=[like(TOK, D, dtype=F32), like(DEVICES * TOK, D), like(D, 2 * F), like(D, OWN_WIDTH), like(DEVICES, 8, TOK, dtype=F32), like(E, D // DEVICES, F)],
        scratch_shapes=[pltpu.VMEM((R, D), BF16)] * 4
        + [
            pltpu.VMEM((D, 2 * F), BF16), pltpu.VMEM((D, OWN_WIDTH), BF16), pltpu.VMEM((DEVICES, 8, TOK), F32),
            pltpu.VMEM((2, 256, 2 * F), BF16), pltpu.VMEM((2, 256, OWN_WIDTH), BF16),
        ]
        + Experts.scratch()
        + [DMA((2,)), DMA((2,)), DMA, DMA((2, 2))]
        + spaces + sems + Direct.scratch(3),
        compiler_params=pltpu.CompilerParams(collective_id=1, has_side_effects=True, vmem_limit_bytes=63 * 2**20),
    )(picks, probs, tokens, cots, wf, wo)


WORK = (
    ("gl", (TOK, TOK), F32),
    ("gm", (TOK, D), F32),
    ("gain2", (TOK, D), F32),
    ("branch", (TOK, D), BF16),
    ("ga", (TOK, D), BF16),
    ("gjf", (TOK, Q_WIDTH + 2 * K_WIDTH), F32),
    ("gj", (TOK, Q_WIDTH + 2 * K_WIDTH), BF16),
    ("gn", (TOK, D), F32),
)


def last_kernel(*refs):
    (x, cot, gin, gates, cos, sin), results, (qkv_full, out_full, out_part, dwf, dwo), outs, work, weights, (small_src, load_sem), refs = cut_up(
        refs, 6, 9, 5, 6, len(WORK), 2, 2
    )
    input_grad, combined, qkv_grad, out_grad, small_grad, grad_gu = outs
    spaces1, sems1, spaces2, sems2, direct_sems, _ = cut_up(refs, 5, 9, 12, 9, 3)
    greet_all()
    p = Place()
    r = Results()
    for name, ref in zip(ATT_NAMES + tuple(w[0] for w in WORK), tuple(results) + tuple(work)):
        setattr(r, name, ref)
    r.input_grad = input_grad
    qkv_ref, out_ref = weights
    s1 = Scatter(p, ROW_HALVES, [out_part], [combined], spaces1, sems1)
    s2 = Scatter(p, DENSE_PARTS, [qkv_ref, out_ref, small_src], [qkv_grad, out_grad, small_grad], spaces2, sems2, in_place=True)
    direct = Direct(gate_up_back, (dwf, dwo, grad_gu), direct_sems)
    s1.begin_all()
    loads = [pltpu.make_async_copy(a, b, load_sem.at[i]) for i, (a, b) in enumerate(((out_full, out_ref), (qkv_full, qkv_ref)))]
    for l in loads:
        l.start()
    direct.own()
    direct.start(12)

    def put_qkv(t, value):
        qkv_ref[t * 256 : t * 256 + 256, :] = value

    def put_out(t, value):
        out_ref[t * 256 : t * 256 + 256, :] = value

    def put_small(value):
        small_src[...] = value

    begin, heads, end = attention_backward(x, cot, gin, gates, cos, sin, qkv_ref, out_ref, r, put_qkv, put_out, put_small)
    for l in loads:
        l.wait()
    for i, chunk in enumerate(begin + heads + end):
        chunk()
        if i % 3 == 2:
            s1.step()
            direct.start(2)
    s2.begin_all()
    s1.step(12)
    while s2.left:
        s2.step()
        direct.start(2)
    direct.start(DEVICES)
    s1.finish()
    s2.finish()
    direct.finish()


def last(x, cot, gin, gates, cos, sin, results, qkv_full, out_full, out_part, dwf, dwo):
    small = like(D, TOK)
    spaces1, sems1 = Scatter.scratch([out_part], ROW_HALVES)
    spaces2, sems2 = Scatter.scratch([qkv_full, out_full, small], DENSE_PARTS, in_place=True)
    own = D // DEVICES
    return pl.pallas_call(
        last_kernel,
        in_specs=[VMEM] * 15 + [HBM] * 5,
        out_specs=[VMEM] * 5 + [HBM],
        out_shape=[
            like(TOK, D), like(TOK, D, dtype=F32), like(own, qkv_full.shape[1], dtype=F32), like(own, D, dtype=F32),
            like(own, TOK, dtype=F32), like(E, own, 2 * F),
        ],
        scratch_shapes=[pltpu.VMEM(s, t) for _, s, t in WORK]
        + [pltpu.VMEM(qkv_full.shape, BF16), pltpu.VMEM(out_full.shape, BF16), pltpu.VMEM(small.shape, BF16), DMA((2,))]
        + spaces1 + sems1 + spaces2 + sems2
        + Direct.scratch(3),
        compiler_params=pltpu.CompilerParams(collective_id=2, has_side_effects=True, vmem_limit_bytes=63 * 2**20),
    )(x, cot, gin, gates, cos, sin, *results, qkv_full, out_full, out_part, dwf, dwo)


def fast(
    layer_input, cotangent, sequence_ids, expert_ids, attention_gain, qkv_weight, output_weight, moe_gain, router, gate_up, down_proj
):
    n, own_rows, T = DEVICES, gate_up.shape[0], layer_input.shape[0]
    me = lax.axis_index("fsdp")
    small = jnp.concatenate(
        [router, attention_gain[:, None], moe_gain[:, None], jnp.zeros((own_rows, 86), BF16)], axis=1
    )
    cosine, sine = rope_tables(positions(sequence_ids), HEAD_WIDTH)
    cos = jnp.concatenate([cosine] * 4, axis=1)
    sin = jnp.concatenate([-sine, sine] * 2, axis=1)
    place_in = jnp.arange(T, dtype=jnp.int32)
    allowed = (sequence_ids[:, None] == sequence_ids[None, :]) & (place_in[None, :] <= place_in[:, None])
    bias = jnp.where(allowed, 0.0, -jnp.inf).astype(F32)

    ids_t = expert_ids.T
    qkv_full, out_full, small_full, ids_all, cots, tokens, shares, wf, wo, *results = first(
        layer_input, cos, sin, bias, ids_t, [qkv_weight, output_weight, small, ids_t], cotangent,
        jnp.transpose(gate_up, (1, 0, 2)), jnp.transpose(down_proj, (1, 0, 2)),
    )

    owned = jnp.stack([(me // 4) * 5 + lax.rem(me, 4), (me // 4) * 5 + 4])
    named = ids_all.reshape(n, TOP, T)[:, :, None, :] == owned[None, None, :, None]
    probs = jnp.sum(jnp.where(named, shares.reshape(n, TOP, 1, T), 0.0), axis=1)
    probs = jnp.broadcast_to(probs[:, :, None, :], (n, 2, CAP, T)).reshape(n * 64, T)
    named = jnp.any(named, axis=1)
    before = (place_in[:, None] < place_in[None, :]).astype(BF16)
    ranks = jnp.dot(named.astype(BF16).reshape(2 * n, T), before, preferred_element_type=F32).reshape(n, 2, 1, T)
    picks = ((ranks == jnp.arange(CAP, dtype=F32)[:, None]) & named[:, :, None, :]).astype(BF16).reshape(n * 64, T)
    gin, out_part, dwf, dwo, gates, grad_down = middle(picks, probs, tokens, cots, wf, wo)
    gates = gates.reshape(8, 4, 8, T)
    gates = jnp.concatenate([gates[:, :, 0], jnp.sum(gates[:, :, 1], axis=1, keepdims=True)], axis=1).reshape(E, T)
    gates = jnp.pad(gates, ((0, 64 - E), (0, 0)))
    input_grad, combined, qkv_grad, out_grad, small_grad, grad_gu = last(
        layer_input, cotangent, gin, gates, cos, sin, results, qkv_full, out_full, out_part, dwf, dwo
    )
    layer_output = (results[ATT_NAMES.index("middle")] + combined).astype(BF16)
    gate_up_grad = jnp.transpose(grad_gu, (1, 0, 2)).astype(F32)
    down_grad = jnp.transpose(grad_down, (1, 0, 2)).astype(F32)
    return (
        layer_output,
        input_grad,
        small_grad[:, E],
        qkv_grad,
        out_grad,
        small_grad[:, E + 1],
        small_grad[:, :E],
        gate_up_grad,
        down_grad,
    )


def solution(mesh):
    rows, flat, cube = P("fsdp", None), P("fsdp"), P("fsdp", None, None)
    return jax.shard_map(
        fast if mesh.shape["fsdp"] == 32 else on_device,
        mesh=mesh,
        in_specs=(rows, rows, flat, rows, flat, rows, rows, flat, rows, cube, cube),
        out_specs=(rows, rows, flat, rows, rows, flat, rows, cube, cube),
        check_vma=False,
    )
```

```python
import functools
import math
import jax
import jax.numpy as jnp
import numpy as np
from jax import lax
from jax.experimental import pallas as pl
from jax.experimental.pallas import tpu as pltpu
from jax.sharding import PartitionSpec as P

MODEL_WIDTH = 1536
QUERY_HEADS = 24
KEY_VALUE_HEADS = 8
HEAD_WIDTH = 64
E = 40
F = 512
TOP = 8
CAP = 32


EPSILON = 1e-06
ATTN_SCALE = 0.015625
RESIDUAL_SCALE = 0.22
ROPE_BASE = 10000.0
PRECISE_ARITHMETIC = lax.Precision.HIGHEST


def positions(sequence_ids):
    sequence_length = sequence_ids.shape[0]
    places = jnp.arange(sequence_length, dtype=jnp.int32)
    same = (sequence_ids[:, None] == sequence_ids[None, :]) & (places[None, :] < places[:, None])
    return jnp.sum(same.astype(jnp.int32), axis=1, dtype=jnp.int32)


def rope_tables(places, head_size):
    half_size = head_size // 2
    exponents = jnp.arange(half_size, dtype=jnp.float32) * (2.0 / head_size)
    inverse = jnp.exp(exponents * -math.log(ROPE_BASE))
    angles = places.astype(jnp.float32)[:, None] * inverse[None, :]
    return (jnp.cos(angles), jnp.sin(angles))


def apply_rotary(tensor, cosine_lookup, sine_lookup):
    half_size = tensor.shape[-1] // 2
    first_half = tensor[..., :half_size]
    second_half = tensor[..., half_size:]
    cosine_rows = cosine_lookup[:, None, :]
    sine_rows = sine_lookup[:, None, :]
    return jnp.concatenate(
        [
            first_half * cosine_rows - second_half * sine_rows,
            second_half * cosine_rows + first_half * sine_rows,
        ],
        axis=-1,
    )


def rotate_back(tensor, cosine_lookup, sine_lookup):
    half_size = tensor.shape[-1] // 2
    first_half = tensor[..., :half_size]
    second_half = tensor[..., half_size:]
    cosine_rows = cosine_lookup[:, None, :]
    sine_rows = sine_lookup[:, None, :]
    return jnp.concatenate(
        [
            first_half * cosine_rows + second_half * sine_rows,
            second_half * cosine_rows - first_half * sine_rows,
        ],
        axis=-1,
    )


def norm_scale(hidden_state):
    return lax.rsqrt(jnp.mean(hidden_state * hidden_state, axis=-1, keepdims=True) + EPSILON)


def norm_back(hidden_state, gain_vector, scale_rows, upstream):
    weighted = upstream * gain_vector.astype(jnp.float32)
    inner_mean = jnp.mean(weighted * hidden_state, axis=-1, keepdims=True)
    grad_hidden = scale_rows * weighted - hidden_state * scale_rows**3 * inner_mean
    grad_gain = jnp.sum(upstream * hidden_state * scale_rows, axis=0)
    return (grad_hidden, grad_gain)


def expert_slots(expert_ids, experts, capacity):
    rows = expert_ids.shape[0]
    picked = expert_ids[:, :, None] == jnp.arange(experts, dtype=jnp.int32)[None, None, :]
    named = jnp.any(picked, axis=1).astype(jnp.bfloat16)
    places = jnp.arange(rows, dtype=jnp.int32)
    before = (places[None, :] < places[:, None]).astype(jnp.bfloat16)
    ranks = jnp.dot(before, named, preferred_element_type=jnp.float32)
    ranks = jnp.sum(jnp.where(picked, ranks[:, None, :], 0.0), axis=-1).astype(jnp.int32)
    return (expert_ids * capacity + ranks).reshape(-1)


def owner_tables(devices):
    width_owned = E * F // devices
    span_count = (F + width_owned - 2) // F + 1
    first_expert = np.arange(devices) * width_owned // F
    send_table = np.minimum(first_expert[:, None] + np.arange(span_count)[None, :], E).reshape(-1)
    combine_table = (send_table[None, :] == np.arange(E)[:, None]).astype(np.float32)
    return (width_owned, span_count, send_table, combine_table)


def dispatch_rows(buffer_rows, send_table, devices, span_count):
    padded = jnp.concatenate(
        [buffer_rows, jnp.zeros((1, CAP, MODEL_WIDTH), buffer_rows.dtype)], axis=0
    )
    chosen = jnp.asarray(send_table[:, None] == np.arange(E + 1)[None, :], dtype=buffer_rows.dtype)
    picked_rows = jnp.einsum(
        "se,ecd->scd", chosen, padded, preferred_element_type=jnp.float32
    ).astype(buffer_rows.dtype)
    return picked_rows.reshape(devices, span_count, CAP, MODEL_WIDTH)


def merge_entries(returned, combine_table):
    flat_rows = returned.reshape(returned.shape[0] * returned.shape[1], CAP * MODEL_WIDTH)
    summed = jnp.dot(
        jnp.asarray(combine_table),
        flat_rows,
        precision=PRECISE_ARITHMETIC,
        preferred_element_type=jnp.float32,
    )
    return summed.reshape(E, CAP, MODEL_WIDTH)


def on_device(
    layer_input,
    cotangent,
    sequence_ids,
    expert_ids,
    attention_gain,
    qkv_weight,
    output_weight,
    moe_gain,
    router,
    gate_up,
    down_proj,
):
    sequence_length = layer_input.shape[0]
    shard_rows = gate_up.shape[0]
    query_group_count = QUERY_HEADS // KEY_VALUE_HEADS
    query_feature_width = QUERY_HEADS * HEAD_WIDTH
    key_feature_width = KEY_VALUE_HEADS * HEAD_WIDTH
    rows_per_block = min(512, sequence_length)
    devices = lax.axis_size("fsdp")
    dense_set = (
        lax.all_gather(attention_gain, "fsdp", axis=0, tiled=True),
        lax.all_gather(qkv_weight, "fsdp", axis=0, tiled=True),
        lax.all_gather(output_weight, "fsdp", axis=0, tiled=True),
        lax.all_gather(moe_gain, "fsdp", axis=0, tiled=True),
        lax.all_gather(router, "fsdp", axis=0, tiled=True),
    )
    gain_one, qkv_full, out_full, gain_two, router_full = dense_set
    width_owned, span_count, send_table, combine_table = owner_tables(devices)
    gate_cols = jnp.transpose(gate_up.reshape(shard_rows, E, 2, F), (0, 2, 1, 3)).reshape(
        shard_rows, 2, E * F
    )
    down_cols = down_proj.reshape(shard_rows, 1, E * F)
    owned_weights = lax.all_to_all(
        jnp.concatenate([gate_cols, down_cols], axis=1),
        "fsdp",
        split_axis=2,
        concat_axis=0,
        tiled=True,
    )
    owned_gate_up = owned_weights[:, :2, :]
    owned_down = owned_weights[:, 2, :]
    owner_index = lax.axis_index("fsdp")
    owned_start = owner_index * width_owned
    owned_columns = owned_start + jnp.arange(width_owned, dtype=jnp.int32)
    slot_of = owned_columns // F - owned_start // F
    column_mask = (slot_of[None, :] == jnp.arange(span_count, dtype=jnp.int32)[:, None]).astype(
        jnp.float32
    )
    inputs = layer_input.astype(jnp.float32)
    scale_one = norm_scale(inputs)
    normed_one = (inputs * scale_one * gain_one.astype(jnp.float32)).astype(jnp.bfloat16)
    joined_projection = jnp.dot(normed_one, qkv_full, preferred_element_type=jnp.float32)
    places = positions(sequence_ids)
    cosine_lookup, sine_lookup = rope_tables(places, HEAD_WIDTH)
    query_rows = apply_rotary(
        joined_projection[:, :query_feature_width].reshape(
            sequence_length, QUERY_HEADS, HEAD_WIDTH
        ),
        cosine_lookup,
        sine_lookup,
    ).astype(jnp.bfloat16)
    query_rows = query_rows.reshape(sequence_length, KEY_VALUE_HEADS, query_group_count, HEAD_WIDTH)
    rotated_keys = apply_rotary(
        joined_projection[:, query_feature_width : query_feature_width + key_feature_width].reshape(
            sequence_length, KEY_VALUE_HEADS, HEAD_WIDTH
        ),
        cosine_lookup,
        sine_lookup,
    ).astype(jnp.bfloat16)
    value_inputs = (
        joined_projection[:, query_feature_width + key_feature_width :]
        .reshape(sequence_length, KEY_VALUE_HEADS, HEAD_WIDTH)
        .astype(jnp.bfloat16)
    )
    token_index = jnp.arange(sequence_length, dtype=jnp.int32)

    def block_scores(offset):
        scores = (
            jnp.einsum(
                "qkgd,tkd->kgqt", query_rows, rotated_keys, preferred_element_type=jnp.float32
            )
            * ATTN_SCALE
        )
        allowed = (
            sequence_ids[offset : offset + rows_per_block, None] == sequence_ids[None, :]
        ) & (token_index[None, :] <= token_index[offset : offset + rows_per_block, None])
        return jnp.where(allowed, scores, -jnp.inf)

    offset = 0
    scores = block_scores(offset)
    row_peak = jnp.max(scores, axis=-1, keepdims=True)
    log_total = row_peak + jnp.log(jnp.sum(jnp.exp(scores - row_peak), axis=-1, keepdims=True))
    probs_half = jnp.exp(scores - log_total).astype(jnp.bfloat16)
    mixed_heads = jnp.einsum(
        "kgqt,tkd->qkgd", probs_half, value_inputs, preferred_element_type=jnp.float32
    )
    attention_output_list = mixed_heads.reshape(rows_per_block, query_feature_width).astype(
        jnp.bfloat16
    )
    total_list = [log_total]
    branch = jnp.dot(attention_output_list, out_full, preferred_element_type=jnp.float32)
    middle = inputs + RESIDUAL_SCALE * branch
    scale_two = norm_scale(middle)
    normed_two = (middle * scale_two * gain_two.astype(jnp.float32)).astype(jnp.bfloat16)
    logits = jnp.dot(normed_two, router_full, preferred_element_type=jnp.float32)
    gate_probs = jax.nn.softmax(logits, axis=-1)
    picked = (expert_ids[:, :, None] == jnp.arange(E, dtype=jnp.int32)[None, None, :]).astype(
        jnp.float32
    )
    route_weight = jnp.einsum("tke,te->tk", picked, gate_probs, precision=PRECISE_ARITHMETIC)
    slot_rows = expert_slots(expert_ids, E, CAP)
    received_storage = (
        jnp.zeros((E * CAP, MODEL_WIDTH), jnp.bfloat16)
        .at[slot_rows]
        .set(jnp.repeat(normed_two, TOP, axis=0))
        .reshape(E, CAP, MODEL_WIDTH)
    )
    send_in = dispatch_rows(received_storage, send_table, devices, span_count)
    pre_cols = jnp.einsum(
        "nrkd,dgw->nrkgw",
        lax.all_to_all(send_in, "fsdp", split_axis=0, concat_axis=0, tiled=True),
        owned_gate_up,
        preferred_element_type=jnp.float32,
    )
    pre_cols = pre_cols * column_mask[None, :, None, None, :]
    gate_cols_pre = pre_cols[..., 0, :]
    up_cols_pre = pre_cols[..., 1, :]
    acted = (gate_cols_pre * jax.nn.sigmoid(gate_cols_pre) * up_cols_pre).astype(jnp.bfloat16)
    partial_out = jnp.einsum("nrkw,dw->nrkd", acted, owned_down, preferred_element_type=jnp.float32)
    returned_out = lax.all_to_all(partial_out, "fsdp", split_axis=0, concat_axis=0, tiled=True)
    buffer_out = merge_entries(returned_out, combine_table)
    routed_out = buffer_out.reshape(E * CAP, MODEL_WIDTH)[slot_rows].reshape(
        sequence_length, TOP, MODEL_WIDTH
    )
    combined = jnp.einsum("tk,tkd->td", route_weight, routed_out, precision=PRECISE_ARITHMETIC)
    layer_output = (middle + RESIDUAL_SCALE * combined).astype(jnp.bfloat16)
    upstream = cotangent.astype(jnp.float32)
    grad_mix = RESIDUAL_SCALE * upstream
    grad_weight = jnp.einsum("td,tkd->tk", grad_mix, routed_out, precision=PRECISE_ARITHMETIC)
    grad_rows = (
        (route_weight[:, :, None] * grad_mix[:, None, :])
        .astype(jnp.bfloat16)
        .reshape(sequence_length * TOP, MODEL_WIDTH)
    )
    buffer_grad = (
        jnp.zeros((E * CAP, MODEL_WIDTH), jnp.bfloat16)
        .at[slot_rows]
        .set(grad_rows)
        .reshape(E, CAP, MODEL_WIDTH)
    )
    gain_one_back, qkv_back, out_back, gain_two_back, router_back = dense_set
    send_grad = dispatch_rows(buffer_grad, send_table, devices, span_count)
    rows_in = lax.all_to_all(send_in, "fsdp", split_axis=0, concat_axis=0, tiled=True)
    rows_grad = lax.all_to_all(send_grad, "fsdp", split_axis=0, concat_axis=0, tiled=True)
    pre_cols = jnp.einsum(
        "nrkd,dgw->nrkgw", rows_in, owned_gate_up, preferred_element_type=jnp.float32
    )
    pre_cols = pre_cols * column_mask[None, :, None, None, :]
    gate_cols_pre = pre_cols[..., 0, :]
    up_cols_pre = pre_cols[..., 1, :]
    sigmoid_cols = jax.nn.sigmoid(gate_cols_pre)
    silu_cols = gate_cols_pre * sigmoid_cols
    acted = (silu_cols * up_cols_pre).astype(jnp.bfloat16)
    grad_act_cols = jnp.einsum(
        "nrkd,dw->nrkw", rows_grad, owned_down, preferred_element_type=jnp.float32
    )
    grad_gate_cols = (
        grad_act_cols * up_cols_pre * sigmoid_cols * (1.0 + gate_cols_pre * (1.0 - sigmoid_cols))
    )
    grad_up_cols = grad_act_cols * silu_cols
    grad_pair = jnp.stack([grad_gate_cols, grad_up_cols], axis=3).astype(jnp.bfloat16)
    partial_back = jnp.einsum(
        "nrkgw,dgw->nrkd", grad_pair, owned_gate_up, preferred_element_type=jnp.float32
    )
    returned_back = lax.all_to_all(partial_back, "fsdp", split_axis=0, concat_axis=0, tiled=True)
    results = (returned_back, rows_in, rows_grad, grad_pair, acted)
    returned_back, rows_in_all, rows_grad_all, grad_pair_all, acted_all = results
    backward_buffer = merge_entries(returned_back, combine_table)
    owned_gate_up_grad = jnp.einsum(
        "nrkd,nrkgw->dgw", rows_in_all, grad_pair_all, preferred_element_type=jnp.float32
    )
    owned_down_grad = jnp.einsum(
        "nrkd,nrkw->dw", rows_grad_all, acted_all, preferred_element_type=jnp.float32
    )
    owned_grads = jnp.concatenate([owned_gate_up_grad, owned_down_grad[:, None, :]], axis=1)
    relaid = lax.all_to_all(owned_grads, "fsdp", split_axis=0, concat_axis=2, tiled=True)
    gate_up_grad = jnp.transpose(
        relaid[:, :2, :].reshape(shard_rows, 2, E, F), (0, 2, 1, 3)
    ).reshape(shard_rows, E, 2 * F)
    down_grad = relaid[:, 2, :].reshape(shard_rows, E, F)
    grad_normed = jnp.sum(
        backward_buffer.reshape(E * CAP, MODEL_WIDTH)[slot_rows].reshape(
            sequence_length, TOP, MODEL_WIDTH
        ),
        axis=1,
    )
    grad_gates = jnp.einsum("tk,tke->te", grad_weight, picked, precision=PRECISE_ARITHMETIC)
    grad_logits = gate_probs * (
        grad_gates - jnp.sum(gate_probs * grad_gates, axis=-1, keepdims=True)
    )
    grad_normed = grad_normed + jnp.einsum(
        "te,de->td", grad_logits, router_back.astype(jnp.float32), precision=PRECISE_ARITHMETIC
    )
    router_part = jnp.einsum(
        "td,te->de", normed_two.astype(jnp.float32), grad_logits, precision=PRECISE_ARITHMETIC
    )
    grad_middle, gain_two_part = norm_back(middle, gain_two_back, scale_two, grad_normed)
    grad_middle = grad_middle + upstream
    grad_branch = (RESIDUAL_SCALE * grad_middle).astype(jnp.bfloat16)
    out_part = jnp.einsum(
        "tq,td->qd", attention_output_list, grad_branch, preferred_element_type=jnp.float32
    )
    attention_output_gradient = jnp.einsum(
        "td,qd->tq", grad_branch, out_back, preferred_element_type=jnp.float32
    ).astype(jnp.bfloat16)
    value_gradient = jnp.zeros((sequence_length, KEY_VALUE_HEADS, HEAD_WIDTH), jnp.float32)
    key_gradient = jnp.zeros((sequence_length, KEY_VALUE_HEADS, HEAD_WIDTH), jnp.float32)
    query_grads = []
    for block_number, offset in enumerate(range(0, sequence_length, rows_per_block)):
        scores = block_scores(offset)
        attn_probs = jnp.exp(scores - total_list[block_number])
        block_gradient = attention_output_gradient.reshape(
            rows_per_block, KEY_VALUE_HEADS, query_group_count, HEAD_WIDTH
        )
        attention_output_block = attention_output_list.reshape(
            rows_per_block, KEY_VALUE_HEADS, query_group_count, HEAD_WIDTH
        )
        row_delta = jnp.sum(
            block_gradient.astype(jnp.float32) * attention_output_block.astype(jnp.float32), axis=-1
        )
        row_delta = jnp.transpose(row_delta, (1, 2, 0))[..., None]
        value_gradient = jnp.einsum(
            "kgqt,qkgd->tkd",
            attn_probs.astype(jnp.bfloat16),
            block_gradient,
            preferred_element_type=jnp.float32,
        )
        grad_probs = jnp.einsum(
            "qkgd,tkd->kgqt", block_gradient, value_inputs, preferred_element_type=jnp.float32
        )
        grad_scores = (attn_probs * (grad_probs - row_delta) * ATTN_SCALE).astype(jnp.bfloat16)
        query_grads.append(
            jnp.einsum(
                "kgqt,tkd->qkgd", grad_scores, rotated_keys, preferred_element_type=jnp.float32
            )
        )
        key_gradient = jnp.einsum(
            "kgqt,qkgd->tkd", grad_scores, query_rows, preferred_element_type=jnp.float32
        )
    grad_queries = query_grads[0].reshape(sequence_length, QUERY_HEADS, HEAD_WIDTH)
    grad_joined = jnp.concatenate(
        [
            rotate_back(grad_queries, cosine_lookup, sine_lookup).reshape(
                sequence_length, query_feature_width
            ),
            rotate_back(key_gradient, cosine_lookup, sine_lookup).reshape(
                sequence_length, key_feature_width
            ),
            value_gradient.reshape(sequence_length, key_feature_width),
        ],
        axis=-1,
    ).astype(jnp.bfloat16)
    qkv_part = jnp.einsum("td,tm->dm", normed_one, grad_joined, preferred_element_type=jnp.float32)
    grad_normed_one = jnp.einsum(
        "tm,dm->td", grad_joined, qkv_back, preferred_element_type=jnp.float32
    )
    grad_inputs, gain_one_part = norm_back(inputs, gain_one_back, scale_one, grad_normed_one)
    input_grad = (grad_inputs + grad_middle).astype(jnp.bfloat16)
    dense_grads = (
        lax.psum_scatter(gain_one_part, "fsdp", scatter_dimension=0, tiled=True),
        lax.psum_scatter(qkv_part, "fsdp", scatter_dimension=0, tiled=True),
        lax.psum_scatter(out_part, "fsdp", scatter_dimension=0, tiled=True),
        lax.psum_scatter(gain_two_part, "fsdp", scatter_dimension=0, tiled=True),
        lax.psum_scatter(router_part, "fsdp", scatter_dimension=0, tiled=True),
    )
    return (
        layer_output,
        input_grad,
        dense_grads[0],
        dense_grads[1],
        dense_grads[2],
        dense_grads[3],
        dense_grads[4],
        gate_up_grad,
        down_grad,
    )


D = MODEL_WIDTH
SRC = 8
STEPS = 4
M = SRC * CAP
F32, BF16 = jnp.float32, jnp.bfloat16

def nt(a, b):
    return lax.dot_general(a, b, (((1,), (1,)), ((), ())), preferred_element_type=F32)
def nn(a, b):
    return lax.dot_general(a, b, (((1,), (0,)), ((), ())), preferred_element_type=F32)
def tn(a, b):
    return lax.dot_general(a, b, (((0,), (0,)), ((), ())), preferred_element_type=F32)

QUARTER, DOWN_WHOLE, DOWN_QUARTER, OWN_WIDTH = 0, 256, 768, 896

class Experts:
    NAMES = ("x", "c", "rw", "gw", "act", "dgu", "actq", "dguq", "ow", "gi")

    @staticmethod
    def scratch():
        R = STEPS * M
        return [
            pltpu.VMEM((2, R, D), BF16), pltpu.VMEM((2, R, D), BF16), pltpu.VMEM((2, M, 128), F32), pltpu.VMEM((2, M, 128), F32),
            pltpu.VMEM((R, F), BF16), pltpu.VMEM((R, 2 * F), BF16), pltpu.VMEM((R, 128), BF16), pltpu.VMEM((R, 256), BF16),
            pltpu.VMEM((2, M, D), BF16), pltpu.VMEM((2, M, D), BF16),
        ]

    def __init__(self, refs, wf_ref, wo_ref, pick_ref, ids_ref, share_ref, gates_ref):
        for name, ref in zip(self.NAMES, refs):
            setattr(self, name, ref)
        self.wf, self.wo, self.pick, self.ids, self.shares, self.gates = wf_ref, wo_ref, pick_ref, ids_ref, share_ref, gates_ref

    def picks(self, plane, s):
        return self.pick[pl.ds(pl.multiple_of(plane * (SRC * 64) + s * 64, 64), 64), :]

    def load(self, step, plane, t_ref, c_ref):
        def one(s):
            pick = self.picks(plane, s)
            block = pl.ds(pl.multiple_of(s * 128, 128), 128)
            xs = nn(pick, t_ref[block, :]).astype(BF16)
            cs = nn(pick, c_ref[block, :]).astype(BF16)
            wide = pick.astype(F32)
            eight = pl.ds(pl.multiple_of(plane * (SRC * TOP) + s * TOP, TOP), TOP)
            share = []
            for k, own in enumerate(owned_experts()):
                prob = jnp.sum(jnp.where(self.ids[eight, :] == own, self.shares[eight, :], 0.0), axis=0, keepdims=True)
                share.append(jnp.sum(wide[k * CAP:k * CAP + CAP] * prob, axis=1, keepdims=True) * RESIDUAL_SCALE)
            here = pl.ds(pl.multiple_of(s * CAP, CAP), CAP)
            to = pl.ds(pl.multiple_of(step * M + s * CAP, CAP), CAP)
            for k in range(2):
                self.x[k, to, :] = xs[k * CAP:k * CAP + CAP]
                self.c[k, to, :] = cs[k * CAP:k * CAP + CAP]
                self.rw[k, here, :] = jnp.broadcast_to(share[k], (CAP, 128))
        for s in range(SRC):
            one(s)

    def run(self, step):
        at = slice(step * M, step * M + M)
        sets = (
            (self.act, self.dgu, 512, lambda: self.wf[...], DOWN_WHOLE),
            (self.actq, self.dguq, 128, lambda: self.wo[:, QUARTER:QUARTER + 256], DOWN_QUARTER),
        )
        for k, (acts, dgus, w, w_gu, d0) in enumerate(sets):
            pre = nn(self.x[k, at, :], w_gu())
            gate, up = pre[:, :w], pre[:, w:]
            sig = jax.nn.sigmoid(gate)
            silu = gate * sig
            act = silu * up
            share = self.rw[k, :, 0:1]
            scaled = (share * act).astype(BF16)
            acts[at, :] = scaled
            da = nn(self.c[k, at, :], self.wo[:, d0:d0 + w])
            gw = RESIDUAL_SCALE * jnp.sum(act.astype(BF16).astype(F32) * da, axis=1, keepdims=True)
            self.gw[k] = jnp.broadcast_to(gw, (M, 128))
            self.ow[k] = nt(scaled, self.wo[:, d0:d0 + w]).astype(BF16)
            da = share * da
            dgus[at, :w] = (da * up * sig * (1.0 + gate * (1.0 - sig))).astype(BF16)
            dgus[at, w:] = (da * silu).astype(BF16)
            self.gi[k] = nt(dgus[at, :], w_gu()).astype(BF16)

    def give(self, plane, out_ref, gin_ref):
        def one(s):
            r = pl.ds(pl.multiple_of(s * CAP, CAP), CAP)
            pick = self.picks(plane, s)
            to = pl.ds(pl.multiple_of(s * 128, 128), 128)
            out_ref[to, :] = tn(pick, jnp.concatenate([self.ow[0, r, :], self.ow[1, r, :]], axis=0)).astype(BF16)
            gin_ref[to, :] = tn(pick, jnp.concatenate([self.gi[0, r, :], self.gi[1, r, :]], axis=0)).astype(BF16)
            wide = pick.astype(F32)
            rows = [jnp.sum(wide[k * CAP:k * CAP + CAP] * self.gw[k, r, :], axis=0, keepdims=True) for k in range(2)]
            self.gates[plane * SRC + s] = jnp.concatenate(rows + [jnp.zeros((6, 128), F32)], axis=0)
        for s in range(SRC):
            one(s)

    def own_grads(self, j, ref):
        c = slice(j * 256, j * 256 + 256)
        ref[:, QUARTER:QUARTER + 256] = tn(self.x[1, :, c], self.dguq[...]).astype(BF16)
        ref[:, DOWN_WHOLE:DOWN_WHOLE + 512] = tn(self.c[0, :, c], self.act[...]).astype(BF16)
        ref[:, DOWN_QUARTER:DOWN_QUARTER + 128] = tn(self.c[1, :, c], self.actq[...]).astype(BF16)

    def whole_grads(self, j, ref):
        ref[...] = tn(self.x[0, :, j * 256:j * 256 + 256], self.dgu[...]).astype(BF16)


MESH = pl.DeviceIdType.MESH
DEVICES = 32
TURNS = tuple(sorted(range(1, DEVICES), key=lambda k: (k % 8 * 5 % 8, k)))
DMA = pltpu.SemaphoreType.DMA


def dev(z, y, x, c):
    return ((z * 2 + y) * 2 + x) * 2 + c


class Place:
    def __init__(self):
        me = lax.axis_index("fsdp")
        self.me = me
        z, y, x, c = me // 8, lax.rem(me // 4, 2), lax.rem(me // 2, 2), lax.rem(me, 2)
        self.z, self.y, self.x, self.c = z, y, x, c
        self.sib, self.xn, self.yn = dev(z, y, x, 1 - c), dev(z, y, 1 - x, c), dev(z, 1 - y, x, c)
        self.up, self.down = dev(z + 1, y, x, c), dev(z - 1, y, x, c)
        table = ((0, 1, 2, 3), (1, 0, 2, 3), (2, 3, 1, 0), (3, 2, 1, 0))
        self.zq = []
        for q in range(4):
            v = jnp.int32(table[0][q])
            for k in range(1, 4):
                v = jnp.where(z == k, table[k][q], v)
            self.zq.append(v)


def greet_all():
    me = lax.axis_index("fsdp")
    barrier = pltpu.get_barrier_semaphore()
    for k in range(1, DEVICES):
        pl.semaphore_signal(barrier, inc=1, device_id=(lax.rem(me + k, DEVICES),), device_id_type=MESH)
    pl.semaphore_wait(barrier, DEVICES - 1)


def rc(src, dst, ss, rs, to):
    return pltpu.make_async_remote_copy(src_ref=src, dst_ref=dst, send_sem=ss, recv_sem=rs, device_id=(to,), device_id_type=MESH)


class Direct:
    def __init__(self, pieces, refs, sems):
        self.pieces, self.refs, (self.ss, self.rs, self.ls) = pieces, refs, sems
        self.me = lax.axis_index("fsdp")
        self.left = list(TURNS)

    @staticmethod
    def scratch(count):
        return [DMA((DEVICES, count)), DMA((DEVICES, count)), DMA((count,))]

    def own(self):
        self.local = [pltpu.make_async_copy(a, b, self.ls.at[i]) for i, (a, b) in enumerate(self.pieces(self.me, self.me, self.refs))]
        for l in self.local:
            l.start()

    def start(self, number):
        turns, self.left = self.left[:number], self.left[number:]
        for k in turns:
            to = lax.rem(self.me + k, DEVICES)
            for i, (a, b) in enumerate(self.pieces(self.me, to, self.refs)):
                rc(a, b, self.ss.at[k, i], self.rs.at[k, i], to).start()

    def finish(self):
        self.start(DEVICES)
        for k in TURNS:
            src = lax.rem(self.me + DEVICES - k, DEVICES)
            for i, (a, b) in enumerate(self.pieces(src, self.me, self.refs)):
                rc(a, b, self.ss.at[k, i], self.rs.at[k, i], src).wait_recv()
        for k in TURNS:
            to = lax.rem(self.me + k, DEVICES)
            for i, (a, b) in enumerate(self.pieces(self.me, to, self.refs)):
                rc(a, b, self.ss.at[k, i], self.rs.at[k, i], to).wait_send()
        for l in self.local:
            l.wait()


class Gather:
    ORDER = ((1, 0), (1, 1), (2, 0), (1, 2), (2, 1), (3, 0), (1, 3), (2, 2), (3, 1), (2, 3), (3, 2), (3, 3))

    def __init__(self, p, parts, shards, outs, sems):
        self.p, self.parts, self.shards, self.outs, self.sems = p, parts, shards, outs, sems
        self.P, self.sends, self.locals = len(parts), [], []
        self.left = list(self.ORDER)

    @staticmethod
    def scratch(arrays, parts):
        P = len(parts)
        return [DMA((arrays,)), DMA((4, P)), DMA((P,))] + [DMA((4, P))] * 7 + [DMA((4, 4, P))] * 2

    def at(self, i, d):
        a, c0, w, _ = self.parts[i]
        rows = self.shards[a].shape[0]
        return self.outs[a].at[pl.ds(pl.multiple_of(d * rows, rows), rows), pl.ds(c0, w)]

    def spot(self, i, q, k, core):
        p = self.p
        flip_x, flip_y = ((0, 0), (1, 0), (0, 1), (1, 1))[k] if self.parts[i][3] == 0 else ((0, 0), (0, 1), (1, 0), (1, 1))[k]
        return self.at(i, dev(p.zq[q], 1 - p.y if flip_y else p.y, 1 - p.x if flip_x else p.x, core))

    def go(self, copy):
        copy.start()
        self.sends.append(copy)

    def step(self, number=1):
        for f, q in self.left[:number]:
            (self.stage1, self.stage2, self.stage3)[f - 1](q)
        self.left = self.left[number:]

    def stage1(self, q):
        p = self.p
        _, zs, zs2, zr, fs, fr, s1s, s1r, s2s, s2r, cs, cr = self.sems
        for i in range(self.P):
            a, c0, w, mode = self.parts[i]
            first, second = (p.xn, p.yn) if mode == 0 else (p.yn, p.xn)
            here = self.spot(i, q, 0, p.c)
            if q == 0:
                src = self.shards[a].at[:, pl.ds(c0, w)]

                @pl.when(p.z < 3)
                def _():
                    rc(src, here, zs.at[0, i], zr.at[p.z, i], p.up).start()

                @pl.when(p.z > 0)
                def _():
                    rc(src, here, zs2.at[i], zr.at[p.z, i], p.down).start()
            else:
                src, zq = here, p.zq[q]
                rc(here, here, zs.at[q, i], zr.at[zq, i], p.up).wait_recv()

                @pl.when((zq < p.z) & (p.z < 3))
                def _():
                    rc(src, here, zs.at[q, i], zr.at[zq, i], p.up).start()

                @pl.when((zq > p.z) & (p.z > 0))
                def _():
                    rc(src, here, zs.at[q, i], zr.at[zq, i], p.down).start()
            self.go(rc(src, here, fs.at[q, i], fr.at[q, i], first))
            self.go(rc(src, here, s1s.at[q, i], s1r.at[q, i], second))
            self.go(rc(src, here, cs.at[0, q, i], cr.at[0, q, i], p.sib))
        if q == 0:
            for a, (shard, out) in enumerate(zip(self.shards, self.outs)):
                rows = shard.shape[0]
                l = pltpu.make_async_copy(shard, out.at[pl.ds(pl.multiple_of(p.me * rows, rows), rows)], self.sems[0].at[a])
                l.start()
                self.locals.append(l)

    def stage2(self, q):
        p = self.p
        fs, fr, s2s, s2r, cs, cr = self.sems[4:6] + self.sems[8:12]
        for i in range(self.P):
            second = p.yn if self.parts[i][3] == 0 else p.xn
            there = self.spot(i, q, 1, p.c)
            rc(there, there, fs.at[q, i], fr.at[q, i], second).wait_recv()
            self.go(rc(there, there, s2s.at[q, i], s2r.at[q, i], second))
            self.go(rc(there, there, cs.at[1, q, i], cr.at[1, q, i], p.sib))

    def stage3(self, q):
        p = self.p
        cs, cr = self.sems[10:12]
        for k, (ss, rs) in ((2, self.sems[6:8]), (3, self.sems[8:10])):
            for i in range(self.P):
                there = self.spot(i, q, k, p.c)
                rc(there, there, ss.at[q, i], rs.at[q, i], p.sib).wait_recv()
                self.go(rc(there, there, cs.at[k, q, i], cr.at[k, q, i], p.sib))

    def arrived(self):
        self.step(12)
        cs, cr = self.sems[10:12]
        for q in range(4):
            for k in range(4):
                for i in range(self.P):
                    there = self.spot(i, q, k, 1 - self.p.c)
                    rc(there, there, cs.at[k, q, i], cr.at[k, q, i], self.p.sib).wait_recv()
        for l in self.locals:
            l.wait()

    def finish(self):
        p = self.p
        zs, zs2, zr = self.sems[1:4]
        for copy in self.sends:
            copy.wait_send()
        for i in range(self.P):
            here = self.at(i, p.me)

            @pl.when(p.z < 3)
            def _():
                rc(here, here, zs.at[0, i], zr.at[p.z, i], p.up).wait_send()

            @pl.when(p.z > 0)
            def _():
                rc(here, here, zs2.at[i], zr.at[p.z, i], p.down).wait_send()

            for q in range(1, 4):
                zq = p.zq[q]

                @pl.when(((zq < p.z) & (p.z < 3)) | ((zq > p.z) & (p.z > 0)))
                def _():
                    rc(here, here, zs.at[q, i], zr.at[zq, i], p.up).wait_send()


class Scatter:
    ORDER = ((1, 3), (1, 2), (2, 3), (1, 1), (2, 2), (3, 3), (1, 0), (2, 1), (3, 2), (2, 0), (3, 1), (3, 0))
    STEP = 16

    def __init__(self, p, parts, fulls, outs, spaces, sems, in_place=False, by_plane=False):
        self.by_plane, self.reads = by_plane, []
        self.p, self.parts, self.fulls, self.outs, self.sems, self.in_place = p, parts, fulls, outs, sems, in_place
        count = len(fulls)
        if in_place:
            spaces = (None,) * count + tuple(spaces)
        self.held, self.r0, self.r1, self.r2, self.r3 = (spaces[i * count : (i + 1) * count] for i in range(5))
        self.rows = [f.shape[0] // (8 if by_plane else DEVICES) for f in fulls]
        self.P, self.sends = len(parts), []
        self.left = list(self.ORDER)

    def begin_all(self):
        self.reads = self.begin()

    @staticmethod
    def scratch(arrays, parts, in_place=False):
        P = len(parts)
        spaces = []
        for cnt in (16, 8, 4, 5) if in_place else (16, 16, 8, 4, 5):
            spaces += [pltpu.VMEM((cnt, a.shape[0] // DEVICES, a.shape[1]), a.dtype) for a in arrays]
        return spaces, [DMA((4, 4, P))] * 3 + [DMA((4, 2, P))] * 2 + [DMA((4, P))] * 3 + [DMA((5, P))]

    def go(self, copy):
        copy.start()
        self.sends.append(copy)

    def cut(self, i):
        return pl.ds(self.parts[i][1], self.parts[i][2])

    def spot(self, i, k):
        x, y = self.p.x, self.p.y
        if self.parts[i][3] == 0:
            return ((1 - y, 1 - x), (1 - y, x), (y, 1 - x), (y, x))[k]
        return ((1 - y, 1 - x), (y, 1 - x), (1 - y, x), (y, x))[k]

    def slot(self, q, yy, xx):
        return (yy * 2 + xx) * 4 + self.p.zq[q]

    def hold(self, a, q, yy, xx):
        if self.in_place:
            start = dev(self.p.zq[q], yy, xx, self.p.c) * self.rows[a]
            return self.fulls[a].at[pl.ds(pl.multiple_of(start, self.rows[a]), self.rows[a])]
        return self.held[a].at[self.slot(q, yy, xx)]

    def source(self, i, q, k, core):
        a = self.parts[i][0]
        d = dev(0 if self.by_plane else self.p.zq[q], *self.spot(i, k), core)
        return self.fulls[a].at[pl.ds(pl.multiple_of(d * self.rows[a], self.rows[a]), self.rows[a]), self.cut(i)]

    def begin(self, planes=(3, 2, 1, 0)):
        ls, s0, e0 = self.sems[:3]
        made = []
        for q in planes:
            for k in range(4):
                for i in range(self.P):
                    a = self.parts[i][0]
                    s = self.slot(q, *self.spot(i, k))
                    copy = rc(self.source(i, q, k, 1 - self.p.c), self.r0[a].at[s, :, self.cut(i)], s0.at[q, k, i], e0.at[q, k, i], self.p.sib)
                    copy.start()
                    made.append(copy.wait_send)
                    if not self.in_place:
                        l = pltpu.make_async_copy(self.source(i, q, k, self.p.c), self.held[a].at[s, :, self.cut(i)], ls.at[q, k, i])
                        l.start()
                        made.append(l.wait)
        return made

    def step(self, number=1):
        for f, q in self.left[:number]:
            (self.stage1, self.stage2, self.stage3)[f - 1](q)
        self.left = self.left[number:]

    def chunks(self, a, body):
        def one(n, carry):
            body(pl.ds(pl.multiple_of(n * self.STEP, self.STEP), self.STEP))
            return carry

        lax.fori_loop(0, self.rows[a] // self.STEP, one, 0)

    def add(self, i, dst, src, s_src):
        a, c0, w, _ = self.parts[i]

        def body(r):
            v = dst[r, c0 : c0 + w].astype(F32) + src[s_src, r, c0 : c0 + w].astype(F32)
            dst[r, c0 : c0 + w] = v.astype(dst.dtype)

        self.chunks(a, body)

    def stage1(self, q):
        p = self.p
        _, s0, e0, s1, e1 = self.sems[:5]
        for k in range(4):
            for i in range(self.P):
                a = self.parts[i][0]
                first = p.yn if self.parts[i][3] == 0 else p.xn
                s = self.slot(q, *self.spot(i, k))
                sums = self.hold(a, q, *self.spot(i, k))
                here = sums.at[:, self.cut(i)]
                rc(here, self.r0[a].at[s, :, self.cut(i)], s0.at[q, k, i], e0.at[q, k, i], p.sib).wait_recv()
                if self.reads and not self.in_place:
                    self.reads[self.reading(q, k, i) * 2 + 1]()
                self.add(i, sums, self.r0[a], s)
                if k < 2:
                    self.go(rc(here, self.r1[a].at[q * 2 + k, :, self.cut(i)], s1.at[q, k, i], e1.at[q, k, i], first))

    def reading(self, q, k, i):
        return ((3 - q) * 4 + k) * self.P + i

    def stage2(self, q):
        p = self.p
        s1, e1, s2, e2 = self.sems[3:7]
        for k in range(2):
            for i in range(self.P):
                a = self.parts[i][0]
                second = p.xn if self.parts[i][3] == 0 else p.yn
                sums = self.hold(a, q, *self.spot(i, k + 2))
                here = sums.at[:, self.cut(i)]
                rc(here, self.r1[a].at[q * 2 + k, :, self.cut(i)], s1.at[q, k, i], e1.at[q, k, i], p.sib).wait_recv()
                self.add(i, sums, self.r1[a], q * 2 + k)
                if k == 0:
                    self.go(rc(here, self.r2[a].at[q, :, self.cut(i)], s2.at[q, i], e2.at[q, i], second))

    def stage3(self, q):
        p = self.p
        s2, e2, s3, e3 = self.sems[5:9]
        zq, z = p.zq[q], p.z
        for i in range(self.P):
            a, c0, w, _ = self.parts[i]
            r3, out, sums = self.r3[a], self.outs[a], self.hold(a, q, p.y, p.x)
            here = sums.at[:, self.cut(i)]
            rc(here, self.r2[a].at[q, :, self.cut(i)], s2.at[q, i], e2.at[q, i], p.sib).wait_recv()
            self.add(i, sums, self.r2[a], q)
            if q > 0:

                @pl.when((zq > z) & (z > 0) | (zq < z) & (z < 3))
                def _():
                    rc(here, r3.at[zq, :, self.cut(i)], s3.at[q, i], e3.at[zq, i], p.sib).wait_recv()
                    self.add(i, sums, r3, zq)

                @pl.when(zq > z)
                def _():
                    rc(here, r3.at[zq, :, self.cut(i)], s3.at[q, i], e3.at[zq, i], p.up).start()

                @pl.when((zq < z) & (zq == z - 1))
                def _():
                    rc(here, r3.at[4, :, self.cut(i)], s3.at[q, i], e3.at[4, i], p.down).start()

                @pl.when(zq < z - 1)
                def _():
                    rc(here, r3.at[zq, :, self.cut(i)], s3.at[q, i], e3.at[zq, i], p.down).start()
            else:

                def first_sum(r):
                    out[r, c0 : c0 + w] = sums[r, c0 : c0 + w].astype(F32)

                self.chunks(a, first_sum)
                for cond, where in ((z > 0, z), (z < 3, 4)):

                    @pl.when(cond)
                    def _():
                        rc(here, r3.at[where, :, self.cut(i)], s3.at[q, i], e3.at[where, i], p.sib).wait_recv()

                        def more(r):
                            out[r, c0 : c0 + w] += r3[where, r, c0 : c0 + w].astype(F32)

                        self.chunks(a, more)

    def finish(self):
        p = self.p
        s3, e3 = self.sems[7:9]
        for wait in self.reads[:: 1 if self.in_place else 2]:
            wait()
        for copy in self.sends:
            copy.wait_send()
        for q in range(1, 4):
            for i in range(self.P):
                here = self.hold(self.parts[i][0], q, p.y, p.x).at[:, self.cut(i)]
                rc(here, here, s3.at[q, i], e3.at[0, i], p.sib).wait_send()


HBM = pl.BlockSpec(memory_space=pl.ANY)
VMEM = pl.BlockSpec(memory_space=pltpu.VMEM)


def like(*shape, dtype=None):
    return jax.ShapeDtypeStruct(shape, dtype or jnp.bfloat16)


def cut_up(refs, *counts):
    out, i = [], 0
    for c in counts:
        out.append(refs[i : i + c])
        i += c
    return out + [refs[i:]]


GROUP = QUERY_HEADS // KEY_VALUE_HEADS
Q_WIDTH, K_WIDTH = QUERY_HEADS * HEAD_WIDTH, KEY_VALUE_HEADS * HEAD_WIDTH
TOK = 128


def partner(v):
    lane = lax.broadcasted_iota(jnp.int32, v.shape, 1) % HEAD_WIDTH
    return jnp.where(lane < HEAD_WIDTH // 2, pltpu.roll(v, 96, 1), pltpu.roll(v, 32, 1))


def attention_forward(x_ref, cos_ref, sin_ref, bias_ref, qkv_ref, out_ref, small_ref, r):
    def norm_one():
        r.small_t[...] = nt(jnp.eye(TOK, dtype=BF16), small_ref[...])
        x = x_ref[...].astype(F32)
        r.n1[...] = (x * norm_scale(x) * r.small_t[E : E + 1, :]).astype(BF16)

    def project(t):
        def run():
            tile = nn(r.n1[...], qkv_ref[:, t * 512 : t * 512 + 512])
            for b in range(4):
                col = t * 512 + b * 128
                v = tile[:, b * 128 : b * 128 + 128]
                if col < Q_WIDTH + K_WIDTH:
                    v = v * cos_ref[...] + partner(v) * sin_ref[...]
                v = v.astype(BF16)
                for half in range(2):
                    piece = v[:, half * 64 : half * 64 + 64]
                    head = col // 64 + half
                    if col < Q_WIDTH:
                        r.q[head // GROUP, head % GROUP * TOK : head % GROUP * TOK + TOK, :] = piece
                    elif col < Q_WIDTH + K_WIDTH:
                        r.k[head - QUERY_HEADS] = piece
                    else:
                        r.v[head - QUERY_HEADS - KEY_VALUE_HEADS] = piece

        return run

    def attend(j):
        def run():
            s = nt(r.q[j], r.k[j]) * ATTN_SCALE
            s = s + jnp.concatenate([bias_ref[...]] * GROUP, axis=0)
            e = jnp.exp(s - jnp.max(s, axis=1, keepdims=True))
            probs = e / jnp.sum(e, axis=1, keepdims=True)
            r.probs[j] = probs
            o = nn(probs.astype(BF16), r.v[j]).astype(BF16)
            for g in range(GROUP):
                h = j * GROUP + g
                r.att[:, h * 64 : h * 64 + 64] = o[g * TOK : g * TOK + TOK]

        return run

    def output(t):
        def run():
            c = slice(t * 512, t * 512 + 512)
            r.middle[:, c] = x_ref[:, c].astype(F32) + RESIDUAL_SCALE * nn(r.att[...], out_ref[:, c])

        return run

    def norm_two():
        m = r.middle[...]
        r.n2[...] = (m * norm_scale(m) * r.small_t[E + 1 : E + 2, :]).astype(BF16)

    return (
        [norm_one]
        + [project(t) for t in range((Q_WIDTH + 2 * K_WIDTH) // 512)]
        + [attend(j) for j in range(KEY_VALUE_HEADS)]
        + [output(t) for t in range(D // 512)]
        + [norm_two]
    )


def split_dot(form, a, b):
    one = b.astype(BF16)
    rest = b - one.astype(F32)
    two = rest.astype(BF16)
    three = (rest - two.astype(F32)).astype(BF16)
    return form(a, one) + form(a, two) + form(a, three)


def norm_back_rows(hidden, gain, upstream):
    scale = norm_scale(hidden)
    weighted = upstream * gain
    inner = jnp.mean(weighted * hidden, axis=-1, keepdims=True)
    return scale * weighted - hidden * scale**3 * inner, upstream * hidden * scale


def gate_probs(r):
    logits = nt(r.small_t[:64, :].astype(BF16), r.n2[...])
    row = lax.broadcasted_iota(jnp.int32, logits.shape, 0)
    logits = jnp.where(row < E, logits, -jnp.inf)
    e = jnp.exp(logits - jnp.max(logits, axis=0, keepdims=True))
    return e / jnp.sum(e, axis=0, keepdims=True)


def attention_backward(x_ref, cot_ref, gin_ref, gates_ref, cos_ref, sin_ref, qkv_ref, out_ref, r, put_qkv, put_out, put_small):
    def router():
        m = r.middle[...]
        probs = gate_probs(r)
        r.gates[...] = jnp.zeros_like(r.gates)
        for g in range(8):
            for j in range(4):
                r.gates[g * 5 + j : g * 5 + j + 1, :] = gates_ref[g * 4 + j, 0:1, :]
            r.gates[g * 5 + 4 : g * 5 + 5, :] = sum(gates_ref[g * 4 + j, 1:2, :] for j in range(4))
        gates = r.gates[...]
        gl = probs * (gates - jnp.sum(probs * gates, axis=0, keepdims=True))
        gl = jnp.concatenate([gl, jnp.zeros((64, TOK), F32)], axis=0).T
        r.gl[...] = gl
        back = nn(gl.astype(BF16), r.small_t[...].astype(BF16))
        low = gl - gl.astype(BF16).astype(F32)
        back = back + nn(low.astype(BF16), r.small_t[...].astype(BF16))
        low = low - low.astype(BF16).astype(F32)
        back = back + nn(low.astype(BF16), r.small_t[...].astype(BF16))
        up = gin_ref[...] + back
        gm, gain_rows = norm_back_rows(m, r.small_t[E + 1 : E + 2, :], up)
        gm = gm + cot_ref[...].astype(F32)
        r.gm[...] = gm
        r.gain2[...] = gain_rows
        r.branch[...] = (RESIDUAL_SCALE * gm).astype(BF16)

    def attended(t):
        def run():
            c = slice(t * 512, t * 512 + 512)
            r.ga[:, c] = nt(r.branch[...], out_ref[c, :]).astype(BF16)

        return run

    def out_part(t):
        def run():
            put_out(t, tn(r.att[:, t * 256 : t * 256 + 256], r.branch[...]).astype(BF16))

        return run

    def head(j):
        def run():
            cols = [slice((j * GROUP + g) * 64, (j * GROUP + g) * 64 + 64) for g in range(GROUP)]
            ga = jnp.concatenate([r.ga[:, c] for c in cols], axis=0)
            at = jnp.concatenate([r.att[:, c] for c in cols], axis=0)
            delta = jnp.sum(ga.astype(F32) * at.astype(F32), axis=1, keepdims=True)
            probs = r.probs[j]
            ds = (probs * (nt(ga, r.v[j]) - delta) * ATTN_SCALE).astype(BF16)
            gq = nn(ds, r.k[j])
            for g, c in enumerate(cols):
                r.gjf[:, c] = gq[g * TOK : g * TOK + TOK]
            r.gjf[:, Q_WIDTH + j * 64 : Q_WIDTH + j * 64 + 64] = tn(ds, r.q[j])
            r.gjf[:, Q_WIDTH + K_WIDTH + j * 64 : Q_WIDTH + K_WIDTH + j * 64 + 64] = tn(probs.astype(BF16), ga)

        return run

    def rotate():
        for col in range(0, Q_WIDTH + 2 * K_WIDTH, 128):
            v = r.gjf[:, col : col + 128]
            if col < Q_WIDTH + K_WIDTH:
                v = v * cos_ref[...] - partner(v) * sin_ref[...]
            r.gj[:, col : col + 128] = v.astype(BF16)

    def qkv_part(t):
        def run():
            put_qkv(t, tn(r.n1[:, t * 256 : t * 256 + 256], r.gj[...]).astype(BF16))

        return run

    def into_normed(t):
        def run():
            c = slice(t * 256, t * 256 + 256)
            r.gn[:, c] = nt(r.gj[...], qkv_ref[c, :])

        return run

    def input_back():
        x = x_ref[...].astype(F32)
        gx, gain_rows = norm_back_rows(x, r.small_t[E : E + 1, :], r.gn[...])
        r.input_grad[...] = (gx + r.gm[...]).astype(BF16)
        lane = lax.broadcasted_iota(jnp.int32, (TOK, TOK), 1)
        small = split_dot(tn, r.n2[...], r.gl[...])
        for rows, at in ((gain_rows, E), (r.gain2[...], E + 1)):
            ones = jnp.where(lane == at, 1.0, 0.0).astype(BF16)
            hi = rows.astype(BF16)
            lo = (rows - hi.astype(F32)).astype(BF16)
            small = small + tn(hi, ones) + tn(lo, ones)
        put_small(small.astype(BF16))

    first = [router] + [attended(t) for t in range(3)] + [out_part(t) for t in range(6)]
    heads = [head(j) for j in range(KEY_VALUE_HEADS)] + [rotate]
    last = [into_normed(t) for t in range(6)] + [input_back] + [qkv_part(t) for t in range(6)]
    return first, heads, last


class Results:
    pass


ATT_NAMES = ("small_t", "n1", "q", "k", "v", "probs", "att", "middle", "n2")
ATT_SHAPES = (
    ((TOK, D), F32),
    ((TOK, D), BF16),
    ((KEY_VALUE_HEADS, GROUP * TOK, HEAD_WIDTH), BF16),
    ((KEY_VALUE_HEADS, TOK, HEAD_WIDTH), BF16),
    ((KEY_VALUE_HEADS, TOK, HEAD_WIDTH), BF16),
    ((KEY_VALUE_HEADS, GROUP * TOK, TOK), F32),
    ((TOK, Q_WIDTH), BF16),
    ((TOK, D), F32),
    ((TOK, D), BF16),
)
ROW_HALVES = ((0, 0, 768, 0), (0, 768, 768, 1))
DENSE_PARTS = ((0, 0, 1280, 0), (0, 1280, 1280, 1), (1, 0, 768, 0), (1, 768, 768, 1), (2, 0, 128, 1))
TOKEN_PARTS = ROW_HALVES + ((1, 0, 128, 1),)
FIRST_PARTS = DENSE_PARTS + ((3, 0, 128, 0),)


def lanes(start):
    return pl.ds(pl.multiple_of(start, 128), 128)


def weights_out(src, dst, refs):
    g_ref, d_ref, wf_ref, wo_ref = refs
    group, own, quarter = dst // 4, lax.rem(dst, 4), lax.rem(dst, 4) * 128
    rows = pl.ds(pl.multiple_of(src * 48, 48), 48)
    fifth = group * 5 + 4
    return (
        (g_ref.at[fifth, :, lanes(quarter)], wo_ref.at[rows, pl.ds(QUARTER, 128)]),
        (g_ref.at[fifth, :, lanes(F + quarter)], wo_ref.at[rows, pl.ds(QUARTER + 128, 128)]),
        (d_ref.at[group * 5 + own], wo_ref.at[rows, pl.ds(DOWN_WHOLE, F)]),
        (d_ref.at[fifth, :, lanes(quarter)], wo_ref.at[rows, pl.ds(DOWN_QUARTER, 128)]),
        (g_ref.at[group * 5 + own], wf_ref.at[rows]),
    )


def down_back(src, dst, refs):
    dwo_ref, gates_ref, d_ref, all_gates_ref = refs
    group, quarter = src // 4, lax.rem(src, 4) * 128
    rows = pl.ds(pl.multiple_of(dst * 48, 48), 48)
    return (
        (gates_ref.at[dst], all_gates_ref.at[src]),
        (dwo_ref.at[rows, pl.ds(DOWN_WHOLE, F)], d_ref.at[group * 5 + lax.rem(src, 4)]),
        (dwo_ref.at[rows, pl.ds(DOWN_QUARTER, 128)], d_ref.at[group * 5 + 4, :, lanes(quarter)]),
    )


def gate_up_back(src, dst, refs):
    dwf_ref, dwo_ref, g_ref = refs
    group, quarter = src // 4, lax.rem(src, 4) * 128
    rows = pl.ds(pl.multiple_of(dst * 48, 48), 48)
    return (
        (dwf_ref.at[rows], g_ref.at[group * 5 + lax.rem(src, 4)]),
        (dwo_ref.at[rows, pl.ds(QUARTER, 128)], g_ref.at[group * 5 + 4, :, lanes(quarter)]),
        (dwo_ref.at[rows, pl.ds(QUARTER + 128, 128)], g_ref.at[group * 5 + 4, :, lanes(F + quarter)]),
    )


def owned_experts():
    me = lax.axis_index("fsdp")
    return (me // 4) * 5 + lax.rem(me, 4), (me // 4) * 5 + 4


def make_picks(ids, named, picks):
    for s in range(DEVICES):
        block = ids[s * TOP : s * TOP + TOP, :]
        for k, e in enumerate(owned_experts()):
            named[s * 2 + k : s * 2 + k + 1, :] = jnp.max(jnp.where(block == e, 1.0, 0.0), axis=0, keepdims=True)
    row = lax.broadcasted_iota(jnp.int32, (TOK, TOK), 0)
    before = jnp.where(row < lax.broadcasted_iota(jnp.int32, (TOK, TOK), 1), 1.0, 0.0).astype(BF16)
    ranks = nn(named[...].astype(BF16), before)
    ranks = jnp.where(named[...] > 0.0, ranks, -1.0)
    slot = lax.broadcasted_iota(jnp.int32, (CAP, TOK), 0).astype(F32)
    for i in range(DEVICES * 2):
        picks[i * CAP : i * CAP + CAP, :] = jnp.where(ranks[i : i + 1, :] == slot, 1.0, 0.0).astype(BF16)


def route_weights(ids, r, rw):
    probs = gate_probs(r)
    row = lax.broadcasted_iota(jnp.int32, probs.shape, 0)
    for k in range(TOP):
        rw[k : k + 1, :] = jnp.sum(jnp.where(row == ids[k : k + 1, :], probs, 0.0), axis=0, keepdims=True)


def first_kernel(*refs):
    (x, cos, sin, bias, ids), dense, (cot,), experts_in, dense_out, outs, results, weights, work, refs = cut_up(
        refs, 5, 4, 1, 2, 4, 6, 9, 4, 7
    )
    cots, tokens, shares, wf, wo, picks = outs
    natural, turned, (rw, named, load_sem) = work[:2], work[2:4], work[4:]
    sems1, sems2, sems3, direct_sems, _ = cut_up(refs, 12, 12, 12, 3)
    greet_all()
    p = Place()
    r = Results()
    for name, ref in zip(ATT_NAMES, results):
        setattr(r, name, ref)
    g1 = Gather(p, FIRST_PARTS, dense, dense_out, sems1)
    g2 = Gather(p, ROW_HALVES, [cot], [cots], sems2)
    g3 = Gather(p, TOKEN_PARTS, [r.n2, rw], [tokens, shares], sems3)
    direct = Direct(weights_out, tuple(turned) + (wf, wo), direct_sems)
    g1.step()
    loads = [pltpu.make_async_copy(a, b, load_sem.at[i]) for i, (a, b) in enumerate(zip(experts_in, natural))]
    for l in loads:
        l.start()
    for l, a, b in zip(loads, natural, turned):
        l.wait()

        def turn(i, carry):
            c = lanes(i * 128)
            b[:, :, c] = jnp.swapaxes(a[:, :, c].astype(F32), 0, 1).astype(BF16)
            return carry

        lax.fori_loop(0, a.shape[2] // 128, turn, 0)
    direct.own()
    for n in FIRST_BATCHES:
        g1.step()
        direct.start(n)
    g2.step(2)
    direct.start(DEVICES)
    g1.arrived()
    loads = [pltpu.make_async_copy(a, b, load_sem.at[i]) for i, (a, b) in enumerate(zip(dense_out, weights))]
    for l in loads:
        l.start()
    g2.step(2)
    for l in loads:
        l.wait()
    for i, chunk in enumerate(attention_forward(x, cos, sin, bias, *weights[:3], r)):
        chunk()
        if i % 2 == 1:
            g2.step()
    route_weights(ids, r, rw)
    g3.step(2)
    make_picks(weights[3], named, picks)
    g2.arrived()
    g3.arrived()
    for g in (g1, g2, g3):
        g.finish()
    direct.finish()


FIRST_BATCHES = (1, 1, 1, 1, 1, 1, 1, 1, 1, 1)


def first(x, cos, sin, bias, ids, dense, cot, gu, dp):
    wide = lambda a: like(DEVICES * a.shape[0], a.shape[1], dtype=a.dtype)
    dense_full = [wide(a) for a in dense]
    return pl.pallas_call(
        first_kernel,
        in_specs=[VMEM] * 5 + [HBM] * 7,
        out_specs=[HBM] * 9 + [VMEM] * 10,
        out_shape=dense_full + [wide(cot), wide(cot), like(DEVICES * TOP, TOK, dtype=F32), like(D, 2 * F), like(D, OWN_WIDTH), like(DEVICES * 64, TOK)] + [like(*s, dtype=t) for s, t in ATT_SHAPES],
        scratch_shapes=[pltpu.VMEM(a.shape, a.dtype) for a in dense_full]
        + [pltpu.VMEM(a.shape, a.dtype) for a in (gu, dp)]
        + [pltpu.VMEM((a.shape[1], a.shape[0], a.shape[2]), a.dtype) for a in (gu, dp)]
        + [pltpu.VMEM((TOP, TOK), F32), pltpu.VMEM((DEVICES * 2, TOK), F32), DMA((4,))]
        + Gather.scratch(4, FIRST_PARTS)
        + Gather.scratch(1, ROW_HALVES)
        + Gather.scratch(2, TOKEN_PARTS)
        + Direct.scratch(5),
        compiler_params=pltpu.CompilerParams(collective_id=0, has_side_effects=True, vmem_limit_bytes=60 * 2**20),
    )(x, cos, sin, bias, ids, *dense, cot, gu, dp)


def middle_kernel(*refs):
    (picks, ids, shares), (tokens, cots, wf_in, wo_in), (gin,), outs, blocks, work, refs = cut_up(refs, 3, 4, 1, 5, 9, 10)
    out_part, dwf, dwo, all_gates, grad_down = outs
    t, c, out_block, gin_block, wf, wo, gates, whole, own = blocks
    (weight_sem, load_sem, out_sem, grad_sem), spaces, sems, direct_sems, _ = cut_up(refs, 4, 5, 9, 3)
    greet_all()
    p = Place()
    s = Scatter(p, ROW_HALVES, [gin_block], [gin], spaces, sems, by_plane=True)
    direct = Direct(down_back, (dwo, gates, grad_down, all_gates), direct_sems)
    e = Experts(work, wf, wo, picks, ids, shares, gates)
    R = SRC * TOK

    def plane_rows(q):
        return pl.ds(pl.multiple_of(p.zq[q] * R, R), R)

    def load(q):
        made = [pltpu.make_async_copy(src.at[plane_rows(q)], dst, load_sem.at[i]) for i, (src, dst) in enumerate(((tokens, t), (cots, c)))]
        for l in made:
            l.start()
        return made

    order = (3, 2, 1, 0)
    loads = load(order[0])
    weights = [pltpu.make_async_copy(a, b, weight_sem.at[i]) for i, (a, b) in enumerate(((wf_in, wf), (wo_in, wo)))]
    for l in weights:
        l.start()
    reads, store = [], None
    for step, q in enumerate(order):
        for l in loads:
            l.wait()
        e.load(step, p.zq[q], t, c)
        if step < 3:
            loads = load(order[step + 1])
        if step == 0:
            for l in weights:
                l.wait()
        for wait in reads:
            wait()
        s.step(step)
        e.run(step)
        if store is not None:
            store.wait()
        e.give(p.zq[q], out_block, gin_block)
        reads = s.begin((q,))
        store = pltpu.make_async_copy(out_block, out_part.at[plane_rows(q)], out_sem)
        store.start()
    stores = []
    for n in range(2 * (D // 256)):
        a, j, b = n // (D // 256), n % (D // 256), n % 2
        block, out, make = ((own, dwo, e.own_grads), (whole, dwf, e.whole_grads))[a]
        if j >= 2:
            stores[n - 2].wait()
        make(j, block.at[b])
        l = pltpu.make_async_copy(block.at[b], out.at[pl.ds(j * 256, 256)], grad_sem.at[b, a])
        l.start()
        stores.append(l)
        if j == D // 256 - 1:
            for l in stores[-2:]:
                l.wait()
            if a == 0:
                direct.own()
                direct.start(DEVICES)
        if n == 1:
            for wait in reads:
                wait()
        if n % 2 == 1:
            s.step()
    s.step(12)
    store.wait()
    s.finish()
    direct.finish()


def middle(picks, ids, shares, tokens, cots, wf, wo):
    R = SRC * TOK
    spaces, sems = Scatter.scratch([tokens], ROW_HALVES)
    return pl.pallas_call(
        middle_kernel,
        in_specs=[VMEM] * 3 + [HBM] * 4,
        out_specs=[VMEM] + [HBM] * 5,
        out_shape=[like(TOK, D, dtype=F32), like(DEVICES * TOK, D), like(D, 2 * F), like(D, OWN_WIDTH), like(DEVICES, 8, TOK, dtype=F32), like(E, D // DEVICES, F)],
        scratch_shapes=[pltpu.VMEM((R, D), BF16)] * 4
        + [
            pltpu.VMEM((D, 2 * F), BF16), pltpu.VMEM((D, OWN_WIDTH), BF16), pltpu.VMEM((DEVICES, 8, TOK), F32),
            pltpu.VMEM((2, 256, 2 * F), BF16), pltpu.VMEM((2, 256, OWN_WIDTH), BF16),
        ]
        + Experts.scratch()
        + [DMA((2,)), DMA((2,)), DMA, DMA((2, 2))]
        + spaces + sems + Direct.scratch(3),
        compiler_params=pltpu.CompilerParams(collective_id=1, has_side_effects=True, vmem_limit_bytes=63 * 2**20),
    )(picks, ids, shares, tokens, cots, wf, wo)


WORK = (
    ("gl", (TOK, TOK), F32),
    ("gm", (TOK, D), F32),
    ("gain2", (TOK, D), F32),
    ("branch", (TOK, D), BF16),
    ("ga", (TOK, D), BF16),
    ("gjf", (TOK, Q_WIDTH + 2 * K_WIDTH), F32),
    ("gj", (TOK, Q_WIDTH + 2 * K_WIDTH), BF16),
    ("gn", (TOK, D), F32),
    ("gates", (64, TOK), F32),
)


def last_kernel(*refs):
    (x, cot, gin, gates, cos, sin), results, (qkv_full, out_full, out_part, dwf, dwo), outs, work, weights, (small_src, load_sem), refs = cut_up(
        refs, 6, 9, 5, 6, len(WORK), 2, 2
    )
    input_grad, layer_output, qkv_grad, out_grad, small_grad, grad_gu = outs
    spaces1, sems1, spaces2, sems2, direct_sems, _ = cut_up(refs, 5, 9, 12, 9, 3)
    greet_all()
    p = Place()
    r = Results()
    for name, ref in zip(ATT_NAMES + tuple(w[0] for w in WORK), tuple(results) + tuple(work)):
        setattr(r, name, ref)
    r.input_grad = input_grad
    r.combined = r.gn
    qkv_ref, out_ref = weights
    s1 = Scatter(p, ROW_HALVES, [out_part], [r.combined], spaces1, sems1)
    s2 = Scatter(p, DENSE_PARTS, [qkv_ref, out_ref, small_src], [qkv_grad, out_grad, small_grad], spaces2, sems2, in_place=True)
    direct = Direct(gate_up_back, (dwf, dwo, grad_gu), direct_sems)
    s1.begin_all()
    loads = [pltpu.make_async_copy(a, b, load_sem.at[i]) for i, (a, b) in enumerate(((out_full, out_ref), (qkv_full, qkv_ref)))]
    for l in loads:
        l.start()
    direct.own()
    direct.start(12)

    def put_qkv(t, value):
        qkv_ref[t * 256 : t * 256 + 256, :] = value

    def put_out(t, value):
        out_ref[t * 256 : t * 256 + 256, :] = value

    def put_small(value):
        small_src[...] = value

    begin, heads, end = attention_backward(x, cot, gin, gates, cos, sin, qkv_ref, out_ref, r, put_qkv, put_out, put_small)
    for l in loads:
        l.wait()
    for i, chunk in enumerate(begin + heads + end):
        chunk()
        if i % 3 == 2:
            s1.step()
            direct.start(2)
    s2.begin_all()
    s1.step(12)
    s2.step(3)
    direct.start(DEVICES)
    layer_output[...] = (r.middle[...] + r.combined[...]).astype(BF16)
    s2.step(12)
    direct.start(DEVICES)
    s1.finish()
    s2.finish()
    direct.finish()


def last(x, cot, gin, gates, cos, sin, results, qkv_full, out_full, out_part, dwf, dwo):
    small = like(D, TOK)
    spaces1, sems1 = Scatter.scratch([out_part], ROW_HALVES)
    spaces2, sems2 = Scatter.scratch([qkv_full, out_full, small], DENSE_PARTS, in_place=True)
    own = D // DEVICES
    return pl.pallas_call(
        last_kernel,
        in_specs=[VMEM] * 15 + [HBM] * 5,
        out_specs=[VMEM] * 5 + [HBM],
        out_shape=[
            like(TOK, D), like(TOK, D), like(own, qkv_full.shape[1], dtype=F32), like(own, D, dtype=F32),
            like(own, TOK, dtype=F32), like(E, own, 2 * F),
        ],
        scratch_shapes=[pltpu.VMEM(s, t) for _, s, t in WORK]
        + [pltpu.VMEM(qkv_full.shape, BF16), pltpu.VMEM(out_full.shape, BF16), pltpu.VMEM(small.shape, BF16), DMA((2,))]
        + spaces1 + sems1 + spaces2 + sems2
        + Direct.scratch(3),
        compiler_params=pltpu.CompilerParams(collective_id=2, has_side_effects=True, vmem_limit_bytes=63 * 2**20),
    )(x, cot, gin, gates, cos, sin, *results, qkv_full, out_full, out_part, dwf, dwo)


def turn_kernel(x_ref, o_ref):
    o_ref[...] = jnp.swapaxes(x_ref[...].astype(F32), 0, 1)


def turned_back(x):
    e, rows, w = x.shape
    return pl.pallas_call(
        turn_kernel,
        grid=(w // 256,),
        in_specs=[pl.BlockSpec((e, rows, 256), lambda i: (0, 0, i))],
        out_specs=pl.BlockSpec((rows, e, 256), lambda i: (0, 0, i)),
        out_shape=like(rows, e, w, dtype=F32),
        compiler_params=pltpu.CompilerParams(vmem_limit_bytes=48 * 2**20),
    )(x)


def fast(
    layer_input, cotangent, sequence_ids, expert_ids, attention_gain, qkv_weight, output_weight, moe_gain, router, gate_up, down_proj
):
    own_rows, T = gate_up.shape[0], layer_input.shape[0]
    small = jnp.concatenate(
        [router, attention_gain[:, None], moe_gain[:, None], jnp.zeros((own_rows, 86), BF16)], axis=1
    )
    cosine, sine = rope_tables(positions(sequence_ids), HEAD_WIDTH)
    cos = jnp.concatenate([cosine] * 4, axis=1)
    sin = jnp.concatenate([-sine, sine] * 2, axis=1)
    place_in = jnp.arange(T, dtype=jnp.int32)
    allowed = (sequence_ids[:, None] == sequence_ids[None, :]) & (place_in[None, :] <= place_in[:, None])
    bias = jnp.where(allowed, 0.0, -jnp.inf).astype(F32)

    ids_t = expert_ids.T
    qkv_full, out_full, small_full, ids_all, cots, tokens, shares, wf, wo, picks, *results = first(
        layer_input, cos, sin, bias, ids_t, [qkv_weight, output_weight, small, ids_t], cotangent,
        gate_up, down_proj,
    )

    gin, out_part, dwf, dwo, gates, grad_down = middle(picks, ids_all, shares, tokens, cots, wf, wo)
    input_grad, layer_output, qkv_grad, out_grad, small_grad, grad_gu = last(
        layer_input, cotangent, gin, gates, cos, sin, results, qkv_full, out_full, out_part, dwf, dwo
    )
    gate_up_grad, down_grad = turned_back(grad_gu), turned_back(grad_down)
    return (
        layer_output,
        input_grad,
        small_grad[:, E],
        qkv_grad,
        out_grad,
        small_grad[:, E + 1],
        small_grad[:, :E],
        gate_up_grad,
        down_grad,
    )


def solution(mesh):
    rows, flat, cube = P("fsdp", None), P("fsdp"), P("fsdp", None, None)
    return jax.shard_map(
        fast if mesh.shape["fsdp"] == 32 else on_device,
        mesh=mesh,
        in_specs=(rows, rows, flat, rows, flat, rows, rows, flat, rows, cube, cube),
        out_specs=(rows, rows, flat, rows, rows, flat, rows, cube, cube),
        check_vma=False,
    )
```

```python
import functools
import math
import jax
import jax.numpy as jnp
import numpy as np
from jax import lax
from jax.experimental import pallas as pl
from jax.experimental.pallas import tpu as pltpu
from jax.sharding import PartitionSpec as P

MODEL_WIDTH = 1536
QUERY_HEADS = 24
KEY_VALUE_HEADS = 8
HEAD_WIDTH = 64
E = 40
F = 512
TOP = 8
CAP = 32


EPSILON = 1e-06
ATTN_SCALE = 0.015625
RESIDUAL_SCALE = 0.22
ROPE_BASE = 10000.0
PRECISE_ARITHMETIC = lax.Precision.HIGHEST


def positions(sequence_ids):
    sequence_length = sequence_ids.shape[0]
    places = jnp.arange(sequence_length, dtype=jnp.int32)
    same = (sequence_ids[:, None] == sequence_ids[None, :]) & (places[None, :] < places[:, None])
    return jnp.sum(same.astype(jnp.int32), axis=1, dtype=jnp.int32)


def rope_tables(places, head_size):
    half_size = head_size // 2
    exponents = jnp.arange(half_size, dtype=jnp.float32) * (2.0 / head_size)
    inverse = jnp.exp(exponents * -math.log(ROPE_BASE))
    angles = places.astype(jnp.float32)[:, None] * inverse[None, :]
    return (jnp.cos(angles), jnp.sin(angles))


def apply_rotary(tensor, cosine_lookup, sine_lookup):
    half_size = tensor.shape[-1] // 2
    first_half = tensor[..., :half_size]
    second_half = tensor[..., half_size:]
    cosine_rows = cosine_lookup[:, None, :]
    sine_rows = sine_lookup[:, None, :]
    return jnp.concatenate(
        [
            first_half * cosine_rows - second_half * sine_rows,
            second_half * cosine_rows + first_half * sine_rows,
        ],
        axis=-1,
    )


def rotate_back(tensor, cosine_lookup, sine_lookup):
    half_size = tensor.shape[-1] // 2
    first_half = tensor[..., :half_size]
    second_half = tensor[..., half_size:]
    cosine_rows = cosine_lookup[:, None, :]
    sine_rows = sine_lookup[:, None, :]
    return jnp.concatenate(
        [
            first_half * cosine_rows + second_half * sine_rows,
            second_half * cosine_rows - first_half * sine_rows,
        ],
        axis=-1,
    )


def norm_scale(hidden_state):
    return lax.rsqrt(jnp.mean(hidden_state * hidden_state, axis=-1, keepdims=True) + EPSILON)


def norm_back(hidden_state, gain_vector, scale_rows, upstream):
    weighted = upstream * gain_vector.astype(jnp.float32)
    inner_mean = jnp.mean(weighted * hidden_state, axis=-1, keepdims=True)
    grad_hidden = scale_rows * weighted - hidden_state * scale_rows**3 * inner_mean
    grad_gain = jnp.sum(upstream * hidden_state * scale_rows, axis=0)
    return (grad_hidden, grad_gain)


def expert_slots(expert_ids, experts, capacity):
    rows = expert_ids.shape[0]
    picked = expert_ids[:, :, None] == jnp.arange(experts, dtype=jnp.int32)[None, None, :]
    named = jnp.any(picked, axis=1).astype(jnp.bfloat16)
    places = jnp.arange(rows, dtype=jnp.int32)
    before = (places[None, :] < places[:, None]).astype(jnp.bfloat16)
    ranks = jnp.dot(before, named, preferred_element_type=jnp.float32)
    ranks = jnp.sum(jnp.where(picked, ranks[:, None, :], 0.0), axis=-1).astype(jnp.int32)
    return (expert_ids * capacity + ranks).reshape(-1)


def owner_tables(devices):
    width_owned = E * F // devices
    span_count = (F + width_owned - 2) // F + 1
    first_expert = np.arange(devices) * width_owned // F
    send_table = np.minimum(first_expert[:, None] + np.arange(span_count)[None, :], E).reshape(-1)
    combine_table = (send_table[None, :] == np.arange(E)[:, None]).astype(np.float32)
    return (width_owned, span_count, send_table, combine_table)


def dispatch_rows(buffer_rows, send_table, devices, span_count):
    padded = jnp.concatenate(
        [buffer_rows, jnp.zeros((1, CAP, MODEL_WIDTH), buffer_rows.dtype)], axis=0
    )
    chosen = jnp.asarray(send_table[:, None] == np.arange(E + 1)[None, :], dtype=buffer_rows.dtype)
    picked_rows = jnp.einsum(
        "se,ecd->scd", chosen, padded, preferred_element_type=jnp.float32
    ).astype(buffer_rows.dtype)
    return picked_rows.reshape(devices, span_count, CAP, MODEL_WIDTH)


def merge_entries(returned, combine_table):
    flat_rows = returned.reshape(returned.shape[0] * returned.shape[1], CAP * MODEL_WIDTH)
    summed = jnp.dot(
        jnp.asarray(combine_table),
        flat_rows,
        precision=PRECISE_ARITHMETIC,
        preferred_element_type=jnp.float32,
    )
    return summed.reshape(E, CAP, MODEL_WIDTH)


def on_device(
    layer_input,
    cotangent,
    sequence_ids,
    expert_ids,
    attention_gain,
    qkv_weight,
    output_weight,
    moe_gain,
    router,
    gate_up,
    down_proj,
):
    sequence_length = layer_input.shape[0]
    shard_rows = gate_up.shape[0]
    query_group_count = QUERY_HEADS // KEY_VALUE_HEADS
    query_feature_width = QUERY_HEADS * HEAD_WIDTH
    key_feature_width = KEY_VALUE_HEADS * HEAD_WIDTH
    rows_per_block = min(512, sequence_length)
    devices = lax.axis_size("fsdp")
    dense_set = (
        lax.all_gather(attention_gain, "fsdp", axis=0, tiled=True),
        lax.all_gather(qkv_weight, "fsdp", axis=0, tiled=True),
        lax.all_gather(output_weight, "fsdp", axis=0, tiled=True),
        lax.all_gather(moe_gain, "fsdp", axis=0, tiled=True),
        lax.all_gather(router, "fsdp", axis=0, tiled=True),
    )
    gain_one, qkv_full, out_full, gain_two, router_full = dense_set
    width_owned, span_count, send_table, combine_table = owner_tables(devices)
    gate_cols = jnp.transpose(gate_up.reshape(shard_rows, E, 2, F), (0, 2, 1, 3)).reshape(
        shard_rows, 2, E * F
    )
    down_cols = down_proj.reshape(shard_rows, 1, E * F)
    owned_weights = lax.all_to_all(
        jnp.concatenate([gate_cols, down_cols], axis=1),
        "fsdp",
        split_axis=2,
        concat_axis=0,
        tiled=True,
    )
    owned_gate_up = owned_weights[:, :2, :]
    owned_down = owned_weights[:, 2, :]
    owner_index = lax.axis_index("fsdp")
    owned_start = owner_index * width_owned
    owned_columns = owned_start + jnp.arange(width_owned, dtype=jnp.int32)
    slot_of = owned_columns // F - owned_start // F
    column_mask = (slot_of[None, :] == jnp.arange(span_count, dtype=jnp.int32)[:, None]).astype(
        jnp.float32
    )
    inputs = layer_input.astype(jnp.float32)
    scale_one = norm_scale(inputs)
    normed_one = (inputs * scale_one * gain_one.astype(jnp.float32)).astype(jnp.bfloat16)
    joined_projection = jnp.dot(normed_one, qkv_full, preferred_element_type=jnp.float32)
    places = positions(sequence_ids)
    cosine_lookup, sine_lookup = rope_tables(places, HEAD_WIDTH)
    query_rows = apply_rotary(
        joined_projection[:, :query_feature_width].reshape(
            sequence_length, QUERY_HEADS, HEAD_WIDTH
        ),
        cosine_lookup,
        sine_lookup,
    ).astype(jnp.bfloat16)
    query_rows = query_rows.reshape(sequence_length, KEY_VALUE_HEADS, query_group_count, HEAD_WIDTH)
    rotated_keys = apply_rotary(
        joined_projection[:, query_feature_width : query_feature_width + key_feature_width].reshape(
            sequence_length, KEY_VALUE_HEADS, HEAD_WIDTH
        ),
        cosine_lookup,
        sine_lookup,
    ).astype(jnp.bfloat16)
    value_inputs = (
        joined_projection[:, query_feature_width + key_feature_width :]
        .reshape(sequence_length, KEY_VALUE_HEADS, HEAD_WIDTH)
        .astype(jnp.bfloat16)
    )
    token_index = jnp.arange(sequence_length, dtype=jnp.int32)

    def block_scores(offset):
        scores = (
            jnp.einsum(
                "qkgd,tkd->kgqt", query_rows, rotated_keys, preferred_element_type=jnp.float32
            )
            * ATTN_SCALE
        )
        allowed = (
            sequence_ids[offset : offset + rows_per_block, None] == sequence_ids[None, :]
        ) & (token_index[None, :] <= token_index[offset : offset + rows_per_block, None])
        return jnp.where(allowed, scores, -jnp.inf)

    offset = 0
    scores = block_scores(offset)
    row_peak = jnp.max(scores, axis=-1, keepdims=True)
    log_total = row_peak + jnp.log(jnp.sum(jnp.exp(scores - row_peak), axis=-1, keepdims=True))
    probs_half = jnp.exp(scores - log_total).astype(jnp.bfloat16)
    mixed_heads = jnp.einsum(
        "kgqt,tkd->qkgd", probs_half, value_inputs, preferred_element_type=jnp.float32
    )
    attention_output_list = mixed_heads.reshape(rows_per_block, query_feature_width).astype(
        jnp.bfloat16
    )
    total_list = [log_total]
    branch = jnp.dot(attention_output_list, out_full, preferred_element_type=jnp.float32)
    middle = inputs + RESIDUAL_SCALE * branch
    scale_two = norm_scale(middle)
    normed_two = (middle * scale_two * gain_two.astype(jnp.float32)).astype(jnp.bfloat16)
    logits = jnp.dot(normed_two, router_full, preferred_element_type=jnp.float32)
    gate_probs = jax.nn.softmax(logits, axis=-1)
    picked = (expert_ids[:, :, None] == jnp.arange(E, dtype=jnp.int32)[None, None, :]).astype(
        jnp.float32
    )
    route_weight = jnp.einsum("tke,te->tk", picked, gate_probs, precision=PRECISE_ARITHMETIC)
    slot_rows = expert_slots(expert_ids, E, CAP)
    received_storage = (
        jnp.zeros((E * CAP, MODEL_WIDTH), jnp.bfloat16)
        .at[slot_rows]
        .set(jnp.repeat(normed_two, TOP, axis=0))
        .reshape(E, CAP, MODEL_WIDTH)
    )
    send_in = dispatch_rows(received_storage, send_table, devices, span_count)
    pre_cols = jnp.einsum(
        "nrkd,dgw->nrkgw",
        lax.all_to_all(send_in, "fsdp", split_axis=0, concat_axis=0, tiled=True),
        owned_gate_up,
        preferred_element_type=jnp.float32,
    )
    pre_cols = pre_cols * column_mask[None, :, None, None, :]
    gate_cols_pre = pre_cols[..., 0, :]
    up_cols_pre = pre_cols[..., 1, :]
    acted = (gate_cols_pre * jax.nn.sigmoid(gate_cols_pre) * up_cols_pre).astype(jnp.bfloat16)
    partial_out = jnp.einsum("nrkw,dw->nrkd", acted, owned_down, preferred_element_type=jnp.float32)
    returned_out = lax.all_to_all(partial_out, "fsdp", split_axis=0, concat_axis=0, tiled=True)
    buffer_out = merge_entries(returned_out, combine_table)
    routed_out = buffer_out.reshape(E * CAP, MODEL_WIDTH)[slot_rows].reshape(
        sequence_length, TOP, MODEL_WIDTH
    )
    combined = jnp.einsum("tk,tkd->td", route_weight, routed_out, precision=PRECISE_ARITHMETIC)
    layer_output = (middle + RESIDUAL_SCALE * combined).astype(jnp.bfloat16)
    upstream = cotangent.astype(jnp.float32)
    grad_mix = RESIDUAL_SCALE * upstream
    grad_weight = jnp.einsum("td,tkd->tk", grad_mix, routed_out, precision=PRECISE_ARITHMETIC)
    grad_rows = (
        (route_weight[:, :, None] * grad_mix[:, None, :])
        .astype(jnp.bfloat16)
        .reshape(sequence_length * TOP, MODEL_WIDTH)
    )
    buffer_grad = (
        jnp.zeros((E * CAP, MODEL_WIDTH), jnp.bfloat16)
        .at[slot_rows]
        .set(grad_rows)
        .reshape(E, CAP, MODEL_WIDTH)
    )
    gain_one_back, qkv_back, out_back, gain_two_back, router_back = dense_set
    send_grad = dispatch_rows(buffer_grad, send_table, devices, span_count)
    rows_in = lax.all_to_all(send_in, "fsdp", split_axis=0, concat_axis=0, tiled=True)
    rows_grad = lax.all_to_all(send_grad, "fsdp", split_axis=0, concat_axis=0, tiled=True)
    pre_cols = jnp.einsum(
        "nrkd,dgw->nrkgw", rows_in, owned_gate_up, preferred_element_type=jnp.float32
    )
    pre_cols = pre_cols * column_mask[None, :, None, None, :]
    gate_cols_pre = pre_cols[..., 0, :]
    up_cols_pre = pre_cols[..., 1, :]
    sigmoid_cols = jax.nn.sigmoid(gate_cols_pre)
    silu_cols = gate_cols_pre * sigmoid_cols
    acted = (silu_cols * up_cols_pre).astype(jnp.bfloat16)
    grad_act_cols = jnp.einsum(
        "nrkd,dw->nrkw", rows_grad, owned_down, preferred_element_type=jnp.float32
    )
    grad_gate_cols = (
        grad_act_cols * up_cols_pre * sigmoid_cols * (1.0 + gate_cols_pre * (1.0 - sigmoid_cols))
    )
    grad_up_cols = grad_act_cols * silu_cols
    grad_pair = jnp.stack([grad_gate_cols, grad_up_cols], axis=3).astype(jnp.bfloat16)
    partial_back = jnp.einsum(
        "nrkgw,dgw->nrkd", grad_pair, owned_gate_up, preferred_element_type=jnp.float32
    )
    returned_back = lax.all_to_all(partial_back, "fsdp", split_axis=0, concat_axis=0, tiled=True)
    results = (returned_back, rows_in, rows_grad, grad_pair, acted)
    returned_back, rows_in_all, rows_grad_all, grad_pair_all, acted_all = results
    backward_buffer = merge_entries(returned_back, combine_table)
    owned_gate_up_grad = jnp.einsum(
        "nrkd,nrkgw->dgw", rows_in_all, grad_pair_all, preferred_element_type=jnp.float32
    )
    owned_down_grad = jnp.einsum(
        "nrkd,nrkw->dw", rows_grad_all, acted_all, preferred_element_type=jnp.float32
    )
    owned_grads = jnp.concatenate([owned_gate_up_grad, owned_down_grad[:, None, :]], axis=1)
    relaid = lax.all_to_all(owned_grads, "fsdp", split_axis=0, concat_axis=2, tiled=True)
    gate_up_grad = jnp.transpose(
        relaid[:, :2, :].reshape(shard_rows, 2, E, F), (0, 2, 1, 3)
    ).reshape(shard_rows, E, 2 * F)
    down_grad = relaid[:, 2, :].reshape(shard_rows, E, F)
    grad_normed = jnp.sum(
        backward_buffer.reshape(E * CAP, MODEL_WIDTH)[slot_rows].reshape(
            sequence_length, TOP, MODEL_WIDTH
        ),
        axis=1,
    )
    grad_gates = jnp.einsum("tk,tke->te", grad_weight, picked, precision=PRECISE_ARITHMETIC)
    grad_logits = gate_probs * (
        grad_gates - jnp.sum(gate_probs * grad_gates, axis=-1, keepdims=True)
    )
    grad_normed = grad_normed + jnp.einsum(
        "te,de->td", grad_logits, router_back.astype(jnp.float32), precision=PRECISE_ARITHMETIC
    )
    router_part = jnp.einsum(
        "td,te->de", normed_two.astype(jnp.float32), grad_logits, precision=PRECISE_ARITHMETIC
    )
    grad_middle, gain_two_part = norm_back(middle, gain_two_back, scale_two, grad_normed)
    grad_middle = grad_middle + upstream
    grad_branch = (RESIDUAL_SCALE * grad_middle).astype(jnp.bfloat16)
    out_part = jnp.einsum(
        "tq,td->qd", attention_output_list, grad_branch, preferred_element_type=jnp.float32
    )
    attention_output_gradient = jnp.einsum(
        "td,qd->tq", grad_branch, out_back, preferred_element_type=jnp.float32
    ).astype(jnp.bfloat16)
    value_gradient = jnp.zeros((sequence_length, KEY_VALUE_HEADS, HEAD_WIDTH), jnp.float32)
    key_gradient = jnp.zeros((sequence_length, KEY_VALUE_HEADS, HEAD_WIDTH), jnp.float32)
    query_grads = []
    for block_number, offset in enumerate(range(0, sequence_length, rows_per_block)):
        scores = block_scores(offset)
        attn_probs = jnp.exp(scores - total_list[block_number])
        block_gradient = attention_output_gradient.reshape(
            rows_per_block, KEY_VALUE_HEADS, query_group_count, HEAD_WIDTH
        )
        attention_output_block = attention_output_list.reshape(
            rows_per_block, KEY_VALUE_HEADS, query_group_count, HEAD_WIDTH
        )
        row_delta = jnp.sum(
            block_gradient.astype(jnp.float32) * attention_output_block.astype(jnp.float32), axis=-1
        )
        row_delta = jnp.transpose(row_delta, (1, 2, 0))[..., None]
        value_gradient = jnp.einsum(
            "kgqt,qkgd->tkd",
            attn_probs.astype(jnp.bfloat16),
            block_gradient,
            preferred_element_type=jnp.float32,
        )
        grad_probs = jnp.einsum(
            "qkgd,tkd->kgqt", block_gradient, value_inputs, preferred_element_type=jnp.float32
        )
        grad_scores = (attn_probs * (grad_probs - row_delta) * ATTN_SCALE).astype(jnp.bfloat16)
        query_grads.append(
            jnp.einsum(
                "kgqt,tkd->qkgd", grad_scores, rotated_keys, preferred_element_type=jnp.float32
            )
        )
        key_gradient = jnp.einsum(
            "kgqt,qkgd->tkd", grad_scores, query_rows, preferred_element_type=jnp.float32
        )
    grad_queries = query_grads[0].reshape(sequence_length, QUERY_HEADS, HEAD_WIDTH)
    grad_joined = jnp.concatenate(
        [
            rotate_back(grad_queries, cosine_lookup, sine_lookup).reshape(
                sequence_length, query_feature_width
            ),
            rotate_back(key_gradient, cosine_lookup, sine_lookup).reshape(
                sequence_length, key_feature_width
            ),
            value_gradient.reshape(sequence_length, key_feature_width),
        ],
        axis=-1,
    ).astype(jnp.bfloat16)
    qkv_part = jnp.einsum("td,tm->dm", normed_one, grad_joined, preferred_element_type=jnp.float32)
    grad_normed_one = jnp.einsum(
        "tm,dm->td", grad_joined, qkv_back, preferred_element_type=jnp.float32
    )
    grad_inputs, gain_one_part = norm_back(inputs, gain_one_back, scale_one, grad_normed_one)
    input_grad = (grad_inputs + grad_middle).astype(jnp.bfloat16)
    dense_grads = (
        lax.psum_scatter(gain_one_part, "fsdp", scatter_dimension=0, tiled=True),
        lax.psum_scatter(qkv_part, "fsdp", scatter_dimension=0, tiled=True),
        lax.psum_scatter(out_part, "fsdp", scatter_dimension=0, tiled=True),
        lax.psum_scatter(gain_two_part, "fsdp", scatter_dimension=0, tiled=True),
        lax.psum_scatter(router_part, "fsdp", scatter_dimension=0, tiled=True),
    )
    return (
        layer_output,
        input_grad,
        dense_grads[0],
        dense_grads[1],
        dense_grads[2],
        dense_grads[3],
        dense_grads[4],
        gate_up_grad,
        down_grad,
    )


D = MODEL_WIDTH
SRC = 8
STEPS = 4
M = SRC * CAP
F32, BF16 = jnp.float32, jnp.bfloat16

def nt(a, b):
    return lax.dot_general(a, b, (((1,), (1,)), ((), ())), preferred_element_type=F32)
def nn(a, b):
    return lax.dot_general(a, b, (((1,), (0,)), ((), ())), preferred_element_type=F32)
def tn(a, b):
    return lax.dot_general(a, b, (((0,), (0,)), ((), ())), preferred_element_type=F32)

QUARTER, DOWN_WHOLE, DOWN_QUARTER, OWN_WIDTH = 0, 256, 768, 896

class Experts:
    NAMES = ("x", "c", "rw", "gw", "act", "dgu", "actq", "dguq", "ow", "gi")

    @staticmethod
    def scratch():
        R = STEPS * M
        return [
            pltpu.VMEM((2, R, D), BF16), pltpu.VMEM((2, R, D), BF16), pltpu.VMEM((2, M, 128), F32), pltpu.VMEM((2, M, 128), F32),
            pltpu.VMEM((R, F), BF16), pltpu.VMEM((R, 2 * F), BF16), pltpu.VMEM((R, 128), BF16), pltpu.VMEM((R, 256), BF16),
            pltpu.VMEM((2, M, D), BF16), pltpu.VMEM((2, M, D), BF16),
        ]

    def __init__(self, refs, wf_ref, wo_ref, pick_ref, ids_ref, share_ref, gates_ref):
        for name, ref in zip(self.NAMES, refs):
            setattr(self, name, ref)
        self.wf, self.wo, self.pick, self.ids, self.shares, self.gates = wf_ref, wo_ref, pick_ref, ids_ref, share_ref, gates_ref

    def picks(self, plane, s):
        return self.pick[pl.ds(pl.multiple_of(plane * (SRC * 64) + s * 64, 64), 64), :]

    def load(self, step, plane, t_ref, c_ref):
        def one(s):
            pick = self.picks(plane, s)
            block = pl.ds(pl.multiple_of(s * 128, 128), 128)
            xs = nn(pick, t_ref[block, :]).astype(BF16)
            cs = nn(pick, c_ref[block, :]).astype(BF16)
            wide = pick.astype(F32)
            eight = pl.ds(pl.multiple_of(plane * (SRC * TOP) + s * TOP, TOP), TOP)
            share = []
            for k, own in enumerate(owned_experts()):
                prob = jnp.sum(jnp.where(self.ids[eight, :] == own, self.shares[eight, :], 0.0), axis=0, keepdims=True)
                share.append(jnp.sum(wide[k * CAP:k * CAP + CAP] * prob, axis=1, keepdims=True) * RESIDUAL_SCALE)
            here = pl.ds(pl.multiple_of(s * CAP, CAP), CAP)
            to = pl.ds(pl.multiple_of(step * M + s * CAP, CAP), CAP)
            for k in range(2):
                self.x[k, to, :] = xs[k * CAP:k * CAP + CAP]
                self.c[k, to, :] = cs[k * CAP:k * CAP + CAP]
                self.rw[k, here, :] = jnp.broadcast_to(share[k], (CAP, 128))
        for s in range(SRC):
            one(s)

    def run(self, step):
        at = slice(step * M, step * M + M)
        sets = (
            (self.act, self.dgu, 512, lambda: self.wf[...], DOWN_WHOLE),
            (self.actq, self.dguq, 128, lambda: self.wo[:, QUARTER:QUARTER + 256], DOWN_QUARTER),
        )
        for k, (acts, dgus, w, w_gu, d0) in enumerate(sets):
            pre = nn(self.x[k, at, :], w_gu())
            gate, up = pre[:, :w], pre[:, w:]
            sig = jax.nn.sigmoid(gate)
            silu = gate * sig
            act = silu * up
            share = self.rw[k, :, 0:1]
            scaled = (share * act).astype(BF16)
            acts[at, :] = scaled
            da = nn(self.c[k, at, :], self.wo[:, d0:d0 + w])
            gw = RESIDUAL_SCALE * jnp.sum(act.astype(BF16).astype(F32) * da, axis=1, keepdims=True)
            self.gw[k] = jnp.broadcast_to(gw, (M, 128))
            self.ow[k] = nt(scaled, self.wo[:, d0:d0 + w]).astype(BF16)
            da = share * da
            dgus[at, :w] = (da * up * sig * (1.0 + gate * (1.0 - sig))).astype(BF16)
            dgus[at, w:] = (da * silu).astype(BF16)
            self.gi[k] = nt(dgus[at, :], w_gu()).astype(BF16)

    def give(self, plane, out_ref, gin_ref):
        def one(s):
            r = pl.ds(pl.multiple_of(s * CAP, CAP), CAP)
            pick = self.picks(plane, s)
            to = pl.ds(pl.multiple_of(s * 128, 128), 128)
            out_ref[to, :] = tn(pick, jnp.concatenate([self.ow[0, r, :], self.ow[1, r, :]], axis=0)).astype(BF16)
            gin_ref[to, :] = tn(pick, jnp.concatenate([self.gi[0, r, :], self.gi[1, r, :]], axis=0)).astype(BF16)
            wide = pick.astype(F32)
            rows = [jnp.sum(wide[k * CAP:k * CAP + CAP] * self.gw[k, r, :], axis=0, keepdims=True) for k in range(2)]
            self.gates[plane * SRC + s] = jnp.concatenate(rows + [jnp.zeros((6, 128), F32)], axis=0)
        for s in range(SRC):
            one(s)

    def own_grads(self, j, ref):
        c = slice(j * 256, j * 256 + 256)
        ref[:, QUARTER:QUARTER + 256] = tn(self.x[1, :, c], self.dguq[...]).astype(BF16)
        ref[:, DOWN_WHOLE:DOWN_WHOLE + 512] = tn(self.c[0, :, c], self.act[...]).astype(BF16)
        ref[:, DOWN_QUARTER:DOWN_QUARTER + 128] = tn(self.c[1, :, c], self.actq[...]).astype(BF16)

    def whole_grads(self, j, ref):
        ref[...] = tn(self.x[0, :, j * 256:j * 256 + 256], self.dgu[...]).astype(BF16)


MESH = pl.DeviceIdType.MESH
DEVICES = 32
TURNS = tuple(sorted(range(1, DEVICES), key=lambda k: (k % 8 * 5 % 8, k)))
DMA = pltpu.SemaphoreType.DMA


def dev(z, y, x, c):
    return ((z * 2 + y) * 2 + x) * 2 + c


class Place:
    def __init__(self):
        me = lax.axis_index("fsdp")
        self.me = me
        z, y, x, c = me // 8, lax.rem(me // 4, 2), lax.rem(me // 2, 2), lax.rem(me, 2)
        self.z, self.y, self.x, self.c = z, y, x, c
        self.sib, self.xn, self.yn = dev(z, y, x, 1 - c), dev(z, y, 1 - x, c), dev(z, 1 - y, x, c)
        self.up, self.down = dev(z + 1, y, x, c), dev(z - 1, y, x, c)
        table = ((0, 1, 2, 3), (1, 0, 2, 3), (2, 3, 1, 0), (3, 2, 1, 0))
        self.zq = []
        for q in range(4):
            v = jnp.int32(table[0][q])
            for k in range(1, 4):
                v = jnp.where(z == k, table[k][q], v)
            self.zq.append(v)


def greet_all():
    me = lax.axis_index("fsdp")
    barrier = pltpu.get_barrier_semaphore()
    for k in range(1, DEVICES):
        pl.semaphore_signal(barrier, inc=1, device_id=(lax.rem(me + k, DEVICES),), device_id_type=MESH)
    pl.semaphore_wait(barrier, DEVICES - 1)


def rc(src, dst, ss, rs, to):
    return pltpu.make_async_remote_copy(src_ref=src, dst_ref=dst, send_sem=ss, recv_sem=rs, device_id=(to,), device_id_type=MESH)


class Direct:
    def __init__(self, pieces, refs, sems):
        self.pieces, self.refs, (self.ss, self.rs, self.ls) = pieces, refs, sems
        self.me = lax.axis_index("fsdp")
        self.left = list(TURNS)

    @staticmethod
    def scratch(count):
        return [DMA((DEVICES, count)), DMA((DEVICES, count)), DMA((count,))]

    def own(self):
        self.local = [pltpu.make_async_copy(a, b, self.ls.at[i]) for i, (a, b) in enumerate(self.pieces(self.me, self.me, self.refs))]
        for l in self.local:
            l.start()

    def start(self, number):
        turns, self.left = self.left[:number], self.left[number:]
        for k in turns:
            to = lax.rem(self.me + k, DEVICES)
            for i, (a, b) in enumerate(self.pieces(self.me, to, self.refs)):
                rc(a, b, self.ss.at[k, i], self.rs.at[k, i], to).start()

    def finish(self):
        self.start(DEVICES)
        for k in TURNS:
            src = lax.rem(self.me + DEVICES - k, DEVICES)
            for i, (a, b) in enumerate(self.pieces(src, self.me, self.refs)):
                rc(a, b, self.ss.at[k, i], self.rs.at[k, i], src).wait_recv()
        for k in TURNS:
            to = lax.rem(self.me + k, DEVICES)
            for i, (a, b) in enumerate(self.pieces(self.me, to, self.refs)):
                rc(a, b, self.ss.at[k, i], self.rs.at[k, i], to).wait_send()
        for l in self.local:
            l.wait()


class Gather:
    ORDER = ((1, 0), (1, 1), (2, 0), (1, 2), (2, 1), (3, 0), (1, 3), (2, 2), (3, 1), (2, 3), (3, 2), (3, 3))

    def __init__(self, p, parts, shards, outs, sems):
        self.p, self.parts, self.shards, self.outs, self.sems = p, parts, shards, outs, sems
        self.P, self.sends, self.locals = len(parts), [], []
        self.left = list(self.ORDER)

    @staticmethod
    def scratch(arrays, parts):
        P = len(parts)
        return [DMA((arrays,)), DMA((4, P)), DMA((P,))] + [DMA((4, P))] * 7 + [DMA((4, 4, P))] * 2

    def at(self, i, d):
        a, c0, w, _ = self.parts[i]
        rows = self.shards[a].shape[0]
        return self.outs[a].at[pl.ds(pl.multiple_of(d * rows, rows), rows), pl.ds(c0, w)]

    def spot(self, i, q, k, core):
        p = self.p
        flip_x, flip_y = ((0, 0), (1, 0), (0, 1), (1, 1))[k] if self.parts[i][3] == 0 else ((0, 0), (0, 1), (1, 0), (1, 1))[k]
        return self.at(i, dev(p.zq[q], 1 - p.y if flip_y else p.y, 1 - p.x if flip_x else p.x, core))

    def go(self, copy):
        copy.start()
        self.sends.append(copy)

    def step(self, number=1):
        for f, q in self.left[:number]:
            (self.stage1, self.stage2, self.stage3)[f - 1](q)
        self.left = self.left[number:]

    def stage1(self, q):
        p = self.p
        _, zs, zs2, zr, fs, fr, s1s, s1r, s2s, s2r, cs, cr = self.sems
        for i in range(self.P):
            a, c0, w, mode = self.parts[i]
            first, second = (p.xn, p.yn) if mode == 0 else (p.yn, p.xn)
            here = self.spot(i, q, 0, p.c)
            if q == 0:
                src = self.shards[a].at[:, pl.ds(c0, w)]

                @pl.when(p.z < 3)
                def _():
                    rc(src, here, zs.at[0, i], zr.at[p.z, i], p.up).start()

                @pl.when(p.z > 0)
                def _():
                    rc(src, here, zs2.at[i], zr.at[p.z, i], p.down).start()
            else:
                src, zq = here, p.zq[q]
                rc(here, here, zs.at[q, i], zr.at[zq, i], p.up).wait_recv()

                @pl.when((zq < p.z) & (p.z < 3))
                def _():
                    rc(src, here, zs.at[q, i], zr.at[zq, i], p.up).start()

                @pl.when((zq > p.z) & (p.z > 0))
                def _():
                    rc(src, here, zs.at[q, i], zr.at[zq, i], p.down).start()
            self.go(rc(src, here, fs.at[q, i], fr.at[q, i], first))
            self.go(rc(src, here, s1s.at[q, i], s1r.at[q, i], second))
            self.go(rc(src, here, cs.at[0, q, i], cr.at[0, q, i], p.sib))
        if q == 0:
            for a, (shard, out) in enumerate(zip(self.shards, self.outs)):
                rows = shard.shape[0]
                l = pltpu.make_async_copy(shard, out.at[pl.ds(pl.multiple_of(p.me * rows, rows), rows)], self.sems[0].at[a])
                l.start()
                self.locals.append(l)

    def stage2(self, q):
        p = self.p
        fs, fr, s2s, s2r, cs, cr = self.sems[4:6] + self.sems[8:12]
        for i in range(self.P):
            second = p.yn if self.parts[i][3] == 0 else p.xn
            there = self.spot(i, q, 1, p.c)
            rc(there, there, fs.at[q, i], fr.at[q, i], second).wait_recv()
            self.go(rc(there, there, s2s.at[q, i], s2r.at[q, i], second))
            self.go(rc(there, there, cs.at[1, q, i], cr.at[1, q, i], p.sib))

    def stage3(self, q):
        p = self.p
        cs, cr = self.sems[10:12]
        for k, (ss, rs) in ((2, self.sems[6:8]), (3, self.sems[8:10])):
            for i in range(self.P):
                there = self.spot(i, q, k, p.c)
                rc(there, there, ss.at[q, i], rs.at[q, i], p.sib).wait_recv()
                self.go(rc(there, there, cs.at[k, q, i], cr.at[k, q, i], p.sib))

    def arrived(self):
        self.step(12)
        cs, cr = self.sems[10:12]
        for q in range(4):
            for k in range(4):
                for i in range(self.P):
                    there = self.spot(i, q, k, 1 - self.p.c)
                    rc(there, there, cs.at[k, q, i], cr.at[k, q, i], self.p.sib).wait_recv()
        for l in self.locals:
            l.wait()

    def finish(self):
        p = self.p
        zs, zs2, zr = self.sems[1:4]
        for copy in self.sends:
            copy.wait_send()
        for i in range(self.P):
            here = self.at(i, p.me)

            @pl.when(p.z < 3)
            def _():
                rc(here, here, zs.at[0, i], zr.at[p.z, i], p.up).wait_send()

            @pl.when(p.z > 0)
            def _():
                rc(here, here, zs2.at[i], zr.at[p.z, i], p.down).wait_send()

            for q in range(1, 4):
                zq = p.zq[q]

                @pl.when(((zq < p.z) & (p.z < 3)) | ((zq > p.z) & (p.z > 0)))
                def _():
                    rc(here, here, zs.at[q, i], zr.at[zq, i], p.up).wait_send()


class Scatter:
    ORDER = ((1, 3), (1, 2), (2, 3), (1, 1), (2, 2), (3, 3), (1, 0), (2, 1), (3, 2), (2, 0), (3, 1), (3, 0))
    STEP = 16

    def __init__(self, p, parts, fulls, outs, spaces, sems, in_place=False, by_plane=False):
        self.by_plane, self.reads = by_plane, []
        self.p, self.parts, self.fulls, self.outs, self.sems, self.in_place = p, parts, fulls, outs, sems, in_place
        count = len(fulls)
        if in_place:
            spaces = (None,) * count + tuple(spaces)
        self.held, self.r0, self.r1, self.r2, self.r3 = (spaces[i * count : (i + 1) * count] for i in range(5))
        self.rows = [f.shape[0] // (8 if by_plane else DEVICES) for f in fulls]
        self.P, self.sends = len(parts), []
        self.left = list(self.ORDER)

    def begin_all(self):
        self.reads = self.begin()

    @staticmethod
    def scratch(arrays, parts, in_place=False):
        P = len(parts)
        spaces = []
        for cnt in (16, 8, 4, 5) if in_place else (16, 16, 8, 4, 5):
            spaces += [pltpu.VMEM((cnt, a.shape[0] // DEVICES, a.shape[1]), a.dtype) for a in arrays]
        return spaces, [DMA((4, 4, P))] * 3 + [DMA((4, 2, P))] * 2 + [DMA((4, P))] * 3 + [DMA((5, P))]

    def go(self, copy):
        copy.start()
        self.sends.append(copy)

    def cut(self, i):
        return pl.ds(self.parts[i][1], self.parts[i][2])

    def spot(self, i, k):
        x, y = self.p.x, self.p.y
        if self.parts[i][3] == 0:
            return ((1 - y, 1 - x), (1 - y, x), (y, 1 - x), (y, x))[k]
        return ((1 - y, 1 - x), (y, 1 - x), (1 - y, x), (y, x))[k]

    def slot(self, q, yy, xx):
        return (yy * 2 + xx) * 4 + self.p.zq[q]

    def hold(self, a, q, yy, xx):
        if self.in_place:
            start = dev(self.p.zq[q], yy, xx, self.p.c) * self.rows[a]
            return self.fulls[a].at[pl.ds(pl.multiple_of(start, self.rows[a]), self.rows[a])]
        return self.held[a].at[self.slot(q, yy, xx)]

    def source(self, i, q, k, core):
        a = self.parts[i][0]
        d = dev(0 if self.by_plane else self.p.zq[q], *self.spot(i, k), core)
        return self.fulls[a].at[pl.ds(pl.multiple_of(d * self.rows[a], self.rows[a]), self.rows[a]), self.cut(i)]

    def begin(self, planes=(3, 2, 1, 0)):
        ls, s0, e0 = self.sems[:3]
        made = []
        for q in planes:
            for k in range(4):
                for i in range(self.P):
                    a = self.parts[i][0]
                    s = self.slot(q, *self.spot(i, k))
                    copy = rc(self.source(i, q, k, 1 - self.p.c), self.r0[a].at[s, :, self.cut(i)], s0.at[q, k, i], e0.at[q, k, i], self.p.sib)
                    copy.start()
                    made.append(copy.wait_send)
                    if not self.in_place:
                        l = pltpu.make_async_copy(self.source(i, q, k, self.p.c), self.held[a].at[s, :, self.cut(i)], ls.at[q, k, i])
                        l.start()
                        made.append(l.wait)
        return made

    def step(self, number=1):
        for f, q in self.left[:number]:
            (self.stage1, self.stage2, self.stage3)[f - 1](q)
        self.left = self.left[number:]

    def chunks(self, a, body):
        def one(n, carry):
            body(pl.ds(pl.multiple_of(n * self.STEP, self.STEP), self.STEP))
            return carry

        lax.fori_loop(0, self.rows[a] // self.STEP, one, 0)

    def add(self, i, dst, src, s_src):
        a, c0, w, _ = self.parts[i]

        def body(r):
            v = dst[r, c0 : c0 + w].astype(F32) + src[s_src, r, c0 : c0 + w].astype(F32)
            dst[r, c0 : c0 + w] = v.astype(dst.dtype)

        self.chunks(a, body)

    def stage1(self, q):
        p = self.p
        _, s0, e0, s1, e1 = self.sems[:5]
        for k in range(4):
            for i in range(self.P):
                a = self.parts[i][0]
                first = p.yn if self.parts[i][3] == 0 else p.xn
                s = self.slot(q, *self.spot(i, k))
                sums = self.hold(a, q, *self.spot(i, k))
                here = sums.at[:, self.cut(i)]
                rc(here, self.r0[a].at[s, :, self.cut(i)], s0.at[q, k, i], e0.at[q, k, i], p.sib).wait_recv()
                if self.reads and not self.in_place:
                    self.reads[self.reading(q, k, i) * 2 + 1]()
                self.add(i, sums, self.r0[a], s)
                if k < 2:
                    self.go(rc(here, self.r1[a].at[q * 2 + k, :, self.cut(i)], s1.at[q, k, i], e1.at[q, k, i], first))

    def reading(self, q, k, i):
        return ((3 - q) * 4 + k) * self.P + i

    def stage2(self, q):
        p = self.p
        s1, e1, s2, e2 = self.sems[3:7]
        for k in range(2):
            for i in range(self.P):
                a = self.parts[i][0]
                second = p.xn if self.parts[i][3] == 0 else p.yn
                sums = self.hold(a, q, *self.spot(i, k + 2))
                here = sums.at[:, self.cut(i)]
                rc(here, self.r1[a].at[q * 2 + k, :, self.cut(i)], s1.at[q, k, i], e1.at[q, k, i], p.sib).wait_recv()
                self.add(i, sums, self.r1[a], q * 2 + k)
                if k == 0:
                    self.go(rc(here, self.r2[a].at[q, :, self.cut(i)], s2.at[q, i], e2.at[q, i], second))

    def stage3(self, q):
        p = self.p
        s2, e2, s3, e3 = self.sems[5:9]
        zq, z = p.zq[q], p.z
        for i in range(self.P):
            a, c0, w, _ = self.parts[i]
            r3, out, sums = self.r3[a], self.outs[a], self.hold(a, q, p.y, p.x)
            here = sums.at[:, self.cut(i)]
            rc(here, self.r2[a].at[q, :, self.cut(i)], s2.at[q, i], e2.at[q, i], p.sib).wait_recv()
            self.add(i, sums, self.r2[a], q)
            if q > 0:

                @pl.when((zq > z) & (z > 0) | (zq < z) & (z < 3))
                def _():
                    rc(here, r3.at[zq, :, self.cut(i)], s3.at[q, i], e3.at[zq, i], p.sib).wait_recv()
                    self.add(i, sums, r3, zq)

                @pl.when(zq > z)
                def _():
                    rc(here, r3.at[zq, :, self.cut(i)], s3.at[q, i], e3.at[zq, i], p.up).start()

                @pl.when((zq < z) & (zq == z - 1))
                def _():
                    rc(here, r3.at[4, :, self.cut(i)], s3.at[q, i], e3.at[4, i], p.down).start()

                @pl.when(zq < z - 1)
                def _():
                    rc(here, r3.at[zq, :, self.cut(i)], s3.at[q, i], e3.at[zq, i], p.down).start()
            else:

                def first_sum(r):
                    out[r, c0 : c0 + w] = sums[r, c0 : c0 + w].astype(F32)

                self.chunks(a, first_sum)
                for cond, where in ((z > 0, z), (z < 3, 4)):

                    @pl.when(cond)
                    def _():
                        rc(here, r3.at[where, :, self.cut(i)], s3.at[q, i], e3.at[where, i], p.sib).wait_recv()

                        def more(r):
                            out[r, c0 : c0 + w] += r3[where, r, c0 : c0 + w].astype(F32)

                        self.chunks(a, more)

    def finish(self):
        p = self.p
        s3, e3 = self.sems[7:9]
        for wait in self.reads[:: 1 if self.in_place else 2]:
            wait()
        for copy in self.sends:
            copy.wait_send()
        for q in range(1, 4):
            for i in range(self.P):
                here = self.hold(self.parts[i][0], q, p.y, p.x).at[:, self.cut(i)]
                rc(here, here, s3.at[q, i], e3.at[0, i], p.sib).wait_send()


HBM = pl.BlockSpec(memory_space=pl.ANY)
VMEM = pl.BlockSpec(memory_space=pltpu.VMEM)


def like(*shape, dtype=None):
    return jax.ShapeDtypeStruct(shape, dtype or jnp.bfloat16)


def cut_up(refs, *counts):
    out, i = [], 0
    for c in counts:
        out.append(refs[i : i + c])
        i += c
    return out + [refs[i:]]


GROUP = QUERY_HEADS // KEY_VALUE_HEADS
Q_WIDTH, K_WIDTH = QUERY_HEADS * HEAD_WIDTH, KEY_VALUE_HEADS * HEAD_WIDTH
TOK = 128


def partner(v):
    lane = lax.broadcasted_iota(jnp.int32, v.shape, 1) % HEAD_WIDTH
    return jnp.where(lane < HEAD_WIDTH // 2, pltpu.roll(v, 96, 1), pltpu.roll(v, 32, 1))


def attention_forward(x_ref, cos_ref, sin_ref, bias_ref, qkv_ref, out_ref, small_ref, r):
    def norm_one():
        r.small_t[...] = nt(jnp.eye(TOK, dtype=BF16), small_ref[...])
        x = x_ref[...].astype(F32)
        r.n1[...] = (x * norm_scale(x) * r.small_t[E : E + 1, :]).astype(BF16)

    def project(t):
        def run():
            tile = nn(r.n1[...], qkv_ref[:, t * 512 : t * 512 + 512])
            for b in range(4):
                col = t * 512 + b * 128
                v = tile[:, b * 128 : b * 128 + 128]
                if col < Q_WIDTH + K_WIDTH:
                    v = v * cos_ref[...] + partner(v) * sin_ref[...]
                v = v.astype(BF16)
                for half in range(2):
                    piece = v[:, half * 64 : half * 64 + 64]
                    head = col // 64 + half
                    if col < Q_WIDTH:
                        r.q[head // GROUP, head % GROUP * TOK : head % GROUP * TOK + TOK, :] = piece
                    elif col < Q_WIDTH + K_WIDTH:
                        r.k[head - QUERY_HEADS] = piece
                    else:
                        r.v[head - QUERY_HEADS - KEY_VALUE_HEADS] = piece

        return run

    def attend(j):
        def run():
            s = nt(r.q[j], r.k[j]) * ATTN_SCALE
            s = s + jnp.concatenate([bias_ref[...]] * GROUP, axis=0)
            e = jnp.exp(s - jnp.max(s, axis=1, keepdims=True))
            probs = e / jnp.sum(e, axis=1, keepdims=True)
            r.probs[j] = probs
            o = nn(probs.astype(BF16), r.v[j]).astype(BF16)
            for g in range(GROUP):
                h = j * GROUP + g
                r.att[:, h * 64 : h * 64 + 64] = o[g * TOK : g * TOK + TOK]

        return run

    def output(t):
        def run():
            c = slice(t * 512, t * 512 + 512)
            r.middle[:, c] = x_ref[:, c].astype(F32) + RESIDUAL_SCALE * nn(r.att[...], out_ref[:, c])

        return run

    def norm_two():
        m = r.middle[...]
        r.n2[...] = (m * norm_scale(m) * r.small_t[E + 1 : E + 2, :]).astype(BF16)

    return (
        [norm_one]
        + [project(t) for t in range((Q_WIDTH + 2 * K_WIDTH) // 512)]
        + [attend(j) for j in range(KEY_VALUE_HEADS)]
        + [output(t) for t in range(D // 512)]
        + [norm_two]
    )


def split_dot(form, a, b):
    one = b.astype(BF16)
    rest = b - one.astype(F32)
    two = rest.astype(BF16)
    three = (rest - two.astype(F32)).astype(BF16)
    return form(a, one) + form(a, two) + form(a, three)


def norm_back_rows(hidden, gain, upstream):
    scale = norm_scale(hidden)
    weighted = upstream * gain
    inner = jnp.mean(weighted * hidden, axis=-1, keepdims=True)
    return scale * weighted - hidden * scale**3 * inner, upstream * hidden * scale


def gate_probs(r):
    logits = nt(r.small_t[:64, :].astype(BF16), r.n2[...])
    row = lax.broadcasted_iota(jnp.int32, logits.shape, 0)
    logits = jnp.where(row < E, logits, -jnp.inf)
    e = jnp.exp(logits - jnp.max(logits, axis=0, keepdims=True))
    return e / jnp.sum(e, axis=0, keepdims=True)


def attention_backward(x_ref, cot_ref, gin_ref, gates_ref, cos_ref, sin_ref, qkv_ref, out_ref, r, put_qkv, put_out, put_small):
    def router():
        m = r.middle[...]
        probs = gate_probs(r)
        r.gates[...] = jnp.zeros_like(r.gates)
        for g in range(8):
            for j in range(4):
                r.gates[g * 5 + j : g * 5 + j + 1, :] = gates_ref[g * 4 + j, 0:1, :]
            r.gates[g * 5 + 4 : g * 5 + 5, :] = sum(gates_ref[g * 4 + j, 1:2, :] for j in range(4))
        gates = r.gates[...]
        gl = probs * (gates - jnp.sum(probs * gates, axis=0, keepdims=True))
        gl = jnp.concatenate([gl, jnp.zeros((64, TOK), F32)], axis=0).T
        r.gl[...] = gl
        back = nn(gl.astype(BF16), r.small_t[...].astype(BF16))
        low = gl - gl.astype(BF16).astype(F32)
        back = back + nn(low.astype(BF16), r.small_t[...].astype(BF16))
        low = low - low.astype(BF16).astype(F32)
        back = back + nn(low.astype(BF16), r.small_t[...].astype(BF16))
        up = gin_ref[...] + back
        gm, gain_rows = norm_back_rows(m, r.small_t[E + 1 : E + 2, :], up)
        gm = gm + cot_ref[...].astype(F32)
        r.gm[...] = gm
        r.gain2[...] = gain_rows
        r.branch[...] = (RESIDUAL_SCALE * gm).astype(BF16)

    def attended(t):
        def run():
            c = slice(t * 512, t * 512 + 512)
            r.ga[:, c] = nt(r.branch[...], out_ref[c, :]).astype(BF16)

        return run

    def out_part(t):
        def run():
            put_out(t, tn(r.att[:, t * 256 : t * 256 + 256], r.branch[...]).astype(BF16))

        return run

    def head(j):
        def run():
            cols = [slice((j * GROUP + g) * 64, (j * GROUP + g) * 64 + 64) for g in range(GROUP)]
            ga = jnp.concatenate([r.ga[:, c] for c in cols], axis=0)
            at = jnp.concatenate([r.att[:, c] for c in cols], axis=0)
            delta = jnp.sum(ga.astype(F32) * at.astype(F32), axis=1, keepdims=True)
            probs = r.probs[j]
            ds = (probs * (nt(ga, r.v[j]) - delta) * ATTN_SCALE).astype(BF16)
            gq = nn(ds, r.k[j])
            for g, c in enumerate(cols):
                r.gjf[:, c] = gq[g * TOK : g * TOK + TOK]
            r.gjf[:, Q_WIDTH + j * 64 : Q_WIDTH + j * 64 + 64] = tn(ds, r.q[j])
            r.gjf[:, Q_WIDTH + K_WIDTH + j * 64 : Q_WIDTH + K_WIDTH + j * 64 + 64] = tn(probs.astype(BF16), ga)

        return run

    def rotate():
        for col in range(0, Q_WIDTH + 2 * K_WIDTH, 128):
            v = r.gjf[:, col : col + 128]
            if col < Q_WIDTH + K_WIDTH:
                v = v * cos_ref[...] - partner(v) * sin_ref[...]
            r.gj[:, col : col + 128] = v.astype(BF16)

    def qkv_part(t):
        def run():
            put_qkv(t, tn(r.n1[:, t * 256 : t * 256 + 256], r.gj[...]).astype(BF16))

        return run

    def into_normed(t):
        def run():
            c = slice(t * 256, t * 256 + 256)
            r.gn[:, c] = nt(r.gj[...], qkv_ref[c, :])

        return run

    def input_back():
        x = x_ref[...].astype(F32)
        gx, gain_rows = norm_back_rows(x, r.small_t[E : E + 1, :], r.gn[...])
        r.input_grad[...] = (gx + r.gm[...]).astype(BF16)
        lane = lax.broadcasted_iota(jnp.int32, (TOK, TOK), 1)
        small = split_dot(tn, r.n2[...], r.gl[...])
        for rows, at in ((gain_rows, E), (r.gain2[...], E + 1)):
            ones = jnp.where(lane == at, 1.0, 0.0).astype(BF16)
            hi = rows.astype(BF16)
            lo = (rows - hi.astype(F32)).astype(BF16)
            small = small + tn(hi, ones) + tn(lo, ones)
        put_small(small.astype(BF16))

    first = [router] + [attended(t) for t in range(3)] + [out_part(t) for t in range(6)]
    heads = [head(j) for j in range(KEY_VALUE_HEADS)] + [rotate]
    last = [into_normed(t) for t in range(6)] + [input_back] + [qkv_part(t) for t in range(6)]
    return first, heads, last


class Results:
    pass


ATT_NAMES = ("small_t", "n1", "q", "k", "v", "probs", "att", "middle", "n2")
ATT_SHAPES = (
    ((TOK, D), F32),
    ((TOK, D), BF16),
    ((KEY_VALUE_HEADS, GROUP * TOK, HEAD_WIDTH), BF16),
    ((KEY_VALUE_HEADS, TOK, HEAD_WIDTH), BF16),
    ((KEY_VALUE_HEADS, TOK, HEAD_WIDTH), BF16),
    ((KEY_VALUE_HEADS, GROUP * TOK, TOK), F32),
    ((TOK, Q_WIDTH), BF16),
    ((TOK, D), F32),
    ((TOK, D), BF16),
)
ROW_HALVES = ((0, 0, 768, 0), (0, 768, 768, 1))
DENSE_PARTS = ((0, 0, 1280, 0), (0, 1280, 1280, 1), (1, 0, 768, 0), (1, 768, 768, 1), (2, 0, 128, 1))
TOKEN_PARTS = ROW_HALVES + ((1, 0, 128, 1),)
FIRST_PARTS = DENSE_PARTS + ((3, 0, 128, 0),)


def lanes(start):
    return pl.ds(pl.multiple_of(start, 128), 128)


def weights_out(src, dst, refs):
    g_ref, d_ref, wf_ref, wo_ref = refs
    group, own, quarter = dst // 4, lax.rem(dst, 4), lax.rem(dst, 4) * 128
    rows = pl.ds(pl.multiple_of(src * 48, 48), 48)
    fifth = group * 5 + 4
    return (
        (g_ref.at[fifth, :, lanes(quarter)], wo_ref.at[rows, pl.ds(QUARTER, 128)]),
        (g_ref.at[fifth, :, lanes(F + quarter)], wo_ref.at[rows, pl.ds(QUARTER + 128, 128)]),
        (d_ref.at[group * 5 + own], wo_ref.at[rows, pl.ds(DOWN_WHOLE, F)]),
        (d_ref.at[fifth, :, lanes(quarter)], wo_ref.at[rows, pl.ds(DOWN_QUARTER, 128)]),
        (g_ref.at[group * 5 + own], wf_ref.at[rows]),
    )


def down_back(src, dst, refs):
    dwo_ref, gates_ref, d_ref, all_gates_ref = refs
    group, quarter = src // 4, lax.rem(src, 4) * 128
    rows = pl.ds(pl.multiple_of(dst * 48, 48), 48)
    return (
        (gates_ref.at[dst], all_gates_ref.at[src]),
        (dwo_ref.at[rows, pl.ds(DOWN_WHOLE, F)], d_ref.at[group * 5 + lax.rem(src, 4)]),
        (dwo_ref.at[rows, pl.ds(DOWN_QUARTER, 128)], d_ref.at[group * 5 + 4, :, lanes(quarter)]),
    )


def gate_up_back(src, dst, refs):
    dwf_ref, dwo_ref, g_ref = refs
    group, quarter = src // 4, lax.rem(src, 4) * 128
    rows = pl.ds(pl.multiple_of(dst * 48, 48), 48)
    return (
        (dwf_ref.at[rows], g_ref.at[group * 5 + lax.rem(src, 4)]),
        (dwo_ref.at[rows, pl.ds(QUARTER, 128)], g_ref.at[group * 5 + 4, :, lanes(quarter)]),
        (dwo_ref.at[rows, pl.ds(QUARTER + 128, 128)], g_ref.at[group * 5 + 4, :, lanes(F + quarter)]),
    )


def owned_experts():
    me = lax.axis_index("fsdp")
    return (me // 4) * 5 + lax.rem(me, 4), (me // 4) * 5 + 4


def make_picks(ids, named, picks):
    for s in range(DEVICES):
        block = ids[s * TOP : s * TOP + TOP, :]
        for k, e in enumerate(owned_experts()):
            named[s * 2 + k : s * 2 + k + 1, :] = jnp.max(jnp.where(block == e, 1.0, 0.0), axis=0, keepdims=True)
    row = lax.broadcasted_iota(jnp.int32, (TOK, TOK), 0)
    before = jnp.where(row < lax.broadcasted_iota(jnp.int32, (TOK, TOK), 1), 1.0, 0.0).astype(BF16)
    ranks = nn(named[...].astype(BF16), before)
    ranks = jnp.where(named[...] > 0.0, ranks, -1.0)
    slot = lax.broadcasted_iota(jnp.int32, (CAP, TOK), 0).astype(F32)
    for i in range(DEVICES * 2):
        picks[i * CAP : i * CAP + CAP, :] = jnp.where(ranks[i : i + 1, :] == slot, 1.0, 0.0).astype(BF16)


def route_weights(ids, r, rw):
    probs = gate_probs(r)
    row = lax.broadcasted_iota(jnp.int32, probs.shape, 0)
    for k in range(TOP):
        rw[k : k + 1, :] = jnp.sum(jnp.where(row == ids[k : k + 1, :], probs, 0.0), axis=0, keepdims=True)


def first_kernel(*refs):
    (x, cos, sin, bias, ids), dense, (cot,), experts_in, dense_out, outs, results, weights, work, refs = cut_up(
        refs, 5, 4, 1, 2, 4, 6, 9, 4, 7
    )
    cots, tokens, shares, wf, wo, picks = outs
    natural, turned, (rw, named, load_sem) = work[:2], work[2:4], work[4:]
    sems1, sems2, sems3, direct_sems, _ = cut_up(refs, 12, 12, 12, 3)
    greet_all()
    p = Place()
    r = Results()
    for name, ref in zip(ATT_NAMES, results):
        setattr(r, name, ref)
    g1 = Gather(p, FIRST_PARTS, dense, dense_out, sems1)
    g2 = Gather(p, ROW_HALVES, [cot], [cots], sems2)
    g3 = Gather(p, TOKEN_PARTS, [r.n2, rw], [tokens, shares], sems3)
    direct = Direct(weights_out, tuple(turned) + (wf, wo), direct_sems)
    g1.step()
    loads = [pltpu.make_async_copy(a, b, load_sem.at[i]) for i, (a, b) in enumerate(zip(experts_in, natural))]
    for l in loads:
        l.start()
    for l, a, b in zip(loads, natural, turned):
        l.wait()

        def turn(i, carry):
            c = lanes(i * 128)
            b[:, :, c] = jnp.swapaxes(a[:, :, c].astype(F32), 0, 1).astype(BF16)
            return carry

        lax.fori_loop(0, a.shape[2] // 128, turn, 0)
    direct.own()
    for n in FIRST_BATCHES:
        g1.step()
        direct.start(n)
    g2.step(2)
    direct.start(DEVICES)
    g1.arrived()
    loads = [pltpu.make_async_copy(a, b, load_sem.at[i]) for i, (a, b) in enumerate(zip(dense_out, weights))]
    for l in loads:
        l.start()
    g2.step(2)
    for l in loads:
        l.wait()
    for i, chunk in enumerate(attention_forward(x, cos, sin, bias, *weights[:3], r)):
        chunk()
        if i % 2 == 1:
            g2.step()
    route_weights(ids, r, rw)
    g3.step(2)
    make_picks(weights[3], named, picks)
    g2.arrived()
    g3.arrived()
    for g in (g1, g2, g3):
        g.finish()
    direct.finish()


FIRST_BATCHES = (1, 1, 1, 1, 1, 1, 1, 1, 1, 1)


def first(x, cos, sin, bias, ids, dense, cot, gu, dp):
    wide = lambda a: like(DEVICES * a.shape[0], a.shape[1], dtype=a.dtype)
    dense_full = [wide(a) for a in dense]
    return pl.pallas_call(
        first_kernel,
        in_specs=[VMEM] * 5 + [HBM] * 7,
        out_specs=[HBM] * 9 + [VMEM] * 10,
        out_shape=dense_full + [wide(cot), wide(cot), like(DEVICES * TOP, TOK, dtype=F32), like(D, 2 * F), like(D, OWN_WIDTH), like(DEVICES * 64, TOK)] + [like(*s, dtype=t) for s, t in ATT_SHAPES],
        scratch_shapes=[pltpu.VMEM(a.shape, a.dtype) for a in dense_full]
        + [pltpu.VMEM(a.shape, a.dtype) for a in (gu, dp)]
        + [pltpu.VMEM((a.shape[1], a.shape[0], a.shape[2]), a.dtype) for a in (gu, dp)]
        + [pltpu.VMEM((TOP, TOK), F32), pltpu.VMEM((DEVICES * 2, TOK), F32), DMA((4,))]
        + Gather.scratch(4, FIRST_PARTS)
        + Gather.scratch(1, ROW_HALVES)
        + Gather.scratch(2, TOKEN_PARTS)
        + Direct.scratch(5),
        compiler_params=pltpu.CompilerParams(collective_id=0, has_side_effects=True, vmem_limit_bytes=60 * 2**20),
    )(x, cos, sin, bias, ids, *dense, cot, gu, dp)


def middle_kernel(*refs):
    (picks, ids, shares), (tokens, cots, wf_in, wo_in), (gin,), outs, blocks, work, refs = cut_up(refs, 3, 4, 1, 5, 9, 10)
    out_part, dwf, dwo, all_gates, grad_down = outs
    t, c, out_block, gin_block, wf, wo, gates, whole, own = blocks
    (weight_sem, load_sem, out_sem, grad_sem), spaces, sems, direct_sems, _ = cut_up(refs, 4, 5, 9, 3)
    greet_all()
    p = Place()
    s = Scatter(p, ROW_HALVES, [gin_block], [gin], spaces, sems, by_plane=True)
    direct = Direct(down_back, (dwo, gates, grad_down, all_gates), direct_sems)
    e = Experts(work, wf, wo, picks, ids, shares, gates)
    R = SRC * TOK

    def plane_rows(q):
        return pl.ds(pl.multiple_of(p.zq[q] * R, R), R)

    def load(q):
        made = [pltpu.make_async_copy(src.at[plane_rows(q)], dst, load_sem.at[i]) for i, (src, dst) in enumerate(((tokens, t), (cots, c)))]
        for l in made:
            l.start()
        return made

    order = (3, 2, 1, 0)
    loads = load(order[0])
    weights = [pltpu.make_async_copy(a, b, weight_sem.at[i]) for i, (a, b) in enumerate(((wf_in, wf), (wo_in, wo)))]
    for l in weights:
        l.start()
    reads, store = [], None
    for step, q in enumerate(order):
        for l in loads:
            l.wait()
        e.load(step, p.zq[q], t, c)
        if step < 3:
            loads = load(order[step + 1])
        if step == 0:
            for l in weights:
                l.wait()
        for wait in reads:
            wait()
        s.step((0, 1, 1, 2)[step])
        e.run(step)
        s.step((0, 0, 1, 1)[step])
        if store is not None:
            store.wait()
        e.give(p.zq[q], out_block, gin_block)
        reads = s.begin((q,))
        store = pltpu.make_async_copy(out_block, out_part.at[plane_rows(q)], out_sem)
        store.start()
    stores = []
    for n in range(2 * (D // 256)):
        a, j, b = n // (D // 256), n % (D // 256), n % 2
        block, out, make = ((own, dwo, e.own_grads), (whole, dwf, e.whole_grads))[a]
        if j >= 2:
            stores[n - 2].wait()
        make(j, block.at[b])
        l = pltpu.make_async_copy(block.at[b], out.at[pl.ds(j * 256, 256)], grad_sem.at[b, a])
        l.start()
        stores.append(l)
        if j == D // 256 - 1:
            for l in stores[-2:]:
                l.wait()
            if a == 0:
                direct.own()
                direct.start(DEVICES)
        if n == 1:
            for wait in reads:
                wait()
        if n in (1, 6, 8, 10, 11):
            s.step()
    s.step(12)
    store.wait()
    s.finish()
    direct.finish()


def middle(picks, ids, shares, tokens, cots, wf, wo):
    R = SRC * TOK
    spaces, sems = Scatter.scratch([tokens], ROW_HALVES)
    return pl.pallas_call(
        middle_kernel,
        in_specs=[VMEM] * 3 + [HBM] * 4,
        out_specs=[VMEM] + [HBM] * 5,
        out_shape=[like(TOK, D, dtype=F32), like(DEVICES * TOK, D), like(D, 2 * F), like(D, OWN_WIDTH), like(DEVICES, 8, TOK, dtype=F32), like(E, D // DEVICES, F)],
        scratch_shapes=[pltpu.VMEM((R, D), BF16)] * 4
        + [
            pltpu.VMEM((D, 2 * F), BF16), pltpu.VMEM((D, OWN_WIDTH), BF16), pltpu.VMEM((DEVICES, 8, TOK), F32),
            pltpu.VMEM((2, 256, 2 * F), BF16), pltpu.VMEM((2, 256, OWN_WIDTH), BF16),
        ]
        + Experts.scratch()
        + [DMA((2,)), DMA((2,)), DMA, DMA((2, 2))]
        + spaces + sems + Direct.scratch(3),
        compiler_params=pltpu.CompilerParams(collective_id=1, has_side_effects=True, vmem_limit_bytes=63 * 2**20),
    )(picks, ids, shares, tokens, cots, wf, wo)


WORK = (
    ("gl", (TOK, TOK), F32),
    ("gm", (TOK, D), F32),
    ("gain2", (TOK, D), F32),
    ("branch", (TOK, D), BF16),
    ("ga", (TOK, D), BF16),
    ("gjf", (TOK, Q_WIDTH + 2 * K_WIDTH), F32),
    ("gj", (TOK, Q_WIDTH + 2 * K_WIDTH), BF16),
    ("gn", (TOK, D), F32),
    ("gates", (64, TOK), F32),
)


def last_kernel(*refs):
    (x, cot, gin, gates, cos, sin), results, (qkv_full, out_full, out_part, dwf, dwo), outs, work, weights, (small_src, load_sem), refs = cut_up(
        refs, 6, 9, 5, 6, len(WORK), 2, 2
    )
    input_grad, layer_output, qkv_grad, out_grad, small_grad, grad_gu = outs
    spaces1, sems1, spaces2, sems2, direct_sems, _ = cut_up(refs, 5, 9, 12, 9, 3)
    greet_all()
    p = Place()
    r = Results()
    for name, ref in zip(ATT_NAMES + tuple(w[0] for w in WORK), tuple(results) + tuple(work)):
        setattr(r, name, ref)
    r.input_grad = input_grad
    r.combined = r.gn
    qkv_ref, out_ref = weights
    s1 = Scatter(p, ROW_HALVES, [out_part], [r.combined], spaces1, sems1)
    s2 = Scatter(p, DENSE_PARTS, [qkv_ref, out_ref, small_src], [qkv_grad, out_grad, small_grad], spaces2, sems2, in_place=True)
    direct = Direct(gate_up_back, (dwf, dwo, grad_gu), direct_sems)
    s1.begin_all()
    loads = [pltpu.make_async_copy(a, b, load_sem.at[i]) for i, (a, b) in enumerate(((out_full, out_ref), (qkv_full, qkv_ref)))]
    for l in loads:
        l.start()
    direct.own()
    direct.start(12)

    def put_qkv(t, value):
        qkv_ref[t * 256 : t * 256 + 256, :] = value

    def put_out(t, value):
        out_ref[t * 256 : t * 256 + 256, :] = value

    def put_small(value):
        small_src[...] = value

    begin, heads, end = attention_backward(x, cot, gin, gates, cos, sin, qkv_ref, out_ref, r, put_qkv, put_out, put_small)
    for l in loads:
        l.wait()
    for i, chunk in enumerate(begin + heads + end):
        chunk()
        if i % 3 == 2:
            s1.step()
            direct.start(2)
    s2.begin_all()
    s1.step(12)
    s2.step(3)
    direct.start(DEVICES)
    layer_output[...] = (r.middle[...] + r.combined[...]).astype(BF16)
    s2.step(12)
    direct.start(DEVICES)
    s1.finish()
    s2.finish()
    direct.finish()


def last(x, cot, gin, gates, cos, sin, results, qkv_full, out_full, out_part, dwf, dwo):
    small = like(D, TOK)
    spaces1, sems1 = Scatter.scratch([out_part], ROW_HALVES)
    spaces2, sems2 = Scatter.scratch([qkv_full, out_full, small], DENSE_PARTS, in_place=True)
    own = D // DEVICES
    return pl.pallas_call(
        last_kernel,
        in_specs=[VMEM] * 15 + [HBM] * 5,
        out_specs=[VMEM] * 5 + [HBM],
        out_shape=[
            like(TOK, D), like(TOK, D), like(own, qkv_full.shape[1], dtype=F32), like(own, D, dtype=F32),
            like(own, TOK, dtype=F32), like(E, own, 2 * F),
        ],
        scratch_shapes=[pltpu.VMEM(s, t) for _, s, t in WORK]
        + [pltpu.VMEM(qkv_full.shape, BF16), pltpu.VMEM(out_full.shape, BF16), pltpu.VMEM(small.shape, BF16), DMA((2,))]
        + spaces1 + sems1 + spaces2 + sems2
        + Direct.scratch(3),
        compiler_params=pltpu.CompilerParams(collective_id=2, has_side_effects=True, vmem_limit_bytes=63 * 2**20),
    )(x, cot, gin, gates, cos, sin, *results, qkv_full, out_full, out_part, dwf, dwo)


def finish_kernel(gu_ref, down_ref, small_ref, *refs):
    whole, (gu_out, down_out, router_out, gain1_out, gain2_out), copies = refs[:4], refs[4:9], refs[9:]
    i = pl.program_id(0)

    @pl.when(i == 0)
    def _():
        for a, b in zip(whole, copies):
            b[...] = a[...]
        small = small_ref[...]
        rows = small.shape[0]
        turned = jnp.concatenate([small, jnp.zeros((TOK - rows, TOK), F32)], axis=0).T
        router_out[...] = turned[:E, :rows]
        gain1_out[...] = turned[E : E + 1, :rows]
        gain2_out[...] = turned[E + 1 : E + 2, :rows]

    @pl.when(i < 4)
    def _():
        gu_out[...] = jnp.swapaxes(gu_ref[...].astype(F32), 0, 1)

    @pl.when(i >= 4)
    def _():
        down_out[...] = jnp.swapaxes(down_ref[...].astype(F32), 0, 1)


def finish(gu, down, small, arrays):
    e, rows, _ = gu.shape
    early = lambda i: (0, 0, jnp.minimum(i, 3))
    late = lambda i: (0, 0, jnp.maximum(i - 4, 0))
    once = lambda a: pl.BlockSpec(a.shape, lambda i: (0, 0), pipeline_mode=pl.Buffered(1))
    outs = [like(E, rows, dtype=F32), like(1, rows, dtype=F32), like(1, rows, dtype=F32)] + [like(*a.shape, dtype=a.dtype) for a in arrays]
    return pl.pallas_call(
        finish_kernel,
        grid=(6,),
        in_specs=[pl.BlockSpec((e, rows, 256), early), pl.BlockSpec((e, rows, 256), late), once(small)] + [once(a) for a in arrays],
        out_specs=[pl.BlockSpec((rows, e, 256), early), pl.BlockSpec((rows, e, 256), late)] + [once(o) for o in outs],
        out_shape=[like(rows, e, gu.shape[2], dtype=F32), like(rows, e, down.shape[2], dtype=F32)] + outs,
        compiler_params=pltpu.CompilerParams(vmem_limit_bytes=63 * 2**20),
    )(gu, down, small, *arrays)


def fast(
    layer_input, cotangent, sequence_ids, expert_ids, attention_gain, qkv_weight, output_weight, moe_gain, router, gate_up, down_proj
):
    own_rows, T = gate_up.shape[0], layer_input.shape[0]
    small = jnp.concatenate(
        [router, attention_gain[:, None], moe_gain[:, None], jnp.zeros((own_rows, 86), BF16)], axis=1
    )
    cosine, sine = rope_tables(positions(sequence_ids), HEAD_WIDTH)
    cos = jnp.concatenate([cosine] * 4, axis=1)
    sin = jnp.concatenate([-sine, sine] * 2, axis=1)
    place_in = jnp.arange(T, dtype=jnp.int32)
    allowed = (sequence_ids[:, None] == sequence_ids[None, :]) & (place_in[None, :] <= place_in[:, None])
    bias = jnp.where(allowed, 0.0, -jnp.inf).astype(F32)

    ids_t = expert_ids.T
    qkv_full, out_full, small_full, ids_all, cots, tokens, shares, wf, wo, picks, *results = first(
        layer_input, cos, sin, bias, ids_t, [qkv_weight, output_weight, small, ids_t], cotangent,
        gate_up, down_proj,
    )

    gin, out_part, dwf, dwo, gates, grad_down = middle(picks, ids_all, shares, tokens, cots, wf, wo)
    input_grad, layer_output, qkv_grad, out_grad, small_grad, grad_gu = last(
        layer_input, cotangent, gin, gates, cos, sin, results, qkv_full, out_full, out_part, dwf, dwo
    )
    gate_up_grad, down_grad, router_grad, gain_one, gain_two, layer_output, input_grad, qkv_grad, out_grad = finish(
        grad_gu, grad_down, small_grad, (layer_output, input_grad, qkv_grad, out_grad)
    )
    return (
        layer_output,
        input_grad,
        gain_one.reshape(own_rows),
        qkv_grad,
        out_grad,
        gain_two.reshape(own_rows),
        router_grad.T,
        gate_up_grad,
        down_grad,
    )


def solution(mesh):
    rows, flat, cube = P("fsdp", None), P("fsdp"), P("fsdp", None, None)
    return jax.shard_map(
        fast if mesh.shape["fsdp"] == 32 else on_device,
        mesh=mesh,
        in_specs=(rows, rows, flat, rows, flat, rows, rows, flat, rows, cube, cube),
        out_specs=(rows, rows, flat, rows, rows, flat, rows, cube, cube),
        check_vma=False,
    )
```

```python
import functools
import math
import jax
import jax.numpy as jnp
import numpy as np
from jax import lax
from jax.experimental import pallas as pl
from jax.experimental.pallas import tpu as pltpu
from jax.sharding import PartitionSpec as P

MODEL_WIDTH = 1536
QUERY_HEADS = 24
KEY_VALUE_HEADS = 8
HEAD_WIDTH = 64
E = 40
F = 512
TOP = 8
CAP = 32


EPSILON = 1e-06
ATTN_SCALE = 0.015625
RESIDUAL_SCALE = 0.22
ROPE_BASE = 10000.0
PRECISE_ARITHMETIC = lax.Precision.HIGHEST


def positions(sequence_ids):
    sequence_length = sequence_ids.shape[0]
    places = jnp.arange(sequence_length, dtype=jnp.int32)
    same = (sequence_ids[:, None] == sequence_ids[None, :]) & (places[None, :] < places[:, None])
    return jnp.sum(same.astype(jnp.int32), axis=1, dtype=jnp.int32)


def rope_tables(places, head_size):
    half_size = head_size // 2
    exponents = jnp.arange(half_size, dtype=jnp.float32) * (2.0 / head_size)
    inverse = jnp.exp(exponents * -math.log(ROPE_BASE))
    angles = places.astype(jnp.float32)[:, None] * inverse[None, :]
    return (jnp.cos(angles), jnp.sin(angles))


def apply_rotary(tensor, cosine_lookup, sine_lookup):
    half_size = tensor.shape[-1] // 2
    first_half = tensor[..., :half_size]
    second_half = tensor[..., half_size:]
    cosine_rows = cosine_lookup[:, None, :]
    sine_rows = sine_lookup[:, None, :]
    return jnp.concatenate(
        [
            first_half * cosine_rows - second_half * sine_rows,
            second_half * cosine_rows + first_half * sine_rows,
        ],
        axis=-1,
    )


def rotate_back(tensor, cosine_lookup, sine_lookup):
    half_size = tensor.shape[-1] // 2
    first_half = tensor[..., :half_size]
    second_half = tensor[..., half_size:]
    cosine_rows = cosine_lookup[:, None, :]
    sine_rows = sine_lookup[:, None, :]
    return jnp.concatenate(
        [
            first_half * cosine_rows + second_half * sine_rows,
            second_half * cosine_rows - first_half * sine_rows,
        ],
        axis=-1,
    )


def norm_scale(hidden_state):
    return lax.rsqrt(jnp.mean(hidden_state * hidden_state, axis=-1, keepdims=True) + EPSILON)


def norm_back(hidden_state, gain_vector, scale_rows, upstream):
    weighted = upstream * gain_vector.astype(jnp.float32)
    inner_mean = jnp.mean(weighted * hidden_state, axis=-1, keepdims=True)
    grad_hidden = scale_rows * weighted - hidden_state * scale_rows**3 * inner_mean
    grad_gain = jnp.sum(upstream * hidden_state * scale_rows, axis=0)
    return (grad_hidden, grad_gain)


def expert_slots(expert_ids, experts, capacity):
    rows = expert_ids.shape[0]
    picked = expert_ids[:, :, None] == jnp.arange(experts, dtype=jnp.int32)[None, None, :]
    named = jnp.any(picked, axis=1).astype(jnp.bfloat16)
    places = jnp.arange(rows, dtype=jnp.int32)
    before = (places[None, :] < places[:, None]).astype(jnp.bfloat16)
    ranks = jnp.dot(before, named, preferred_element_type=jnp.float32)
    ranks = jnp.sum(jnp.where(picked, ranks[:, None, :], 0.0), axis=-1).astype(jnp.int32)
    return (expert_ids * capacity + ranks).reshape(-1)


def owner_tables(devices):
    width_owned = E * F // devices
    span_count = (F + width_owned - 2) // F + 1
    first_expert = np.arange(devices) * width_owned // F
    send_table = np.minimum(first_expert[:, None] + np.arange(span_count)[None, :], E).reshape(-1)
    combine_table = (send_table[None, :] == np.arange(E)[:, None]).astype(np.float32)
    return (width_owned, span_count, send_table, combine_table)


def dispatch_rows(buffer_rows, send_table, devices, span_count):
    padded = jnp.concatenate(
        [buffer_rows, jnp.zeros((1, CAP, MODEL_WIDTH), buffer_rows.dtype)], axis=0
    )
    chosen = jnp.asarray(send_table[:, None] == np.arange(E + 1)[None, :], dtype=buffer_rows.dtype)
    picked_rows = jnp.einsum(
        "se,ecd->scd", chosen, padded, preferred_element_type=jnp.float32
    ).astype(buffer_rows.dtype)
    return picked_rows.reshape(devices, span_count, CAP, MODEL_WIDTH)


def merge_entries(returned, combine_table):
    flat_rows = returned.reshape(returned.shape[0] * returned.shape[1], CAP * MODEL_WIDTH)
    summed = jnp.dot(
        jnp.asarray(combine_table),
        flat_rows,
        precision=PRECISE_ARITHMETIC,
        preferred_element_type=jnp.float32,
    )
    return summed.reshape(E, CAP, MODEL_WIDTH)


def on_device(
    layer_input,
    cotangent,
    sequence_ids,
    expert_ids,
    attention_gain,
    qkv_weight,
    output_weight,
    moe_gain,
    router,
    gate_up,
    down_proj,
):
    sequence_length = layer_input.shape[0]
    shard_rows = gate_up.shape[0]
    query_group_count = QUERY_HEADS // KEY_VALUE_HEADS
    query_feature_width = QUERY_HEADS * HEAD_WIDTH
    key_feature_width = KEY_VALUE_HEADS * HEAD_WIDTH
    rows_per_block = min(512, sequence_length)
    devices = lax.axis_size("fsdp")
    dense_set = (
        lax.all_gather(attention_gain, "fsdp", axis=0, tiled=True),
        lax.all_gather(qkv_weight, "fsdp", axis=0, tiled=True),
        lax.all_gather(output_weight, "fsdp", axis=0, tiled=True),
        lax.all_gather(moe_gain, "fsdp", axis=0, tiled=True),
        lax.all_gather(router, "fsdp", axis=0, tiled=True),
    )
    gain_one, qkv_full, out_full, gain_two, router_full = dense_set
    width_owned, span_count, send_table, combine_table = owner_tables(devices)
    gate_cols = jnp.transpose(gate_up.reshape(shard_rows, E, 2, F), (0, 2, 1, 3)).reshape(
        shard_rows, 2, E * F
    )
    down_cols = down_proj.reshape(shard_rows, 1, E * F)
    owned_weights = lax.all_to_all(
        jnp.concatenate([gate_cols, down_cols], axis=1),
        "fsdp",
        split_axis=2,
        concat_axis=0,
        tiled=True,
    )
    owned_gate_up = owned_weights[:, :2, :]
    owned_down = owned_weights[:, 2, :]
    owner_index = lax.axis_index("fsdp")
    owned_start = owner_index * width_owned
    owned_columns = owned_start + jnp.arange(width_owned, dtype=jnp.int32)
    slot_of = owned_columns // F - owned_start // F
    column_mask = (slot_of[None, :] == jnp.arange(span_count, dtype=jnp.int32)[:, None]).astype(
        jnp.float32
    )
    inputs = layer_input.astype(jnp.float32)
    scale_one = norm_scale(inputs)
    normed_one = (inputs * scale_one * gain_one.astype(jnp.float32)).astype(jnp.bfloat16)
    joined_projection = jnp.dot(normed_one, qkv_full, preferred_element_type=jnp.float32)
    places = positions(sequence_ids)
    cosine_lookup, sine_lookup = rope_tables(places, HEAD_WIDTH)
    query_rows = apply_rotary(
        joined_projection[:, :query_feature_width].reshape(
            sequence_length, QUERY_HEADS, HEAD_WIDTH
        ),
        cosine_lookup,
        sine_lookup,
    ).astype(jnp.bfloat16)
    query_rows = query_rows.reshape(sequence_length, KEY_VALUE_HEADS, query_group_count, HEAD_WIDTH)
    rotated_keys = apply_rotary(
        joined_projection[:, query_feature_width : query_feature_width + key_feature_width].reshape(
            sequence_length, KEY_VALUE_HEADS, HEAD_WIDTH
        ),
        cosine_lookup,
        sine_lookup,
    ).astype(jnp.bfloat16)
    value_inputs = (
        joined_projection[:, query_feature_width + key_feature_width :]
        .reshape(sequence_length, KEY_VALUE_HEADS, HEAD_WIDTH)
        .astype(jnp.bfloat16)
    )
    token_index = jnp.arange(sequence_length, dtype=jnp.int32)

    def block_scores(offset):
        scores = (
            jnp.einsum(
                "qkgd,tkd->kgqt", query_rows, rotated_keys, preferred_element_type=jnp.float32
            )
            * ATTN_SCALE
        )
        allowed = (
            sequence_ids[offset : offset + rows_per_block, None] == sequence_ids[None, :]
        ) & (token_index[None, :] <= token_index[offset : offset + rows_per_block, None])
        return jnp.where(allowed, scores, -jnp.inf)

    offset = 0
    scores = block_scores(offset)
    row_peak = jnp.max(scores, axis=-1, keepdims=True)
    log_total = row_peak + jnp.log(jnp.sum(jnp.exp(scores - row_peak), axis=-1, keepdims=True))
    probs_half = jnp.exp(scores - log_total).astype(jnp.bfloat16)
    mixed_heads = jnp.einsum(
        "kgqt,tkd->qkgd", probs_half, value_inputs, preferred_element_type=jnp.float32
    )
    attention_output_list = mixed_heads.reshape(rows_per_block, query_feature_width).astype(
        jnp.bfloat16
    )
    total_list = [log_total]
    branch = jnp.dot(attention_output_list, out_full, preferred_element_type=jnp.float32)
    middle = inputs + RESIDUAL_SCALE * branch
    scale_two = norm_scale(middle)
    normed_two = (middle * scale_two * gain_two.astype(jnp.float32)).astype(jnp.bfloat16)
    logits = jnp.dot(normed_two, router_full, preferred_element_type=jnp.float32)
    gate_probs = jax.nn.softmax(logits, axis=-1)
    picked = (expert_ids[:, :, None] == jnp.arange(E, dtype=jnp.int32)[None, None, :]).astype(
        jnp.float32
    )
    route_weight = jnp.einsum("tke,te->tk", picked, gate_probs, precision=PRECISE_ARITHMETIC)
    slot_rows = expert_slots(expert_ids, E, CAP)
    received_storage = (
        jnp.zeros((E * CAP, MODEL_WIDTH), jnp.bfloat16)
        .at[slot_rows]
        .set(jnp.repeat(normed_two, TOP, axis=0))
        .reshape(E, CAP, MODEL_WIDTH)
    )
    send_in = dispatch_rows(received_storage, send_table, devices, span_count)
    pre_cols = jnp.einsum(
        "nrkd,dgw->nrkgw",
        lax.all_to_all(send_in, "fsdp", split_axis=0, concat_axis=0, tiled=True),
        owned_gate_up,
        preferred_element_type=jnp.float32,
    )
    pre_cols = pre_cols * column_mask[None, :, None, None, :]
    gate_cols_pre = pre_cols[..., 0, :]
    up_cols_pre = pre_cols[..., 1, :]
    acted = (gate_cols_pre * jax.nn.sigmoid(gate_cols_pre) * up_cols_pre).astype(jnp.bfloat16)
    partial_out = jnp.einsum("nrkw,dw->nrkd", acted, owned_down, preferred_element_type=jnp.float32)
    returned_out = lax.all_to_all(partial_out, "fsdp", split_axis=0, concat_axis=0, tiled=True)
    buffer_out = merge_entries(returned_out, combine_table)
    routed_out = buffer_out.reshape(E * CAP, MODEL_WIDTH)[slot_rows].reshape(
        sequence_length, TOP, MODEL_WIDTH
    )
    combined = jnp.einsum("tk,tkd->td", route_weight, routed_out, precision=PRECISE_ARITHMETIC)
    layer_output = (middle + RESIDUAL_SCALE * combined).astype(jnp.bfloat16)
    upstream = cotangent.astype(jnp.float32)
    grad_mix = RESIDUAL_SCALE * upstream
    grad_weight = jnp.einsum("td,tkd->tk", grad_mix, routed_out, precision=PRECISE_ARITHMETIC)
    grad_rows = (
        (route_weight[:, :, None] * grad_mix[:, None, :])
        .astype(jnp.bfloat16)
        .reshape(sequence_length * TOP, MODEL_WIDTH)
    )
    buffer_grad = (
        jnp.zeros((E * CAP, MODEL_WIDTH), jnp.bfloat16)
        .at[slot_rows]
        .set(grad_rows)
        .reshape(E, CAP, MODEL_WIDTH)
    )
    gain_one_back, qkv_back, out_back, gain_two_back, router_back = dense_set
    send_grad = dispatch_rows(buffer_grad, send_table, devices, span_count)
    rows_in = lax.all_to_all(send_in, "fsdp", split_axis=0, concat_axis=0, tiled=True)
    rows_grad = lax.all_to_all(send_grad, "fsdp", split_axis=0, concat_axis=0, tiled=True)
    pre_cols = jnp.einsum(
        "nrkd,dgw->nrkgw", rows_in, owned_gate_up, preferred_element_type=jnp.float32
    )
    pre_cols = pre_cols * column_mask[None, :, None, None, :]
    gate_cols_pre = pre_cols[..., 0, :]
    up_cols_pre = pre_cols[..., 1, :]
    sigmoid_cols = jax.nn.sigmoid(gate_cols_pre)
    silu_cols = gate_cols_pre * sigmoid_cols
    acted = (silu_cols * up_cols_pre).astype(jnp.bfloat16)
    grad_act_cols = jnp.einsum(
        "nrkd,dw->nrkw", rows_grad, owned_down, preferred_element_type=jnp.float32
    )
    grad_gate_cols = (
        grad_act_cols * up_cols_pre * sigmoid_cols * (1.0 + gate_cols_pre * (1.0 - sigmoid_cols))
    )
    grad_up_cols = grad_act_cols * silu_cols
    grad_pair = jnp.stack([grad_gate_cols, grad_up_cols], axis=3).astype(jnp.bfloat16)
    partial_back = jnp.einsum(
        "nrkgw,dgw->nrkd", grad_pair, owned_gate_up, preferred_element_type=jnp.float32
    )
    returned_back = lax.all_to_all(partial_back, "fsdp", split_axis=0, concat_axis=0, tiled=True)
    results = (returned_back, rows_in, rows_grad, grad_pair, acted)
    returned_back, rows_in_all, rows_grad_all, grad_pair_all, acted_all = results
    backward_buffer = merge_entries(returned_back, combine_table)
    owned_gate_up_grad = jnp.einsum(
        "nrkd,nrkgw->dgw", rows_in_all, grad_pair_all, preferred_element_type=jnp.float32
    )
    owned_down_grad = jnp.einsum(
        "nrkd,nrkw->dw", rows_grad_all, acted_all, preferred_element_type=jnp.float32
    )
    owned_grads = jnp.concatenate([owned_gate_up_grad, owned_down_grad[:, None, :]], axis=1)
    relaid = lax.all_to_all(owned_grads, "fsdp", split_axis=0, concat_axis=2, tiled=True)
    gate_up_grad = jnp.transpose(
        relaid[:, :2, :].reshape(shard_rows, 2, E, F), (0, 2, 1, 3)
    ).reshape(shard_rows, E, 2 * F)
    down_grad = relaid[:, 2, :].reshape(shard_rows, E, F)
    grad_normed = jnp.sum(
        backward_buffer.reshape(E * CAP, MODEL_WIDTH)[slot_rows].reshape(
            sequence_length, TOP, MODEL_WIDTH
        ),
        axis=1,
    )
    grad_gates = jnp.einsum("tk,tke->te", grad_weight, picked, precision=PRECISE_ARITHMETIC)
    grad_logits = gate_probs * (
        grad_gates - jnp.sum(gate_probs * grad_gates, axis=-1, keepdims=True)
    )
    grad_normed = grad_normed + jnp.einsum(
        "te,de->td", grad_logits, router_back.astype(jnp.float32), precision=PRECISE_ARITHMETIC
    )
    router_part = jnp.einsum(
        "td,te->de", normed_two.astype(jnp.float32), grad_logits, precision=PRECISE_ARITHMETIC
    )
    grad_middle, gain_two_part = norm_back(middle, gain_two_back, scale_two, grad_normed)
    grad_middle = grad_middle + upstream
    grad_branch = (RESIDUAL_SCALE * grad_middle).astype(jnp.bfloat16)
    out_part = jnp.einsum(
        "tq,td->qd", attention_output_list, grad_branch, preferred_element_type=jnp.float32
    )
    attention_output_gradient = jnp.einsum(
        "td,qd->tq", grad_branch, out_back, preferred_element_type=jnp.float32
    ).astype(jnp.bfloat16)
    value_gradient = jnp.zeros((sequence_length, KEY_VALUE_HEADS, HEAD_WIDTH), jnp.float32)
    key_gradient = jnp.zeros((sequence_length, KEY_VALUE_HEADS, HEAD_WIDTH), jnp.float32)
    query_grads = []
    for block_number, offset in enumerate(range(0, sequence_length, rows_per_block)):
        scores = block_scores(offset)
        attn_probs = jnp.exp(scores - total_list[block_number])
        block_gradient = attention_output_gradient.reshape(
            rows_per_block, KEY_VALUE_HEADS, query_group_count, HEAD_WIDTH
        )
        attention_output_block = attention_output_list.reshape(
            rows_per_block, KEY_VALUE_HEADS, query_group_count, HEAD_WIDTH
        )
        row_delta = jnp.sum(
            block_gradient.astype(jnp.float32) * attention_output_block.astype(jnp.float32), axis=-1
        )
        row_delta = jnp.transpose(row_delta, (1, 2, 0))[..., None]
        value_gradient = jnp.einsum(
            "kgqt,qkgd->tkd",
            attn_probs.astype(jnp.bfloat16),
            block_gradient,
            preferred_element_type=jnp.float32,
        )
        grad_probs = jnp.einsum(
            "qkgd,tkd->kgqt", block_gradient, value_inputs, preferred_element_type=jnp.float32
        )
        grad_scores = (attn_probs * (grad_probs - row_delta) * ATTN_SCALE).astype(jnp.bfloat16)
        query_grads.append(
            jnp.einsum(
                "kgqt,tkd->qkgd", grad_scores, rotated_keys, preferred_element_type=jnp.float32
            )
        )
        key_gradient = jnp.einsum(
            "kgqt,qkgd->tkd", grad_scores, query_rows, preferred_element_type=jnp.float32
        )
    grad_queries = query_grads[0].reshape(sequence_length, QUERY_HEADS, HEAD_WIDTH)
    grad_joined = jnp.concatenate(
        [
            rotate_back(grad_queries, cosine_lookup, sine_lookup).reshape(
                sequence_length, query_feature_width
            ),
            rotate_back(key_gradient, cosine_lookup, sine_lookup).reshape(
                sequence_length, key_feature_width
            ),
            value_gradient.reshape(sequence_length, key_feature_width),
        ],
        axis=-1,
    ).astype(jnp.bfloat16)
    qkv_part = jnp.einsum("td,tm->dm", normed_one, grad_joined, preferred_element_type=jnp.float32)
    grad_normed_one = jnp.einsum(
        "tm,dm->td", grad_joined, qkv_back, preferred_element_type=jnp.float32
    )
    grad_inputs, gain_one_part = norm_back(inputs, gain_one_back, scale_one, grad_normed_one)
    input_grad = (grad_inputs + grad_middle).astype(jnp.bfloat16)
    dense_grads = (
        lax.psum_scatter(gain_one_part, "fsdp", scatter_dimension=0, tiled=True),
        lax.psum_scatter(qkv_part, "fsdp", scatter_dimension=0, tiled=True),
        lax.psum_scatter(out_part, "fsdp", scatter_dimension=0, tiled=True),
        lax.psum_scatter(gain_two_part, "fsdp", scatter_dimension=0, tiled=True),
        lax.psum_scatter(router_part, "fsdp", scatter_dimension=0, tiled=True),
    )
    return (
        layer_output,
        input_grad,
        dense_grads[0],
        dense_grads[1],
        dense_grads[2],
        dense_grads[3],
        dense_grads[4],
        gate_up_grad,
        down_grad,
    )


D = MODEL_WIDTH
SRC = 8
STEPS = 4
M = SRC * CAP
F32, BF16 = jnp.float32, jnp.bfloat16

def nt(a, b):
    return lax.dot_general(a, b, (((1,), (1,)), ((), ())), preferred_element_type=F32)
def nn(a, b):
    return lax.dot_general(a, b, (((1,), (0,)), ((), ())), preferred_element_type=F32)
def tn(a, b):
    return lax.dot_general(a, b, (((0,), (0,)), ((), ())), preferred_element_type=F32)

QUARTER, DOWN_WHOLE, DOWN_QUARTER, OWN_WIDTH = 0, 256, 768, 896

class Experts:
    NAMES = ("x", "c", "rw", "gw", "act", "dgu", "actq", "dguq", "ow", "gi")

    @staticmethod
    def scratch():
        R = STEPS * M
        return [
            pltpu.VMEM((2, R, D), BF16), pltpu.VMEM((2, R, D), BF16), pltpu.VMEM((2, M, 128), F32), pltpu.VMEM((2, M, 128), F32),
            pltpu.VMEM((R, F), BF16), pltpu.VMEM((R, 2 * F), BF16), pltpu.VMEM((R, 128), BF16), pltpu.VMEM((R, 256), BF16),
            pltpu.VMEM((2, M, D), BF16), pltpu.VMEM((2, M, D), BF16),
        ]

    def __init__(self, refs, wf_ref, wo_ref, pick_ref, ids_ref, share_ref, gates_ref):
        for name, ref in zip(self.NAMES, refs):
            setattr(self, name, ref)
        self.wf, self.wo, self.pick, self.ids, self.shares, self.gates = wf_ref, wo_ref, pick_ref, ids_ref, share_ref, gates_ref

    def picks(self, plane, s):
        return self.pick[pl.ds(pl.multiple_of(plane * (SRC * 64) + s * 64, 64), 64), :]

    def load(self, step, plane, t_ref, c_ref):
        def one(s):
            pick = self.picks(plane, s)
            block = pl.ds(pl.multiple_of(s * 128, 128), 128)
            xs = nn(pick, t_ref[block, :]).astype(BF16)
            cs = nn(pick, c_ref[block, :]).astype(BF16)
            wide = pick.astype(F32)
            eight = pl.ds(pl.multiple_of(plane * (SRC * TOP) + s * TOP, TOP), TOP)
            share = []
            for k, own in enumerate(owned_experts()):
                prob = jnp.sum(jnp.where(self.ids[eight, :] == own, self.shares[eight, :], 0.0), axis=0, keepdims=True)
                share.append(jnp.sum(wide[k * CAP:k * CAP + CAP] * prob, axis=1, keepdims=True) * RESIDUAL_SCALE)
            here = pl.ds(pl.multiple_of(s * CAP, CAP), CAP)
            to = pl.ds(pl.multiple_of(step * M + s * CAP, CAP), CAP)
            for k in range(2):
                self.x[k, to, :] = xs[k * CAP:k * CAP + CAP]
                self.c[k, to, :] = cs[k * CAP:k * CAP + CAP]
                self.rw[k, here, :] = jnp.broadcast_to(share[k], (CAP, 128))
        for s in range(SRC):
            one(s)

    def run(self, step):
        at = slice(step * M, step * M + M)
        sets = (
            (self.act, self.dgu, 512, lambda: self.wf[...], DOWN_WHOLE),
            (self.actq, self.dguq, 128, lambda: self.wo[:, QUARTER:QUARTER + 256], DOWN_QUARTER),
        )
        for k, (acts, dgus, w, w_gu, d0) in enumerate(sets):
            pre = nn(self.x[k, at, :], w_gu())
            gate, up = pre[:, :w], pre[:, w:]
            sig = jax.nn.sigmoid(gate)
            silu = gate * sig
            act = silu * up
            share = self.rw[k, :, 0:1]
            scaled = (share * act).astype(BF16)
            acts[at, :] = scaled
            da = nn(self.c[k, at, :], self.wo[:, d0:d0 + w])
            gw = RESIDUAL_SCALE * jnp.sum(act.astype(BF16).astype(F32) * da, axis=1, keepdims=True)
            self.gw[k] = jnp.broadcast_to(gw, (M, 128))
            self.ow[k] = nt(scaled, self.wo[:, d0:d0 + w]).astype(BF16)
            da = share * da
            dgus[at, :w] = (da * up * sig * (1.0 + gate * (1.0 - sig))).astype(BF16)
            dgus[at, w:] = (da * silu).astype(BF16)
            self.gi[k] = nt(dgus[at, :], w_gu()).astype(BF16)

    def give(self, plane, out_ref, gin_ref):
        def one(s):
            r = pl.ds(pl.multiple_of(s * CAP, CAP), CAP)
            pick = self.picks(plane, s)
            to = pl.ds(pl.multiple_of(s * 128, 128), 128)
            out_ref[to, :] = tn(pick, jnp.concatenate([self.ow[0, r, :], self.ow[1, r, :]], axis=0)).astype(BF16)
            gin_ref[to, :] = tn(pick, jnp.concatenate([self.gi[0, r, :], self.gi[1, r, :]], axis=0)).astype(BF16)
            wide = pick.astype(F32)
            rows = [jnp.sum(wide[k * CAP:k * CAP + CAP] * self.gw[k, r, :], axis=0, keepdims=True) for k in range(2)]
            self.gates[plane * SRC + s] = jnp.concatenate(rows + [jnp.zeros((6, 128), F32)], axis=0)
        for s in range(SRC):
            one(s)

    def own_grads(self, j, ref):
        c = slice(j * 256, j * 256 + 256)
        ref[:, QUARTER:QUARTER + 256] = tn(self.x[1, :, c], self.dguq[...]).astype(BF16)
        ref[:, DOWN_WHOLE:DOWN_WHOLE + 512] = tn(self.c[0, :, c], self.act[...]).astype(BF16)
        ref[:, DOWN_QUARTER:DOWN_QUARTER + 128] = tn(self.c[1, :, c], self.actq[...]).astype(BF16)

    def whole_grads(self, j, ref):
        ref[...] = tn(self.x[0, :, j * 256:j * 256 + 256], self.dgu[...]).astype(BF16)


MESH = pl.DeviceIdType.MESH
DEVICES = 32
TURNS = tuple(sorted(range(1, DEVICES), key=lambda k: (k % 8 * 5 % 8, k)))
DMA = pltpu.SemaphoreType.DMA


def dev(z, y, x, c):
    return ((z * 2 + y) * 2 + x) * 2 + c


class Place:
    def __init__(self):
        me = lax.axis_index("fsdp")
        self.me = me
        z, y, x, c = me // 8, lax.rem(me // 4, 2), lax.rem(me // 2, 2), lax.rem(me, 2)
        self.z, self.y, self.x, self.c = z, y, x, c
        self.sib, self.xn, self.yn = dev(z, y, x, 1 - c), dev(z, y, 1 - x, c), dev(z, 1 - y, x, c)
        self.up, self.down = dev(z + 1, y, x, c), dev(z - 1, y, x, c)
        table = ((0, 1, 2, 3), (1, 0, 2, 3), (2, 3, 1, 0), (3, 2, 1, 0))
        self.zq = []
        for q in range(4):
            v = jnp.int32(table[0][q])
            for k in range(1, 4):
                v = jnp.where(z == k, table[k][q], v)
            self.zq.append(v)


def greet_all():
    me = lax.axis_index("fsdp")
    barrier = pltpu.get_barrier_semaphore()
    for k in range(1, DEVICES):
        pl.semaphore_signal(barrier, inc=1, device_id=(lax.rem(me + k, DEVICES),), device_id_type=MESH)
    pl.semaphore_wait(barrier, DEVICES - 1)


def rc(src, dst, ss, rs, to):
    return pltpu.make_async_remote_copy(src_ref=src, dst_ref=dst, send_sem=ss, recv_sem=rs, device_id=(to,), device_id_type=MESH)


class Direct:
    def __init__(self, pieces, refs, sems):
        self.pieces, self.refs, (self.ss, self.rs, self.ls) = pieces, refs, sems
        self.me = lax.axis_index("fsdp")
        self.left = list(TURNS)

    @staticmethod
    def scratch(count):
        return [DMA((DEVICES, count)), DMA((DEVICES, count)), DMA((count,))]

    def own(self):
        self.local = [pltpu.make_async_copy(a, b, self.ls.at[i]) for i, (a, b) in enumerate(self.pieces(self.me, self.me, self.refs))]
        for l in self.local:
            l.start()

    def start(self, number):
        turns, self.left = self.left[:number], self.left[number:]
        for k in turns:
            to = lax.rem(self.me + k, DEVICES)
            for i, (a, b) in enumerate(self.pieces(self.me, to, self.refs)):
                rc(a, b, self.ss.at[k, i], self.rs.at[k, i], to).start()

    def finish(self):
        self.start(DEVICES)
        for k in TURNS:
            src = lax.rem(self.me + DEVICES - k, DEVICES)
            for i, (a, b) in enumerate(self.pieces(src, self.me, self.refs)):
                rc(a, b, self.ss.at[k, i], self.rs.at[k, i], src).wait_recv()
        for k in TURNS:
            to = lax.rem(self.me + k, DEVICES)
            for i, (a, b) in enumerate(self.pieces(self.me, to, self.refs)):
                rc(a, b, self.ss.at[k, i], self.rs.at[k, i], to).wait_send()
        for l in self.local:
            l.wait()


class Gather:
    ORDER = ((1, 0), (1, 1), (2, 0), (1, 2), (2, 1), (3, 0), (1, 3), (2, 2), (3, 1), (2, 3), (3, 2), (3, 3))

    def __init__(self, p, parts, shards, outs, sems):
        self.p, self.parts, self.shards, self.outs, self.sems = p, parts, shards, outs, sems
        self.P, self.sends, self.locals = len(parts), [], []
        self.left = list(self.ORDER)

    @staticmethod
    def scratch(arrays, parts):
        P = len(parts)
        return [DMA((arrays,)), DMA((4, P)), DMA((P,))] + [DMA((4, P))] * 7 + [DMA((4, 4, P))] * 2

    def at(self, i, d):
        a, c0, w, _ = self.parts[i]
        rows = self.shards[a].shape[0]
        return self.outs[a].at[pl.ds(pl.multiple_of(d * rows, rows), rows), pl.ds(c0, w)]

    def spot(self, i, q, k, core):
        p = self.p
        flip_x, flip_y = ((0, 0), (1, 0), (0, 1), (1, 1))[k] if self.parts[i][3] == 0 else ((0, 0), (0, 1), (1, 0), (1, 1))[k]
        return self.at(i, dev(p.zq[q], 1 - p.y if flip_y else p.y, 1 - p.x if flip_x else p.x, core))

    def go(self, copy):
        copy.start()
        self.sends.append(copy)

    def step(self, number=1):
        for f, q in self.left[:number]:
            (self.stage1, self.stage2, self.stage3)[f - 1](q)
        self.left = self.left[number:]

    def stage1(self, q):
        p = self.p
        _, zs, zs2, zr, fs, fr, s1s, s1r, s2s, s2r, cs, cr = self.sems
        for i in range(self.P):
            a, c0, w, mode = self.parts[i]
            first, second = (p.xn, p.yn) if mode == 0 else (p.yn, p.xn)
            here = self.spot(i, q, 0, p.c)
            if q == 0:
                src = self.shards[a].at[:, pl.ds(c0, w)]

                @pl.when(p.z < 3)
                def _():
                    rc(src, here, zs.at[0, i], zr.at[p.z, i], p.up).start()

                @pl.when(p.z > 0)
                def _():
                    rc(src, here, zs2.at[i], zr.at[p.z, i], p.down).start()
            else:
                src, zq = here, p.zq[q]
                rc(here, here, zs.at[q, i], zr.at[zq, i], p.up).wait_recv()

                @pl.when((zq < p.z) & (p.z < 3))
                def _():
                    rc(src, here, zs.at[q, i], zr.at[zq, i], p.up).start()

                @pl.when((zq > p.z) & (p.z > 0))
                def _():
                    rc(src, here, zs.at[q, i], zr.at[zq, i], p.down).start()
            self.go(rc(src, here, fs.at[q, i], fr.at[q, i], first))
            self.go(rc(src, here, s1s.at[q, i], s1r.at[q, i], second))
            self.go(rc(src, here, cs.at[0, q, i], cr.at[0, q, i], p.sib))
        if q == 0:
            for a, (shard, out) in enumerate(zip(self.shards, self.outs)):
                rows = shard.shape[0]
                l = pltpu.make_async_copy(shard, out.at[pl.ds(pl.multiple_of(p.me * rows, rows), rows)], self.sems[0].at[a])
                l.start()
                self.locals.append(l)

    def stage2(self, q):
        p = self.p
        fs, fr, s2s, s2r, cs, cr = self.sems[4:6] + self.sems[8:12]
        for i in range(self.P):
            second = p.yn if self.parts[i][3] == 0 else p.xn
            there = self.spot(i, q, 1, p.c)
            rc(there, there, fs.at[q, i], fr.at[q, i], second).wait_recv()
            self.go(rc(there, there, s2s.at[q, i], s2r.at[q, i], second))
            self.go(rc(there, there, cs.at[1, q, i], cr.at[1, q, i], p.sib))

    def stage3(self, q):
        p = self.p
        cs, cr = self.sems[10:12]
        for k, (ss, rs) in ((2, self.sems[6:8]), (3, self.sems[8:10])):
            for i in range(self.P):
                there = self.spot(i, q, k, p.c)
                rc(there, there, ss.at[q, i], rs.at[q, i], p.sib).wait_recv()
                self.go(rc(there, there, cs.at[k, q, i], cr.at[k, q, i], p.sib))

    def arrived(self):
        self.step(12)
        cs, cr = self.sems[10:12]
        for q in range(4):
            for k in range(4):
                for i in range(self.P):
                    there = self.spot(i, q, k, 1 - self.p.c)
                    rc(there, there, cs.at[k, q, i], cr.at[k, q, i], self.p.sib).wait_recv()
        for l in self.locals:
            l.wait()

    def finish(self):
        p = self.p
        zs, zs2, zr = self.sems[1:4]
        for copy in self.sends:
            copy.wait_send()
        for i in range(self.P):
            here = self.at(i, p.me)

            @pl.when(p.z < 3)
            def _():
                rc(here, here, zs.at[0, i], zr.at[p.z, i], p.up).wait_send()

            @pl.when(p.z > 0)
            def _():
                rc(here, here, zs2.at[i], zr.at[p.z, i], p.down).wait_send()

            for q in range(1, 4):
                zq = p.zq[q]

                @pl.when(((zq < p.z) & (p.z < 3)) | ((zq > p.z) & (p.z > 0)))
                def _():
                    rc(here, here, zs.at[q, i], zr.at[zq, i], p.up).wait_send()


class Scatter:
    ORDER = ((1, 3), (1, 2), (2, 3), (1, 1), (2, 2), (3, 3), (1, 0), (2, 1), (3, 2), (2, 0), (3, 1), (3, 0))
    STEP = 16

    def __init__(self, p, parts, fulls, outs, spaces, sems, in_place=False, by_plane=False):
        self.by_plane, self.reads = by_plane, []
        self.p, self.parts, self.fulls, self.outs, self.sems, self.in_place = p, parts, fulls, outs, sems, in_place
        count = len(fulls)
        if in_place:
            spaces = (None,) * count + tuple(spaces)
        self.held, self.r0, self.r1, self.r2, self.r3 = (spaces[i * count : (i + 1) * count] for i in range(5))
        self.rows = [f.shape[0] // (8 if by_plane else DEVICES) for f in fulls]
        self.P, self.sends = len(parts), []
        self.left = list(self.ORDER)

    def begin_all(self):
        self.reads = self.begin()

    @staticmethod
    def scratch(arrays, parts, in_place=False):
        P = len(parts)
        spaces = []
        for cnt in (16, 8, 4, 5) if in_place else (16, 16, 8, 4, 5):
            spaces += [pltpu.VMEM((cnt, a.shape[0] // DEVICES, a.shape[1]), a.dtype) for a in arrays]
        return spaces, [DMA((4, 4, P))] * 3 + [DMA((4, 2, P))] * 2 + [DMA((4, P))] * 3 + [DMA((5, P))]

    def go(self, copy):
        copy.start()
        self.sends.append(copy)

    def cut(self, i):
        return pl.ds(self.parts[i][1], self.parts[i][2])

    def spot(self, i, k):
        x, y = self.p.x, self.p.y
        if self.parts[i][3] == 0:
            return ((1 - y, 1 - x), (1 - y, x), (y, 1 - x), (y, x))[k]
        return ((1 - y, 1 - x), (y, 1 - x), (1 - y, x), (y, x))[k]

    def slot(self, q, yy, xx):
        return (yy * 2 + xx) * 4 + self.p.zq[q]

    def hold(self, a, q, yy, xx):
        if self.in_place:
            start = dev(self.p.zq[q], yy, xx, self.p.c) * self.rows[a]
            return self.fulls[a].at[pl.ds(pl.multiple_of(start, self.rows[a]), self.rows[a])]
        return self.held[a].at[self.slot(q, yy, xx)]

    def source(self, i, q, k, core):
        a = self.parts[i][0]
        d = dev(0 if self.by_plane else self.p.zq[q], *self.spot(i, k), core)
        return self.fulls[a].at[pl.ds(pl.multiple_of(d * self.rows[a], self.rows[a]), self.rows[a]), self.cut(i)]

    def begin(self, planes=(3, 2, 1, 0)):
        ls, s0, e0 = self.sems[:3]
        made = []
        for q in planes:
            for k in range(4):
                for i in range(self.P):
                    a = self.parts[i][0]
                    s = self.slot(q, *self.spot(i, k))
                    copy = rc(self.source(i, q, k, 1 - self.p.c), self.r0[a].at[s, :, self.cut(i)], s0.at[q, k, i], e0.at[q, k, i], self.p.sib)
                    copy.start()
                    made.append(copy.wait_send)
                    if not self.in_place:
                        l = pltpu.make_async_copy(self.source(i, q, k, self.p.c), self.held[a].at[s, :, self.cut(i)], ls.at[q, k, i])
                        l.start()
                        made.append(l.wait)
        return made

    def step(self, number=1):
        for f, q in self.left[:number]:
            (self.stage1, self.stage2, self.stage3)[f - 1](q)
        self.left = self.left[number:]

    def chunks(self, a, body):
        def one(n, carry):
            body(pl.ds(pl.multiple_of(n * self.STEP, self.STEP), self.STEP))
            return carry

        lax.fori_loop(0, self.rows[a] // self.STEP, one, 0)

    def add(self, i, dst, src, s_src):
        a, c0, w, _ = self.parts[i]

        def body(r):
            v = dst[r, c0 : c0 + w].astype(F32) + src[s_src, r, c0 : c0 + w].astype(F32)
            dst[r, c0 : c0 + w] = v.astype(dst.dtype)

        self.chunks(a, body)

    def stage1(self, q):
        p = self.p
        _, s0, e0, s1, e1 = self.sems[:5]
        for k in range(4):
            for i in range(self.P):
                a = self.parts[i][0]
                first = p.yn if self.parts[i][3] == 0 else p.xn
                s = self.slot(q, *self.spot(i, k))
                sums = self.hold(a, q, *self.spot(i, k))
                here = sums.at[:, self.cut(i)]
                rc(here, self.r0[a].at[s, :, self.cut(i)], s0.at[q, k, i], e0.at[q, k, i], p.sib).wait_recv()
                if self.reads and not self.in_place:
                    self.reads[self.reading(q, k, i) * 2 + 1]()
                self.add(i, sums, self.r0[a], s)
                if k < 2:
                    self.go(rc(here, self.r1[a].at[q * 2 + k, :, self.cut(i)], s1.at[q, k, i], e1.at[q, k, i], first))

    def reading(self, q, k, i):
        return ((3 - q) * 4 + k) * self.P + i

    def stage2(self, q):
        p = self.p
        s1, e1, s2, e2 = self.sems[3:7]
        for k in range(2):
            for i in range(self.P):
                a = self.parts[i][0]
                second = p.xn if self.parts[i][3] == 0 else p.yn
                sums = self.hold(a, q, *self.spot(i, k + 2))
                here = sums.at[:, self.cut(i)]
                rc(here, self.r1[a].at[q * 2 + k, :, self.cut(i)], s1.at[q, k, i], e1.at[q, k, i], p.sib).wait_recv()
                self.add(i, sums, self.r1[a], q * 2 + k)
                if k == 0:
                    self.go(rc(here, self.r2[a].at[q, :, self.cut(i)], s2.at[q, i], e2.at[q, i], second))

    def stage3(self, q):
        p = self.p
        s2, e2, s3, e3 = self.sems[5:9]
        zq, z = p.zq[q], p.z
        for i in range(self.P):
            a, c0, w, _ = self.parts[i]
            r3, out, sums = self.r3[a], self.outs[a], self.hold(a, q, p.y, p.x)
            here = sums.at[:, self.cut(i)]
            rc(here, self.r2[a].at[q, :, self.cut(i)], s2.at[q, i], e2.at[q, i], p.sib).wait_recv()
            self.add(i, sums, self.r2[a], q)
            if q > 0:

                @pl.when((zq > z) & (z > 0) | (zq < z) & (z < 3))
                def _():
                    rc(here, r3.at[zq, :, self.cut(i)], s3.at[q, i], e3.at[zq, i], p.sib).wait_recv()
                    self.add(i, sums, r3, zq)

                @pl.when(zq > z)
                def _():
                    rc(here, r3.at[zq, :, self.cut(i)], s3.at[q, i], e3.at[zq, i], p.up).start()

                @pl.when((zq < z) & (zq == z - 1))
                def _():
                    rc(here, r3.at[4, :, self.cut(i)], s3.at[q, i], e3.at[4, i], p.down).start()

                @pl.when(zq < z - 1)
                def _():
                    rc(here, r3.at[zq, :, self.cut(i)], s3.at[q, i], e3.at[zq, i], p.down).start()
            else:

                def first_sum(r):
                    out[r, c0 : c0 + w] = sums[r, c0 : c0 + w].astype(F32)

                self.chunks(a, first_sum)
                for cond, where in ((z > 0, z), (z < 3, 4)):

                    @pl.when(cond)
                    def _():
                        rc(here, r3.at[where, :, self.cut(i)], s3.at[q, i], e3.at[where, i], p.sib).wait_recv()

                        def more(r):
                            out[r, c0 : c0 + w] += r3[where, r, c0 : c0 + w].astype(F32)

                        self.chunks(a, more)

    def finish(self):
        p = self.p
        s3, e3 = self.sems[7:9]
        for wait in self.reads[:: 1 if self.in_place else 2]:
            wait()
        for copy in self.sends:
            copy.wait_send()
        for q in range(1, 4):
            for i in range(self.P):
                here = self.hold(self.parts[i][0], q, p.y, p.x).at[:, self.cut(i)]
                rc(here, here, s3.at[q, i], e3.at[0, i], p.sib).wait_send()


HBM = pl.BlockSpec(memory_space=pl.ANY)
VMEM = pl.BlockSpec(memory_space=pltpu.VMEM)


def like(*shape, dtype=None):
    return jax.ShapeDtypeStruct(shape, dtype or jnp.bfloat16)


def cut_up(refs, *counts):
    out, i = [], 0
    for c in counts:
        out.append(refs[i : i + c])
        i += c
    return out + [refs[i:]]


GROUP = QUERY_HEADS // KEY_VALUE_HEADS
Q_WIDTH, K_WIDTH = QUERY_HEADS * HEAD_WIDTH, KEY_VALUE_HEADS * HEAD_WIDTH
TOK = 128


def partner(v):
    lane = lax.broadcasted_iota(jnp.int32, v.shape, 1) % HEAD_WIDTH
    return jnp.where(lane < HEAD_WIDTH // 2, pltpu.roll(v, 96, 1), pltpu.roll(v, 32, 1))


def attention_forward(x_ref, cos_ref, sin_ref, bias_ref, qkv_ref, out_ref, small_ref, r):
    def norm_one():
        r.small_t[...] = nt(jnp.eye(TOK, dtype=BF16), small_ref[...])
        x = x_ref[...].astype(F32)
        r.n1[...] = (x * norm_scale(x) * r.small_t[E : E + 1, :]).astype(BF16)

    def project(t):
        def run():
            tile = nn(r.n1[...], qkv_ref[:, t * 512 : t * 512 + 512])
            for b in range(4):
                col = t * 512 + b * 128
                v = tile[:, b * 128 : b * 128 + 128]
                if col < Q_WIDTH + K_WIDTH:
                    v = v * cos_ref[...] + partner(v) * sin_ref[...]
                v = v.astype(BF16)
                for half in range(2):
                    piece = v[:, half * 64 : half * 64 + 64]
                    head = col // 64 + half
                    if col < Q_WIDTH:
                        r.q[head // GROUP, head % GROUP * TOK : head % GROUP * TOK + TOK, :] = piece
                    elif col < Q_WIDTH + K_WIDTH:
                        r.k[head - QUERY_HEADS] = piece
                    else:
                        r.v[head - QUERY_HEADS - KEY_VALUE_HEADS] = piece

        return run

    def attend(j):
        def run():
            s = nt(r.q[j], r.k[j]) * ATTN_SCALE
            s = s + jnp.concatenate([bias_ref[...]] * GROUP, axis=0)
            e = jnp.exp(s - jnp.max(s, axis=1, keepdims=True))
            probs = e / jnp.sum(e, axis=1, keepdims=True)
            r.probs[j] = probs
            o = nn(probs.astype(BF16), r.v[j]).astype(BF16)
            for g in range(GROUP):
                h = j * GROUP + g
                r.att[:, h * 64 : h * 64 + 64] = o[g * TOK : g * TOK + TOK]

        return run

    def output(t):
        def run():
            c = slice(t * 512, t * 512 + 512)
            r.middle[:, c] = x_ref[:, c].astype(F32) + RESIDUAL_SCALE * nn(r.att[...], out_ref[:, c])

        return run

    def norm_two():
        m = r.middle[...]
        r.n2[...] = (m * norm_scale(m) * r.small_t[E + 1 : E + 2, :]).astype(BF16)

    return (
        [norm_one]
        + [project(t) for t in range((Q_WIDTH + 2 * K_WIDTH) // 512)]
        + [attend(j) for j in range(KEY_VALUE_HEADS)]
        + [output(t) for t in range(D // 512)]
        + [norm_two]
    )


def split_dot(form, a, b):
    one = b.astype(BF16)
    rest = b - one.astype(F32)
    two = rest.astype(BF16)
    three = (rest - two.astype(F32)).astype(BF16)
    return form(a, one) + form(a, two) + form(a, three)


def norm_back_rows(hidden, gain, upstream):
    scale = norm_scale(hidden)
    weighted = upstream * gain
    inner = jnp.mean(weighted * hidden, axis=-1, keepdims=True)
    return scale * weighted - hidden * scale**3 * inner, upstream * hidden * scale


def gate_probs(r):
    logits = nt(r.small_t[:64, :].astype(BF16), r.n2[...])
    row = lax.broadcasted_iota(jnp.int32, logits.shape, 0)
    logits = jnp.where(row < E, logits, -jnp.inf)
    e = jnp.exp(logits - jnp.max(logits, axis=0, keepdims=True))
    return e / jnp.sum(e, axis=0, keepdims=True)


def attention_backward(x_ref, cot_ref, gin_ref, gates_ref, cos_ref, sin_ref, qkv_ref, out_ref, r, put_qkv, put_out, put_small):
    def router():
        m = r.middle[...]
        probs = gate_probs(r)
        r.gates[...] = jnp.zeros_like(r.gates)
        for g in range(8):
            for j in range(4):
                r.gates[g * 5 + j : g * 5 + j + 1, :] = gates_ref[g * 4 + j, 0:1, :]
            r.gates[g * 5 + 4 : g * 5 + 5, :] = sum(gates_ref[g * 4 + j, 1:2, :] for j in range(4))
        gates = r.gates[...]
        gl = probs * (gates - jnp.sum(probs * gates, axis=0, keepdims=True))
        gl = jnp.concatenate([gl, jnp.zeros((64, TOK), F32)], axis=0).T
        r.gl[...] = gl
        back = nn(gl.astype(BF16), r.small_t[...].astype(BF16))
        low = gl - gl.astype(BF16).astype(F32)
        back = back + nn(low.astype(BF16), r.small_t[...].astype(BF16))
        low = low - low.astype(BF16).astype(F32)
        back = back + nn(low.astype(BF16), r.small_t[...].astype(BF16))
        up = gin_ref[...] + back
        gm, gain_rows = norm_back_rows(m, r.small_t[E + 1 : E + 2, :], up)
        gm = gm + cot_ref[...].astype(F32)
        r.gm[...] = gm
        r.gain2[...] = gain_rows
        r.branch[...] = (RESIDUAL_SCALE * gm).astype(BF16)

    def attended(t):
        def run():
            c = slice(t * 512, t * 512 + 512)
            r.ga[:, c] = nt(r.branch[...], out_ref[c, :]).astype(BF16)

        return run

    def out_part(t):
        def run():
            put_out(t, tn(r.att[:, t * 256 : t * 256 + 256], r.branch[...]).astype(BF16))

        return run

    def head(j):
        def run():
            cols = [slice((j * GROUP + g) * 64, (j * GROUP + g) * 64 + 64) for g in range(GROUP)]
            ga = jnp.concatenate([r.ga[:, c] for c in cols], axis=0)
            at = jnp.concatenate([r.att[:, c] for c in cols], axis=0)
            delta = jnp.sum(ga.astype(F32) * at.astype(F32), axis=1, keepdims=True)
            probs = r.probs[j]
            ds = (probs * (nt(ga, r.v[j]) - delta) * ATTN_SCALE).astype(BF16)
            gq = nn(ds, r.k[j])
            for g, c in enumerate(cols):
                r.gjf[:, c] = gq[g * TOK : g * TOK + TOK]
            r.gjf[:, Q_WIDTH + j * 64 : Q_WIDTH + j * 64 + 64] = tn(ds, r.q[j])
            r.gjf[:, Q_WIDTH + K_WIDTH + j * 64 : Q_WIDTH + K_WIDTH + j * 64 + 64] = tn(probs.astype(BF16), ga)

        return run

    def rotate():
        for col in range(0, Q_WIDTH + 2 * K_WIDTH, 128):
            v = r.gjf[:, col : col + 128]
            if col < Q_WIDTH + K_WIDTH:
                v = v * cos_ref[...] - partner(v) * sin_ref[...]
            r.gj[:, col : col + 128] = v.astype(BF16)

    def qkv_part(t):
        def run():
            put_qkv(t, tn(r.n1[:, t * 256 : t * 256 + 256], r.gj[...]).astype(BF16))

        return run

    def into_normed(t):
        def run():
            c = slice(t * 256, t * 256 + 256)
            r.gn[:, c] = nt(r.gj[...], qkv_ref[c, :])

        return run

    def input_back():
        x = x_ref[...].astype(F32)
        gx, gain_rows = norm_back_rows(x, r.small_t[E : E + 1, :], r.gn[...])
        r.input_grad[...] = (gx + r.gm[...]).astype(BF16)
        lane = lax.broadcasted_iota(jnp.int32, (TOK, TOK), 1)
        small = split_dot(tn, r.n2[...], r.gl[...])
        for rows, at in ((gain_rows, E), (r.gain2[...], E + 1)):
            ones = jnp.where(lane == at, 1.0, 0.0).astype(BF16)
            hi = rows.astype(BF16)
            lo = (rows - hi.astype(F32)).astype(BF16)
            small = small + tn(hi, ones) + tn(lo, ones)
        put_small(small.astype(BF16))

    first = [router] + [attended(t) for t in range(3)] + [out_part(t) for t in range(6)]
    heads = [head(j) for j in range(KEY_VALUE_HEADS)] + [rotate]
    last = [into_normed(t) for t in range(6)] + [input_back] + [qkv_part(t) for t in range(6)]
    return first, heads, last


class Results:
    pass


ATT_NAMES = ("small_t", "n1", "q", "k", "v", "probs", "att", "middle", "n2")
ATT_SHAPES = (
    ((TOK, D), F32),
    ((TOK, D), BF16),
    ((KEY_VALUE_HEADS, GROUP * TOK, HEAD_WIDTH), BF16),
    ((KEY_VALUE_HEADS, TOK, HEAD_WIDTH), BF16),
    ((KEY_VALUE_HEADS, TOK, HEAD_WIDTH), BF16),
    ((KEY_VALUE_HEADS, GROUP * TOK, TOK), F32),
    ((TOK, Q_WIDTH), BF16),
    ((TOK, D), F32),
    ((TOK, D), BF16),
)
ROW_HALVES = ((0, 0, 768, 0), (0, 768, 768, 1))
DENSE_PARTS = ((0, 0, 1280, 0), (0, 1280, 1280, 1), (1, 0, 768, 0), (1, 768, 768, 1), (2, 0, 128, 1))
TOKEN_PARTS = ROW_HALVES + ((1, 0, 128, 1),)
FIRST_PARTS = DENSE_PARTS + ((3, 0, 128, 0),)


def lanes(start):
    return pl.ds(pl.multiple_of(start, 128), 128)


def weights_out(src, dst, refs):
    g_ref, d_ref, wf_ref, wo_ref = refs
    group, own, quarter = dst // 4, lax.rem(dst, 4), lax.rem(dst, 4) * 128
    rows = pl.ds(pl.multiple_of(src * 48, 48), 48)
    fifth = group * 5 + 4
    return (
        (g_ref.at[fifth, :, lanes(quarter)], wo_ref.at[rows, pl.ds(QUARTER, 128)]),
        (g_ref.at[fifth, :, lanes(F + quarter)], wo_ref.at[rows, pl.ds(QUARTER + 128, 128)]),
        (d_ref.at[group * 5 + own], wo_ref.at[rows, pl.ds(DOWN_WHOLE, F)]),
        (d_ref.at[fifth, :, lanes(quarter)], wo_ref.at[rows, pl.ds(DOWN_QUARTER, 128)]),
        (g_ref.at[group * 5 + own], wf_ref.at[rows]),
    )


def down_back(src, dst, refs):
    dwo_ref, gates_ref, d_ref, all_gates_ref = refs
    group, quarter = src // 4, lax.rem(src, 4) * 128
    rows = pl.ds(pl.multiple_of(dst * 48, 48), 48)
    return (
        (gates_ref.at[dst], all_gates_ref.at[src]),
        (dwo_ref.at[rows, pl.ds(DOWN_WHOLE, F)], d_ref.at[group * 5 + lax.rem(src, 4)]),
        (dwo_ref.at[rows, pl.ds(DOWN_QUARTER, 128)], d_ref.at[group * 5 + 4, :, lanes(quarter)]),
    )


def gate_up_back(src, dst, refs):
    dwf_ref, dwo_ref, g_ref = refs
    group, quarter = src // 4, lax.rem(src, 4) * 128
    rows = pl.ds(pl.multiple_of(dst * 48, 48), 48)
    return (
        (dwf_ref.at[rows], g_ref.at[group * 5 + lax.rem(src, 4)]),
        (dwo_ref.at[rows, pl.ds(QUARTER, 128)], g_ref.at[group * 5 + 4, :, lanes(quarter)]),
        (dwo_ref.at[rows, pl.ds(QUARTER + 128, 128)], g_ref.at[group * 5 + 4, :, lanes(F + quarter)]),
    )


def tables(seq, cos, sin, bias):
    rows = jnp.broadcast_to(seq[...], (TOK, TOK))
    same = rows == rows.T
    t = lax.broadcasted_iota(jnp.int32, (TOK, TOK), 0)
    s = lax.broadcasted_iota(jnp.int32, (TOK, TOK), 1)
    places = jnp.sum(jnp.where(same, jnp.where(s < t, 1.0, 0.0), 0.0), axis=1, keepdims=True)
    bias[...] = jnp.where(same, jnp.where(s <= t, 0.0, -jnp.inf), -jnp.inf)
    half = HEAD_WIDTH // 2
    exponents = (s % half).astype(F32) * (2.0 / HEAD_WIDTH)
    angles = places * jnp.exp(exponents * -math.log(ROPE_BASE))
    cos[...] = jnp.cos(angles)
    sine = jnp.sin(angles)
    sin[...] = jnp.where(s % HEAD_WIDTH < half, -sine, sine)


def owned_experts():
    me = lax.axis_index("fsdp")
    return (me // 4) * 5 + lax.rem(me, 4), (me // 4) * 5 + 4


def make_picks(ids, named, picks):
    for s in range(DEVICES):
        block = ids[s * TOP : s * TOP + TOP, :]
        for k, e in enumerate(owned_experts()):
            named[s * 2 + k : s * 2 + k + 1, :] = jnp.max(jnp.where(block == e, 1.0, 0.0), axis=0, keepdims=True)
    row = lax.broadcasted_iota(jnp.int32, (TOK, TOK), 0)
    before = jnp.where(row < lax.broadcasted_iota(jnp.int32, (TOK, TOK), 1), 1.0, 0.0).astype(BF16)
    ranks = nn(named[...].astype(BF16), before)
    ranks = jnp.where(named[...] > 0.0, ranks, -1.0)
    slot = lax.broadcasted_iota(jnp.int32, (CAP, TOK), 0).astype(F32)
    for i in range(DEVICES * 2):
        picks[i * CAP : i * CAP + CAP, :] = jnp.where(ranks[i : i + 1, :] == slot, 1.0, 0.0).astype(BF16)


def route_weights(ids, r, rw):
    probs = gate_probs(r)
    row = lax.broadcasted_iota(jnp.int32, probs.shape, 0)
    for k in range(TOP):
        rw[k : k + 1, :] = jnp.sum(jnp.where(row == ids[k : k + 1, :], probs, 0.0), axis=0, keepdims=True)


def first_kernel(*refs):
    (x, seq, ids), dense, (cot,), experts_in, dense_out, outs, results, weights, work, refs = cut_up(
        refs, 3, 4, 1, 2, 4, 6, 11, 4, 8
    )
    cots, tokens, shares, wf, wo, picks = outs
    natural, turned, (rw, named, bias, load_sem) = work[:2], work[2:4], work[4:]
    cos, sin = results[9:]
    sems1, sems2, sems3, direct_sems, _ = cut_up(refs, 12, 12, 12, 3)
    greet_all()
    p = Place()
    r = Results()
    for name, ref in zip(ATT_NAMES, results):
        setattr(r, name, ref)
    g1 = Gather(p, FIRST_PARTS, dense, dense_out, sems1)
    g2 = Gather(p, ROW_HALVES, [cot], [cots], sems2)
    g3 = Gather(p, TOKEN_PARTS, [r.n2, rw], [tokens, shares], sems3)
    direct = Direct(weights_out, tuple(turned) + (wf, wo), direct_sems)
    g1.step()
    loads = [pltpu.make_async_copy(a, b, load_sem.at[i]) for i, (a, b) in enumerate(zip(experts_in, natural))]
    for l in loads:
        l.start()
    for l, a, b in zip(loads, natural, turned):
        l.wait()

        def turn(i, carry):
            c = lanes(i * 128)
            b[:, :, c] = jnp.swapaxes(a[:, :, c].astype(F32), 0, 1).astype(BF16)
            return carry

        lax.fori_loop(0, a.shape[2] // 128, turn, 0)
    direct.own()
    tables(seq, cos, sin, bias)
    for n in FIRST_BATCHES:
        g1.step()
        direct.start(n)
    g2.step(2)
    direct.start(DEVICES)
    g1.arrived()
    loads = [pltpu.make_async_copy(a, b, load_sem.at[i]) for i, (a, b) in enumerate(zip(dense_out, weights))]
    for l in loads:
        l.start()
    g2.step(2)
    for l in loads:
        l.wait()
    for i, chunk in enumerate(attention_forward(x, cos, sin, bias, *weights[:3], r)):
        chunk()
        if i % 2 == 1:
            g2.step()
    route_weights(ids, r, rw)
    g3.step(2)
    make_picks(weights[3], named, picks)
    g2.arrived()
    g3.arrived()
    for g in (g1, g2, g3):
        g.finish()
    direct.finish()


FIRST_BATCHES = (1, 1, 1, 1, 1, 1, 1, 1, 1, 1)


def first(x, seq, ids, dense, cot, gu, dp):
    wide = lambda a: like(DEVICES * a.shape[0], a.shape[1], dtype=a.dtype)
    dense_full = [wide(a) for a in dense]
    return pl.pallas_call(
        first_kernel,
        in_specs=[VMEM] * 3 + [HBM] * 7,
        out_specs=[HBM] * 9 + [VMEM] * 12,
        out_shape=dense_full + [wide(cot), wide(cot), like(DEVICES * TOP, TOK, dtype=F32), like(D, 2 * F), like(D, OWN_WIDTH), like(DEVICES * 64, TOK)] + [like(*s, dtype=t) for s, t in ATT_SHAPES] + [like(TOK, TOK, dtype=F32)] * 2,
        scratch_shapes=[pltpu.VMEM(a.shape, a.dtype) for a in dense_full]
        + [pltpu.VMEM(a.shape, a.dtype) for a in (gu, dp)]
        + [pltpu.VMEM((a.shape[1], a.shape[0], a.shape[2]), a.dtype) for a in (gu, dp)]
        + [pltpu.VMEM((TOP, TOK), F32), pltpu.VMEM((DEVICES * 2, TOK), F32), pltpu.VMEM((TOK, TOK), F32), DMA((4,))]
        + Gather.scratch(4, FIRST_PARTS)
        + Gather.scratch(1, ROW_HALVES)
        + Gather.scratch(2, TOKEN_PARTS)
        + Direct.scratch(5),
        compiler_params=pltpu.CompilerParams(collective_id=0, has_side_effects=True, vmem_limit_bytes=60 * 2**20),
    )(x, seq, ids, *dense, cot, gu, dp)


def middle_kernel(*refs):
    (picks, ids, shares), (tokens, cots, wf_in, wo_in), (gin,), outs, blocks, work, refs = cut_up(refs, 3, 4, 1, 5, 9, 10)
    out_part, dwf, dwo, all_gates, grad_down = outs
    t, c, out_block, gin_block, wf, wo, gates, whole, own = blocks
    (weight_sem, load_sem, out_sem, grad_sem), spaces, sems, direct_sems, _ = cut_up(refs, 4, 5, 9, 3)
    greet_all()
    p = Place()
    s = Scatter(p, ROW_HALVES, [gin_block], [gin], spaces, sems, by_plane=True)
    direct = Direct(down_back, (dwo, gates, grad_down, all_gates), direct_sems)
    e = Experts(work, wf, wo, picks, ids, shares, gates)
    R = SRC * TOK

    def plane_rows(q):
        return pl.ds(pl.multiple_of(p.zq[q] * R, R), R)

    def load(q):
        made = [pltpu.make_async_copy(src.at[plane_rows(q)], dst, load_sem.at[i]) for i, (src, dst) in enumerate(((tokens, t), (cots, c)))]
        for l in made:
            l.start()
        return made

    order = (3, 2, 1, 0)
    loads = load(order[0])
    weights = [pltpu.make_async_copy(a, b, weight_sem.at[i]) for i, (a, b) in enumerate(((wf_in, wf), (wo_in, wo)))]
    for l in weights:
        l.start()
    reads, store = [], None
    for step, q in enumerate(order):
        for l in loads:
            l.wait()
        e.load(step, p.zq[q], t, c)
        if step < 3:
            loads = load(order[step + 1])
        if step == 0:
            for l in weights:
                l.wait()
        for wait in reads:
            wait()
        s.step((0, 1, 1, 2)[step])
        e.run(step)
        s.step((0, 0, 1, 1)[step])
        if store is not None:
            store.wait()
        e.give(p.zq[q], out_block, gin_block)
        reads = s.begin((q,))
        store = pltpu.make_async_copy(out_block, out_part.at[plane_rows(q)], out_sem)
        store.start()
    stores = []
    for n in range(2 * (D // 256)):
        a, j, b = n // (D // 256), n % (D // 256), n % 2
        block, out, make = ((own, dwo, e.own_grads), (whole, dwf, e.whole_grads))[a]
        if j >= 2:
            stores[n - 2].wait()
        make(j, block.at[b])
        l = pltpu.make_async_copy(block.at[b], out.at[pl.ds(j * 256, 256)], grad_sem.at[b, a])
        l.start()
        stores.append(l)
        if j == D // 256 - 1:
            for l in stores[-2:]:
                l.wait()
            if a == 0:
                direct.own()
                direct.start(DEVICES)
        if n == 1:
            for wait in reads:
                wait()
        if n in (1, 6, 8, 10, 11):
            s.step()
    s.step(12)
    store.wait()
    s.finish()
    direct.finish()


def middle(picks, ids, shares, tokens, cots, wf, wo):
    R = SRC * TOK
    spaces, sems = Scatter.scratch([tokens], ROW_HALVES)
    return pl.pallas_call(
        middle_kernel,
        in_specs=[VMEM] * 3 + [HBM] * 4,
        out_specs=[VMEM] + [HBM] * 5,
        out_shape=[like(TOK, D, dtype=F32), like(DEVICES * TOK, D), like(D, 2 * F), like(D, OWN_WIDTH), like(DEVICES, 8, TOK, dtype=F32), like(E, D // DEVICES, F)],
        scratch_shapes=[pltpu.VMEM((R, D), BF16)] * 4
        + [
            pltpu.VMEM((D, 2 * F), BF16), pltpu.VMEM((D, OWN_WIDTH), BF16), pltpu.VMEM((DEVICES, 8, TOK), F32),
            pltpu.VMEM((2, 256, 2 * F), BF16), pltpu.VMEM((2, 256, OWN_WIDTH), BF16),
        ]
        + Experts.scratch()
        + [DMA((2,)), DMA((2,)), DMA, DMA((2, 2))]
        + spaces + sems + Direct.scratch(3),
        compiler_params=pltpu.CompilerParams(collective_id=1, has_side_effects=True, vmem_limit_bytes=63 * 2**20),
    )(picks, ids, shares, tokens, cots, wf, wo)


WORK = (
    ("gl", (TOK, TOK), F32),
    ("gm", (TOK, D), F32),
    ("gain2", (TOK, D), F32),
    ("branch", (TOK, D), BF16),
    ("ga", (TOK, D), BF16),
    ("gjf", (TOK, Q_WIDTH + 2 * K_WIDTH), F32),
    ("gj", (TOK, Q_WIDTH + 2 * K_WIDTH), BF16),
    ("gn", (TOK, D), F32),
    ("gates", (64, TOK), F32),
)


def last_kernel(*refs):
    (x, cot, gin, gates, cos, sin), results, (qkv_full, out_full, out_part, dwf, dwo), outs, work, weights, (small_src, load_sem), refs = cut_up(
        refs, 6, 9, 5, 6, len(WORK), 2, 2
    )
    input_grad, layer_output, qkv_grad, out_grad, small_grad, grad_gu = outs
    spaces1, sems1, spaces2, sems2, direct_sems, _ = cut_up(refs, 5, 9, 12, 9, 3)
    greet_all()
    p = Place()
    r = Results()
    for name, ref in zip(ATT_NAMES + tuple(w[0] for w in WORK), tuple(results) + tuple(work)):
        setattr(r, name, ref)
    r.input_grad = input_grad
    r.combined = r.gn
    qkv_ref, out_ref = weights
    s1 = Scatter(p, ROW_HALVES, [out_part], [r.combined], spaces1, sems1)
    s2 = Scatter(p, DENSE_PARTS, [qkv_ref, out_ref, small_src], [qkv_grad, out_grad, small_grad], spaces2, sems2, in_place=True)
    direct = Direct(gate_up_back, (dwf, dwo, grad_gu), direct_sems)
    s1.begin_all()
    loads = [pltpu.make_async_copy(a, b, load_sem.at[i]) for i, (a, b) in enumerate(((out_full, out_ref), (qkv_full, qkv_ref)))]
    for l in loads:
        l.start()
    direct.own()
    direct.start(12)

    def put_qkv(t, value):
        qkv_ref[t * 256 : t * 256 + 256, :] = value

    def put_out(t, value):
        out_ref[t * 256 : t * 256 + 256, :] = value

    def put_small(value):
        small_src[...] = value

    begin, heads, end = attention_backward(x, cot, gin, gates, cos, sin, qkv_ref, out_ref, r, put_qkv, put_out, put_small)
    for l in loads:
        l.wait()
    for i, chunk in enumerate(begin + heads + end):
        chunk()
        if i % 3 == 2:
            s1.step()
            direct.start(2)
    s2.begin_all()
    s1.step(12)
    s2.step(3)
    direct.start(DEVICES)
    layer_output[...] = (r.middle[...] + r.combined[...]).astype(BF16)
    s2.step(12)
    direct.start(DEVICES)
    s1.finish()
    s2.finish()
    direct.finish()


def last(x, cot, gin, gates, cos, sin, results, qkv_full, out_full, out_part, dwf, dwo):
    small = like(D, TOK)
    spaces1, sems1 = Scatter.scratch([out_part], ROW_HALVES)
    spaces2, sems2 = Scatter.scratch([qkv_full, out_full, small], DENSE_PARTS, in_place=True)
    own = D // DEVICES
    return pl.pallas_call(
        last_kernel,
        in_specs=[VMEM] * 15 + [HBM] * 5,
        out_specs=[VMEM] * 5 + [HBM],
        out_shape=[
            like(TOK, D), like(TOK, D), like(own, qkv_full.shape[1], dtype=F32), like(own, D, dtype=F32),
            like(own, TOK, dtype=F32), like(E, own, 2 * F),
        ],
        scratch_shapes=[pltpu.VMEM(s, t) for _, s, t in WORK]
        + [pltpu.VMEM(qkv_full.shape, BF16), pltpu.VMEM(out_full.shape, BF16), pltpu.VMEM(small.shape, BF16), DMA((2,))]
        + spaces1 + sems1 + spaces2 + sems2
        + Direct.scratch(3),
        compiler_params=pltpu.CompilerParams(collective_id=2, has_side_effects=True, vmem_limit_bytes=63 * 2**20),
    )(x, cot, gin, gates, cos, sin, *results, qkv_full, out_full, out_part, dwf, dwo)


def finish_kernel(gu_ref, down_ref, small_ref, *refs):
    whole, (gu_out, down_out, router_out, gain1_out, gain2_out), copies = refs[:4], refs[4:9], refs[9:]
    i = pl.program_id(0)

    @pl.when(i == 0)
    def _():
        for a, b in zip(whole, copies):
            b[...] = a[...]
        small = small_ref[...]
        rows = small.shape[0]
        turned = jnp.concatenate([small, jnp.zeros((TOK - rows, TOK), F32)], axis=0).T
        router_out[...] = turned[:E, :rows]
        gain1_out[...] = turned[E : E + 1, :rows]
        gain2_out[...] = turned[E + 1 : E + 2, :rows]

    @pl.when(i < 4)
    def _():
        gu_out[...] = jnp.swapaxes(gu_ref[...].astype(F32), 0, 1)

    @pl.when(i >= 4)
    def _():
        down_out[...] = jnp.swapaxes(down_ref[...].astype(F32), 0, 1)


def finish(gu, down, small, arrays):
    e, rows, _ = gu.shape
    early = lambda i: (0, 0, jnp.minimum(i, 3))
    late = lambda i: (0, 0, jnp.maximum(i - 4, 0))
    once = lambda a: pl.BlockSpec(a.shape, lambda i: (0, 0), pipeline_mode=pl.Buffered(1))
    outs = [like(E, rows, dtype=F32), like(1, rows, dtype=F32), like(1, rows, dtype=F32)] + [like(*a.shape, dtype=a.dtype) for a in arrays]
    return pl.pallas_call(
        finish_kernel,
        grid=(6,),
        in_specs=[pl.BlockSpec((e, rows, 256), early), pl.BlockSpec((e, rows, 256), late), once(small)] + [once(a) for a in arrays],
        out_specs=[pl.BlockSpec((rows, e, 256), early), pl.BlockSpec((rows, e, 256), late)] + [once(o) for o in outs],
        out_shape=[like(rows, e, gu.shape[2], dtype=F32), like(rows, e, down.shape[2], dtype=F32)] + outs,
        compiler_params=pltpu.CompilerParams(vmem_limit_bytes=63 * 2**20),
    )(gu, down, small, *arrays)


def fast(
    layer_input, cotangent, sequence_ids, expert_ids, attention_gain, qkv_weight, output_weight, moe_gain, router, gate_up, down_proj
):
    own_rows, T = gate_up.shape[0], layer_input.shape[0]
    small = jnp.concatenate(
        [router, attention_gain[:, None], moe_gain[:, None], jnp.zeros((own_rows, 86), BF16)], axis=1
    )
    ids_t = expert_ids.T
    qkv_full, out_full, small_full, ids_all, cots, tokens, shares, wf, wo, picks, *results, cos, sin = first(
        layer_input, sequence_ids.astype(F32).reshape(1, T), ids_t, [qkv_weight, output_weight, small, ids_t], cotangent,
        gate_up, down_proj,
    )

    gin, out_part, dwf, dwo, gates, grad_down = middle(picks, ids_all, shares, tokens, cots, wf, wo)
    input_grad, layer_output, qkv_grad, out_grad, small_grad, grad_gu = last(
        layer_input, cotangent, gin, gates, cos, sin, results, qkv_full, out_full, out_part, dwf, dwo
    )
    gate_up_grad, down_grad, router_grad, gain_one, gain_two, layer_output, input_grad, qkv_grad, out_grad = finish(
        grad_gu, grad_down, small_grad, (layer_output, input_grad, qkv_grad, out_grad)
    )
    return (
        layer_output,
        input_grad,
        gain_one.reshape(own_rows),
        qkv_grad,
        out_grad,
        gain_two.reshape(own_rows),
        router_grad.T,
        gate_up_grad,
        down_grad,
    )


def solution(mesh):
    rows, flat, cube = P("fsdp", None), P("fsdp"), P("fsdp", None, None)
    return jax.shard_map(
        fast if mesh.shape["fsdp"] == 32 else on_device,
        mesh=mesh,
        in_specs=(rows, rows, flat, rows, flat, rows, rows, flat, rows, cube, cube),
        out_specs=(rows, rows, flat, rows, rows, flat, rows, cube, cube),
        check_vma=False,
    )
```
